32 devices in a mesh: dp: 8 (over y, x, core), context: 4 (over z).
Axes of the slice: x: 2, y: 2, z: 4, core: 2. Of those that a mesh axis runs over, the one named last changes fastest.
Arguments:
- span_order: int32 [8, 4], P('dp'), may hold values from 0 to 3, each once within a row
- queries: bfloat16 [12288, 1024], P(('dp', 'context')), may hold values from -9 to 9
- keys: bfloat16 [12288, 128], P(('dp', 'context')), may hold values from -6 to 6
- values: bfloat16 [12288, 128], P(('dp', 'context')), may hold values from -6 to 6
- out_grad: bfloat16 [12288, 1024], P(('dp', 'context')), may hold values from -6 to 6
- activations: bfloat16 [12288, 8192], P(('dp', 'context')), may hold values from -6 to 6
- error_feedback: float32 [8, 4, 8192, 256], P('dp', 'context')
Outputs:
- query_grad: bfloat16 [12288, 1024], P(('dp', 'context'))
- key_grad: bfloat16 [12288, 128], P(('dp', 'context'))
- value_grad: bfloat16 [12288, 128], P(('dp', 'context'))
- payload: float32 [8192, 256], P(('dp', 'context'))
- block_scale: float32 [256], replicated
The draws below stay inside these ranges and needn't reach their ends.
Inputs may be any that keep to these rules, and one draw needn't show every extreme that they name: `span_order`: each row is a permutation: the indices of context hold the blocks of a sequence in the order that the row gives.
All inputs are finite; a program needn't handle non-finite values.
Results may differ from the reference program's by a relative error of at most 0.0061.
Values may be sent and summed in bfloat16 or wider, within the bound.
No kernel may reach another device: no remote copies, remote signals or barrier semaphores. Data moves between devices by JAX's collectives and lax.ppermute only.
A program may use at most 128 MiB of HBM per device.

```python
import jax
import jax.numpy as jnp
from jax import lax

D = 8192
HD = 128
HQ = 8
TOK_DEV = 384
QROWS = 32
SEQ = 1536
TOKENS = 12288
BLOCKS = 256
N_DP = 8
N_CONTEXT = 4


def paired_rows(key, spike):
    active = jnp.minimum(spike, 1.0)
    sign_pattern = jnp.where(jax.random.bernoulli(jax.random.fold_in(key, 101), 0.5, (TOKENS, HD)), 1.0, -1.0)
    row_index = jnp.arange(TOKENS, dtype=jnp.int32)
    offset_rows = row_index % TOK_DEV
    lead_rows = (offset_rows % 64 == 1).astype(jnp.float32)[:, None] * active
    follow_rows = ((offset_rows % 64 == 0) & (offset_rows + 1 < TOK_DEV)).astype(jnp.float32)[:, None] * active
    lead_keys = spike * sign_pattern
    return (lead_rows, follow_rows, lead_keys, row_index)


def draw_keys(key, part):
    lead_rows, follow_rows, lead_keys, row_index = paired_rows(key, 0.0)
    key = jax.random.fold_in(key, 7)
    base_draw = jnp.clip(jax.random.normal(key, (TOKENS, HD), jnp.float32), -6.0, 6.0)
    mixed = base_draw * (1.0 - lead_rows - follow_rows)
    return mixed.astype(jnp.bfloat16)


def draw_queries(key, part):
    lead_rows, follow_rows, lead_keys, row_index = paired_rows(key, 0.0)
    key = jax.random.fold_in(key, 13)
    strength_table = jnp.array([1.25, 2.0, 3.0], jnp.float32)
    strength = strength_table[row_index // 64 % 3][:, None]
    aligned = jnp.tile(strength * lead_keys, (1, HQ))
    base_draw = jnp.clip(jax.random.normal(key, (TOKENS, HQ * HD), jnp.float32), -6.0, 6.0)
    mixed = base_draw * (1.0 - lead_rows) + lead_rows * aligned
    return mixed.astype(jnp.bfloat16)


def draw_error_feedback(key, part):
    key = jax.random.fold_in(key, 23)
    device_rank = (jnp.arange(N_DP, dtype=jnp.float32)[:, None] * N_CONTEXT + jnp.arange(N_CONTEXT, dtype=jnp.float32)[None, :]) / (N_DP * N_CONTEXT - 1)
    rise_factor = (3.0 ** device_rank)[:, :, None, None]
    row_scale = jnp.exp(jax.random.uniform(jax.random.fold_in(key, 1), (D, 1), jnp.float32, 0.0, 2.302585))
    shape_full = (N_DP, N_CONTEXT, D, 2 * HD)
    noise_draw = jax.random.normal(jax.random.fold_in(key, 2), shape_full, jnp.float32)
    return 1.5 * rise_factor * row_scale[None, None, :, :] * noise_draw


def levels(key, extent, pieces, least, high):
    def one(position, blocks):
        draws = jax.random.uniform(jax.random.fold_in(jax.random.fold_in(key, 6), position), (blocks,), jnp.float32, least / len(pieces), high / len(pieces))
        return jnp.repeat(jnp.exp(draws), extent[position] // blocks).reshape((-1,) + (1,) * (len(extent) - position - 1))

    gain = one(*pieces[0])
    for cut in pieces[1:]:
        gain = gain * one(*cut)
    return gain


def gaussian(stream_key, shape, scale, reach, shards=(), kind=jnp.bfloat16):
    drawn = jax.random.normal(stream_key, shape, jnp.float32) * scale
    if len(shards) > 0:
        drawn = levels(stream_key, shape, shards, -0.22, 0.18) * drawn
    return jnp.clip(drawn, min=-reach, max=reach).astype(kind)


def setup_inputs(seed: int = 0) -> dict:
    seeds = jax.random.split(jax.random.key(seed), 8)
    return {
        "span_order": jax.vmap(lambda own: jax.random.permutation(own, N_CONTEXT))(jax.random.split(seeds[0], N_DP)).reshape((N_DP, N_CONTEXT)).astype(jnp.int32),
        "queries": draw_queries(jax.random.fold_in(seeds[7], 71), 0),
        "keys": draw_keys(jax.random.fold_in(seeds[7], 71), 0),
        "values": gaussian(seeds[3], (TOKENS, HD), 1.0, 6.0, ((0, 32),)),
        "out_grad": gaussian(seeds[4], (TOKENS, HQ * HD), 1.0, 6.0, ((0, 32),)),
        "activations": gaussian(seeds[5], (TOKENS, D), 1.0, 6.0, ((0, 32),)),
        "error_feedback": draw_error_feedback(jax.random.fold_in(seeds[7], 71), 0),
    }


def head_backward(query_head, all_keys, all_values, grad_head, query_positions, key_positions):
    inverse = 1.0 / (query_head.shape[1] ** 0.5)
    scores = jnp.dot(query_head, all_keys.T, preferred_element_type=jnp.float32) * inverse
    allowed = key_positions[None, :] <= query_positions[:, None]
    scores = jnp.where(allowed, scores, -jnp.inf)
    row_top = jnp.max(scores, axis=1, keepdims=True)
    expo_terms = jnp.exp(scores - row_top)
    probs = expo_terms / jnp.sum(expo_terms, axis=1, keepdims=True)
    prob_grad = jnp.dot(grad_head, all_values.T, preferred_element_type=jnp.float32)
    row_delta = jnp.sum(probs * prob_grad, axis=1, keepdims=True)
    score_grad = (probs * (prob_grad - row_delta)).astype(jnp.bfloat16)
    probs_low = probs.astype(jnp.bfloat16)
    query_part = jnp.dot(score_grad, all_keys, preferred_element_type=jnp.float32) * inverse
    key_part = jnp.dot(score_grad.T, query_head, preferred_element_type=jnp.float32) * inverse
    value_part = jnp.dot(probs_low.T, grad_head, preferred_element_type=jnp.float32)
    return query_part, key_part, value_part


def reference(span_order, queries, keys, values, out_grad, activations, error_feedback):
    offsets = jnp.arange(TOK_DEV, dtype=jnp.int32)

    def one_sequence(inputs):
        order_row, query_seq, key_seq, value_seq, grad_seq = inputs
        positions = (order_row[:, None] * TOK_DEV + offsets[None, :]).reshape(SEQ)

        def one_head(totals, head_index):
            column_start = (head_index * HD).astype(jnp.int32)
            query_head = lax.dynamic_slice_in_dim(query_seq, column_start, HD, 1)
            grad_head = lax.dynamic_slice_in_dim(grad_seq, column_start, HD, 1)
            query_part, key_part, value_part = head_backward(query_head, key_seq, value_seq, grad_head, positions, positions)
            return (totals[0] + key_part, totals[1] + value_part), query_part

        zero_rows = jnp.zeros((SEQ, HD), jnp.float32)
        (key_total, value_total), query_parts = lax.scan(one_head, (zero_rows, zero_rows), jnp.arange(HQ, dtype=jnp.int32))
        query_total = jnp.transpose(query_parts, (1, 0, 2)).reshape(SEQ, HQ * HD)
        return query_total.astype(jnp.bfloat16), key_total.astype(jnp.bfloat16), value_total.astype(jnp.bfloat16)

    query_grad, key_grad, value_grad = lax.map(one_sequence, (
        span_order,
        queries.reshape(N_DP, SEQ, HQ * HD),
        keys.reshape(N_DP, SEQ, HD),
        values.reshape(N_DP, SEQ, HD),
        out_grad.reshape(N_DP, SEQ, HQ * HD)))
    query_grad = query_grad.reshape(TOKENS, HQ * HD)
    key_grad = key_grad.reshape(TOKENS, HD)
    value_grad = value_grad.reshape(TOKENS, HD)

    device_count = N_DP * N_CONTEXT
    pair_grads = jnp.concatenate([key_grad, value_grad], axis=1).reshape(device_count, TOK_DEV, 2 * HD)
    device_acts = activations.reshape(device_count, TOK_DEV, D)
    device_errors = error_feedback.reshape(device_count, D, 2 * HD)

    def corrected_of(acts_block, grads_block, error_block):
        return jnp.dot(acts_block.T, grads_block, preferred_element_type=jnp.float32) + error_block

    def max_step(running, device_item):
        corrected = corrected_of(*device_item)
        block_top = jnp.max(jnp.abs(corrected).reshape(BLOCKS, QROWS * 2 * HD), axis=1)
        return jnp.maximum(running, block_top), None

    block_max, _ = lax.scan(max_step, jnp.zeros((BLOCKS,), jnp.float32), (device_acts, pair_grads, device_errors))
    block_scale = block_max + 1e-6
    row_factor = jnp.repeat(7.0 / block_scale, QROWS)

    def sum_step(running, device_item):
        corrected = corrected_of(*device_item)
        normalized = lax.optimization_barrier((corrected * row_factor[:, None]).astype(jnp.bfloat16))
        return running + normalized.astype(jnp.float32), None

    payload, _ = lax.scan(sum_step, jnp.zeros((D, 2 * HD), jnp.float32), (device_acts, pair_grads, device_errors))
    return query_grad, key_grad, value_grad, payload, block_scale
```

```python
import functools

import jax
import jax.numpy as jnp
from jax import lax
from jax.experimental import pallas as pl
from jax.experimental.pallas import tpu as pltpu
from jax.sharding import PartitionSpec as P

QROWS = 32
LOG2E = 1.4426950408889634
FAR = 1e30
MIB = 1024 * 1024


def xor_perm(size, mask):
    return [(i, i ^ mask) for i in range(size)]


def attention_kernel(n_blocks, keep_ref, q_ref, do_ref, *refs):
    k_refs, v_refs = refs[:n_blocks], refs[n_blocks : 2 * n_blocks]
    dq_ref, own_ref, other_ref, k_all, v_all, q_cat, do_cat, p_buf, ds_buf, dk_acc, dv_acc = refs[2 * n_blocks :]
    rows, hd = k_refs[0].shape
    inverse = 1.0 / hd**0.5
    factor = inverse * LOG2E
    step = pl.program_id(0)
    width = 256
    f32 = jnp.float32

    @pl.when(step == 0)
    def _():
        for b in range(n_blocks):
            k_all[b * rows : (b + 1) * rows, :] = k_refs[b][...]
            v_all[b * rows : (b + 1) * rows, :] = v_refs[b][...]
        dk_acc[...] = jnp.zeros_like(dk_acc)
        dv_acc[...] = jnp.zeros_like(dv_acc)

    for h in range(2):
        q_cat[h * rows : (h + 1) * rows, :] = q_ref[:, h * hd : (h + 1) * hd]
        do_cat[h * rows : (h + 1) * rows, :] = do_ref[:, h * hd : (h + 1) * hd]

    for t in range(2 * rows // width):
        lanes = slice(t * width, (t + 1) * width)
        qc, dc = q_cat[lanes, :], do_cat[lanes, :]
        nt = (((1,), (1,)), ((), ()))
        s = [
            lax.dot_general(k_all[b * rows : (b + 1) * rows, :], qc, nt, preferred_element_type=f32)
            for b in range(n_blocks)
        ]
        dp = [
            lax.dot_general(v_all[b * rows : (b + 1) * rows, :], dc, nt, preferred_element_type=f32)
            for b in range(n_blocks)
        ]
        key_at = lax.broadcasted_iota(jnp.int32, (rows, width), 0)
        query_at = lax.broadcasted_iota(jnp.int32, (rows, width), 1) + t * width
        query_at = jnp.where(query_at >= rows, query_at - rows, query_at)
        s[0] = jnp.where(key_at <= query_at, s[0], -FAR)
        top = jnp.max(s[0], axis=0, keepdims=True)
        for b in range(1, n_blocks):
            block_top = jnp.max(s[b], axis=0, keepdims=True)
            top = jnp.maximum(top, jnp.where(keep_ref[b] > 0, block_top, -FAR))
        top = top * factor
        e, total, weighted = [], 0.0, 0.0
        for b in range(n_blocks):
            shift = top if b == 0 else jnp.where(keep_ref[b] > 0, top, FAR)
            e_b = jnp.exp2(s[b] * factor - shift)
            total = total + jnp.sum(e_b, axis=0, keepdims=True)
            weighted = weighted + jnp.sum(e_b * dp[b], axis=0, keepdims=True)
            e.append(e_b)
        inv = 1.0 / total
        delta = weighted * inv
        for b in range(n_blocks):
            p = e[b] * inv
            p_buf[b * rows : (b + 1) * rows, lanes] = p.astype(jnp.bfloat16)
            ds_buf[b * rows : (b + 1) * rows, lanes] = (p * (dp[b] - delta)).astype(jnp.bfloat16)

    dk_acc[...] += jnp.dot(ds_buf[...], q_cat[...], preferred_element_type=f32)
    dv_acc[...] += jnp.dot(p_buf[...], do_cat[...], preferred_element_type=f32)
    dq = lax.dot_general(ds_buf[...], k_all[...], (((0,), (0,)), ((), ())), preferred_element_type=f32) * inverse
    for h in range(2):
        dq_ref[:, h * hd : (h + 1) * hd] = dq[h * rows : (h + 1) * rows, :].astype(jnp.bfloat16)

    @pl.when(step == pl.num_programs(0) - 1)
    def _():
        own_ref[:, :hd] = dk_acc[:rows, :] * inverse
        own_ref[:, hd:] = dv_acc[:rows, :]
        for b in range(1, n_blocks):
            part = slice(b * rows, (b + 1) * rows)
            other_ref[b - 1, :, :hd] = (dk_acc[part, :] * inverse).astype(jnp.bfloat16)
            other_ref[b - 1, :, hd:] = dv_acc[part, :].astype(jnp.bfloat16)


def attention(keep, queries, out_grad, k_blocks, v_blocks):
    n = len(k_blocks)
    rows, hd = k_blocks[0].shape
    heads = queries.shape[1] // hd
    whole = pl.BlockSpec((rows, hd), lambda i, *_: (0, 0))
    pair = pl.BlockSpec((rows, 2 * hd), lambda i, *_: (0, i))
    bf16, f32 = jnp.bfloat16, jnp.float32
    return pl.pallas_call(
        functools.partial(attention_kernel, n),
        grid_spec=pltpu.PrefetchScalarGridSpec(
            num_scalar_prefetch=1,
            grid=(heads // 2,),
            in_specs=[pair, pair] + [whole] * (2 * n),
            out_specs=[
                pair,
                pl.BlockSpec((rows, 2 * hd), lambda i, *_: (0, 0)),
                pl.BlockSpec((n - 1, rows, 2 * hd), lambda i, *_: (0, 0, 0)),
            ],
            scratch_shapes=[
                pltpu.VMEM((n * rows, hd), bf16),
                pltpu.VMEM((n * rows, hd), bf16),
                pltpu.VMEM((2 * rows, hd), bf16),
                pltpu.VMEM((2 * rows, hd), bf16),
                pltpu.VMEM((n * rows, 2 * rows), bf16),
                pltpu.VMEM((n * rows, 2 * rows), bf16),
                pltpu.VMEM((n * rows, hd), f32),
                pltpu.VMEM((n * rows, hd), f32),
            ],
        ),
        out_shape=[
            jax.ShapeDtypeStruct(queries.shape, bf16),
            jax.ShapeDtypeStruct((rows, 2 * hd), f32),
            jax.ShapeDtypeStruct((n - 1, rows, 2 * hd), bf16),
        ],
        compiler_params=pltpu.CompilerParams(vmem_limit_bytes=48 * MIB),
        cost_estimate=pl.CostEstimate(
            flops=10 * rows * n * rows * hd * heads, bytes_accessed=6 * rows * heads * hd, transcendentals=n * rows * rows * heads
        ),
        name="attention_backward",
    )(keep, queries, out_grad, *k_blocks, *v_blocks)


def corrected_kernel(n_parts, shrink, with_grads, side_ref, *refs):
    own_ref, part_refs = refs[0], refs[1 : n_parts + 1]
    a_ref, e_ref, *outs = refs[n_parts + 1 :]
    if with_grads:
        low_ref, high_ref, top_ref, kg_ref, vg_ref, grads = outs
    else:
        low_ref, high_ref, top_ref, grads = outs
    hd = low_ref.shape[-1]

    @pl.when(pl.program_id(0) == 0)
    def _():
        total = own_ref[...]
        for part in part_refs:
            total = total + part[...].astype(jnp.float32)
        total = total.astype(jnp.bfloat16)
        grads[...] = total
        if with_grads:
            kg_ref[...] = total[:, :hd]
            vg_ref[...] = total[:, hd:]

    c = lax.dot_general(a_ref[...], grads[...], (((0,), (0,)), ((), ())), preferred_element_type=jnp.float32)
    c = c + e_ref[...]
    tile = c.shape[0]
    mags = jnp.max(jnp.abs(c).reshape(tile // QROWS, QROWS, c.shape[1]), axis=1)
    top_ref[0] = jnp.max(mags.T, axis=0, keepdims=True)
    low = (c * shrink).astype(jnp.bfloat16)
    low_ref[0] = low[:, :hd]
    high_ref[0] = low[:, hd:]


def corrected_tiles(side, own, parts, activations, errors, n_dp, shrink, with_grads):
    rows, width = own.shape
    model = activations.shape[1]
    tile = model // n_dp
    hd = width // 2
    whole = pl.BlockSpec((rows, width), lambda i, side: (0, 0))
    half = pl.BlockSpec((1, tile, hd), lambda i, side: (i, 0, 0))
    bf16, f32 = jnp.bfloat16, jnp.float32
    out_specs = [half, half, pl.BlockSpec((1, 1, tile // QROWS), lambda i, side: (i, 0, 0))]
    out_shape = [
        jax.ShapeDtypeStruct((n_dp // 2, tile, hd), bf16),
        jax.ShapeDtypeStruct((n_dp // 2, tile, hd), bf16),
        jax.ShapeDtypeStruct((n_dp // 2, 1, tile // QROWS), f32),
    ]
    if with_grads:
        out_specs += [pl.BlockSpec((rows, hd), lambda i, side: (0, 0))] * 2
        out_shape += [jax.ShapeDtypeStruct((rows, hd), bf16)] * 2
    return pl.pallas_call(
        functools.partial(corrected_kernel, len(parts), shrink, with_grads),
        grid_spec=pltpu.PrefetchScalarGridSpec(
            num_scalar_prefetch=1,
            grid=(n_dp // 2,),
            in_specs=[whole] * (1 + len(parts))
            + [
                pl.BlockSpec((rows, tile), lambda i, side: (0, 2 * i + side[0])),
                pl.BlockSpec((tile, width), lambda i, side: (2 * i + side[0], 0)),
            ],
            out_specs=out_specs,
            scratch_shapes=[pltpu.VMEM((rows, width), bf16)],
        ),
        out_shape=out_shape,
        compiler_params=pltpu.CompilerParams(vmem_limit_bytes=48 * MIB),
        cost_estimate=pl.CostEstimate(
            flops=rows * width * model, bytes_accessed=rows * model + 3 * width * model, transcendentals=0
        ),
        name="corrected_tiles",
    )(side, own, *parts, activations, errors)


def add_low(a, b):
    return (a.astype(jnp.float32) + b.astype(jnp.float32)).astype(jnp.bfloat16)


def local(n_dp, n_ctx, span_order, queries, keys, values, out_grad, activations, error_feedback):
    hd = keys.shape[1]
    me_dp, me_ctx = lax.axis_index("dp"), lax.axis_index("context")
    dp_bits = n_dp.bit_length() - 1

    def swap_dp(x, bit):
        return lax.ppermute(x, "dp", xor_perm(n_dp, 1 << bit))

    def swap_ctx(x, mask):
        return lax.ppermute(x, "context", xor_perm(n_ctx, mask))

    k_blocks = [keys] + [swap_ctx(keys, b) for b in range(1, n_ctx)]
    v_blocks = [values] + [swap_ctx(values, b) for b in range(1, n_ctx)]
    spans = span_order[0]
    block_spans = spans[me_ctx ^ jnp.arange(n_ctx, dtype=jnp.int32)]
    keep = (block_spans < block_spans[0]).astype(jnp.int32)
    query_grad, own, others = attention(keep, queries, out_grad, k_blocks, v_blocks)

    parts = [swap_ctx(others[b - 1], b) for b in range(1, n_ctx)]
    shrink = 1.0 / (n_dp * n_ctx)
    errors = error_feedback[0, 0]
    side = (me_dp & 1).astype(jnp.int32)
    send_low, send_high, send_top, key_grad, value_grad = corrected_tiles(
        (1 - side)[None], own, parts, activations, errors, n_dp, shrink, True
    )
    got = (swap_dp(send_low, 0), swap_dp(send_high, 0))
    keep_low, keep_high, keep_top = corrected_tiles(
        side[None], own, parts, activations, errors, n_dp, shrink, False
    )

    send_top, keep_top = send_top[:, 0], keep_top[:, 0]
    first = jnp.where(side == 0, keep_top, send_top)
    second = jnp.where(side == 0, send_top, keep_top)
    tops = jnp.stack([first, second], axis=1).reshape(-1)
    for bit in range(dp_bits):
        tops = jnp.maximum(tops, swap_dp(tops, bit))
    mask = 1
    while mask < n_ctx:
        tops = jnp.maximum(tops, swap_ctx(tops, mask))
        mask *= 2
    block_scale = tops + 1e-06

    results = []
    for half, (kept, received) in enumerate(zip((keep_low, keep_high), got)):
        current = add_low(kept, received)
        bits = list(range(1, dp_bits))
        current = current.reshape((2,) * len(bits) + current.shape[1:])
        order = bits if half == 0 else bits[::-1]
        left = bits[::-1]
        for bit in order:
            axis = left.index(bit)
            mine = (me_dp >> bit) & 1
            away = lax.dynamic_index_in_dim(current, 1 - mine, axis, keepdims=False)
            stay = lax.dynamic_index_in_dim(current, mine, axis, keepdims=False)
            current = add_low(stay, swap_dp(away, bit))
            left.remove(bit)
        chunks = current.reshape(n_ctx, -1, hd)
        total = lax.dynamic_index_in_dim(chunks, me_ctx, 0, keepdims=False).astype(jnp.float32)
        for b in range(1, n_ctx):
            away = lax.dynamic_index_in_dim(chunks, me_ctx ^ b, 0, keepdims=False)
            total = total + swap_ctx(away, b).astype(jnp.float32)
        results.append(total)
    own_blocks = block_scale.shape[0] // (n_dp * n_ctx)
    own_scale = lax.dynamic_slice_in_dim(block_scale, (me_dp * n_ctx + me_ctx) * own_blocks, own_blocks)
    row_factor = jnp.repeat((7.0 / shrink) / own_scale, QROWS)
    payload = jnp.concatenate(results, axis=1) * row_factor[:, None]
    return (query_grad, key_grad, value_grad, payload, block_scale)


def solution(mesh):
    tokens = P(("dp", "context"), None)
    return jax.shard_map(
        functools.partial(local, mesh.shape["dp"], mesh.shape["context"]),
        mesh=mesh,
        in_specs=(P("dp", None), tokens, tokens, tokens, tokens, tokens, P("dp", "context", None, None)),
        out_specs=(tokens, tokens, tokens, tokens, P()),
        check_vma=False,
    )
```

```python
import functools

import jax
import jax.numpy as jnp
from jax import lax
from jax.experimental import pallas as pl
from jax.experimental.pallas import tpu as pltpu
from jax.sharding import PartitionSpec as P

QROWS = 32
LOG2E = 1.4426950408889634
FAR = 1e30
MIB = 1024 * 1024
BF16, F32 = jnp.bfloat16, jnp.float32


def xor_perm(size, mask):
    return [(i, i ^ mask) for i in range(size)]


def whole(shape):
    return pl.BlockSpec(shape, lambda *_: (0,) * len(shape))


def params(mib):
    return pltpu.CompilerParams(vmem_limit_bytes=mib * MIB)


def prepare_kernel(q_ref, do_ref, a_ref, q_out, do_out, a_out):
    q_out[...] = q_ref[...]
    do_out[...] = do_ref[...]
    a_out[...] = a_ref[...].T


def prepare(queries, out_grad, activations, hd):
    rows, columns = queries.shape
    heads = columns // hd
    model = activations.shape[1]
    tile = model // heads
    head = pl.BlockSpec((rows, hd), lambda i: (0, i))
    stacked = pl.BlockSpec((rows, hd), lambda i: (i, 0))
    return pl.pallas_call(
        prepare_kernel,
        grid=(heads,),
        in_specs=[head, head, pl.BlockSpec((rows, tile), lambda i: (0, i))],
        out_specs=[stacked, stacked, pl.BlockSpec((tile, rows), lambda i: (i, 0))],
        out_shape=[
            jax.ShapeDtypeStruct((heads * rows, hd), BF16),
            jax.ShapeDtypeStruct((heads * rows, hd), BF16),
            jax.ShapeDtypeStruct((model, rows), BF16),
        ],
        compiler_params=params(12),
        cost_estimate=pl.CostEstimate(flops=0, bytes_accessed=4 * rows * (model + 2 * columns), transcendentals=0),
        name="prepare",
    )(queries, out_grad, activations)


def attention_kernel(n_blocks, me_ref, span_ref, q_ref, do_ref, *refs):
    kv_refs = refs[:n_blocks]
    dq_ref, own_ref, *rest = refs[n_blocks:]
    other_refs = rest[: n_blocks - 1]
    k_all, v_all, p_buf, ds_buf, dk_acc, dv_acc = rest[n_blocks - 1 :]
    rows, hd = dk_acc.shape[0] // n_blocks, dk_acc.shape[1]
    inverse = 1.0 / hd**0.5
    factor = inverse * LOG2E
    step = pl.program_id(0)
    width = 256
    me = me_ref[0]
    keep = [None] + [span_ref[me ^ b] < span_ref[me] for b in range(1, n_blocks)]

    @pl.when(step == 0)
    def _():
        for b in range(n_blocks):
            k_all[b * rows : (b + 1) * rows, :] = kv_refs[b][:, :hd]
            v_all[b * rows : (b + 1) * rows, :] = kv_refs[b][:, hd:]
        dk_acc[...] = jnp.zeros_like(dk_acc)
        dv_acc[...] = jnp.zeros_like(dv_acc)

    for t in range(2 * rows // width):
        lanes = slice(t * width, (t + 1) * width)
        qc, dc = q_ref[lanes, :], do_ref[lanes, :]
        nt = (((1,), (1,)), ((), ()))
        s = [
            lax.dot_general(k_all[b * rows : (b + 1) * rows, :], qc, nt, preferred_element_type=F32)
            for b in range(n_blocks)
        ]
        dp = [
            lax.dot_general(v_all[b * rows : (b + 1) * rows, :], dc, nt, preferred_element_type=F32)
            for b in range(n_blocks)
        ]
        key_at = lax.broadcasted_iota(jnp.int32, (rows, width), 0)
        query_at = lax.broadcasted_iota(jnp.int32, (rows, width), 1) + t * width
        query_at = jnp.where(query_at >= rows, query_at - rows, query_at)
        s[0] = jnp.where(key_at <= query_at, s[0], -FAR)
        top = jnp.max(s[0], axis=0, keepdims=True)
        for b in range(1, n_blocks):
            block_top = jnp.max(s[b], axis=0, keepdims=True)
            top = jnp.maximum(top, jnp.where(keep[b], block_top, -FAR))
        top = top * factor
        e, total, weighted = [], 0.0, 0.0
        for b in range(n_blocks):
            shift = top if b == 0 else jnp.where(keep[b], top, FAR)
            e_b = jnp.exp2(s[b] * factor - shift)
            total = total + jnp.sum(e_b, axis=0, keepdims=True)
            weighted = weighted + jnp.sum(e_b * dp[b], axis=0, keepdims=True)
            e.append(e_b)
        inv = 1.0 / total
        delta = weighted * inv
        for b in range(n_blocks):
            p = e[b] * inv
            p_buf[b * rows : (b + 1) * rows, lanes] = p.astype(BF16)
            ds_buf[b * rows : (b + 1) * rows, lanes] = (p * (dp[b] - delta)).astype(BF16)

    dk_acc[...] += jnp.dot(ds_buf[...], q_ref[...], preferred_element_type=F32)
    dv_acc[...] += jnp.dot(p_buf[...], do_ref[...], preferred_element_type=F32)
    dq = lax.dot_general(ds_buf[...], k_all[...], (((0,), (0,)), ((), ())), preferred_element_type=F32) * inverse
    for h in range(2):
        dq_ref[:, h * hd : (h + 1) * hd] = dq[h * rows : (h + 1) * rows, :].astype(BF16)

    @pl.when(step == pl.num_programs(0) - 1)
    def _():
        own_ref[:, :hd] = dk_acc[:rows, :] * inverse
        own_ref[:, hd:] = dv_acc[:rows, :]
        for b in range(1, n_blocks):
            part = slice(b * rows, (b + 1) * rows)
            other_refs[b - 1][:, :hd] = (dk_acc[part, :] * inverse).astype(BF16)
            other_refs[b - 1][:, hd:] = dv_acc[part, :].astype(BF16)


def attention(me, spans, stacked_q, stacked_do, kv_blocks):
    n = len(kv_blocks)
    rows, hd = kv_blocks[0].shape[0], stacked_q.shape[1]
    heads = stacked_q.shape[0] // rows
    pair = pl.BlockSpec((2 * rows, hd), lambda i, *_: (i, 0))
    return pl.pallas_call(
        functools.partial(attention_kernel, n),
        grid_spec=pltpu.PrefetchScalarGridSpec(
            num_scalar_prefetch=2,
            grid=(heads // 2,),
            in_specs=[pair, pair] + [whole((rows, 2 * hd))] * n,
            out_specs=[pl.BlockSpec((rows, 2 * hd), lambda i, *_: (0, i))] + [whole((rows, 2 * hd))] * n,
            scratch_shapes=[
                pltpu.VMEM((n * rows, hd), BF16),
                pltpu.VMEM((n * rows, hd), BF16),
                pltpu.VMEM((n * rows, 2 * rows), BF16),
                pltpu.VMEM((n * rows, 2 * rows), BF16),
                pltpu.VMEM((n * rows, hd), F32),
                pltpu.VMEM((n * rows, hd), F32),
            ],
        ),
        out_shape=[jax.ShapeDtypeStruct((rows, heads * hd), BF16), jax.ShapeDtypeStruct((rows, 2 * hd), F32)]
        + [jax.ShapeDtypeStruct((rows, 2 * hd), BF16)] * (n - 1),
        compiler_params=params(36),
        cost_estimate=pl.CostEstimate(
            flops=10 * rows * n * rows * hd * heads,
            bytes_accessed=6 * rows * heads * hd,
            transcendentals=n * rows * rows * heads,
        ),
        name="attention_backward",
    )(me, spans, stacked_q, stacked_do, *kv_blocks)


def tile_of(step, me_dp, bits, flip):
    dest = me_dp ^ flip
    for j in range(1, bits):
        stays = (step >> (bits - 1 - j)) & 1
        dest = dest ^ ((1 - stays) << j)
    return dest


def reversed_step(step, bits):
    out = 0
    for j in range(1, bits):
        out = out + (((step >> (bits - 1 - j)) & 1) << (j - 1))
    return out


def corrected_tile(shrink, chosen, row, grads, a_ref, e_ref, top_ref):
    _, n_ctx, _, rows_set, rows = a_ref.shape
    tall = n_ctx * rows_set
    a = a_ref[0, :, 0].reshape(tall, rows)
    e = e_ref[0, :, 0].reshape(tall, e_ref.shape[4])
    c = jnp.dot(a, grads, preferred_element_type=F32) + e

    @pl.when(pl.program_id(0) == 0)
    def _():
        top_ref[...] = jnp.zeros_like(top_ref)

    mags = jnp.max(jnp.abs(c).reshape(tall // QROWS, QROWS, c.shape[1]), axis=1)
    mags = jnp.max(mags, axis=1, keepdims=True)
    per_set = rows_set // QROWS
    lanes = top_ref.shape[1]
    block = lax.broadcasted_iota(jnp.int32, (tall // QROWS, lanes), 0)
    lane = lax.broadcasted_iota(jnp.int32, (tall // QROWS, lanes), 1)
    shift = per_set.bit_length() - 1
    place = ((block >> shift) * (lanes // n_ctx)) + chosen * per_set + (block & (per_set - 1))
    top_ref[pl.ds(row, 1), :] = jnp.max(jnp.where(lane == place, mags, 0.0), axis=0, keepdims=True)
    return c * shrink


def send_kernel(n_parts, bits, shrink, chosen, with_grads, me_ref, own_ref, *refs):
    part_refs = refs[:n_parts]
    a_ref, e_ref, out_ref, top_ref, *grad_refs, grads = refs[n_parts:]
    step = pl.program_id(0)

    @pl.when(step == 0)
    def _():
        total = own_ref[...].astype(F32)
        for part in part_refs:
            total = total + part[...].astype(F32)
        total = total.astype(BF16)
        grads[...] = total
        if with_grads:
            hd = total.shape[1] // 2
            grad_refs[0][...] = total[:, :hd]
            grad_refs[1][...] = total[:, hd:]
            grad_refs[2][...] = total

    dest = tile_of(step, me_ref[0], bits, 1)
    out_ref[0] = corrected_tile(shrink, chosen, dest, grads[...], a_ref, e_ref, top_ref).astype(BF16)


def keep_kernel(bits, shrink, chosen, me_ref, grads, got_ref, a_ref, e_ref, low_away, low_stay, high_away, high_stay, top_ref):
    step = pl.program_id(0)
    half = low_away.shape[0]
    hd = low_away.shape[2]
    dest = tile_of(step, me_ref[0], bits, 0)
    c = corrected_tile(shrink, chosen, dest, grads[...], a_ref, e_ref, top_ref)
    c = (c + got_ref[0].astype(F32)).astype(BF16)
    back = reversed_step(step, bits)
    for at, part, away, stay in ((step, c[:, :hd], low_away, low_stay), (back, c[:, hd:], high_away, high_stay)):

        @pl.when(at < half)
        def _():
            away[at] = part

        @pl.when(at >= half)
        def _():
            stay[at - half] = part


def tile_specs(bits, flip, chosen, a, e):
    def block(x):
        _, n_ctx, _, rows_set, width = x.shape
        return pl.BlockSpec(
            (1, n_ctx, 1, rows_set, width), lambda i, me: (tile_of(i, me[0], bits, flip), 0, chosen, 0, 0)
        )

    return [block(a), block(e)]


def tile_cost(a, e):
    n_dp, n_ctx, sets, rows_set, rows = a.shape
    tall = n_dp // 2 * n_ctx * rows_set
    width = e.shape[4]
    return pl.CostEstimate(
        flops=2 * tall * rows * width, bytes_accessed=tall * (2 * rows + 6 * width), transcendentals=0
    )


def send_tiles(me, own, parts, a, e, chosen, shrink, with_grads):
    n_dp, n_ctx, sets, rows_set, rows = a.shape
    bits = n_dp.bit_length() - 1
    width = e.shape[4]
    tall = n_ctx * rows_set
    lanes = sets * tall // QROWS
    grad_shapes = [(rows, width // 2), (rows, width // 2), (rows, width)] if with_grads else []
    return pl.pallas_call(
        functools.partial(send_kernel, len(parts), bits, shrink, chosen, with_grads),
        grid_spec=pltpu.PrefetchScalarGridSpec(
            num_scalar_prefetch=1,
            grid=(n_dp // 2,),
            in_specs=[whole((rows, width))] * (1 + len(parts)) + tile_specs(bits, 1, chosen, a, e),
            out_specs=[pl.BlockSpec((1, tall, width), lambda i, me: (i, 0, 0)), whole((n_dp, lanes))]
            + [whole(s) for s in grad_shapes],
            scratch_shapes=[pltpu.VMEM((rows, width), BF16)],
        ),
        out_shape=[jax.ShapeDtypeStruct((n_dp // 2, tall, width), BF16), jax.ShapeDtypeStruct((n_dp, lanes), F32)]
        + [jax.ShapeDtypeStruct(s, BF16) for s in grad_shapes],
        compiler_params=params(16),
        cost_estimate=tile_cost(a, e),
        name="send_tiles",
    )(me, own, *parts, a, e)


def keep_tiles(me, grads, got, a, e, chosen, shrink):
    n_dp, n_ctx, sets, rows_set, rows = a.shape
    bits = n_dp.bit_length() - 1
    width = e.shape[4]
    tall = n_ctx * rows_set
    lanes = sets * tall // QROWS
    half = (n_dp // 4, tall, width // 2)
    return pl.pallas_call(
        functools.partial(keep_kernel, bits, shrink, chosen),
        grid_spec=pltpu.PrefetchScalarGridSpec(
            num_scalar_prefetch=1,
            grid=(n_dp // 2,),
            in_specs=[whole((rows, width)), pl.BlockSpec((1, tall, width), lambda i, me: (i, 0, 0))]
            + tile_specs(bits, 0, chosen, a, e),
            out_specs=[whole(half)] * 4 + [whole((n_dp, lanes))],
        ),
        out_shape=[jax.ShapeDtypeStruct(half, BF16)] * 4 + [jax.ShapeDtypeStruct((n_dp, lanes), F32)],
        compiler_params=params(16),
        cost_estimate=tile_cost(a, e),
        name="keep_tiles",
    )(me, grads, got, a, e)


def largest(tops, top_out):
    if tops:
        top = tops[0][...]
        for other in tops[1:]:
            top = jnp.maximum(top, other[...])
        top_out[0][...] = top


def add_kernel(n_tops, *refs):
    low, low_got, high, high_got = refs[:4]
    tops = refs[4 : 4 + n_tops]
    low_away, low_stay, high_away, high_stay, *top_out = refs[4 + n_tops :]
    half = low_away.shape[0]
    for mine, got, away, stay in ((low, low_got, low_away, low_stay), (high, high_got, high_away, high_stay)):
        away[...] = (mine[:half].astype(F32) + got[:half].astype(F32)).astype(BF16)
        stay[...] = (mine[half:].astype(F32) + got[half:].astype(F32)).astype(BF16)
    largest(tops, top_out)


def add_stage(low, low_got, high, high_got, tops):
    m, tall, hd = low.shape
    half = jax.ShapeDtypeStruct((m // 2, tall, hd), BF16)
    return pl.pallas_call(
        functools.partial(add_kernel, len(tops)),
        out_shape=[half] * 4 + [jax.ShapeDtypeStruct(top.shape, F32) for top in tops[:1]],
        compiler_params=params(16),
        cost_estimate=pl.CostEstimate(flops=2 * low.size, bytes_accessed=12 * low.size, transcendentals=0),
        name="add_stage",
    )(low, low_got, high, high_got, *tops)


def last_kernel(n_ctx, n_tops, me_ref, *refs):
    low, low_got, high, high_got = refs[:4]
    tops = refs[4 : 4 + n_tops]
    outs, top_out = refs[4 + n_tops : 4 + n_tops + n_ctx], refs[4 + n_tops + n_ctx :]
    hd = low.shape[2]
    rows_set = low.shape[1] // n_ctx
    for b in range(n_ctx):
        part = pl.ds(pl.multiple_of((me_ref[0] ^ b) * rows_set, rows_set), rows_set)
        for at, mine, got in ((0, low, low_got), (hd, high, high_got)):
            total = mine[0, part, :].astype(F32) + got[0, part, :].astype(F32)
            outs[b][:, at : at + hd] = total.astype(outs[b].dtype)
    largest(tops, top_out)


def last_stage(me_ctx, low, low_got, high, high_got, tops, n_ctx):
    _, tall, hd = low.shape
    shape = (tall // n_ctx, 2 * hd)
    return pl.pallas_call(
        functools.partial(last_kernel, n_ctx, len(tops)),
        grid_spec=pltpu.PrefetchScalarGridSpec(
            num_scalar_prefetch=1,
            grid=(1,),
            in_specs=[whole(low.shape)] * 4 + [whole(top.shape) for top in tops],
            out_specs=[whole(shape)] * n_ctx + [whole(top.shape) for top in tops[:1]],
        ),
        out_shape=[jax.ShapeDtypeStruct(shape, F32)]
        + [jax.ShapeDtypeStruct(shape, BF16)] * (n_ctx - 1)
        + [jax.ShapeDtypeStruct(top.shape, F32) for top in tops[:1]],
        compiler_params=params(16),
        cost_estimate=pl.CostEstimate(flops=2 * low.size, bytes_accessed=12 * low.size, transcendentals=0),
        name="last_stage",
    )(me_ctx, low, low_got, high, high_got, *tops)


def final_kernel(sets, n_ctx, gain, me_dp_ref, me_ctx_ref, *refs):
    groups = [refs[chosen * n_ctx : (chosen + 1) * n_ctx] for chosen in range(sets)]
    tops = refs[sets * n_ctx : sets * n_ctx + n_ctx]
    out_ref, scale_ref = refs[sets * n_ctx + n_ctx :]
    scale = tops[0][...]
    for other in tops[1:]:
        scale = jnp.maximum(scale, other[...])
    scale_ref[...] = scale + 1e-06
    factors = gain / scale_ref[pl.ds(me_dp_ref[0], 1), :]
    lane = lax.broadcasted_iota(jnp.int32, factors.shape, 1)
    rows_set = groups[0][0].shape[0]
    per_set = rows_set // QROWS
    first = me_ctx_ref[0] * (sets * per_set)
    for chosen, group in enumerate(groups):
        for r in range(per_set):
            part = slice(r * QROWS, (r + 1) * QROWS)
            total = group[0][part, :]
            for other in group[1:]:
                total = total + other[part, :].astype(F32)
            mine = jnp.where(lane == first + (chosen * per_set + r), factors, 0.0)
            at = chosen * rows_set + r * QROWS
            out_ref[at : at + QROWS, :] = total * jnp.sum(mine, axis=1, keepdims=True)


def final_stage(me_dp, me_ctx, groups, tops, gain):
    sets, n_ctx = len(groups), len(groups[0])
    rows_set, width = groups[0][0].shape
    return pl.pallas_call(
        functools.partial(final_kernel, sets, n_ctx, gain),
        grid_spec=pltpu.PrefetchScalarGridSpec(
            num_scalar_prefetch=2,
            grid=(1,),
            in_specs=[whole((rows_set, width))] * (sets * n_ctx) + [whole(tops[0].shape)] * n_ctx,
            out_specs=[whole((sets * rows_set, width)), whole(tops[0].shape)],
        ),
        out_shape=[
            jax.ShapeDtypeStruct((sets * rows_set, width), F32),
            jax.ShapeDtypeStruct(tops[0].shape, F32),
        ],
        compiler_params=params(8),
        cost_estimate=pl.CostEstimate(
            flops=4 * sets * rows_set * width, bytes_accessed=16 * sets * rows_set * width, transcendentals=0
        ),
        name="final_stage",
    )(me_dp, me_ctx, *[x for group in groups for x in group], *tops)


def local(n_dp, n_ctx, sets, span_order, queries, keys, values, out_grad, activations, error_feedback):
    rows, hd = keys.shape
    model = activations.shape[1]
    rows_set = model // (n_dp * n_ctx * sets)
    me_dp = lax.axis_index("dp").astype(jnp.int32)[None]
    me_ctx = lax.axis_index("context").astype(jnp.int32)[None]
    bits = n_dp.bit_length() - 1

    def swap_dp(x, mask):
        return lax.ppermute(x, "dp", xor_perm(n_dp, mask))

    def swap_ctx(x, mask):
        return lax.ppermute(x, "context", xor_perm(n_ctx, mask))

    pairs = jnp.concatenate([keys, values], axis=1)
    kv_blocks = [pairs] + [swap_ctx(pairs, b) for b in range(1, n_ctx)]
    stacked_q, stacked_do, acts = prepare(queries, out_grad, activations, hd)
    query_grad, own, *others = attention(me_ctx, span_order[0], stacked_q, stacked_do, kv_blocks)
    parts = [swap_ctx(other, b + 1) for b, other in enumerate(others)]

    shrink = 1.0 / (n_dp * n_ctx)
    acts = acts.reshape(n_dp, n_ctx, sets, rows_set, rows)
    errors = error_feedback.reshape(n_dp, n_ctx, sets, rows_set, 2 * hd)
    got, tops = [], []
    for chosen in range(sets):
        if chosen == 0:
            out, top, key_grad, value_grad, grads = send_tiles(me_dp, own, parts, acts, errors, 0, shrink, True)
        else:
            out, top = send_tiles(me_dp, grads, [], acts, errors, chosen, shrink, False)
        got.append(swap_dp(out, 1))
        tops.append(top)

    halves = []
    for chosen in range(sets):
        *half, top = keep_tiles(me_dp, grads, got[chosen], acts, errors, chosen, shrink)
        halves.append(half)
        tops.append(top)
    top = functools.reduce(jnp.maximum, tops)

    groups = []
    for chosen in range(sets):
        low_away, low, high_away, high = halves[chosen]
        for stage in range(1, bits):
            low_got = swap_dp(low_away, 1 << stage)
            high_got = swap_dp(high_away, 1 << (bits - stage))
            tops = []
            if chosen == sets - 1:
                masks = [1] if stage == 1 else range(2, n_dp, 2) if stage == 2 else []
                tops = [top] + [swap_dp(top, mask) for mask in masks]
            if stage < bits - 1:
                low_away, low, high_away, high, *top_out = add_stage(low, low_got, high, high_got, tops)
            else:
                outs = last_stage(me_ctx, low, low_got, high, high_got, tops, n_ctx)
                mine, *away = outs[:n_ctx]
                top_out = outs[n_ctx:]
            if tops:
                top = top_out[0]
        groups.append([mine] + [swap_ctx(part, b + 1) for b, part in enumerate(away)])
    tops = [top] + [swap_ctx(top, b) for b in range(1, n_ctx)]
    payload, scale = final_stage(me_dp, me_ctx, groups, tops, 7.0 / shrink)
    return query_grad, key_grad, value_grad, payload, scale.reshape(-1)


def solution(mesh):
    tokens = P(("dp", "context"), None)
    return jax.shard_map(
        functools.partial(local, mesh.shape["dp"], mesh.shape["context"], 2),
        mesh=mesh,
        in_specs=(P("dp", None), tokens, tokens, tokens, tokens, tokens, P("dp", "context", None, None)),
        out_specs=(tokens, tokens, tokens, tokens, P()),
        check_vma=False,
    )
```

```python
import functools

import jax
import jax.numpy as jnp
from jax import lax
from jax.experimental import pallas as pl
from jax.experimental.pallas import tpu as pltpu
from jax.sharding import PartitionSpec as P

QROWS = 32
LOG2E = 1.4426950408889634
FAR = 1e30
MIB = 1024 * 1024
BF16, F32 = jnp.bfloat16, jnp.float32


def xor_perm(size, mask):
    return [(i, i ^ mask) for i in range(size)]


def whole(shape):
    return pl.BlockSpec(shape, lambda *_: (0,) * len(shape))


def params(mib):
    return pltpu.CompilerParams(vmem_limit_bytes=mib * MIB)


def prepare_kernel(q_ref, do_ref, a_ref, e_ref, q_out, do_out, a_out, e_out):
    q_out[...] = q_ref[...]
    do_out[...] = do_ref[...]
    a_out[...] = a_ref[...].T
    e_out[...] = e_ref[...]


def prepare(queries, out_grad, activations, errors, hd):
    rows, columns = queries.shape
    heads = columns // hd
    model = activations.shape[1]
    tile = model // heads
    width = errors.shape[1]
    head = pl.BlockSpec((rows, hd), lambda i: (0, i))
    stacked = pl.BlockSpec((rows, hd), lambda i: (i, 0))
    error_tile = pl.BlockSpec((tile, width), lambda i: (i, 0))
    return pl.pallas_call(
        prepare_kernel,
        grid=(heads,),
        in_specs=[head, head, pl.BlockSpec((rows, tile), lambda i: (0, i)), error_tile],
        out_specs=[stacked, stacked, pl.BlockSpec((tile, rows), lambda i: (i, 0)), error_tile],
        out_shape=[
            jax.ShapeDtypeStruct((heads * rows, hd), BF16),
            jax.ShapeDtypeStruct((heads * rows, hd), BF16),
            jax.ShapeDtypeStruct((model, rows), BF16),
            jax.ShapeDtypeStruct((model, width), F32),
        ],
        compiler_params=params(56),
        cost_estimate=pl.CostEstimate(
            flops=0, bytes_accessed=4 * rows * (model + 2 * columns) + 8 * model * width, transcendentals=0
        ),
        name="prepare",
    )(queries, out_grad, activations, errors)


CHUNK = 256


def key_value(refs):
    if len(refs) == 2:
        return refs[0][...], refs[1][...]
    hd = refs[0].shape[1] // 2
    return refs[0][:, :hd], refs[0][:, hd:]


def score_chunk(k, v, q_ref, do_ref, at, own, first_lane):
    nt = (((1,), (1,)), ((), ()))
    lanes = pl.ds(at, CHUNK)
    s = lax.dot_general(k, q_ref[lanes, :], nt, preferred_element_type=F32)
    dp = lax.dot_general(v, do_ref[lanes, :], nt, preferred_element_type=F32)
    if own:
        rows = k.shape[0]
        key_at = lax.broadcasted_iota(jnp.int32, s.shape, 0)
        query_at = lax.broadcasted_iota(jnp.int32, s.shape, 1) + first_lane
        query_at = jnp.where(query_at >= rows, query_at - rows, query_at)
        s = jnp.where(key_at <= query_at, s, -FAR)
    return s, dp


def counted(b, me_ref, span_ref):
    me = me_ref[0]
    return span_ref[me ^ b] < span_ref[me]


def stats_kernel(b, me_ref, span_ref, q_ref, do_ref, *refs):
    if b == 0:
        kv, out = refs[:2], refs[2]
    else:
        kv, before, out = refs[:1], refs[1], refs[2]
    hd = q_ref.shape[1]

    def run():
        k, v = key_value(kv)
        pair = 2 * k.shape[0]
        factor = LOG2E / hd**0.5

        def heads(i, carry):
            for t in range(pair // CHUNK):
                at = pl.multiple_of(i * pair + t * CHUNK, CHUNK)
                lanes = pl.ds(at, CHUNK)
                s, dp = score_chunk(k, v, q_ref, do_ref, at, b == 0, t * CHUNK)
                top = jnp.max(s, axis=0, keepdims=True) * factor
                e = jnp.exp2(s * factor - top)
                total = jnp.sum(e, axis=0, keepdims=True)
                weighted = jnp.sum(e * dp, axis=0, keepdims=True)
                if b > 0:
                    old = before[0:1, lanes]
                    both = jnp.maximum(old, top)
                    old_part, new_part = jnp.exp2(old - both), jnp.exp2(top - both)
                    total = before[1:2, lanes] * old_part + total * new_part
                    weighted = before[2:3, lanes] * old_part + weighted * new_part
                    top = both
                out[0:1, lanes] = top
                out[1:2, lanes] = total
                out[2:3, lanes] = weighted
            return carry

        lax.fori_loop(0, q_ref.shape[0] // pair, heads, 0)

    if b == 0:
        run()
    else:
        keep = counted(b, me_ref, span_ref)
        pl.when(keep)(run)

        @pl.when(jnp.logical_not(keep))
        def _():
            out[...] = before[...]


def block_gradients(own, stats, q_ref, do_ref, kv, p_buf, ds_buf, dk, dv, ds_at):
    k, v = key_value(kv)
    hd = q_ref.shape[1]
    pair = 2 * k.shape[0]
    factor = LOG2E / hd**0.5
    dk[...] = jnp.zeros_like(dk)
    dv[...] = jnp.zeros_like(dv)

    def heads(i, carry):
        for t in range(pair // CHUNK):
            at = pl.multiple_of(i * pair + t * CHUNK, CHUNK)
            lanes = pl.ds(at, CHUNK)
            s, dp = score_chunk(k, v, q_ref, do_ref, at, own, t * CHUNK)
            total = stats[1:2, lanes]
            level = stats[0:1, lanes] + jnp.log(total) * LOG2E
            p = jnp.exp2(s * factor - level)
            ds = (p * (dp - stats[2:3, lanes] / total)).astype(BF16)
            p_buf[:, t * CHUNK : (t + 1) * CHUNK] = p.astype(BF16)
            ds_buf[:, t * CHUNK : (t + 1) * CHUNK] = ds
            ds_at(lanes, ds)
        part = pl.ds(pl.multiple_of(i * pair, pair), pair)
        dk[...] += jnp.dot(ds_buf[...], q_ref[part, :], preferred_element_type=F32)
        dv[...] += jnp.dot(p_buf[...], do_ref[part, :], preferred_element_type=F32)
        return carry

    lax.fori_loop(0, q_ref.shape[0] // pair, heads, 0)
    inverse = 1.0 / hd**0.5
    return dk[...] * inverse, dv[...]


def other_kernel(b, me_ref, span_ref, stats, q_ref, do_ref, kv, out_ref, ds_out, p_buf, ds_buf, dk, dv):
    keep = counted(b, me_ref, span_ref)
    hd = q_ref.shape[1]

    @pl.when(keep)
    def _():
        def ds_at(lanes, ds):
            ds_out[:, lanes] = ds

        dk_sum, dv_sum = block_gradients(False, stats, q_ref, do_ref, (kv,), p_buf, ds_buf, dk, dv, ds_at)
        out_ref[:, :hd] = dk_sum.astype(BF16)
        out_ref[:, hd:] = dv_sum.astype(BF16)

    @pl.when(jnp.logical_not(keep))
    def _():
        out_ref[...] = jnp.zeros_like(out_ref)
        ds_out[...] = jnp.zeros_like(ds_out)


def own_kernel(n, me_ref, span_ref, stats, q_ref, do_ref, k_ref, v_ref, *refs):
    kv_refs, ds_refs = refs[: n - 1], refs[n - 1 : 2 * n - 2]
    out_ref, dq_ref, ds_own, p_buf, ds_buf, dk, dv = refs[2 * n - 2 :]
    rows, hd = k_ref.shape

    def ds_at(lanes, ds):
        ds_own[:, lanes] = ds

    dk_sum, dv_sum = block_gradients(True, stats, q_ref, do_ref, (k_ref, v_ref), p_buf, ds_buf, dk, dv, ds_at)
    out_ref[:, :hd] = dk_sum
    out_ref[:, hd:] = dv_sum
    tn = (((0,), (0,)), ((), ()))

    def head(h, carry):
        lanes = pl.ds(pl.multiple_of(h * rows, 128), rows)
        dq = lax.dot_general(ds_own[:, lanes], k_ref[...], tn, preferred_element_type=F32)
        for kv, ds in zip(kv_refs, ds_refs):
            dq = dq + lax.dot_general(ds[:, lanes], kv[:, :hd], tn, preferred_element_type=F32)
        dq_ref[:, pl.ds(pl.multiple_of(h * hd, hd), hd)] = (dq / hd**0.5).astype(BF16)
        return carry

    lax.fori_loop(0, q_ref.shape[0] // rows, head, 0)


def block_call(kernel, name, products, operands, me, spans, stacked_q, out_shape, scratch):
    tall, hd = stacked_q.shape
    rows = operands[-1].shape[0] if name == "block_stats" else out_shape[0].shape[0]
    return pl.pallas_call(
        kernel,
        grid_spec=pltpu.PrefetchScalarGridSpec(
            num_scalar_prefetch=2,
            grid=(1,),
            in_specs=[whole(x.shape) for x in operands],
            out_specs=[whole(x.shape) for x in out_shape],
            scratch_shapes=scratch,
        ),
        out_shape=out_shape,
        compiler_params=params(24),
        cost_estimate=pl.CostEstimate(
            flops=4 * products * rows * tall * hd, bytes_accessed=8 * tall * hd, transcendentals=rows * tall
        ),
        name=name,
    )(me, spans, *operands)


def attention(me, spans, stacked_q, stacked_do, keys, values, received, swap):
    n = len(received) + 1
    rows, hd = keys.shape
    tall = stacked_q.shape[0]
    stats_shape = [jax.ShapeDtypeStruct((8, tall), F32)]

    def stats_call(b, operands):
        return block_call(
            functools.partial(stats_kernel, b), "block_stats", 2, operands, me, spans, stacked_q, stats_shape, []
        )[0]

    stats = stats_call(0, [stacked_q, stacked_do, keys, values])
    for b, kv in enumerate(received, 1):
        stats = stats_call(b, [stacked_q, stacked_do, kv, stats])
    pair_scratch = [
        pltpu.VMEM((rows, 2 * rows), BF16),
        pltpu.VMEM((rows, 2 * rows), BF16),
        pltpu.VMEM((rows, hd), F32),
        pltpu.VMEM((rows, hd), F32),
    ]
    parts, score_grads = [None] * (n - 1), [None] * (n - 1)
    for b in range(n - 1, 0, -1):
        part, score_grads[b - 1] = block_call(
            functools.partial(other_kernel, b),
            "block_gradients",
            4,
            [stats, stacked_q, stacked_do, received[b - 1]],
            me,
            spans,
            stacked_q,
            [jax.ShapeDtypeStruct((rows, 2 * hd), BF16), jax.ShapeDtypeStruct((rows, tall), BF16)],
            pair_scratch,
        )
        parts[b - 1] = swap(part, b)
    own, query_grad = block_call(
        functools.partial(own_kernel, n),
        "own_gradients",
        8,
        [stats, stacked_q, stacked_do, keys, values, *received, *score_grads],
        me,
        spans,
        stacked_q,
        [jax.ShapeDtypeStruct((rows, 2 * hd), F32), jax.ShapeDtypeStruct((rows, tall // rows * hd), BF16)],
        [pltpu.VMEM((rows, tall), BF16)] + pair_scratch,
    )
    return query_grad, own, parts


def tile_of(step, me_dp, bits, flip):
    mask = flip
    for j in range(1, bits):
        if not (step >> (bits - 1 - j)) & 1:
            mask |= 1 << j
    return me_dp ^ mask


def reversed_step(step, bits):
    return sum(((step >> (bits - 1 - j)) & 1) << (j - 1) for j in range(1, bits))


def corrected_tile(chosen, dest, grads, a_ref, e_ref, top_ref):
    _, n_ctx, _, rows_set, rows = a_ref.shape
    tall = n_ctx * rows_set
    a = a_ref[dest, :, chosen].reshape(tall, rows)
    e = e_ref[dest, :, chosen].reshape(tall, e_ref.shape[4])
    c = jnp.dot(a, grads, preferred_element_type=F32) + e

    mags = jnp.max(jnp.abs(c).reshape(tall // QROWS, QROWS, c.shape[1]), axis=1)
    mags = jnp.max(mags, axis=1, keepdims=True)
    per_set = rows_set // QROWS
    lanes = top_ref.shape[1]
    block = lax.broadcasted_iota(jnp.int32, (tall // QROWS, lanes), 0)
    lane = lax.broadcasted_iota(jnp.int32, (tall // QROWS, lanes), 1)
    shift = per_set.bit_length() - 1
    place = ((block >> shift) * (lanes // n_ctx)) + chosen * per_set + (block & (per_set - 1))
    top_ref[pl.ds(dest, 1), :] = jnp.max(jnp.where(lane == place, mags, 0.0), axis=0, keepdims=True)
    return c


def send_kernel(n_parts, bits, shrink, chosen, with_grads, me_ref, own_ref, *refs):
    part_refs = refs[:n_parts]
    a_ref, e_ref, out_ref, top_ref, *grad_refs = refs[n_parts:]
    if with_grads:
        total = own_ref[...]
        for part in part_refs:
            total = total + part[...].astype(F32)
        total = total.astype(BF16)
        hd = total.shape[1] // 2
        grad_refs[0][...] = total[:, :hd]
        grad_refs[1][...] = total[:, hd:]
        grad_refs[2][...] = total
    else:
        total = own_ref[...]
    top_ref[...] = jnp.zeros_like(top_ref)
    for step in range(out_ref.shape[0]):
        dest = tile_of(step, me_ref[0], bits, 1)
        c = corrected_tile(chosen, dest, total, a_ref, e_ref, top_ref)
        out_ref[step] = (c * shrink).astype(BF16)


def keep_kernel(bits, shrink, chosen, me_ref, grads, got_ref, a_ref, e_ref, *outs):
    low_away, low_stay, high_away, high_stay, top_ref = outs
    half = low_away.shape[0]
    hd = low_away.shape[2]
    total = grads[...]
    top_ref[...] = jnp.zeros_like(top_ref)
    for step in range(2 * half):
        dest = tile_of(step, me_ref[0], bits, 0)
        c = corrected_tile(chosen, dest, total, a_ref, e_ref, top_ref)
        c = (c * shrink + got_ref[step].astype(F32)).astype(BF16)
        back = reversed_step(step, bits)
        for at, part, away, stay in ((step, c[:, :hd], low_away, low_stay), (back, c[:, hd:], high_away, high_stay)):
            if at < half:
                away[at] = part
            else:
                stay[at - half] = part


def tile_call(kernel, name, me, operands, out_shape, a, e):
    n_dp, n_ctx, _, rows_set, rows = a.shape
    tall = n_dp // 2 * n_ctx * rows_set
    width = e.shape[4]
    return pl.pallas_call(
        kernel,
        grid_spec=pltpu.PrefetchScalarGridSpec(
            num_scalar_prefetch=1,
            grid=(1,),
            in_specs=[whole(x.shape) for x in operands] + [whole(a.shape), whole(e.shape)],
            out_specs=[whole(x.shape) for x in out_shape],
        ),
        out_shape=out_shape,
        compiler_params=params(28),
        cost_estimate=pl.CostEstimate(
            flops=2 * tall * rows * width, bytes_accessed=tall * (2 * rows + 6 * width), transcendentals=0
        ),
        name=name,
    )(me, *operands, a, e)


def send_tiles(me, own, parts, a, e, chosen, shrink, with_grads):
    n_dp, n_ctx, sets, rows_set, rows = a.shape
    bits = n_dp.bit_length() - 1
    width = e.shape[4]
    tall = n_ctx * rows_set
    out_shape = [
        jax.ShapeDtypeStruct((n_dp // 2, tall, width), BF16),
        jax.ShapeDtypeStruct((n_dp, sets * tall // QROWS), F32),
    ]
    if with_grads:
        out_shape += [jax.ShapeDtypeStruct((rows, columns), BF16) for columns in (width // 2, width // 2, width)]
    kernel = functools.partial(send_kernel, len(parts), bits, shrink, chosen, with_grads)
    return tile_call(kernel, "send_tiles", me, [own, *parts], out_shape, a, e)


def keep_tiles(me, grads, got, a, e, chosen, shrink):
    n_dp, n_ctx, sets, rows_set, rows = a.shape
    bits = n_dp.bit_length() - 1
    tall = n_ctx * rows_set
    half = jax.ShapeDtypeStruct((n_dp // 4, tall, e.shape[4] // 2), BF16)
    out_shape = [half] * 4 + [jax.ShapeDtypeStruct((n_dp, sets * tall // QROWS), F32)]
    kernel = functools.partial(keep_kernel, bits, shrink, chosen)
    return tile_call(kernel, "keep_tiles", me, [grads, got], out_shape, a, e)


def largest(tops, top_out):
    if tops:
        top = tops[0][...]
        for other in tops[1:]:
            top = jnp.maximum(top, other[...])
        top_out[0][...] = top


def add_kernel(n_tops, *refs):
    low, low_got, high, high_got = refs[:4]
    tops = refs[4 : 4 + n_tops]
    low_away, low_stay, high_away, high_stay, *top_out = refs[4 + n_tops :]
    half = low_away.shape[0]
    for mine, got, away, stay in ((low, low_got, low_away, low_stay), (high, high_got, high_away, high_stay)):
        away[...] = (mine[:half].astype(F32) + got[:half].astype(F32)).astype(BF16)
        stay[...] = (mine[half:].astype(F32) + got[half:].astype(F32)).astype(BF16)
    largest(tops, top_out)


def add_stage(low, low_got, high, high_got, tops):
    m, tall, hd = low.shape
    half = jax.ShapeDtypeStruct((m // 2, tall, hd), BF16)
    return pl.pallas_call(
        functools.partial(add_kernel, len(tops)),
        out_shape=[half] * 4 + [jax.ShapeDtypeStruct(top.shape, F32) for top in tops[:1]],
        compiler_params=params(16),
        cost_estimate=pl.CostEstimate(flops=2 * low.size, bytes_accessed=12 * low.size, transcendentals=0),
        name="add_stage",
    )(low, low_got, high, high_got, *tops)


def last_kernel(n_ctx, n_tops, me_ref, *refs):
    low, low_got, high, high_got = refs[:4]
    tops = refs[4 : 4 + n_tops]
    outs, top_out = refs[4 + n_tops : 4 + n_tops + n_ctx], refs[4 + n_tops + n_ctx :]
    hd = low.shape[2]
    rows_set = low.shape[1] // n_ctx
    for b in range(n_ctx):
        part = pl.ds(pl.multiple_of((me_ref[0] ^ b) * rows_set, rows_set), rows_set)
        for at, mine, got in ((0, low, low_got), (hd, high, high_got)):
            total = mine[0, part, :].astype(F32) + got[0, part, :].astype(F32)
            outs[b][:, at : at + hd] = total.astype(outs[b].dtype)
    largest(tops, top_out)


def last_stage(me_ctx, low, low_got, high, high_got, tops, n_ctx):
    _, tall, hd = low.shape
    shape = (tall // n_ctx, 2 * hd)
    return pl.pallas_call(
        functools.partial(last_kernel, n_ctx, len(tops)),
        grid_spec=pltpu.PrefetchScalarGridSpec(
            num_scalar_prefetch=1,
            grid=(1,),
            in_specs=[whole(low.shape)] * 4 + [whole(top.shape) for top in tops],
            out_specs=[whole(shape)] * n_ctx + [whole(top.shape) for top in tops[:1]],
        ),
        out_shape=[jax.ShapeDtypeStruct(shape, F32)]
        + [jax.ShapeDtypeStruct(shape, BF16)] * (n_ctx - 1)
        + [jax.ShapeDtypeStruct(top.shape, F32) for top in tops[:1]],
        compiler_params=params(16),
        cost_estimate=pl.CostEstimate(flops=2 * low.size, bytes_accessed=12 * low.size, transcendentals=0),
        name="last_stage",
    )(me_ctx, low, low_got, high, high_got, *tops)


def final_kernel(sets, n_ctx, gain, me_dp_ref, me_ctx_ref, *refs):
    groups = [refs[chosen * n_ctx : (chosen + 1) * n_ctx] for chosen in range(sets)]
    tops = refs[sets * n_ctx : sets * n_ctx + n_ctx]
    out_ref, scale_ref = refs[sets * n_ctx + n_ctx :]
    scale = tops[0][...]
    for other in tops[1:]:
        scale = jnp.maximum(scale, other[...])
    scale_ref[...] = scale + 1e-06
    factors = gain / scale_ref[pl.ds(me_dp_ref[0], 1), :]
    lane = lax.broadcasted_iota(jnp.int32, factors.shape, 1)
    rows_set = groups[0][0].shape[0]
    per_set = rows_set // QROWS
    first = me_ctx_ref[0] * (sets * per_set)
    for chosen, group in enumerate(groups):
        for r in range(per_set):
            part = slice(r * QROWS, (r + 1) * QROWS)
            total = group[0][part, :]
            for other in group[1:]:
                total = total + other[part, :].astype(F32)
            mine = jnp.where(lane == first + (chosen * per_set + r), factors, 0.0)
            at = chosen * rows_set + r * QROWS
            out_ref[at : at + QROWS, :] = total * jnp.sum(mine, axis=1, keepdims=True)


def final_stage(me_dp, me_ctx, groups, tops, gain):
    sets, n_ctx = len(groups), len(groups[0])
    rows_set, width = groups[0][0].shape
    return pl.pallas_call(
        functools.partial(final_kernel, sets, n_ctx, gain),
        grid_spec=pltpu.PrefetchScalarGridSpec(
            num_scalar_prefetch=2,
            grid=(1,),
            in_specs=[whole((rows_set, width))] * (sets * n_ctx) + [whole(tops[0].shape)] * n_ctx,
            out_specs=[whole((sets * rows_set, width)), whole(tops[0].shape)],
        ),
        out_shape=[
            jax.ShapeDtypeStruct((sets * rows_set, width), F32),
            jax.ShapeDtypeStruct(tops[0].shape, F32),
        ],
        compiler_params=params(8),
        cost_estimate=pl.CostEstimate(
            flops=4 * sets * rows_set * width, bytes_accessed=16 * sets * rows_set * width, transcendentals=0
        ),
        name="final_stage",
    )(me_dp, me_ctx, *[x for group in groups for x in group], *tops)


def local(n_dp, n_ctx, sets, span_order, queries, keys, values, out_grad, activations, error_feedback):
    rows, hd = keys.shape
    model = activations.shape[1]
    rows_set = model // (n_dp * n_ctx * sets)
    me_dp = lax.axis_index("dp").astype(jnp.int32)[None]
    me_ctx = lax.axis_index("context").astype(jnp.int32)[None]
    bits = n_dp.bit_length() - 1

    def swap_dp(x, mask):
        return lax.ppermute(x, "dp", xor_perm(n_dp, mask))

    def swap_ctx(x, mask):
        return lax.ppermute(x, "context", xor_perm(n_ctx, mask))

    pairs = jnp.concatenate([keys, values], axis=1)
    received = [swap_ctx(pairs, b) for b in range(1, n_ctx)]
    stacked_q, stacked_do, acts, errors = prepare(queries, out_grad, activations, error_feedback[0, 0], hd)
    query_grad, own, parts = attention(
        me_ctx, span_order[0], stacked_q, stacked_do, keys, values, received, swap_ctx
    )

    shrink = 1.0 / (n_dp * n_ctx)
    acts = acts.reshape(n_dp, n_ctx, sets, rows_set, rows)
    errors = errors.reshape(n_dp, n_ctx, sets, rows_set, 2 * hd)
    got, tops = [], []
    for chosen in range(sets):
        if chosen == 0:
            out, top, key_grad, value_grad, grads = send_tiles(me_dp, own, parts, acts, errors, 0, shrink, True)
        else:
            out, top = send_tiles(me_dp, grads, [], acts, errors, chosen, shrink, False)
        got.append(swap_dp(out, 1))
        tops.append(top)

    halves = []
    for chosen in range(sets):
        *half, top = keep_tiles(me_dp, grads, got[chosen], acts, errors, chosen, shrink)
        halves.append(half)
        tops.append(top)
    top = functools.reduce(jnp.maximum, tops)

    groups = []
    for chosen in range(sets):
        low_away, low, high_away, high = halves[chosen]
        for stage in range(1, bits):
            low_got = swap_dp(low_away, 1 << stage)
            high_got = swap_dp(high_away, 1 << (bits - stage))
            tops = []
            if chosen == sets - 1:
                masks = [1] if stage == 1 else range(2, n_dp, 2) if stage == 2 else []
                tops = [top] + [swap_dp(top, mask) for mask in masks]
            if stage < bits - 1:
                low_away, low, high_away, high, *top_out = add_stage(low, low_got, high, high_got, tops)
            else:
                outs = last_stage(me_ctx, low, low_got, high, high_got, tops, n_ctx)
                mine, *away = outs[:n_ctx]
                top_out = outs[n_ctx:]
            if tops:
                top = top_out[0]
        groups.append([mine] + [swap_ctx(part, b + 1) for b, part in enumerate(away)])
    tops = [top] + [swap_ctx(top, b) for b in range(1, n_ctx)]
    payload, scale = final_stage(me_dp, me_ctx, groups, tops, 7.0 / shrink)
    return query_grad, key_grad, value_grad, payload, scale.reshape(-1)


def solution(mesh):
    tokens = P(("dp", "context"), None)
    return jax.shard_map(
        functools.partial(local, mesh.shape["dp"], mesh.shape["context"], 2),
        mesh=mesh,
        in_specs=(P("dp", None), tokens, tokens, tokens, tokens, tokens, P("dp", "context", None, None)),
        out_specs=(tokens, tokens, tokens, tokens, P()),
        check_vma=False,
    )
```

```python
import functools

import jax
import jax.numpy as jnp
from jax import lax
from jax.experimental import pallas as pl
from jax.experimental.pallas import tpu as pltpu
from jax.sharding import PartitionSpec as P

QROWS = 32
LOG2E = 1.4426950408889634
FAR = 1e30
MIB = 1024 * 1024
CHUNK = 256
TOP_ROWS, TOP_LANES = 16, 128
BF16, F32 = jnp.bfloat16, jnp.float32
BF16_MAX = float(jnp.finfo(jnp.bfloat16).max)
NT = (((1,), (1,)), ((), ()))
TN = (((0,), (0,)), ((), ()))


def xor_perm(size, mask):
    return [(i, i ^ mask) for i in range(size)]


def whole(x):
    return pl.BlockSpec(x.shape, lambda *_: (0,) * len(x.shape))


def shape(dims, dtype=BF16):
    return jax.ShapeDtypeStruct(dims, dtype)


def whole_call(kernel, name, scalars, operands, out_shape, mib, cost, scratch=()):
    return pl.pallas_call(
        kernel,
        grid_spec=pltpu.PrefetchScalarGridSpec(
            num_scalar_prefetch=len(scalars),
            grid=(1,),
            in_specs=[whole(x) for x in operands],
            out_specs=[whole(x) for x in out_shape],
            scratch_shapes=list(scratch),
        ),
        out_shape=out_shape,
        compiler_params=pltpu.CompilerParams(vmem_limit_bytes=mib * MIB),
        cost_estimate=pl.CostEstimate(flops=cost[0], bytes_accessed=cost[1], transcendentals=0),
        name=name,
    )(*scalars, *operands)


def join_kernel(k_ref, v_ref, out_ref):
    hd = k_ref.shape[1]
    out_ref[:, :hd] = k_ref[...]
    out_ref[:, hd:] = v_ref[...]


def join(keys, values):
    rows, hd = keys.shape
    out = [shape((rows, 2 * hd))]
    return whole_call(join_kernel, "join_keys_values", [], [keys, values], out, 4, (0, 8 * rows * hd))[0]


def prepare_kernel(pieces, a_hbm, e_hbm, a_out, e_out, a_buf, a_sems, e_sems):
    model = a_buf.shape[1]
    tile = model // pieces
    parts = [pl.ds(i * tile, tile) for i in range(pieces)]
    a_copies = [pltpu.make_async_copy(a_hbm.at[:, p], a_buf.at[:, p], a_sems.at[i]) for i, p in enumerate(parts)]
    e_copies = [pltpu.make_async_copy(e_hbm.at[p, :], e_out.at[p, :], e_sems.at[i]) for i, p in enumerate(parts)]
    for copy in a_copies + e_copies:
        copy.start()
    for copy, part in zip(a_copies, parts):
        copy.wait()
        a_out[part, :] = a_buf[:, part].T
    for copy in e_copies:
        copy.wait()


def prepare(activations, errors):
    rows, model = activations.shape
    pieces = 8
    hbm = pl.BlockSpec(memory_space=pltpu.HBM)
    outs = [shape((model, rows)), shape(errors.shape, F32)]
    return pl.pallas_call(
        functools.partial(prepare_kernel, pieces),
        in_specs=[hbm, hbm],
        out_specs=[pl.BlockSpec(memory_space=pltpu.VMEM)] * 2,
        out_shape=outs,
        scratch_shapes=[
            pltpu.VMEM((rows, model), BF16),
            pltpu.SemaphoreType.DMA((pieces,)),
            pltpu.SemaphoreType.DMA((pieces,)),
        ],
        compiler_params=pltpu.CompilerParams(vmem_limit_bytes=28 * MIB),
        cost_estimate=pl.CostEstimate(
            flops=0, bytes_accessed=2 * rows * model + 4 * errors.size, transcendentals=0
        ),
        name="prepare",
    )(activations, errors)


def key_value(refs):
    if len(refs) == 2:
        return refs[0][...], refs[1][...]
    hd = refs[0].shape[1] // 2
    return refs[0][:, :hd], refs[0][:, hd:]


def head_pair(ref, i, hd):
    at = i * (2 * hd)
    first = ref[:, pl.ds(pl.multiple_of(at, hd), hd)]
    second = ref[:, pl.ds(pl.multiple_of(at + hd, hd), hd)]
    return jnp.concatenate([first, second], axis=0)


def score_chunk(k, v, q, do, own, first_lane):
    s = lax.dot_general(k, q, NT, preferred_element_type=F32)
    dp = lax.dot_general(v, do, NT, preferred_element_type=F32)
    if own:
        rows = k.shape[0]
        key_at = lax.broadcasted_iota(jnp.int32, s.shape, 0)
        query_at = lax.broadcasted_iota(jnp.int32, s.shape, 1) + first_lane
        query_at = jnp.where(query_at >= rows, query_at - rows, query_at)
        s = jnp.where(key_at <= query_at, s, -FAR)
    return s, dp


def counted(b, me_ref, span_ref):
    me = me_ref[0]
    return span_ref[me ^ b] < span_ref[me]


def stats_kernel(b, me_ref, span_ref, q_ref, do_ref, *refs):
    if b == 0:
        kv, out = refs[:2], refs[2]
    else:
        kv, before, out = refs[:1], refs[1], refs[2]

    def run():
        k, v = key_value(kv)
        rows, hd = k.shape
        pair = 2 * rows
        factor = LOG2E / hd**0.5

        def heads(i, carry):
            q, do = head_pair(q_ref, i, hd), head_pair(do_ref, i, hd)
            for t in range(pair // CHUNK):
                part = slice(t * CHUNK, (t + 1) * CHUNK)
                lanes = pl.ds(pl.multiple_of(i * pair + t * CHUNK, CHUNK), CHUNK)
                s, dp = score_chunk(k, v, q[part], do[part], b == 0, t * CHUNK)
                top = jnp.max(s, axis=0, keepdims=True) * factor
                e = jnp.exp2(s * factor - top)
                total = jnp.sum(e, axis=0, keepdims=True)
                weighted = jnp.sum(e * dp, axis=0, keepdims=True)
                if b > 0:
                    old = before[0:1, lanes]
                    both = jnp.maximum(old, top)
                    old_part, new_part = jnp.exp2(old - both), jnp.exp2(top - both)
                    total = before[1:2, lanes] * old_part + total * new_part
                    weighted = before[2:3, lanes] * old_part + weighted * new_part
                    top = both
                out[0:1, lanes] = top
                out[1:2, lanes] = total
                out[2:3, lanes] = weighted
            return carry

        lax.fori_loop(0, q_ref.shape[1] // (2 * hd), heads, 0)

    if b == 0:
        run()
    else:
        keep = counted(b, me_ref, span_ref)
        pl.when(keep)(run)

        @pl.when(jnp.logical_not(keep))
        def _():
            out[...] = before[...]


def block_gradients(own, stats, q_ref, do_ref, kv, p_buf, ds_ref, ds_step, dk, dv, after):
    k, v = key_value(kv)
    rows, hd = k.shape
    pair = 2 * rows
    factor = LOG2E / hd**0.5
    dk[...] = jnp.zeros_like(dk)
    dv[...] = jnp.zeros_like(dv)

    def heads(i, carry):
        q, do = head_pair(q_ref, i, hd), head_pair(do_ref, i, hd)
        for t in range(pair // CHUNK):
            part = slice(t * CHUNK, (t + 1) * CHUNK)
            lanes = pl.ds(pl.multiple_of(i * pair + t * CHUNK, CHUNK), CHUNK)
            s, dp = score_chunk(k, v, q[part], do[part], own, t * CHUNK)
            total = stats[1:2, lanes]
            level = stats[0:1, lanes] + jnp.log(total) * LOG2E
            p = jnp.exp2(s * factor - level)
            p_buf[:, part] = p.astype(BF16)
            ds = (p * (dp - stats[2:3, lanes] / total)).astype(BF16)
            ds_ref[:, pl.ds(pl.multiple_of(i * ds_step + t * CHUNK, CHUNK), CHUNK)] = ds
        ds = ds_ref[:, pl.ds(pl.multiple_of(i * ds_step, CHUNK), pair)]
        dk[...] += jnp.dot(ds, q, preferred_element_type=F32)
        dv[...] += jnp.dot(p_buf[...], do, preferred_element_type=F32)
        after(i, ds)
        return carry

    lax.fori_loop(0, q_ref.shape[1] // (2 * hd), heads, 0)
    inverse = 1.0 / hd**0.5
    return dk[...] * inverse, dv[...]


def other_kernel(b, me_ref, span_ref, stats, q_ref, do_ref, kv, out_ref, ds_out, p_buf, dk, dv):
    keep = counted(b, me_ref, span_ref)
    rows, hd = dk.shape

    @pl.when(keep)
    def _():
        dk_sum, dv_sum = block_gradients(
            False, stats, q_ref, do_ref, (kv,), p_buf, ds_out, 2 * rows, dk, dv, lambda i, ds: None
        )
        out_ref[:, :hd] = dk_sum.astype(BF16)
        out_ref[:, hd:] = dv_sum.astype(BF16)

    @pl.when(jnp.logical_not(keep))
    def _():
        out_ref[...] = jnp.zeros_like(out_ref)
        ds_out[...] = jnp.zeros_like(ds_out)


def own_kernel(n, me_ref, span_ref, stats, q_ref, do_ref, k_ref, v_ref, *refs):
    kv_refs, ds_refs = refs[: n - 1], refs[n - 1 : 2 * n - 2]
    out_ref, dq_ref, ds_buf, p_buf, dk, dv = refs[2 * n - 2 :]
    rows, hd = k_ref.shape
    pair = 2 * rows

    def query_part(i, ds):
        lanes = pl.ds(pl.multiple_of(i * pair, CHUNK), pair)
        dq = lax.dot_general(ds, k_ref[...], TN, preferred_element_type=F32)
        for kv, other in zip(kv_refs, ds_refs):
            dq = dq + lax.dot_general(other[:, lanes], kv[:, :hd], TN, preferred_element_type=F32)
        dq = (dq / hd**0.5).astype(BF16)
        for h in range(2):
            at = pl.multiple_of(i * (2 * hd) + h * hd, hd)
            dq_ref[:, pl.ds(at, hd)] = dq[h * rows : (h + 1) * rows]

    dk_sum, dv_sum = block_gradients(
        True, stats, q_ref, do_ref, (k_ref, v_ref), p_buf, ds_buf, 0, dk, dv, query_part
    )
    out_ref[:, :hd] = dk_sum
    out_ref[:, hd:] = dv_sum


def attention(me, spans, queries, out_grad, keys, values, received, swap):
    n = len(received) + 1
    rows, hd = keys.shape
    columns = queries.shape[1]
    tall = columns // hd * rows
    product = 2 * rows * tall * hd
    scalars = [me, spans]

    def stats_call(b, operands):
        outs = [shape((8, tall), F32)]
        cost = (4 * product, 8 * rows * columns)
        return whole_call(functools.partial(stats_kernel, b), "block_stats", scalars, operands, outs, 20, cost)[0]

    stats = stats_call(0, [queries, out_grad, keys, values])
    for b, kv in enumerate(received, 1):
        stats = stats_call(b, [queries, out_grad, kv, stats])
    p_buf = pltpu.VMEM((rows, 2 * rows), BF16)
    sums = [pltpu.VMEM((rows, hd), F32)] * 2
    parts, score_grads = [None] * (n - 1), [None] * (n - 1)
    for b in range(n - 1, 0, -1):
        part, score_grads[b - 1] = whole_call(
            functools.partial(other_kernel, b),
            "block_gradients",
            scalars,
            [stats, queries, out_grad, received[b - 1]],
            [shape((rows, 2 * hd)), shape((rows, tall))],
            24,
            (8 * product, 16 * rows * columns),
            [p_buf, *sums],
        )
        parts[b - 1] = swap(part, b)
    own, query_grad = whole_call(
        functools.partial(own_kernel, n),
        "own_gradients",
        scalars,
        [stats, queries, out_grad, keys, values, *received, *score_grads],
        [shape((rows, 2 * hd), F32), shape((rows, columns))],
        32,
        (16 * product, 16 * rows * columns),
        [p_buf, p_buf, *sums],
    )
    return query_grad, own, parts


def pack_top(top):
    high = jnp.minimum(top, BF16_MAX).astype(BF16)
    rest = top - high.astype(F32)
    middle = rest.astype(BF16)
    low = (rest - middle.astype(F32)).astype(BF16)
    return jnp.concatenate([high, middle, low], axis=0)


def unpack_top(ref, at):
    parts = [ref[at + i * TOP_ROWS : at + (i + 1) * TOP_ROWS, :TOP_LANES].astype(F32) for i in range(3)]
    return parts[0] + (parts[1] + parts[2])


def tile_of(step, me_dp, bits, flip):
    mask = flip
    for j in range(1, bits):
        if not (step >> (bits - 1 - j)) & 1:
            mask |= 1 << j
    return me_dp ^ mask


def reversed_step(step, bits):
    return sum(((step >> (bits - 1 - j)) & 1) << (j - 1) for j in range(1, bits))


def corrected_tile(chosen, dest, grads, a_ref, e_ref, top_ref):
    _, n_ctx, sets, rows_set, rows = a_ref.shape
    tall = n_ctx * rows_set
    a = a_ref[dest, :, chosen].reshape(tall, rows)
    e = e_ref[dest, :, chosen].reshape(tall, e_ref.shape[4])
    c = jnp.dot(a, grads, preferred_element_type=F32) + e

    mags = jnp.max(jnp.abs(c).reshape(tall // QROWS, QROWS, c.shape[1]), axis=1)
    mags = jnp.max(mags, axis=1, keepdims=True)
    per_set = rows_set // QROWS
    block = lax.broadcasted_iota(jnp.int32, (tall // QROWS, TOP_LANES), 0)
    lane = lax.broadcasted_iota(jnp.int32, (tall // QROWS, TOP_LANES), 1)
    shift = per_set.bit_length() - 1
    place = ((block >> shift) * (sets * per_set)) + chosen * per_set + (block & (per_set - 1))
    top = jnp.max(jnp.where(lane == place, mags, 0.0), axis=0, keepdims=True)
    top_ref[pl.ds(dest, 1), :] = jnp.maximum(top_ref[pl.ds(dest, 1), :], top)
    return c


def first_send_kernel(bits, shrink, n_parts, me_ref, own_ref, *refs):
    part_refs = refs[:n_parts]
    a_ref, e_ref, out_ref, top_ref, kg_ref, vg_ref, grads_ref = refs[n_parts:]
    total = own_ref[...]
    for part in part_refs:
        total = total + part[...].astype(F32)
    total = total.astype(BF16)
    hd = total.shape[1] // 2
    kg_ref[...] = total[:, :hd]
    vg_ref[...] = total[:, hd:]
    grads_ref[...] = total
    top_ref[...] = jnp.zeros_like(top_ref)
    send_rows(bits, shrink, 0, me_ref, total, a_ref, e_ref, out_ref, top_ref)


def next_send_kernel(bits, shrink, chosen, me_ref, grads_ref, before_ref, a_ref, e_ref, out_ref, top_ref):
    top_ref[...] = before_ref[...]
    send_rows(bits, shrink, chosen, me_ref, grads_ref[...], a_ref, e_ref, out_ref, top_ref)


def send_rows(bits, shrink, chosen, me_ref, total, a_ref, e_ref, out_ref, top_ref):
    for step in range(out_ref.shape[0]):
        dest = tile_of(step, me_ref[0], bits, 1)
        c = corrected_tile(chosen, dest, total, a_ref, e_ref, top_ref)
        out_ref[step] = (c * shrink).astype(BF16)


def keep_kernel(bits, shrink, chosen, me_ref, grads, got_ref, before_ref, a_ref, e_ref, *outs):
    low_away, low_stay, high_away, high_stay, top_ref = outs
    steps, tall, width = got_ref.shape
    half = steps // 2
    hd = width // 2
    total = grads[...]
    top_ref[...] = before_ref[...]
    for step in range(steps):
        dest = tile_of(step, me_ref[0], bits, 0)
        c = corrected_tile(chosen, dest, total, a_ref, e_ref, top_ref)
        c = (c * shrink + got_ref[step].astype(F32)).astype(BF16)
        back = reversed_step(step, bits)
        for at, part, away, stay in ((step, c[:, :hd], low_away, low_stay), (back, c[:, hd:], high_away, high_stay)):
            if at < half:
                away[at * tall : (at + 1) * tall, :] = part
            else:
                stay[(at - half) * tall : (at - half + 1) * tall, :] = part
    low_away[half * tall :, :] = pack_top(top_ref[...])


def largest(top_ref, low_got, at, others):
    top = jnp.maximum(top_ref[...], unpack_top(low_got, at))
    for other in others:
        top = jnp.maximum(top, other[...])
    return top


def add_kernel(n_others, low, low_got, high, high_got, top_ref, *refs):
    others = refs[:n_others]
    low_away, low_stay, high_away, high_stay, top_out = refs[n_others:]
    size = low.shape[0]
    half = size // 2
    for mine, got, away, stay in ((low, low_got, low_away, low_stay), (high, high_got, high_away, high_stay)):
        away[:half, :] = (mine[:half, :].astype(F32) + got[:half, :].astype(F32)).astype(BF16)
        stay[...] = (mine[half:, :].astype(F32) + got[half:size, :].astype(F32)).astype(BF16)
    top = largest(top_ref, low_got, size, others)
    low_away[half:, :] = pack_top(top)
    top_out[...] = top


def last_kernel(n_ctx, n_others, me_ref, low, low_got, high, high_got, top_ref, *refs):
    others = refs[:n_others]
    *outs, top_out = refs[n_others:]
    size, hd = low.shape
    rows_set = size // n_ctx
    top = largest(top_ref, low_got, size, others)
    packed = pack_top(top)
    for b in range(n_ctx):
        part = pl.ds(pl.multiple_of((me_ref[0] ^ b) * rows_set, rows_set), rows_set)
        for at, mine, got in ((0, low, low_got), (hd, high, high_got)):
            total = mine[part, :].astype(F32) + got[part, :].astype(F32)
            outs[b][:rows_set, at : at + hd] = total.astype(outs[b].dtype)
        if b > 0:
            outs[b][rows_set:, :TOP_LANES] = packed
            outs[b][rows_set:, TOP_LANES:] = jnp.zeros_like(packed)
    top_out[...] = top


def final_kernel(sets, n_ctx, gain, me_dp_ref, me_ctx_ref, *refs):
    groups = [refs[chosen * n_ctx : (chosen + 1) * n_ctx] for chosen in range(sets)]
    top_ref, out_ref, scale_ref, all_tops = refs[sets * n_ctx :]
    n_dp, lanes = scale_ref.shape
    rows_set = groups[0][0].shape[0]
    scale = top_ref[...]
    for other in groups[-1][1:]:
        scale = jnp.maximum(scale, unpack_top(other, rows_set))
    scale = scale + 1e-06
    all_tops[...] = scale
    scale_ref[...] = scale[:n_dp, :lanes]
    factors = gain / all_tops[pl.ds(me_dp_ref[0], 1), :]
    lane = lax.broadcasted_iota(jnp.int32, factors.shape, 1)
    per_set = rows_set // QROWS
    first = me_ctx_ref[0] * (sets * per_set)
    for chosen, group in enumerate(groups):
        for r in range(per_set):
            part = slice(r * QROWS, (r + 1) * QROWS)
            total = group[0][part, :]
            for other in group[1:]:
                total = total + other[part, :].astype(F32)
            mine = jnp.where(lane == first + (chosen * per_set + r), factors, 0.0)
            at = chosen * rows_set + r * QROWS
            out_ref[at : at + QROWS, :] = total * jnp.sum(mine, axis=1, keepdims=True)


def local(n_dp, n_ctx, sets, span_order, queries, keys, values, out_grad, activations, error_feedback):
    rows, hd = keys.shape
    width = 2 * hd
    model = activations.shape[1]
    rows_set = model // (n_dp * n_ctx * sets)
    tall = n_ctx * rows_set
    me_dp = lax.axis_index("dp").astype(jnp.int32)[None]
    me_ctx = lax.axis_index("context").astype(jnp.int32)[None]
    bits = n_dp.bit_length() - 1
    packed_rows = 3 * TOP_ROWS

    def swap_dp(x, mask):
        return lax.ppermute(x, "dp", xor_perm(n_dp, mask))

    def swap_ctx(x, mask):
        return lax.ppermute(x, "context", xor_perm(n_ctx, mask))

    pairs = join(keys, values)
    received = [swap_ctx(pairs, b) for b in range(1, n_ctx)]
    acts, errors = prepare(activations, error_feedback[0, 0])
    query_grad, own, parts = attention(me_ctx, span_order[0], queries, out_grad, keys, values, received, swap_ctx)

    shrink = 1.0 / (n_dp * n_ctx)
    acts = acts.reshape(n_dp, n_ctx, sets, rows_set, rows)
    errors = errors.reshape(n_dp, n_ctx, sets, rows_set, width)
    tops = shape((TOP_ROWS, TOP_LANES), F32)
    steps = n_dp // 2
    cost = (2 * steps * tall * rows * width, steps * tall * (2 * rows + 6 * width))
    message = shape((steps, tall, width))
    got = []
    for chosen in range(sets):
        if chosen == 0:
            out, top, key_grad, value_grad, grads = whole_call(
                functools.partial(first_send_kernel, bits, shrink, n_ctx - 1),
                "send_tiles",
                [me_dp],
                [own, *parts, acts, errors],
                [message, tops, shape((rows, hd)), shape((rows, hd)), shape((rows, width))],
                28,
                cost,
            )
        else:
            out, top = whole_call(
                functools.partial(next_send_kernel, bits, shrink, chosen),
                "send_tiles",
                [me_dp],
                [grads, top, acts, errors],
                [message, tops],
                28,
                cost,
            )
        got.append(swap_dp(out, 1))

    halves = []
    for chosen in range(sets):
        half = steps // 2 * tall
        *arrays, top = whole_call(
            functools.partial(keep_kernel, bits, shrink, chosen),
            "keep_tiles",
            [me_dp],
            [grads, got[chosen], top, acts, errors],
            [shape((half + packed_rows, hd))] + [shape((half, hd))] * 3 + [tops],
            28,
            cost,
        )
        halves.append((arrays, top))

    groups = []
    for chosen in range(sets):
        (low_away, low, high_away, high), top = halves[chosen]
        for stage in range(1, bits):
            low_got = swap_dp(low_away, 1 << stage)
            high_got = swap_dp(high_away, 1 << (bits - stage))
            others = [swap_dp(top, mask) for mask in (1, 3)] if chosen == sets - 1 and stage == 1 else []
            operands = [low, low_got, high, high_got, top, *others]
            size = low.shape[0]
            cost = (4 * size * hd, 12 * size * hd)
            if stage < bits - 1:
                low_away, low, high_away, high, top = whole_call(
                    functools.partial(add_kernel, len(others)),
                    "add_stage",
                    [],
                    operands,
                    [shape((size // 2 + packed_rows, hd))] + [shape((size // 2, hd))] * 3 + [tops],
                    16,
                    cost,
                )
            else:
                mine, *away, top = whole_call(
                    functools.partial(last_kernel, n_ctx, len(others)),
                    "last_stage",
                    [me_ctx],
                    operands,
                    [shape((rows_set, width), F32)] + [shape((rows_set + packed_rows, width))] * (n_ctx - 1) + [tops],
                    16,
                    cost,
                )
        groups.append([mine] + [swap_ctx(part, b + 1) for b, part in enumerate(away)])
    payload, scale = whole_call(
        functools.partial(final_kernel, sets, n_ctx, 7.0 / shrink),
        "final_stage",
        [me_dp, me_ctx],
        [x for group in groups for x in group] + [top],
        [shape((sets * rows_set, width), F32), shape((n_dp, sets * tall // QROWS), F32)],
        8,
        (4 * sets * tall * width, 16 * sets * rows_set * width),
        [pltpu.VMEM((TOP_ROWS, TOP_LANES), F32)],
    )
    return query_grad, key_grad, value_grad, payload, scale.reshape(-1)


def solution(mesh):
    tokens = P(("dp", "context"), None)
    return jax.shard_map(
        functools.partial(local, mesh.shape["dp"], mesh.shape["context"], 2),
        mesh=mesh,
        in_specs=(P("dp", None), tokens, tokens, tokens, tokens, tokens, P("dp", "context", None, None)),
        out_specs=(tokens, tokens, tokens, tokens, P()),
        check_vma=False,
    )
```

```python
import functools

import jax
import jax.numpy as jnp
from jax import lax
from jax.experimental import pallas as pl
from jax.experimental.pallas import tpu as pltpu
from jax.sharding import PartitionSpec as P

QROWS = 32
LOG2E = 1.4426950408889634
FAR = 1e30
MIB = 1024 * 1024
CHUNK = 256
TOP_ROWS, TOP_LANES, PACK_LANES = 16, 128, 32
BF16, F32 = jnp.bfloat16, jnp.float32
BF16_MAX = float(jnp.finfo(jnp.bfloat16).max)
NT = (((1,), (1,)), ((), ()))
TN = (((0,), (0,)), ((), ()))


def xor_perm(size, mask):
    return [(i, i ^ mask) for i in range(size)]


def whole(x):
    return pl.BlockSpec(x.shape, lambda *_: (0,) * len(x.shape))


def shape(dims, dtype=BF16):
    return jax.ShapeDtypeStruct(dims, dtype)


def whole_call(kernel, name, scalars, operands, out_shape, mib, cost, scratch=(), after=()):
    def body(*refs):
        first = len(scalars) + len(operands)
        kernel(*refs[:first], *refs[first + len(after) :])

    return pl.pallas_call(
        body,
        grid_spec=pltpu.PrefetchScalarGridSpec(
            num_scalar_prefetch=len(scalars),
            grid=(1,),
            in_specs=[whole(x) for x in operands] + [pl.BlockSpec(memory_space=pl.ANY)] * len(after),
            out_specs=[whole(x) for x in out_shape],
            scratch_shapes=list(scratch),
        ),
        out_shape=out_shape,
        compiler_params=pltpu.CompilerParams(vmem_limit_bytes=mib * MIB),
        cost_estimate=pl.CostEstimate(flops=cost[0], bytes_accessed=cost[1], transcendentals=0),
        name=name,
    )(*scalars, *operands, *after)


def copy_all(pairs_of_refs, sems):
    copies = [pltpu.make_async_copy(src, dst, sems.at[i]) for i, (src, dst) in enumerate(pairs_of_refs)]
    for copy in copies:
        copy.start()
    for copy in copies:
        copy.wait()


def join_kernel(k_hbm, v_hbm, out_ref, sems):
    hd = k_hbm.shape[1]
    copy_all([(k_hbm, out_ref.at[:, pl.ds(0, hd)]), (v_hbm, out_ref.at[:, pl.ds(hd, hd)])], sems)


def load_call(kernel, name, operands, out_shape, mib):
    return pl.pallas_call(
        kernel,
        in_specs=[pl.BlockSpec(memory_space=pltpu.HBM)] * 2,
        out_specs=[pl.BlockSpec(memory_space=pltpu.VMEM)] * len(out_shape),
        out_shape=out_shape,
        scratch_shapes=[pltpu.SemaphoreType.DMA((2,))],
        compiler_params=pltpu.CompilerParams(vmem_limit_bytes=mib * MIB),
        cost_estimate=pl.CostEstimate(flops=0, bytes_accessed=4 * operands[0].size, transcendentals=0),
        name=name,
    )(*operands)


def prepare_kernel(pieces, a_hbm, e_hbm, _, a_out, e_out, a_buf, a_sems, e_sems):
    model = a_buf.shape[1]
    tile = model // pieces
    parts = [pl.ds(i * tile, tile) for i in range(pieces)]
    a_copies = [pltpu.make_async_copy(a_hbm.at[:, p], a_buf.at[:, p], a_sems.at[i]) for i, p in enumerate(parts)]
    e_copies = [pltpu.make_async_copy(e_hbm.at[p, :], e_out.at[p, :], e_sems.at[i]) for i, p in enumerate(parts)]
    for copy in a_copies + e_copies:
        copy.start()
    for copy, part in zip(a_copies, parts):
        copy.wait()
        a_out[part, :] = a_buf[:, part].T
    for copy in e_copies:
        copy.wait()


def prepare(activations, errors, after):
    rows, model = activations.shape
    pieces = 8
    hbm = pl.BlockSpec(memory_space=pltpu.HBM)
    outs = [shape((model, rows)), shape(errors.shape, F32)]
    return pl.pallas_call(
        functools.partial(prepare_kernel, pieces),
        in_specs=[hbm, hbm, pl.BlockSpec(memory_space=pl.ANY)],
        out_specs=[pl.BlockSpec(memory_space=pltpu.VMEM)] * 2,
        out_shape=outs,
        scratch_shapes=[
            pltpu.VMEM((rows, model), BF16),
            pltpu.SemaphoreType.DMA((pieces,)),
            pltpu.SemaphoreType.DMA((pieces,)),
        ],
        compiler_params=pltpu.CompilerParams(vmem_limit_bytes=28 * MIB),
        cost_estimate=pl.CostEstimate(
            flops=0, bytes_accessed=2 * rows * model + 4 * errors.size, transcendentals=0
        ),
        name="prepare",
    )(activations, errors, *after)


def key_value(ref):
    hd = ref.shape[1] // 2
    return ref[:, :hd], ref[:, hd:]


def head_pair(ref, i, hd):
    at = i * (2 * hd)
    first = ref[:, pl.ds(pl.multiple_of(at, hd), hd)]
    second = ref[:, pl.ds(pl.multiple_of(at + hd, hd), hd)]
    return jnp.concatenate([first, second], axis=0)


def score_chunk(k, v, q, do, own, first_lane):
    s = lax.dot_general(k, q, NT, preferred_element_type=F32)
    dp = lax.dot_general(v, do, NT, preferred_element_type=F32)
    if own:
        rows = k.shape[0]
        key_at = lax.broadcasted_iota(jnp.int32, s.shape, 0)
        query_at = lax.broadcasted_iota(jnp.int32, s.shape, 1) + first_lane
        query_at = jnp.where(query_at >= rows, query_at - rows, query_at)
        s = jnp.where(key_at <= query_at, s, -FAR)
    return s, dp


def counted(b, me_ref, span_ref):
    me = me_ref[0]
    return span_ref[me ^ b] < span_ref[me]


def stats_kernel(b, me_ref, span_ref, q_ref, do_ref, kv, *refs):
    before, out = refs[0], refs[-1]

    def run():
        k, v = key_value(kv)
        rows, hd = k.shape
        pair = 2 * rows
        factor = LOG2E / hd**0.5

        def heads(i, carry):
            q, do = head_pair(q_ref, i, hd), head_pair(do_ref, i, hd)
            for t in range(pair // CHUNK):
                part = slice(t * CHUNK, (t + 1) * CHUNK)
                lanes = pl.ds(pl.multiple_of(i * pair + t * CHUNK, CHUNK), CHUNK)
                s, dp = score_chunk(k, v, q[part], do[part], b == 0, t * CHUNK)
                top = jnp.max(s, axis=0, keepdims=True) * factor
                e = jnp.exp2(s * factor - top)
                total = jnp.sum(e, axis=0, keepdims=True)
                weighted = jnp.sum(e * dp, axis=0, keepdims=True)
                if b > 0:
                    old = before[0:1, lanes]
                    both = jnp.maximum(old, top)
                    old_part, new_part = jnp.exp2(old - both), jnp.exp2(top - both)
                    total = before[1:2, lanes] * old_part + total * new_part
                    weighted = before[2:3, lanes] * old_part + weighted * new_part
                    top = both
                out[0:1, lanes] = top
                out[1:2, lanes] = total
                out[2:3, lanes] = weighted
            return carry

        lax.fori_loop(0, q_ref.shape[1] // (2 * hd), heads, 0, unroll=True)

    if b == 0:
        run()
    else:
        keep = counted(b, me_ref, span_ref)
        pl.when(keep)(run)

        @pl.when(jnp.logical_not(keep))
        def _():
            out[...] = before[...]


def block_gradients(own, stats, q_ref, do_ref, kv, p_buf, ds_ref, dk, dv):
    k, v = key_value(kv)
    rows, hd = k.shape
    pair = 2 * rows
    factor = LOG2E / hd**0.5
    dk[...] = jnp.zeros_like(dk)
    dv[...] = jnp.zeros_like(dv)

    def heads(i, carry):
        q, do = head_pair(q_ref, i, hd), head_pair(do_ref, i, hd)
        for t in range(pair // CHUNK):
            part = slice(t * CHUNK, (t + 1) * CHUNK)
            lanes = pl.ds(pl.multiple_of(i * pair + t * CHUNK, CHUNK), CHUNK)
            s, dp = score_chunk(k, v, q[part], do[part], own, t * CHUNK)
            total = stats[1:2, lanes]
            level = stats[0:1, lanes] + jnp.log(total) * LOG2E
            p = jnp.exp2(s * factor - level)
            p_buf[:, part] = p.astype(BF16)
            ds = (p * (dp - stats[2:3, lanes] / total)).astype(BF16)
            ds_ref[:, lanes] = ds
        ds = ds_ref[:, pl.ds(pl.multiple_of(i * pair, CHUNK), pair)]
        dk[...] += jnp.dot(ds, q, preferred_element_type=F32)
        dv[...] += jnp.dot(p_buf[...], do, preferred_element_type=F32)
        return carry

    lax.fori_loop(0, q_ref.shape[1] // (2 * hd), heads, 0, unroll=True)
    inverse = 1.0 / hd**0.5
    return dk[...] * inverse, dv[...]


def other_kernel(b, me_ref, span_ref, stats, q_ref, do_ref, kv, out_ref, ds_out, p_buf, dk, dv):
    keep = counted(b, me_ref, span_ref)
    rows, hd = dk.shape

    @pl.when(keep)
    def _():
        dk_sum, dv_sum = block_gradients(False, stats, q_ref, do_ref, kv, p_buf, ds_out, dk, dv)
        out_ref[:, :hd] = dk_sum.astype(BF16)
        out_ref[:, hd:] = dv_sum.astype(BF16)

    @pl.when(jnp.logical_not(keep))
    def _():
        out_ref[...] = jnp.zeros_like(out_ref)
        ds_out[...] = jnp.zeros_like(ds_out)


def own_kernel(me_ref, span_ref, stats, q_ref, do_ref, kv, out_ref, ds_out, p_buf, dk, dv):
    hd = dk.shape[1]
    dk_sum, dv_sum = block_gradients(True, stats, q_ref, do_ref, kv, p_buf, ds_out, dk, dv)
    out_ref[:, :hd] = dk_sum
    out_ref[:, hd:] = dv_sum


def query_kernel(n, *refs):
    kv_refs, ds_refs, dq_ref = refs[:n], refs[n : 2 * n], refs[2 * n]
    rows, hd = kv_refs[0].shape[0], kv_refs[0].shape[1] // 2
    for h in range(dq_ref.shape[1] // hd):
        dq = 0.0
        for kv, ds in zip(kv_refs, ds_refs):
            part = ds[:, h * rows : (h + 1) * rows]
            dq = dq + lax.dot_general(part, kv[:, :hd], TN, preferred_element_type=F32)
        dq_ref[:, h * hd : (h + 1) * hd] = (dq / hd**0.5).astype(BF16)


def relay_kernel(block_ref, out_ref):
    out_ref[...] = block_ref[...]


def attention(me, spans, queries, out_grad, pairs, swap, n):
    rows, hd = pairs.shape[0], pairs.shape[1] // 2
    columns = queries.shape[1]
    tall = columns // hd * rows
    product = 2 * rows * tall * hd
    scalars = [me, spans]

    def stats_call(b, operands):
        outs = [shape((8, tall), F32)]
        cost = (4 * product, 8 * rows * columns)
        return whole_call(functools.partial(stats_kernel, b), "block_stats", scalars, operands, outs, 20, cost)[0]

    blocks = [pairs] + [None] * (n - 1)
    for b in range(1, n):
        if b & (b - 1) == 0:
            blocks[b] = swap(pairs, b)
    stats = stats_call(0, [queries, out_grad, pairs])
    for b in range(1, n):
        if blocks[b] is None:
            handed = blocks[b & (b - 1)]
            if b == 3:
                cost = (0, 8 * rows * hd)
                handed = whole_call(relay_kernel, "relay", [], [handed], [shape(handed.shape)], 4, cost, [], first)[0]
            blocks[b] = swap(handed, b & -b)
        stats = stats_call(b, [queries, out_grad, blocks[b], stats])
        if b == 1:
            first = [stats]
    received = blocks[1:]
    p_buf = pltpu.VMEM((rows, 2 * rows), BF16)
    sums = [pltpu.VMEM((rows, hd), F32)] * 2
    parts, score_grads, before = [None] * (n - 1), [None] * (n - 1), []
    for b in range(n - 1, 0, -1):
        part, score_grads[b - 1] = whole_call(
            functools.partial(other_kernel, b),
            "block_gradients",
            scalars,
            [stats, queries, out_grad, received[b - 1]],
            [shape((rows, 2 * hd)), shape((rows, tall))],
            24,
            (8 * product, 16 * rows * columns),
            [p_buf, *sums],
            before,
        )
        parts[b - 1] = swap(part, b)
        before = [part]
    own, own_score_grad = whole_call(
        own_kernel,
        "own_gradients",
        scalars,
        [stats, queries, out_grad, pairs],
        [shape((rows, 2 * hd), F32), shape((rows, tall))],
        24,
        (8 * product, 16 * rows * columns),
        [p_buf, *sums],
        before,
    )
    return own, parts, blocks, [own_score_grad, *score_grads], before


def query_gradients(blocks, score_grads, columns, after):
    n = len(blocks)
    rows, width = blocks[0].shape
    return whole_call(
        functools.partial(query_kernel, n),
        "query_gradients",
        [],
        [*blocks, *score_grads],
        [shape((rows, columns))],
        24,
        (2 * n * rows * rows * columns, 16 * rows * columns),
        [],
        after,
    )[0]


def pack_top(top):
    high = jnp.minimum(top, BF16_MAX).astype(BF16).astype(F32)
    rest = top - high
    middle = rest.astype(BF16).astype(F32)
    low = rest - middle
    return (high + pltpu.roll(middle, PACK_LANES, 1) + pltpu.roll(low, 2 * PACK_LANES, 1)).astype(BF16)


def unpack_top(ref, at):
    x = ref[at : at + TOP_ROWS, :].astype(F32)
    total = x + (pltpu.roll(x, TOP_LANES - PACK_LANES, 1) + pltpu.roll(x, TOP_LANES - 2 * PACK_LANES, 1))
    lane = lax.broadcasted_iota(jnp.int32, x.shape, 1)
    return jnp.where(lane < PACK_LANES, total, 0.0)


def tile_of(step, me_dp, bits, flip):
    mask = flip
    for j in range(1, bits):
        if not (step >> (bits - 1 - j)) & 1:
            mask |= 1 << j
    return me_dp ^ mask


def reversed_step(step, bits):
    return sum(((step >> (bits - 1 - j)) & 1) << (j - 1) for j in range(1, bits))


def corrected_tile(chosen, dest, grads, a_ref, e_ref, top_ref):
    _, n_ctx, sets, rows_set, rows = a_ref.shape
    tall = n_ctx * rows_set
    a = a_ref[dest, :, chosen].reshape(tall, rows)
    e = e_ref[dest, :, chosen].reshape(tall, e_ref.shape[4])
    c = jnp.dot(a, grads, preferred_element_type=F32) + e

    mags = jnp.max(jnp.abs(c).reshape(tall // QROWS, QROWS, c.shape[1]), axis=1)
    mags = jnp.max(mags, axis=1, keepdims=True)
    per_set = rows_set // QROWS
    block = lax.broadcasted_iota(jnp.int32, (tall // QROWS, TOP_LANES), 0)
    lane = lax.broadcasted_iota(jnp.int32, (tall // QROWS, TOP_LANES), 1)
    shift = per_set.bit_length() - 1
    place = ((block >> shift) * (sets * per_set)) + chosen * per_set + (block & (per_set - 1))
    top = jnp.max(jnp.where(lane == place, mags, 0.0), axis=0, keepdims=True)
    top_ref[pl.ds(dest, 1), :] = jnp.maximum(top_ref[pl.ds(dest, 1), :], top)
    return c


def first_send_kernel(bits, shrink, n_parts, me_ref, own_ref, *refs):
    part_refs = refs[:n_parts]
    a_ref, e_ref, out_ref, top_ref, kg_ref, vg_ref, grads_ref = refs[n_parts:]
    total = own_ref[...]
    for part in part_refs:
        total = total + part[...].astype(F32)
    total = total.astype(BF16)
    hd = total.shape[1] // 2
    kg_ref[...] = total[:, :hd]
    vg_ref[...] = total[:, hd:]
    grads_ref[...] = total
    top_ref[...] = jnp.zeros_like(top_ref)
    send_rows(bits, shrink, 0, me_ref, total, a_ref, e_ref, out_ref, top_ref)


def next_send_kernel(bits, shrink, chosen, me_ref, grads_ref, before_ref, a_ref, e_ref, out_ref, top_ref):
    top_ref[...] = before_ref[...]
    send_rows(bits, shrink, chosen, me_ref, grads_ref[...], a_ref, e_ref, out_ref, top_ref)


def send_rows(bits, shrink, chosen, me_ref, total, a_ref, e_ref, out_ref, top_ref):
    for step in range(out_ref.shape[0]):
        dest = tile_of(step, me_ref[0], bits, 1)
        c = corrected_tile(chosen, dest, total, a_ref, e_ref, top_ref)
        out_ref[step] = (c * shrink).astype(BF16)


def keep_kernel(bits, shrink, chosen, me_ref, grads, got_ref, before_ref, a_ref, e_ref, *outs):
    low_away, low_stay, high_away, high_stay, top_ref = outs
    steps, tall, width = got_ref.shape
    half = steps // 2
    hd = width // 2
    total = grads[...]
    top_ref[...] = before_ref[...]
    for step in range(steps):
        dest = tile_of(step, me_ref[0], bits, 0)
        c = corrected_tile(chosen, dest, total, a_ref, e_ref, top_ref)
        c = (c * shrink + got_ref[step].astype(F32)).astype(BF16)
        back = reversed_step(step, bits)
        for at, part, away, stay in ((step, c[:, :hd], low_away, low_stay), (back, c[:, hd:], high_away, high_stay)):
            if at < half:
                away[at * tall : (at + 1) * tall, :] = part
            else:
                stay[(at - half) * tall : (at - half + 1) * tall, :] = part
    if low_away.shape[0] > half * tall:
        low_away[half * tall :, :] = pack_top(top_ref[...])


def largest(tops, low_got, size):
    found = [top[...] for top in tops]
    if low_got.shape[0] > size:
        found.append(unpack_top(low_got, size))
    return functools.reduce(jnp.maximum, found)


def add_kernel(n_tops, low, low_got, high, high_got, *refs):
    tops = refs[:n_tops]
    low_away, low_stay, high_away, high_stay, *top_out = refs[n_tops:]
    size = low.shape[0]
    half = size // 2
    for mine, got, away, stay in ((low, low_got, low_away, low_stay), (high, high_got, high_away, high_stay)):
        away[:half, :] = (mine[:half, :].astype(F32) + got[:half, :].astype(F32)).astype(BF16)
        stay[...] = (mine[half:, :].astype(F32) + got[half:size, :].astype(F32)).astype(BF16)
    if tops:
        top = largest(tops, low_got, size)
        top_out[0][...] = top
        if low_away.shape[0] > half:
            low_away[half:, :] = pack_top(top)


def last_kernel(n_ctx, n_tops, me_ref, low, low_got, high, high_got, *refs):
    tops = refs[:n_tops]
    outs, top_out = refs[n_tops : n_tops + n_ctx], refs[n_tops + n_ctx :]
    size, hd = low.shape
    rows_set = size // n_ctx
    if tops:
        top = largest(tops, low_got, size)
        top_out[0][...] = top
        packed = pack_top(top)
    for b in range(n_ctx):
        part = pl.ds(pl.multiple_of((me_ref[0] ^ b) * rows_set, rows_set), rows_set)
        for at, mine, got in ((0, low, low_got), (rows_set, high, high_got)):
            total = mine[part, :].astype(F32) + got[part, :].astype(F32)
            outs[b][at : at + rows_set, :] = total.astype(outs[b].dtype)
        if b > 0 and tops:
            outs[b][2 * rows_set :, :] = packed


def final_kernel(sets, n_ctx, gain, me_dp_ref, me_ctx_ref, *refs):
    groups = [refs[chosen * n_ctx : (chosen + 1) * n_ctx] for chosen in range(sets)]
    top_ref, out_ref, scale_ref, all_tops = refs[sets * n_ctx :]
    n_dp, lanes = scale_ref.shape
    rows_set, hd = groups[0][0].shape[0] // 2, groups[0][0].shape[1]
    scale = top_ref[...]
    for other in groups[-1][1:]:
        scale = jnp.maximum(scale, unpack_top(other, 2 * rows_set))
    scale = scale + 1e-06
    all_tops[...] = scale
    scale_ref[...] = scale[:n_dp, :lanes]
    factors = gain / all_tops[pl.ds(me_dp_ref[0], 1), :]
    lane = lax.broadcasted_iota(jnp.int32, factors.shape, 1)
    per_set = rows_set // QROWS
    first = me_ctx_ref[0] * (sets * per_set)
    for chosen, group in enumerate(groups):
        for r in range(per_set):
            mine = jnp.where(lane == first + (chosen * per_set + r), factors, 0.0)
            factor = jnp.sum(mine, axis=1, keepdims=True)
            at = chosen * rows_set + r * QROWS
            for h in range(2):
                part = slice(h * rows_set + r * QROWS, h * rows_set + (r + 1) * QROWS)
                total = group[0][part, :]
                for other in group[1:]:
                    total = total + other[part, :].astype(F32)
                out_ref[at : at + QROWS, h * hd : (h + 1) * hd] = total * factor


def local(n_dp, n_ctx, sets, span_order, queries, keys, values, out_grad, activations, error_feedback):
    rows, hd = keys.shape
    width = 2 * hd
    model = activations.shape[1]
    rows_set = model // (n_dp * n_ctx * sets)
    tall = n_ctx * rows_set
    me_dp = lax.axis_index("dp").astype(jnp.int32)[None]
    me_ctx = lax.axis_index("context").astype(jnp.int32)[None]
    bits = n_dp.bit_length() - 1

    def swap_dp(x, mask):
        return lax.ppermute(x, "dp", xor_perm(n_dp, mask))

    def swap_ctx(x, mask):
        return lax.ppermute(x, "context", xor_perm(n_ctx, mask))

    pairs = load_call(join_kernel, "join_keys_values", [keys, values], [shape((rows, width))], 4)[0]
    own, parts, blocks, score_grads, last_part = attention(
        me_ctx, span_order[0], queries, out_grad, pairs, swap_ctx, n_ctx
    )
    acts, errors = prepare(activations, error_feedback[0, 0], last_part)

    shrink = 1.0 / (n_dp * n_ctx)
    acts = acts.reshape(n_dp, n_ctx, sets, rows_set, rows)
    errors = errors.reshape(n_dp, n_ctx, sets, rows_set, width)
    tops = shape((TOP_ROWS, TOP_LANES), F32)
    steps = n_dp // 2
    cost = (2 * steps * tall * rows * width, steps * tall * (2 * rows + 6 * width))
    message = shape((steps, tall, width))
    got = []
    for chosen in range(sets):
        if chosen == 0:
            out, top, key_grad, value_grad, grads = whole_call(
                functools.partial(first_send_kernel, bits, shrink, n_ctx - 1),
                "send_tiles",
                [me_dp],
                [own, *parts, acts, errors],
                [message, tops, shape((rows, hd)), shape((rows, hd)), shape((rows, width))],
                28,
                cost,
            )
        else:
            out, top = whole_call(
                functools.partial(next_send_kernel, bits, shrink, chosen),
                "send_tiles",
                [me_dp],
                [grads, top, acts, errors],
                [message, tops],
                28,
                cost,
            )
        got.append(swap_dp(out, 1))

    halves = []
    for chosen in range(sets):
        half = steps // 2 * tall
        extra = TOP_ROWS if chosen == sets - 1 else 0
        *arrays, top = whole_call(
            functools.partial(keep_kernel, bits, shrink, chosen),
            "keep_tiles",
            [me_dp],
            [grads, got[chosen], top, acts, errors],
            [shape((half + extra, hd))] + [shape((half, hd))] * 3 + [tops],
            28,
            cost,
        )
        halves.append(arrays)

    gathered = [top, swap_dp(top, 1), swap_dp(top, 3)]
    query_grad = query_gradients(blocks, score_grads, queries.shape[1], [top])
    groups = []
    for chosen in range(sets):
        low_away, low, high_away, high = halves[chosen]
        extra = TOP_ROWS if chosen == sets - 1 else 0
        for stage in range(1, bits):
            low_got = swap_dp(low_away, 1 << stage)
            high_got = swap_dp(high_away, 1 << (bits - stage))
            with_tops = extra > 0 or (chosen == 0 and stage == 1)
            operands = [low, low_got, high, high_got] + (gathered if with_tops else [])
            n_tops = len(operands) - 4
            size = low.shape[0]
            cost = (4 * size * hd, 12 * size * hd)
            if stage < bits - 1:
                low_away, low, high_away, high, *top_out = whole_call(
                    functools.partial(add_kernel, n_tops),
                    "add_stage",
                    [],
                    operands,
                    [shape((size // 2 + extra, hd))] + [shape((size // 2, hd))] * 3 + [tops] * with_tops,
                    16,
                    cost,
                    after=[query_grad] if chosen == 0 and stage == 1 else [],
                )
            else:
                outs = whole_call(
                    functools.partial(last_kernel, n_ctx, n_tops),
                    "last_stage",
                    [me_ctx],
                    operands,
                    [shape((2 * rows_set, hd), F32)]
                    + [shape((2 * rows_set + extra, hd))] * (n_ctx - 1)
                    + [tops] * with_tops,
                    16,
                    cost,
                )
                mine, away, top_out = outs[0], outs[1:n_ctx], outs[n_ctx:]
            if with_tops:
                gathered = list(top_out)
        groups.append([mine] + [swap_ctx(away[b - 1], b) for b in range(n_ctx - 1, 0, -1)])
    payload, scale = whole_call(
        functools.partial(final_kernel, sets, n_ctx, 7.0 / shrink),
        "final_stage",
        [me_dp, me_ctx],
        [x for group in groups for x in group] + gathered,
        [shape((sets * rows_set, width), F32), shape((n_dp, sets * tall // QROWS), F32)],
        8,
        (4 * sets * tall * width, 16 * sets * rows_set * width),
        [pltpu.VMEM((TOP_ROWS, TOP_LANES), F32)],
    )
    return query_grad, key_grad, value_grad, payload, scale.reshape(-1)


def solution(mesh):
    tokens = P(("dp", "context"), None)
    return jax.shard_map(
        functools.partial(local, mesh.shape["dp"], mesh.shape["context"], 2),
        mesh=mesh,
        in_specs=(P("dp", None), tokens, tokens, tokens, tokens, tokens, P("dp", "context", None, None)),
        out_specs=(tokens, tokens, tokens, tokens, P()),
        check_vma=False,
    )
```

```python
import functools

import jax
import jax.numpy as jnp
from jax import lax
from jax.experimental import pallas as pl
from jax.experimental.pallas import tpu as pltpu
from jax.sharding import PartitionSpec as P

QROWS = 32
LOG2E = 1.4426950408889634
FAR = 1e30
MIB = 1024 * 1024
CHUNK = 256
TOP_ROWS, TOP_LANES, PACK_LANES = 16, 128, 32
BF16, F32 = jnp.bfloat16, jnp.float32
BF16_MAX = float(jnp.finfo(jnp.bfloat16).max)
NT = (((1,), (1,)), ((), ()))
TN = (((0,), (0,)), ((), ()))


def xor_perm(size, mask):
    return [(i, i ^ mask) for i in range(size)]


def whole(x):
    return pl.BlockSpec(x.shape, lambda *_: (0,) * len(x.shape))


def shape(dims, dtype=BF16):
    return jax.ShapeDtypeStruct(dims, dtype)


def whole_call(kernel, name, scalars, operands, out_shape, mib, cost, scratch=(), after=()):
    def body(*refs):
        first = len(scalars) + len(operands)
        kernel(*refs[:first], *refs[first + len(after) :])

    return pl.pallas_call(
        body,
        grid_spec=pltpu.PrefetchScalarGridSpec(
            num_scalar_prefetch=len(scalars),
            grid=(1,),
            in_specs=[whole(x) for x in operands] + [pl.BlockSpec(memory_space=pl.ANY)] * len(after),
            out_specs=[whole(x) for x in out_shape],
            scratch_shapes=list(scratch),
        ),
        out_shape=out_shape,
        compiler_params=pltpu.CompilerParams(vmem_limit_bytes=mib * MIB),
        cost_estimate=pl.CostEstimate(flops=cost[0], bytes_accessed=cost[1], transcendentals=0),
        name=name,
    )(*scalars, *operands, *after)


def copy_all(pairs_of_refs, sems):
    copies = [pltpu.make_async_copy(src, dst, sems.at[i]) for i, (src, dst) in enumerate(pairs_of_refs)]
    for copy in copies:
        copy.start()
    for copy in copies:
        copy.wait()


def join_kernel(k_hbm, v_hbm, out_ref, sems):
    hd = k_hbm.shape[1]
    copy_all([(k_hbm, out_ref.at[:, pl.ds(0, hd)]), (v_hbm, out_ref.at[:, pl.ds(hd, hd)])], sems)


def load_call(kernel, name, operands, out_shape, mib):
    return pl.pallas_call(
        kernel,
        in_specs=[pl.BlockSpec(memory_space=pltpu.HBM)] * 2,
        out_specs=[pl.BlockSpec(memory_space=pltpu.VMEM)] * len(out_shape),
        out_shape=out_shape,
        scratch_shapes=[pltpu.SemaphoreType.DMA((2,))],
        compiler_params=pltpu.CompilerParams(vmem_limit_bytes=mib * MIB),
        cost_estimate=pl.CostEstimate(flops=0, bytes_accessed=4 * operands[0].size, transcendentals=0),
        name=name,
    )(*operands)


def prepare_kernel(pieces, a_hbm, e_hbm, _, a_out, e_out, a_buf, a_sems, e_sems):
    model = a_buf.shape[1]
    tile = model // pieces
    parts = [pl.ds(i * tile, tile) for i in range(pieces)]
    a_copies = [pltpu.make_async_copy(a_hbm.at[:, p], a_buf.at[:, p], a_sems.at[i]) for i, p in enumerate(parts)]
    e_copies = [pltpu.make_async_copy(e_hbm.at[p, :], e_out.at[p, :], e_sems.at[i]) for i, p in enumerate(parts)]
    for copy in a_copies + e_copies:
        copy.start()
    for copy, part in zip(a_copies, parts):
        copy.wait()
        a_out[part, :] = a_buf[:, part].T
    for copy in e_copies:
        copy.wait()


def prepare(activations, errors, after):
    rows, model = activations.shape
    pieces = 8
    hbm = pl.BlockSpec(memory_space=pltpu.HBM)
    outs = [shape((model, rows)), shape(errors.shape, F32)]
    return pl.pallas_call(
        functools.partial(prepare_kernel, pieces),
        in_specs=[hbm, hbm, pl.BlockSpec(memory_space=pl.ANY)],
        out_specs=[pl.BlockSpec(memory_space=pltpu.VMEM)] * 2,
        out_shape=outs,
        scratch_shapes=[
            pltpu.VMEM((rows, model), BF16),
            pltpu.SemaphoreType.DMA((pieces,)),
            pltpu.SemaphoreType.DMA((pieces,)),
        ],
        compiler_params=pltpu.CompilerParams(vmem_limit_bytes=24 * MIB),
        cost_estimate=pl.CostEstimate(
            flops=0, bytes_accessed=2 * rows * model + 4 * errors.size, transcendentals=0
        ),
        name="prepare",
    )(activations, errors, *after)


def key_value(ref):
    hd = ref.shape[1] // 2
    return ref[:, :hd], ref[:, hd:]


def head_pair(ref, i, hd):
    at = i * (2 * hd)
    first = ref[:, pl.ds(pl.multiple_of(at, hd), hd)]
    second = ref[:, pl.ds(pl.multiple_of(at + hd, hd), hd)]
    return jnp.concatenate([first, second], axis=0)


def score_chunk(k, v, q, do, own, first_lane):
    s = lax.dot_general(k, q, NT, preferred_element_type=F32)
    dp = lax.dot_general(v, do, NT, preferred_element_type=F32)
    if own:
        rows = k.shape[0]
        key_at = lax.broadcasted_iota(jnp.int32, s.shape, 0)
        query_at = lax.broadcasted_iota(jnp.int32, s.shape, 1) + first_lane
        query_at = jnp.where(query_at >= rows, query_at - rows, query_at)
        s = jnp.where(key_at <= query_at, s, -FAR)
    return s, dp


def counted(b, flags):
    lane = lax.broadcasted_iota(jnp.int32, flags.shape, 1)
    return jnp.max(jnp.where(lane == b, flags[...], 0.0)) > 0.5


def stats_of_block(b, q_ref, do_ref, kv, before, out):
    k, v = key_value(kv)
    rows, hd = k.shape
    pair = 2 * rows
    factor = LOG2E / hd**0.5

    def heads(i, carry):
        q, do = head_pair(q_ref, i, hd), head_pair(do_ref, i, hd)
        for t in range(pair // CHUNK):
            part = slice(t * CHUNK, (t + 1) * CHUNK)
            lanes = pl.ds(pl.multiple_of(i * pair + t * CHUNK, CHUNK), CHUNK)
            s, dp = score_chunk(k, v, q[part], do[part], b == 0, t * CHUNK)
            top = jnp.max(s, axis=0, keepdims=True) * factor
            e = jnp.exp2(s * factor - top)
            total = jnp.sum(e, axis=0, keepdims=True)
            weighted = jnp.sum(e * dp, axis=0, keepdims=True)
            if b > 0:
                old = before[0:1, lanes]
                both = jnp.maximum(old, top)
                old_part, new_part = jnp.exp2(old - both), jnp.exp2(top - both)
                total = before[1:2, lanes] * old_part + total * new_part
                weighted = before[2:3, lanes] * old_part + weighted * new_part
                top = both
            out[0:1, lanes] = top
            out[1:2, lanes] = total
            out[2:3, lanes] = weighted
        return carry

    lax.fori_loop(0, q_ref.shape[1] // (2 * hd), heads, 0, unroll=True)


def first_stats_kernel(n, me_ref, span_ref, q_ref, do_ref, kv, out, q_out, do_out, flags):
    me = me_ref[0]
    lane = lax.broadcasted_iota(jnp.int32, flags.shape, 1)
    found = jnp.zeros(flags.shape, F32)
    for b in range(1, n):
        found = jnp.where((lane == b) & (span_ref[me ^ b] < span_ref[me]), 1.0, found)
    flags[...] = found
    q_out[...] = q_ref[...]
    do_out[...] = do_ref[...]
    stats_of_block(0, q_ref, do_ref, kv, None, out)


def next_stats_kernel(b, flags, q_ref, do_ref, kv, before, out):
    keep = counted(b, flags)

    @pl.when(keep)
    def _():
        stats_of_block(b, q_ref, do_ref, kv, before, out)

    @pl.when(jnp.logical_not(keep))
    def _():
        out[...] = before[...]


def block_gradients(own, stats, q_ref, do_ref, kv, p_buf, ds_ref, dk, dv):
    k, v = key_value(kv)
    rows, hd = k.shape
    pair = 2 * rows
    factor = LOG2E / hd**0.5
    dk[...] = jnp.zeros_like(dk)
    dv[...] = jnp.zeros_like(dv)

    def heads(i, carry):
        q, do = head_pair(q_ref, i, hd), head_pair(do_ref, i, hd)
        for t in range(pair // CHUNK):
            part = slice(t * CHUNK, (t + 1) * CHUNK)
            lanes = pl.ds(pl.multiple_of(i * pair + t * CHUNK, CHUNK), CHUNK)
            s, dp = score_chunk(k, v, q[part], do[part], own, t * CHUNK)
            total = stats[1:2, lanes]
            level = stats[0:1, lanes] + jnp.log(total) * LOG2E
            p = jnp.exp2(s * factor - level)
            p_buf[:, part] = p.astype(BF16)
            ds = (p * (dp - stats[2:3, lanes] / total)).astype(BF16)
            ds_ref[:, lanes] = ds
        ds = ds_ref[:, pl.ds(pl.multiple_of(i * pair, CHUNK), pair)]
        dk[...] += jnp.dot(ds, q, preferred_element_type=F32)
        dv[...] += jnp.dot(p_buf[...], do, preferred_element_type=F32)
        return carry

    lax.fori_loop(0, q_ref.shape[1] // (2 * hd), heads, 0, unroll=True)
    inverse = 1.0 / hd**0.5
    return dk[...] * inverse, dv[...]


def other_kernel(b, flags, stats, q_ref, do_ref, kv, out_ref, ds_out, p_buf, dk, dv):
    keep = counted(b, flags)
    rows, hd = dk.shape

    @pl.when(keep)
    def _():
        dk_sum, dv_sum = block_gradients(False, stats, q_ref, do_ref, kv, p_buf, ds_out, dk, dv)
        out_ref[:, :hd] = dk_sum.astype(BF16)
        out_ref[:, hd:] = dv_sum.astype(BF16)

    @pl.when(jnp.logical_not(keep))
    def _():
        out_ref[...] = jnp.zeros_like(out_ref)
        ds_out[...] = jnp.zeros_like(ds_out)


def own_kernel(stats, q_ref, do_ref, kv, out_ref, ds_out, p_buf, dk, dv):
    hd = dk.shape[1]
    dk_sum, dv_sum = block_gradients(True, stats, q_ref, do_ref, kv, p_buf, ds_out, dk, dv)
    out_ref[:, :hd] = dk_sum
    out_ref[:, hd:] = dv_sum


def query_kernel(n, *refs):
    kv_refs, ds_refs, dq_ref, mark_ref = refs[:n], refs[n : 2 * n], refs[2 * n], refs[2 * n + 1]
    mark_ref[...] = jnp.zeros_like(mark_ref)
    rows, hd = kv_refs[0].shape[0], kv_refs[0].shape[1] // 2
    for h in range(dq_ref.shape[1] // hd):
        dq = 0.0
        for kv, ds in zip(kv_refs, ds_refs):
            part = ds[:, h * rows : (h + 1) * rows]
            dq = dq + lax.dot_general(part, kv[:, :hd], TN, preferred_element_type=F32)
        dq_ref[:, h * hd : (h + 1) * hd] = (dq / hd**0.5).astype(BF16)


def attention(me, spans, queries, out_grad, pairs, swap, n):
    rows, hd = pairs.shape[0], pairs.shape[1] // 2
    columns = queries.shape[1]
    tall = columns // hd * rows
    product = 2 * rows * tall * hd
    cost = (4 * product, 8 * rows * columns)

    blocks = [pairs]
    for b in range(1, n):
        blocks.append(swap(blocks[b & (b - 1)], b & -b))
    stats_shape = shape((8, tall), F32)
    stats, queries, out_grad, flags = whole_call(
        functools.partial(first_stats_kernel, n),
        "first_stats",
        [me, spans],
        [queries, out_grad, pairs],
        [stats_shape, shape(queries.shape), shape(out_grad.shape), shape((8, 128), F32)],
        14,
        cost,
    )
    for b in range(1, n):
        stats = whole_call(
            functools.partial(next_stats_kernel, b),
            "next_stats",
            [],
            [flags, queries, out_grad, blocks[b], stats],
            [stats_shape],
            12,
            cost,
            [],
            blocks[2:3] if b == 1 else [],
        )[0]
    received = blocks[1:]
    p_buf = pltpu.VMEM((rows, 2 * rows), BF16)
    sums = [pltpu.VMEM((rows, hd), F32)] * 2
    parts, score_grads, before = [None] * (n - 1), [None] * (n - 1), []
    for b in range(n - 1, 0, -1):
        part, score_grads[b - 1] = whole_call(
            functools.partial(other_kernel, b),
            "block_gradients",
            [],
            [flags, stats, queries, out_grad, received[b - 1]],
            [shape((rows, 2 * hd)), shape((rows, tall))],
            14,
            (8 * product, 16 * rows * columns),
            [p_buf, *sums],
            before,
        )
        parts[b - 1] = swap(part, b)
        before = [part]
    own, own_score_grad = whole_call(
        own_kernel,
        "own_gradients",
        [],
        [stats, queries, out_grad, pairs],
        [shape((rows, 2 * hd), F32), shape((rows, tall))],
        14,
        (8 * product, 16 * rows * columns),
        [p_buf, *sums],
        before,
    )
    return own, parts, blocks, [own_score_grad, *score_grads], before


def query_gradients(blocks, score_grads, columns, after):
    n = len(blocks)
    rows, width = blocks[0].shape
    return whole_call(
        functools.partial(query_kernel, n),
        "query_gradients",
        [],
        [*blocks, *score_grads],
        [shape((rows, columns)), shape((8, 128), F32)],
        5 + 3 * n,
        (2 * n * rows * rows * columns, 16 * rows * columns),
        [],
        after,
    )


def pack_top(top):
    high = jnp.minimum(top, BF16_MAX).astype(BF16).astype(F32)
    rest = top - high
    middle = rest.astype(BF16).astype(F32)
    low = rest - middle
    return (high + pltpu.roll(middle, PACK_LANES, 1) + pltpu.roll(low, 2 * PACK_LANES, 1)).astype(BF16)


def unpack_top(ref, at):
    x = ref[at : at + TOP_ROWS, :TOP_LANES].astype(F32)
    total = x + (pltpu.roll(x, TOP_LANES - PACK_LANES, 1) + pltpu.roll(x, TOP_LANES - 2 * PACK_LANES, 1))
    lane = lax.broadcasted_iota(jnp.int32, x.shape, 1)
    return jnp.where(lane < PACK_LANES, total, 0.0)


def tile_of(step, me_dp, bits, flip):
    mask = flip
    for j in range(1, bits):
        if not (step >> (bits - 1 - j)) & 1:
            mask |= 1 << j
    return me_dp ^ mask


def reversed_step(step, bits):
    return sum(((step >> (bits - 1 - j)) & 1) << (j - 1) for j in range(1, bits))


def corrected_tile(chosen, dest, grads, a_ref, e_ref, top_ref):
    _, n_ctx, sets, rows_set, rows = a_ref.shape
    tall = n_ctx * rows_set
    a = a_ref[dest, :, chosen].reshape(tall, rows)
    e = e_ref[dest, :, chosen].reshape(tall, e_ref.shape[4])
    c = jnp.dot(a, grads, preferred_element_type=F32) + e

    mags = jnp.max(jnp.abs(c).reshape(tall // QROWS, QROWS, c.shape[1]), axis=1)
    mags = jnp.max(mags, axis=1, keepdims=True)
    per_set = rows_set // QROWS
    block = lax.broadcasted_iota(jnp.int32, (tall // QROWS, TOP_LANES), 0)
    lane = lax.broadcasted_iota(jnp.int32, (tall // QROWS, TOP_LANES), 1)
    shift = per_set.bit_length() - 1
    place = ((block >> shift) * (sets * per_set)) + chosen * per_set + (block & (per_set - 1))
    top = jnp.max(jnp.where(lane == place, mags, 0.0), axis=0, keepdims=True)
    top_ref[pl.ds(dest, 1), :] = jnp.maximum(top_ref[pl.ds(dest, 1), :], top)
    return c


def send_rows(bits, shrink, chosen, me_ref, total, a_ref, e_ref, out_ref, top_ref, packed):
    tall = a_ref.shape[1] * a_ref.shape[3]
    steps = a_ref.shape[0] // 2
    for step in range(steps):
        dest = tile_of(step, me_ref[0], bits, 1)
        c = corrected_tile(chosen, dest, total, a_ref, e_ref, top_ref)
        out_ref[step * tall : (step + 1) * tall, :] = (c * shrink).astype(BF16)
    if packed:
        out_ref[steps * tall :, :TOP_LANES] = pack_top(top_ref[...])
        out_ref[steps * tall :, TOP_LANES:] = jnp.zeros((TOP_ROWS, out_ref.shape[1] - TOP_LANES), BF16)


def first_send_kernel(bits, shrink, n_parts, me_ref, own_ref, *refs):
    part_refs = refs[:n_parts]
    a_ref, e_ref, out_ref, top_ref, kg_ref, vg_ref, grads_ref = refs[n_parts:]
    total = own_ref[...]
    for part in part_refs:
        total = total + part[...].astype(F32)
    total = total.astype(BF16)
    hd = total.shape[1] // 2
    kg_ref[...] = total[:, :hd]
    vg_ref[...] = total[:, hd:]
    grads_ref[...] = total
    top_ref[...] = jnp.zeros_like(top_ref)
    send_rows(bits, shrink, 0, me_ref, total, a_ref, e_ref, out_ref, top_ref, False)


def next_send_kernel(bits, shrink, chosen, packed, me_ref, grads_ref, before_ref, a_ref, e_ref, out_ref, top_ref):
    top_ref[...] = before_ref[...]
    send_rows(bits, shrink, chosen, me_ref, grads_ref[...], a_ref, e_ref, out_ref, top_ref, packed)


def kept_kernel(bits, shrink, me_ref, grads_ref, before_ref, a_ref, e_ref, *outs):
    *kept, top_ref = outs
    top_ref[...] = before_ref[...]
    total = grads_ref[...]
    for chosen, out_ref in enumerate(kept):
        for step in range(out_ref.shape[0]):
            dest = tile_of(step, me_ref[0], bits, 0)
            out_ref[step] = corrected_tile(chosen, dest, total, a_ref, e_ref, top_ref) * shrink


def split_kernel(bits, n_tops, kept, got, *refs):
    steps, tall, width = kept.shape
    half = steps // 2
    hd = width // 2
    tops = refs[:n_tops]
    low_away, low_stay, high_away, high_stay, *top_out = refs[n_tops:]
    for step in range(steps):
        c = (kept[step] + got[step * tall : (step + 1) * tall, :].astype(F32)).astype(BF16)
        back = reversed_step(step, bits)
        for at, part, away, stay in ((step, c[:, :hd], low_away, low_stay), (back, c[:, hd:], high_away, high_stay)):
            if at < half:
                away[at * tall : (at + 1) * tall, :] = part
            else:
                stay[(at - half) * tall : (at - half + 1) * tall, :] = part
    if tops:
        top = largest(tops, got, steps * tall)
        top_out[0][...] = top
        low_away[half * tall :, :] = pack_top(top)


def largest(tops, low_got, size):
    found = [top[...] for top in tops]
    if low_got.shape[0] > size:
        found.append(unpack_top(low_got, size))
    return functools.reduce(jnp.maximum, found)


def add_kernel(n_tops, low, low_got, high, high_got, *refs):
    tops = refs[:n_tops]
    low_away, low_stay, high_away, high_stay, *top_out = refs[n_tops:]
    size = low.shape[0]
    half = size // 2
    for mine, got, away, stay in ((low, low_got, low_away, low_stay), (high, high_got, high_away, high_stay)):
        away[:half, :] = (mine[:half, :].astype(F32) + got[:half, :].astype(F32)).astype(BF16)
        stay[...] = (mine[half:, :].astype(F32) + got[half:size, :].astype(F32)).astype(BF16)
    if tops:
        top = largest(tops, low_got, size)
        top_out[0][...] = top
        if low_away.shape[0] > half:
            low_away[half:, :] = pack_top(top)


def last_kernel(n_ctx, n_tops, me_ref, low, low_got, high, high_got, *refs):
    tops = refs[:n_tops]
    outs, top_out = refs[n_tops : n_tops + n_ctx], refs[n_tops + n_ctx :]
    size, hd = low.shape
    rows_set = size // n_ctx
    if tops:
        top = largest(tops, low_got, size)
        top_out[0][...] = top
        packed = pack_top(top)
    for b in range(n_ctx):
        part = pl.ds(pl.multiple_of((me_ref[0] ^ b) * rows_set, rows_set), rows_set)
        for at, mine, got in ((0, low, low_got), (rows_set, high, high_got)):
            total = mine[part, :].astype(F32) + got[part, :].astype(F32)
            outs[b][at : at + rows_set, :] = total.astype(outs[b].dtype)
        if b > 0 and tops:
            outs[b][2 * rows_set :, :] = packed


def final_kernel(sets, n_ctx, gain, me_dp_ref, me_ctx_ref, *refs):
    groups = [refs[chosen * n_ctx : (chosen + 1) * n_ctx] for chosen in range(sets)]
    top_ref, out_ref, scale_ref, all_tops = refs[sets * n_ctx :]
    n_dp, lanes = scale_ref.shape
    rows_set, hd = groups[0][0].shape[0] // 2, groups[0][0].shape[1]
    scale = top_ref[...]
    for other in groups[-1][1:]:
        scale = jnp.maximum(scale, unpack_top(other, 2 * rows_set))
    scale = scale + 1e-06
    all_tops[...] = scale
    scale_ref[...] = scale[:n_dp, :lanes]
    factors = gain / all_tops[pl.ds(me_dp_ref[0], 1), :]
    lane = lax.broadcasted_iota(jnp.int32, factors.shape, 1)
    per_set = rows_set // QROWS
    first = me_ctx_ref[0] * (sets * per_set)
    for chosen, group in enumerate(groups):
        for r in range(per_set):
            mine = jnp.where(lane == first + (chosen * per_set + r), factors, 0.0)
            factor = jnp.sum(mine, axis=1, keepdims=True)
            at = chosen * rows_set + r * QROWS
            for h in range(2):
                part = slice(h * rows_set + r * QROWS, h * rows_set + (r + 1) * QROWS)
                total = group[0][part, :]
                for other in group[1:]:
                    total = total + other[part, :].astype(F32)
                out_ref[at : at + QROWS, h * hd : (h + 1) * hd] = total * factor


def local(n_dp, n_ctx, sets, span_order, queries, keys, values, out_grad, activations, error_feedback):
    rows, hd = keys.shape
    width = 2 * hd
    model = activations.shape[1]
    rows_set = model // (n_dp * n_ctx * sets)
    tall = n_ctx * rows_set
    me_dp = lax.axis_index("dp").astype(jnp.int32)[None]
    me_ctx = lax.axis_index("context").astype(jnp.int32)[None]
    bits = n_dp.bit_length() - 1

    def swap_dp(x, mask):
        return lax.ppermute(x, "dp", xor_perm(n_dp, mask))

    def swap_ctx(x, mask):
        return lax.ppermute(x, "context", xor_perm(n_ctx, mask))

    pairs = load_call(join_kernel, "join_keys_values", [keys, values], [shape((rows, width))], 4)[0]
    own, parts, blocks, score_grads, last_part = attention(
        me_ctx, span_order[0], queries, out_grad, pairs, swap_ctx, n_ctx
    )
    acts, errors = prepare(activations, error_feedback[0, 0], last_part)

    shrink = 1.0 / (n_dp * n_ctx)
    acts = acts.reshape(n_dp, n_ctx, sets, rows_set, rows)
    errors = errors.reshape(n_dp, n_ctx, sets, rows_set, width)
    tops = shape((TOP_ROWS, TOP_LANES), F32)
    steps = n_dp // 2
    cost = (2 * steps * tall * rows * width, steps * tall * (2 * rows + 6 * width))
    out, top, key_grad, value_grad, grads = whole_call(
        functools.partial(first_send_kernel, bits, shrink, n_ctx - 1),
        "send_tiles",
        [me_dp],
        [own, *parts, acts, errors],
        [shape((steps * tall, width)), tops, shape((rows, hd)), shape((rows, hd)), shape((rows, width))],
        22,
        cost,
    )
    got = [swap_dp(out, 1)]
    *kept, top = whole_call(
        functools.partial(kept_kernel, bits, shrink),
        "kept_tiles",
        [me_dp],
        [grads, top, acts, errors],
        [shape((steps, tall, width), F32)] * sets + [tops],
        24,
        (sets * cost[0], sets * cost[1]),
    )
    for chosen in range(1, sets):
        extra = TOP_ROWS if chosen == sets - 1 else 0
        out, top = whole_call(
            functools.partial(next_send_kernel, bits, shrink, chosen, extra > 0),
            "send_tiles",
            [me_dp],
            [grads, top, acts, errors],
            [shape((steps * tall + extra, width)), tops],
            22,
            cost,
        )
        got.append(swap_dp(out, 1))

    halves = []
    for chosen in range(sets):
        half = steps // 2 * tall
        last = chosen == sets - 1
        arrays = whole_call(
            functools.partial(split_kernel, bits, int(last)),
            "split_tiles",
            [],
            [kept[chosen], got[chosen]] + [top] * last,
            [shape((half + TOP_ROWS * last, hd))] + [shape((half, hd))] * 3 + [tops] * last,
            10,
            (4 * half * width, 12 * half * width),
        )
        halves.append(arrays[:4])
    gathered = [arrays[4]]
    query_grad, mark = query_gradients(blocks, score_grads, queries.shape[1], [arrays[1]])
    groups = []
    for chosen in range(sets):
        low_away, low, high_away, high = halves[chosen]
        extra = TOP_ROWS if chosen == sets - 1 else 0
        for stage in range(1, bits):
            low_got = swap_dp(low_away, 1 << stage)
            high_got = swap_dp(high_away, 1 << (bits - stage))
            with_tops = extra > 0
            operands = [low, low_got, high, high_got] + (gathered if with_tops else [])
            n_tops = len(operands) - 4
            size = low.shape[0]
            cost = (4 * size * hd, 12 * size * hd)
            if stage < bits - 1:
                low_away, low, high_away, high, *top_out = whole_call(
                    functools.partial(add_kernel, n_tops),
                    "add_stage",
                    [],
                    operands,
                    [shape((size // 2 + extra, hd))] + [shape((size // 2, hd))] * 3 + [tops] * with_tops,
                    8,
                    cost,
                    after=[mark] if chosen == 0 and stage == 1 else [],
                )
            else:
                outs = whole_call(
                    functools.partial(last_kernel, n_ctx, n_tops),
                    "last_stage",
                    [me_ctx],
                    operands,
                    [shape((2 * rows_set, hd), F32)]
                    + [shape((2 * rows_set + extra, hd))] * (n_ctx - 1)
                    + [tops] * with_tops,
                    8,
                    cost,
                )
                mine, away, top_out = outs[0], outs[1:n_ctx], outs[n_ctx:]
            if with_tops:
                gathered = list(top_out)
        groups.append([mine] + [swap_ctx(away[b - 1], b) for b in range(n_ctx - 1, 0, -1)])
    payload, scale = whole_call(
        functools.partial(final_kernel, sets, n_ctx, 7.0 / shrink),
        "final_stage",
        [me_dp, me_ctx],
        [x for group in groups for x in group] + gathered,
        [shape((sets * rows_set, width), F32), shape((n_dp, sets * tall // QROWS), F32)],
        8,
        (4 * sets * tall * width, 16 * sets * rows_set * width),
        [pltpu.VMEM((TOP_ROWS, TOP_LANES), F32)],
    )
    return query_grad, key_grad, value_grad, payload, scale.reshape(-1)


def solution(mesh):
    tokens = P(("dp", "context"), None)
    return jax.shard_map(
        functools.partial(local, mesh.shape["dp"], mesh.shape["context"], 2),
        mesh=mesh,
        in_specs=(P("dp", None), tokens, tokens, tokens, tokens, tokens, P("dp", "context", None, None)),
        out_specs=(tokens, tokens, tokens, tokens, P()),
        check_vma=False,
    )
```

```python
import functools

import jax
import jax.numpy as jnp
from jax import lax
from jax.experimental import pallas as pl
from jax.experimental.pallas import tpu as pltpu
from jax.sharding import PartitionSpec as P

QROWS = 32
LOG2E = 1.4426950408889634
FAR = 1e30
MIB = 1024 * 1024
CHUNK = 256
TOP_ROWS, TOP_LANES, PACK_LANES = 16, 128, 32
BF16, F32 = jnp.bfloat16, jnp.float32
BF16_MAX = float(jnp.finfo(jnp.bfloat16).max)
NT = (((1,), (1,)), ((), ()))
TN = (((0,), (0,)), ((), ()))


def xor_perm(size, mask):
    return [(i, i ^ mask) for i in range(size)]


def whole(x):
    return pl.BlockSpec(x.shape, lambda *_: (0,) * len(x.shape))


def shape(dims, dtype=BF16):
    return jax.ShapeDtypeStruct(dims, dtype)


def whole_call(kernel, name, scalars, operands, out_shape, mib, cost, scratch=(), after=()):
    def body(*refs):
        first = len(scalars) + len(operands)
        kernel(*refs[:first], *refs[first + len(after) :])

    return pl.pallas_call(
        body,
        grid_spec=pltpu.PrefetchScalarGridSpec(
            num_scalar_prefetch=len(scalars),
            grid=(1,),
            in_specs=[whole(x) for x in operands] + [pl.BlockSpec(memory_space=pl.ANY)] * len(after),
            out_specs=[whole(x) for x in out_shape],
            scratch_shapes=list(scratch),
        ),
        out_shape=out_shape,
        compiler_params=pltpu.CompilerParams(vmem_limit_bytes=mib * MIB),
        cost_estimate=pl.CostEstimate(flops=cost[0], bytes_accessed=cost[1], transcendentals=0),
        name=name,
    )(*scalars, *operands, *after)


def begin_kernel(out_ref):
    out_ref[...] = jnp.zeros_like(out_ref)


def begin():
    mark = [shape((8, 128), F32)]
    return whole_call(begin_kernel, "begin", [], [], mark, 4, (20_000_000_000, 0))[0]


def prepare_kernel(pieces, a_ref, a_out):
    tile = a_ref.shape[1] // pieces
    for i in range(pieces):
        a_out[i * tile : (i + 1) * tile, :] = a_ref[:, i * tile : (i + 1) * tile].T


def prepare(activations, after):
    rows, model = activations.shape
    outs = [shape((model, rows))]
    cost = (0, 4 * rows * model)
    kernel = functools.partial(prepare_kernel, 8)
    return whole_call(kernel, "prepare", [], [activations], outs, 16, cost, [], after)[0]


def head_pair(ref, i, hd):
    at = i * (2 * hd)
    first = ref[:, pl.ds(pl.multiple_of(at, hd), hd)]
    second = ref[:, pl.ds(pl.multiple_of(at + hd, hd), hd)]
    return jnp.concatenate([first, second], axis=0)


def score_chunk(k, v, q, do, own, first_lane):
    s = lax.dot_general(k, q, NT, preferred_element_type=F32)
    dp = lax.dot_general(v, do, NT, preferred_element_type=F32)
    if own:
        rows = k.shape[0]
        key_at = lax.broadcasted_iota(jnp.int32, s.shape, 0)
        query_at = lax.broadcasted_iota(jnp.int32, s.shape, 1) + first_lane
        query_at = jnp.where(query_at >= rows, query_at - rows, query_at)
        s = jnp.where(key_at <= query_at, s, -FAR)
    return s, dp


def counted(b, flags):
    lane = lax.broadcasted_iota(jnp.int32, flags.shape, 1)
    return jnp.max(jnp.where(lane == b, flags[...], 0.0)) > 0.5


def stats_of_block(b, q_ref, do_ref, k_ref, v_ref, before, out):
    k, v = k_ref[...], v_ref[...]
    rows, hd = k.shape
    pair = 2 * rows
    factor = LOG2E / hd**0.5

    def heads(i, carry):
        q, do = head_pair(q_ref, i, hd), head_pair(do_ref, i, hd)
        for t in range(pair // CHUNK):
            part = slice(t * CHUNK, (t + 1) * CHUNK)
            lanes = pl.ds(pl.multiple_of(i * pair + t * CHUNK, CHUNK), CHUNK)
            s, dp = score_chunk(k, v, q[part], do[part], b == 0, t * CHUNK)
            top = jnp.max(s, axis=0, keepdims=True) * factor
            e = jnp.exp2(s * factor - top)
            total = jnp.sum(e, axis=0, keepdims=True)
            weighted = jnp.sum(e * dp, axis=0, keepdims=True)
            if b > 0:
                old = before[0:1, lanes]
                both = jnp.maximum(old, top)
                old_part, new_part = jnp.exp2(old - both), jnp.exp2(top - both)
                total = before[1:2, lanes] * old_part + total * new_part
                weighted = before[2:3, lanes] * old_part + weighted * new_part
                top = both
            out[0:1, lanes] = top
            out[1:2, lanes] = total
            out[2:3, lanes] = weighted
        return carry

    lax.fori_loop(0, q_ref.shape[1] // (2 * hd), heads, 0, unroll=True)


def first_stats_kernel(n, me_ref, span_ref, q_ref, do_ref, k_ref, v_ref, out, q_out, do_out, k_out, v_out, flags):
    me = me_ref[0]
    lane = lax.broadcasted_iota(jnp.int32, flags.shape, 1)
    found = jnp.zeros(flags.shape, F32)
    for b in range(1, n):
        found = jnp.where((lane == b) & (span_ref[me ^ b] < span_ref[me]), 1.0, found)
    flags[...] = found
    q_out[...] = q_ref[...]
    do_out[...] = do_ref[...]
    k_out[...] = k_ref[...]
    v_out[...] = v_ref[...]
    stats_of_block(0, q_ref, do_ref, k_ref, v_ref, None, out)


def next_stats_kernel(b, flags, q_ref, do_ref, k_ref, v_ref, before, out):
    keep = counted(b, flags)

    @pl.when(keep)
    def _():
        stats_of_block(b, q_ref, do_ref, k_ref, v_ref, before, out)

    @pl.when(jnp.logical_not(keep))
    def _():
        out[...] = before[...]


def block_gradients(own, stats, q_ref, do_ref, k_ref, v_ref, p_buf, ds_ref, dk, dv):
    k, v = k_ref[...], v_ref[...]
    rows, hd = k.shape
    pair = 2 * rows
    factor = LOG2E / hd**0.5
    dk[...] = jnp.zeros_like(dk)
    dv[...] = jnp.zeros_like(dv)

    def heads(i, carry):
        q, do = head_pair(q_ref, i, hd), head_pair(do_ref, i, hd)
        for t in range(pair // CHUNK):
            part = slice(t * CHUNK, (t + 1) * CHUNK)
            lanes = pl.ds(pl.multiple_of(i * pair + t * CHUNK, CHUNK), CHUNK)
            s, dp = score_chunk(k, v, q[part], do[part], own, t * CHUNK)
            total = stats[1:2, lanes]
            level = stats[0:1, lanes] + jnp.log(total) * LOG2E
            p = jnp.exp2(s * factor - level)
            p_buf[:, part] = p.astype(BF16)
            ds = (p * (dp - stats[2:3, lanes] / total)).astype(BF16)
            ds_ref[:, lanes] = ds
        ds = ds_ref[:, pl.ds(pl.multiple_of(i * pair, CHUNK), pair)]
        dk[...] += jnp.dot(ds, q, preferred_element_type=F32)
        dv[...] += jnp.dot(p_buf[...], do, preferred_element_type=F32)
        return carry

    lax.fori_loop(0, q_ref.shape[1] // (2 * hd), heads, 0, unroll=True)
    inverse = 1.0 / hd**0.5
    return dk[...] * inverse, dv[...]


def other_kernel(b, flags, stats, q_ref, do_ref, k_ref, v_ref, out_ref, ds_out, p_buf, dk, dv):
    keep = counted(b, flags)
    rows, hd = dk.shape

    @pl.when(keep)
    def _():
        dk_sum, dv_sum = block_gradients(False, stats, q_ref, do_ref, k_ref, v_ref, p_buf, ds_out, dk, dv)
        out_ref[:, :hd] = dk_sum.astype(BF16)
        out_ref[:, hd:] = dv_sum.astype(BF16)

    @pl.when(jnp.logical_not(keep))
    def _():
        out_ref[...] = jnp.zeros_like(out_ref)
        ds_out[...] = jnp.zeros_like(ds_out)


def own_kernel(stats, q_ref, do_ref, k_ref, v_ref, out_ref, ds_out, p_buf, dk, dv):
    hd = dk.shape[1]
    dk_sum, dv_sum = block_gradients(True, stats, q_ref, do_ref, k_ref, v_ref, p_buf, ds_out, dk, dv)
    out_ref[:, :hd] = dk_sum
    out_ref[:, hd:] = dv_sum


def query_kernel(n, *refs):
    k_refs, ds_refs, dq_ref, mark_ref = refs[:n], refs[n : 2 * n], refs[2 * n], refs[2 * n + 1]
    mark_ref[...] = jnp.zeros_like(mark_ref)
    rows, hd = k_refs[0].shape
    for h in range(dq_ref.shape[1] // hd):
        dq = 0.0
        for k, ds in zip(k_refs, ds_refs):
            part = ds[:, h * rows : (h + 1) * rows]
            dq = dq + lax.dot_general(part, k[...], TN, preferred_element_type=F32)
        dq_ref[:, h * hd : (h + 1) * hd] = (dq / hd**0.5).astype(BF16)


def relay_kernel(block_ref, out_ref):
    out_ref[...] = block_ref[...]


def merge_kernel(own_ref, got_ref, out_ref):
    out_ref[...] = (own_ref[...].astype(F32) + got_ref[...].astype(F32)).astype(BF16)


def small_call(kernel, name, operands, after):
    x = operands[0]
    return whole_call(kernel, name, [], operands, [shape(x.shape)], 4, (0, 6 * x.size), [], after)[0]


def attention(me, spans, queries, out_grad, keys, values, swap, n):
    rows, hd = keys.shape
    columns = queries.shape[1]
    tall = columns // hd * rows
    product = 2 * rows * tall * hd
    cost = (8 * product, 8 * rows * columns)

    direct = [b for b in range(1, n) if b & (b - 1) == 0]
    blocks = {b: [swap(keys, b), swap(values, b)] for b in reversed(direct)}
    stats_shape = shape((8, tall), F32)
    stats, queries, out_grad, keys, values, flags = whole_call(
        functools.partial(first_stats_kernel, n),
        "first_stats",
        [me, spans],
        [queries, out_grad, keys, values],
        [stats_shape] + [shape(x.shape) for x in (queries, out_grad, keys, values)] + [shape((8, 128), F32)],
        14,
        cost,
        [],
        [begin()],
    )
    blocks[0] = [keys, values]
    for b in range(1, n):
        if b == 2:
            values_on = small_call(relay_kernel, "relay", [blocks[2][1]], [stats])
            blocks[3] = [swap(blocks[2][0], 1), swap(values_on, 1)]
        if b not in blocks:
            blocks[b] = [swap(x, b & -b) for x in blocks[b & (b - 1)]]
        stats = whole_call(
            functools.partial(next_stats_kernel, b),
            "next_stats",
            [],
            [flags, queries, out_grad, *blocks[b], stats],
            [stats_shape],
            12,
            cost,
            [],
            blocks[2][:1] if b == 1 else blocks[3][:1] if b == 2 else [],
        )[0]
    p_buf = pltpu.VMEM((rows, 2 * rows), BF16)
    sums = [pltpu.VMEM((rows, hd), F32)] * 2
    parts, score_grads, before = [[] for _ in range(n)], [None] * n, []
    for b in range(n - 1, 0, -1):
        part, score_grads[b] = whole_call(
            functools.partial(other_kernel, b),
            "block_gradients",
            [],
            [flags, stats, queries, out_grad, *blocks[b]],
            [shape((rows, 2 * hd)), shape((rows, tall))],
            14,
            (11 * product, 16 * rows * columns),
            [p_buf, *sums],
            before,
        )
        before = [part]
        parts[b].insert(0, part)
    arrived = []
    for b in range(n - 1, 0, -1):
        part, *got = parts[b]
        for other in got:
            part = small_call(merge_kernel, "merge", [part, other], [])
            before = [part]
        to = b & (b - 1)
        (parts[to] if to else arrived).append(swap(part, b & -b))
    own, score_grads[0] = whole_call(
        own_kernel,
        "own_gradients",
        [],
        [stats, queries, out_grad, keys, values],
        [shape((rows, 2 * hd), F32), shape((rows, tall))],
        14,
        (8 * product, 16 * rows * columns),
        [p_buf, *sums],
        before,
    )
    return own, arrived, [blocks[b][0] for b in range(n)], score_grads, before


def query_gradients(key_blocks, score_grads, columns, after):
    n = len(key_blocks)
    rows = key_blocks[0].shape[0]
    return whole_call(
        functools.partial(query_kernel, n),
        "query_gradients",
        [],
        [*key_blocks, *score_grads],
        [shape((rows, columns)), shape((8, 128), F32)],
        5 + 3 * n,
        (2 * n * rows * rows * columns, 16 * rows * columns),
        [],
        after,
    )


def pack_top(top):
    high = jnp.minimum(top, BF16_MAX).astype(BF16).astype(F32)
    rest = top - high
    middle = rest.astype(BF16).astype(F32)
    low = rest - middle
    return (high + pltpu.roll(middle, PACK_LANES, 1) + pltpu.roll(low, 2 * PACK_LANES, 1)).astype(BF16)


def unpack_top(ref, at):
    x = ref[at : at + TOP_ROWS, :TOP_LANES].astype(F32)
    total = x + (pltpu.roll(x, TOP_LANES - PACK_LANES, 1) + pltpu.roll(x, TOP_LANES - 2 * PACK_LANES, 1))
    lane = lax.broadcasted_iota(jnp.int32, x.shape, 1)
    return jnp.where(lane < PACK_LANES, total, 0.0)


def tile_of(step, me_dp, bits, flip):
    mask = flip
    for j in range(1, bits):
        if not (step >> (bits - 1 - j)) & 1:
            mask |= 1 << j
    return me_dp ^ mask


def reversed_step(step, bits):
    return sum(((step >> (bits - 1 - j)) & 1) << (j - 1) for j in range(1, bits))


def corrected_tile(chosen, dest, grads, a_ref, e_ref, top_ref):
    _, n_ctx, sets, rows_set, rows = a_ref.shape
    tall = n_ctx * rows_set
    a = a_ref[dest, :, chosen].reshape(tall, rows)
    e = e_ref[dest, :, chosen].reshape(tall, e_ref.shape[4])
    c = jnp.dot(a, grads, preferred_element_type=F32) + e

    mags = jnp.max(jnp.abs(c).reshape(tall // QROWS, QROWS, c.shape[1]), axis=1)
    mags = jnp.max(mags, axis=1, keepdims=True)
    per_set = rows_set // QROWS
    block = lax.broadcasted_iota(jnp.int32, (tall // QROWS, TOP_LANES), 0)
    lane = lax.broadcasted_iota(jnp.int32, (tall // QROWS, TOP_LANES), 1)
    shift = per_set.bit_length() - 1
    place = ((block >> shift) * (sets * per_set)) + chosen * per_set + (block & (per_set - 1))
    top = jnp.max(jnp.where(lane == place, mags, 0.0), axis=0, keepdims=True)
    top_ref[pl.ds(dest, 1), :] = jnp.maximum(top_ref[pl.ds(dest, 1), :], top)
    return c


def send_rows(bits, shrink, chosen, me_ref, total, a_ref, e_ref, out_ref, top_ref, packed):
    tall = a_ref.shape[1] * a_ref.shape[3]
    steps = a_ref.shape[0] // 2
    for step in range(steps):
        dest = tile_of(step, me_ref[0], bits, 1)
        c = corrected_tile(chosen, dest, total, a_ref, e_ref, top_ref)
        out_ref[step * tall : (step + 1) * tall, :] = (c * shrink).astype(BF16)
    if packed:
        out_ref[steps * tall :, :TOP_LANES] = pack_top(top_ref[...])
        out_ref[steps * tall :, TOP_LANES:] = jnp.zeros((TOP_ROWS, out_ref.shape[1] - TOP_LANES), BF16)


def first_send_kernel(bits, shrink, n_parts, me_ref, own_ref, *refs):
    part_refs = refs[:n_parts]
    a_ref, e_ref, out_ref, top_ref, kg_ref, vg_ref, grads_ref = refs[n_parts:]
    total = own_ref[...]
    for part in part_refs:
        total = total + part[...].astype(F32)
    total = total.astype(BF16)
    hd = total.shape[1] // 2
    kg_ref[...] = total[:, :hd]
    vg_ref[...] = total[:, hd:]
    grads_ref[...] = total
    top_ref[...] = jnp.zeros_like(top_ref)
    send_rows(bits, shrink, 0, me_ref, total, a_ref, e_ref, out_ref, top_ref, False)


def next_send_kernel(bits, shrink, chosen, packed, me_ref, grads_ref, before_ref, a_ref, e_ref, out_ref, top_ref):
    top_ref[...] = before_ref[...]
    send_rows(bits, shrink, chosen, me_ref, grads_ref[...], a_ref, e_ref, out_ref, top_ref, packed)


def kept_kernel(bits, shrink, me_ref, grads_ref, before_ref, a_ref, e_ref, *outs):
    *kept, top_ref = outs
    top_ref[...] = before_ref[...]
    total = grads_ref[...]
    for chosen, out_ref in enumerate(kept):
        for step in range(out_ref.shape[0]):
            dest = tile_of(step, me_ref[0], bits, 0)
            out_ref[step] = corrected_tile(chosen, dest, total, a_ref, e_ref, top_ref) * shrink


def split_kernel(bits, n_tops, kept, got, *refs):
    steps, tall, width = kept.shape
    half = steps // 2
    hd = width // 2
    tops = refs[:n_tops]
    low_away, low_stay, high_away, high_stay, *top_out = refs[n_tops:]
    for step in range(steps):
        c = (kept[step] + got[step * tall : (step + 1) * tall, :].astype(F32)).astype(BF16)
        back = reversed_step(step, bits)
        for at, part, away, stay in ((step, c[:, :hd], low_away, low_stay), (back, c[:, hd:], high_away, high_stay)):
            if at < half:
                away[at * tall : (at + 1) * tall, :] = part
            else:
                stay[(at - half) * tall : (at - half + 1) * tall, :] = part
    if tops:
        top = largest(tops, got, steps * tall)
        top_out[0][...] = top
        low_away[half * tall :, :] = pack_top(top)


def largest(tops, low_got, size):
    found = [top[...] for top in tops]
    if low_got.shape[0] > size:
        found.append(unpack_top(low_got, size))
    return functools.reduce(jnp.maximum, found)


def add_kernel(n_tops, low, low_got, high, high_got, *refs):
    tops = refs[:n_tops]
    low_away, low_stay, high_away, high_stay, *top_out = refs[n_tops:]
    size = low.shape[0]
    half = size // 2
    for mine, got, away, stay in ((low, low_got, low_away, low_stay), (high, high_got, high_away, high_stay)):
        away[:half, :] = (mine[:half, :].astype(F32) + got[:half, :].astype(F32)).astype(BF16)
        stay[...] = (mine[half:, :].astype(F32) + got[half:size, :].astype(F32)).astype(BF16)
    if tops:
        top = largest(tops, low_got, size)
        top_out[0][...] = top
        if low_away.shape[0] > half:
            low_away[half:, :] = pack_top(top)


def last_kernel(n_ctx, n_tops, me_ref, low, low_got, high, high_got, *refs):
    tops = refs[:n_tops]
    outs, top_out = refs[n_tops : n_tops + n_ctx], refs[n_tops + n_ctx :]
    size, hd = low.shape
    rows_set = size // n_ctx
    if tops:
        top = largest(tops, low_got, size)
        top_out[0][...] = top
        packed = pack_top(top)
    for b in range(n_ctx):
        part = pl.ds(pl.multiple_of((me_ref[0] ^ b) * rows_set, rows_set), rows_set)
        for at, mine, got in ((0, low, low_got), (rows_set, high, high_got)):
            total = mine[part, :].astype(F32) + got[part, :].astype(F32)
            outs[b][at : at + rows_set, :] = total.astype(outs[b].dtype)
        if b > 0 and tops:
            outs[b][2 * rows_set :, :] = packed


def final_kernel(sets, n_ctx, gain, me_dp_ref, me_ctx_ref, *refs):
    groups = [refs[chosen * n_ctx : (chosen + 1) * n_ctx] for chosen in range(sets)]
    top_ref, out_ref, scale_ref, all_tops = refs[sets * n_ctx :]
    n_dp, lanes = scale_ref.shape
    rows_set, hd = groups[0][0].shape[0] // 2, groups[0][0].shape[1]
    scale = top_ref[...]
    for other in groups[-1][1:]:
        scale = jnp.maximum(scale, unpack_top(other, 2 * rows_set))
    scale = scale + 1e-06
    all_tops[...] = scale
    scale_ref[...] = scale[:n_dp, :lanes]
    factors = gain / all_tops[pl.ds(me_dp_ref[0], 1), :]
    lane = lax.broadcasted_iota(jnp.int32, factors.shape, 1)
    per_set = rows_set // QROWS
    first = me_ctx_ref[0] * (sets * per_set)
    for chosen, group in enumerate(groups):
        for r in range(per_set):
            mine = jnp.where(lane == first + (chosen * per_set + r), factors, 0.0)
            factor = jnp.sum(mine, axis=1, keepdims=True)
            at = chosen * rows_set + r * QROWS
            for h in range(2):
                part = slice(h * rows_set + r * QROWS, h * rows_set + (r + 1) * QROWS)
                total = group[0][part, :]
                for other in group[1:]:
                    total = total + other[part, :].astype(F32)
                out_ref[at : at + QROWS, h * hd : (h + 1) * hd] = total * factor


def local(n_dp, n_ctx, sets, span_order, queries, keys, values, out_grad, activations, error_feedback):
    rows, hd = keys.shape
    width = 2 * hd
    model = activations.shape[1]
    rows_set = model // (n_dp * n_ctx * sets)
    tall = n_ctx * rows_set
    me_dp = lax.axis_index("dp").astype(jnp.int32)[None]
    me_ctx = lax.axis_index("context").astype(jnp.int32)[None]
    bits = n_dp.bit_length() - 1

    def swap_dp(x, mask):
        return lax.ppermute(x, "dp", xor_perm(n_dp, mask))

    def swap_ctx(x, mask):
        return lax.ppermute(x, "context", xor_perm(n_ctx, mask))

    own, parts, key_blocks, score_grads, last_part = attention(
        me_ctx, span_order[0], queries, out_grad, keys, values, swap_ctx, n_ctx
    )
    acts = prepare(activations, last_part)

    shrink = 1.0 / (n_dp * n_ctx)
    acts = acts.reshape(n_dp, n_ctx, sets, rows_set, rows)
    errors = error_feedback.reshape(n_dp, n_ctx, sets, rows_set, width)
    tops = shape((TOP_ROWS, TOP_LANES), F32)
    steps = n_dp // 2
    cost = (2 * steps * tall * rows * width, steps * tall * (2 * rows + 6 * width))
    out, top, key_grad, value_grad, grads = whole_call(
        functools.partial(first_send_kernel, bits, shrink, len(parts)),
        "send_tiles",
        [me_dp],
        [own, *parts, acts, errors],
        [shape((steps * tall, width)), tops, shape((rows, hd)), shape((rows, hd)), shape((rows, width))],
        22,
        cost,
    )
    got = [swap_dp(out, 1)]
    *kept, top = whole_call(
        functools.partial(kept_kernel, bits, shrink),
        "kept_tiles",
        [me_dp],
        [grads, top, acts, errors],
        [shape((steps, tall, width), F32)] * sets + [tops],
        24,
        (sets * cost[0], sets * cost[1]),
    )
    for chosen in range(1, sets):
        extra = TOP_ROWS if chosen == sets - 1 else 0
        out, top = whole_call(
            functools.partial(next_send_kernel, bits, shrink, chosen, extra > 0),
            "send_tiles",
            [me_dp],
            [grads, top, acts, errors],
            [shape((steps * tall + extra, width)), tops],
            22,
            cost,
        )
        got.append(swap_dp(out, 1))

    halves = []
    for chosen in range(sets):
        half = steps // 2 * tall
        last = chosen == sets - 1
        arrays = whole_call(
            functools.partial(split_kernel, bits, int(last)),
            "split_tiles",
            [],
            [kept[chosen], got[chosen]] + [top] * last,
            [shape((half + TOP_ROWS * last, hd))] + [shape((half, hd))] * 3 + [tops] * last,
            10,
            (4 * half * width, 12 * half * width),
        )
        halves.append(arrays[:4])
    gathered = [arrays[4]]
    query_grad, mark = query_gradients(key_blocks, score_grads, queries.shape[1], [arrays[1]])
    groups = []
    for chosen in range(sets):
        low_away, low, high_away, high = halves[chosen]
        extra = TOP_ROWS if chosen == sets - 1 else 0
        for stage in range(1, bits):
            low_got = swap_dp(low_away, 1 << stage)
            high_got = swap_dp(high_away, 1 << (bits - stage))
            with_tops = extra > 0
            operands = [low, low_got, high, high_got] + (gathered if with_tops else [])
            n_tops = len(operands) - 4
            size = low.shape[0]
            cost = (4 * size * hd, 12 * size * hd)
            if stage < bits - 1:
                low_away, low, high_away, high, *top_out = whole_call(
                    functools.partial(add_kernel, n_tops),
                    "add_stage",
                    [],
                    operands,
                    [shape((size // 2 + extra, hd))] + [shape((size // 2, hd))] * 3 + [tops] * with_tops,
                    8,
                    cost,
                    after=[mark] if chosen == 0 and stage == 1 else [],
                )
            else:
                outs = whole_call(
                    functools.partial(last_kernel, n_ctx, n_tops),
                    "last_stage",
                    [me_ctx],
                    operands,
                    [shape((2 * rows_set, hd), F32)]
                    + [shape((2 * rows_set + extra, hd))] * (n_ctx - 1)
                    + [tops] * with_tops,
                    8,
                    cost,
                )
                mine, away, top_out = outs[0], outs[1:n_ctx], outs[n_ctx:]
            if with_tops:
                gathered = list(top_out)
        groups.append([mine] + [swap_ctx(away[b - 1], b) for b in range(n_ctx - 1, 0, -1)])
    payload, scale = whole_call(
        functools.partial(final_kernel, sets, n_ctx, 7.0 / shrink),
        "final_stage",
        [me_dp, me_ctx],
        [x for group in groups for x in group] + gathered,
        [shape((sets * rows_set, width), F32), shape((n_dp, sets * tall // QROWS), F32)],
        8,
        (4 * sets * tall * width, 16 * sets * rows_set * width),
        [pltpu.VMEM((TOP_ROWS, TOP_LANES), F32)],
    )
    return query_grad, key_grad, value_grad, payload, scale.reshape(-1)


def solution(mesh):
    tokens = P(("dp", "context"), None)
    return jax.shard_map(
        functools.partial(local, mesh.shape["dp"], mesh.shape["context"], 2),
        mesh=mesh,
        in_specs=(P("dp", None), tokens, tokens, tokens, tokens, tokens, P("dp", "context", None, None)),
        out_specs=(tokens, tokens, tokens, tokens, P()),
        check_vma=False,
    )
```

```python
import functools

import jax
import jax.numpy as jnp
from jax import lax
from jax.experimental import pallas as pl
from jax.experimental.pallas import tpu as pltpu
from jax.sharding import PartitionSpec as P

QROWS = 32
LOG2E = 1.4426950408889634
FAR = 1e30
MIB = 1024 * 1024
CHUNK = 256
TOP_ROWS, TOP_LANES, PACK_LANES = 16, 128, 32
BF16, F32 = jnp.bfloat16, jnp.float32
BF16_MAX = float(jnp.finfo(jnp.bfloat16).max)
NT = (((1,), (1,)), ((), ()))
TN = (((0,), (0,)), ((), ()))


def xor_perm(size, mask):
    return [(i, i ^ mask) for i in range(size)]


def whole(x):
    return pl.BlockSpec(x.shape, lambda *_: (0,) * len(x.shape))


def shape(dims, dtype=BF16):
    return jax.ShapeDtypeStruct(dims, dtype)


def whole_call(kernel, name, scalars, operands, out_shape, mib, cost, scratch=(), after=()):
    def body(*refs):
        first = len(scalars) + len(operands)
        kernel(*refs[:first], *refs[first + len(after) :])

    return pl.pallas_call(
        body,
        grid_spec=pltpu.PrefetchScalarGridSpec(
            num_scalar_prefetch=len(scalars),
            grid=(1,),
            in_specs=[whole(x) for x in operands] + [pl.BlockSpec(memory_space=pl.ANY)] * len(after),
            out_specs=[whole(x) for x in out_shape],
            scratch_shapes=list(scratch),
        ),
        out_shape=out_shape,
        compiler_params=pltpu.CompilerParams(vmem_limit_bytes=mib * MIB),
        cost_estimate=pl.CostEstimate(flops=cost[0], bytes_accessed=cost[1], transcendentals=0),
        name=name,
    )(*scalars, *operands, *after)


def begin_kernel(out_ref):
    out_ref[...] = jnp.zeros_like(out_ref)


def begin():
    mark = [shape((8, 128), F32)]
    return whole_call(begin_kernel, "begin", [], [], mark, 4, (20_000_000_000, 0))[0]


def prepare_kernel(pieces, a_ref, a_out):
    tile = a_ref.shape[1] // pieces
    for i in range(pieces):
        a_out[i * tile : (i + 1) * tile, :] = a_ref[:, i * tile : (i + 1) * tile].T


def prepare(activations, after):
    rows, model = activations.shape
    outs = [shape((model, rows))]
    cost = (0, 0)
    kernel = functools.partial(prepare_kernel, 8)
    return whole_call(kernel, "prepare", [], [activations], outs, 16, cost, [], after)[0]


def head_pair(ref, i, hd):
    at = i * (2 * hd)
    first = ref[:, pl.ds(pl.multiple_of(at, hd), hd)]
    second = ref[:, pl.ds(pl.multiple_of(at + hd, hd), hd)]
    return jnp.concatenate([first, second], axis=0)


def score_chunk(k, v, q, do, own, first_lane):
    s = lax.dot_general(k, q, NT, preferred_element_type=F32)
    dp = lax.dot_general(v, do, NT, preferred_element_type=F32)
    if own:
        rows = k.shape[0]
        key_at = lax.broadcasted_iota(jnp.int32, s.shape, 0)
        query_at = lax.broadcasted_iota(jnp.int32, s.shape, 1) + first_lane
        query_at = jnp.where(query_at >= rows, query_at - rows, query_at)
        s = jnp.where(key_at <= query_at, s, -FAR)
    return s, dp


def counted(b, flags):
    lane = lax.broadcasted_iota(jnp.int32, flags.shape, 1)
    return jnp.max(jnp.where(lane == b, flags[...], 0.0)) > 0.5


def stats_of_block(b, q_ref, do_ref, k_ref, v_ref, before, out):
    k, v = k_ref[...], v_ref[...]
    rows, hd = k.shape
    pair = 2 * rows
    factor = LOG2E / hd**0.5

    def heads(i, carry):
        q, do = head_pair(q_ref, i, hd), head_pair(do_ref, i, hd)
        for t in range(pair // CHUNK):
            part = slice(t * CHUNK, (t + 1) * CHUNK)
            lanes = pl.ds(pl.multiple_of(i * pair + t * CHUNK, CHUNK), CHUNK)
            s, dp = score_chunk(k, v, q[part], do[part], b == 0, t * CHUNK)
            top = jnp.max(s, axis=0, keepdims=True) * factor
            e = jnp.exp2(s * factor - top)
            total = jnp.sum(e, axis=0, keepdims=True)
            weighted = jnp.sum(e * dp, axis=0, keepdims=True)
            if b > 0:
                old = before[0:1, lanes]
                both = jnp.maximum(old, top)
                old_part, new_part = jnp.exp2(old - both), jnp.exp2(top - both)
                total = before[1:2, lanes] * old_part + total * new_part
                weighted = before[2:3, lanes] * old_part + weighted * new_part
                top = both
            out[0:1, lanes] = top
            out[1:2, lanes] = total
            out[2:3, lanes] = weighted
        return carry

    lax.fori_loop(0, q_ref.shape[1] // (2 * hd), heads, 0, unroll=True)


def first_stats_kernel(n, me_ref, span_ref, q_ref, do_ref, k_ref, v_ref, out, q_out, do_out, k_out, v_out, flags):
    me = me_ref[0]
    lane = lax.broadcasted_iota(jnp.int32, flags.shape, 1)
    found = jnp.zeros(flags.shape, F32)
    for b in range(1, n):
        found = jnp.where((lane == b) & (span_ref[me ^ b] < span_ref[me]), 1.0, found)
    flags[...] = found
    q_out[...] = q_ref[...]
    do_out[...] = do_ref[...]
    k_out[...] = k_ref[...]
    v_out[...] = v_ref[...]
    stats_of_block(0, q_ref, do_ref, k_ref, v_ref, None, out)


def next_stats_kernel(b, flags, q_ref, do_ref, k_ref, v_ref, before, out):
    keep = counted(b, flags)

    @pl.when(keep)
    def _():
        stats_of_block(b, q_ref, do_ref, k_ref, v_ref, before, out)

    @pl.when(jnp.logical_not(keep))
    def _():
        out[...] = before[...]


def block_gradients(own, stats, q_ref, do_ref, k_ref, v_ref, p_buf, ds_ref, dk, dv):
    k, v = k_ref[...], v_ref[...]
    rows, hd = k.shape
    pair = 2 * rows
    factor = LOG2E / hd**0.5
    dk[...] = jnp.zeros_like(dk)
    dv[...] = jnp.zeros_like(dv)

    def heads(i, carry):
        q, do = head_pair(q_ref, i, hd), head_pair(do_ref, i, hd)
        for t in range(pair // CHUNK):
            part = slice(t * CHUNK, (t + 1) * CHUNK)
            lanes = pl.ds(pl.multiple_of(i * pair + t * CHUNK, CHUNK), CHUNK)
            s, dp = score_chunk(k, v, q[part], do[part], own, t * CHUNK)
            total = stats[1:2, lanes]
            level = stats[0:1, lanes] + jnp.log(total) * LOG2E
            p = jnp.exp2(s * factor - level)
            p_buf[:, part] = p.astype(BF16)
            ds = (p * (dp - stats[2:3, lanes] / total)).astype(BF16)
            ds_ref[:, lanes] = ds
        ds = ds_ref[:, pl.ds(pl.multiple_of(i * pair, CHUNK), pair)]
        dk[...] += jnp.dot(ds, q, preferred_element_type=F32)
        dv[...] += jnp.dot(p_buf[...], do, preferred_element_type=F32)
        return carry

    lax.fori_loop(0, q_ref.shape[1] // (2 * hd), heads, 0, unroll=True)
    inverse = 1.0 / hd**0.5
    return dk[...] * inverse, dv[...]


def other_kernel(b, flags, stats, q_ref, do_ref, k_ref, v_ref, out_ref, ds_out, p_buf, dk, dv):
    keep = counted(b, flags)
    rows, hd = dk.shape

    @pl.when(keep)
    def _():
        dk_sum, dv_sum = block_gradients(False, stats, q_ref, do_ref, k_ref, v_ref, p_buf, ds_out, dk, dv)
        out_ref[:, :hd] = dk_sum.astype(BF16)
        out_ref[:, hd:] = dv_sum.astype(BF16)

    @pl.when(jnp.logical_not(keep))
    def _():
        out_ref[...] = jnp.zeros_like(out_ref)
        ds_out[...] = jnp.zeros_like(ds_out)


def own_kernel(stats, q_ref, do_ref, k_ref, v_ref, out_ref, ds_out, p_buf, dk, dv):
    hd = dk.shape[1]
    dk_sum, dv_sum = block_gradients(True, stats, q_ref, do_ref, k_ref, v_ref, p_buf, ds_out, dk, dv)
    out_ref[:, :hd] = dk_sum
    out_ref[:, hd:] = dv_sum


def query_kernel(n, *refs):
    k_refs, ds_refs, dq_ref, mark_ref = refs[:n], refs[n : 2 * n], refs[2 * n], refs[2 * n + 1]
    mark_ref[...] = jnp.zeros_like(mark_ref)
    rows, hd = k_refs[0].shape
    for h in range(dq_ref.shape[1] // hd):
        dq = 0.0
        for k, ds in zip(k_refs, ds_refs):
            part = ds[:, h * rows : (h + 1) * rows]
            dq = dq + lax.dot_general(part, k[...], TN, preferred_element_type=F32)
        dq_ref[:, h * hd : (h + 1) * hd] = (dq / hd**0.5).astype(BF16)


def merge_kernel(rows, own_ref, got_ref, out_ref):
    out_ref[:rows, :] = (own_ref[:rows, :].astype(F32) + got_ref[:rows, :].astype(F32)).astype(BF16)
    out_ref[rows:, :] = jnp.zeros((out_ref.shape[0] - rows, out_ref.shape[1]), BF16)


def merge(own, got, rows, after):
    outs = [shape((rows + TOP_ROWS, own.shape[1]))]
    kernel = functools.partial(merge_kernel, rows)
    return whole_call(kernel, "merge", [], [own, got], outs, 4, (0, 6 * own.size), [], after)[0]


def attention(me, spans, queries, out_grad, keys, values, swap, n):
    rows, hd = keys.shape
    columns = queries.shape[1]
    tall = columns // hd * rows
    product = 2 * rows * tall * hd
    cost = (8 * product, 8 * rows * columns)

    direct = [b for b in range(1, n) if b & (b - 1) == 0]
    blocks = {b: [swap(keys, b), swap(values, b)] for b in reversed(direct)}
    stats_shape = shape((8, tall), F32)
    stats, queries, out_grad, keys, values, flags = whole_call(
        functools.partial(first_stats_kernel, n),
        "first_stats",
        [me, spans],
        [queries, out_grad, keys, values],
        [stats_shape] + [shape(x.shape) for x in (queries, out_grad, keys, values)] + [shape((8, 128), F32)],
        14,
        cost,
        [],
        [begin()],
    )
    blocks[0] = [keys, values]
    for b in range(1, n):
        if b not in blocks:
            blocks[b] = [swap(x, b & -b) for x in blocks[b & (b - 1)]]
        stats = whole_call(
            functools.partial(next_stats_kernel, b),
            "next_stats",
            [],
            [flags, queries, out_grad, *blocks[b], stats],
            [stats_shape],
            12,
            cost,
            [],
            blocks[2] if b == 1 else [],
        )[0]
    p_buf = pltpu.VMEM((rows, 2 * rows), BF16)
    sums = [pltpu.VMEM((rows, hd), F32)] * 2
    def own_call(after):
        return whole_call(
            own_kernel,
            "own_gradients",
            [],
            [stats, queries, out_grad, keys, values],
            [shape((rows, 2 * hd), F32), shape((rows, tall))],
            14,
            (11 * product, 16 * rows * columns),
            [p_buf, *sums],
            after,
        )

    parts, score_grads, before = [[] for _ in range(n)], [None] * n, []
    for b in range(n - 1, 0, -1):
        part, score_grads[b] = whole_call(
            functools.partial(other_kernel, b),
            "block_gradients",
            [],
            [flags, stats, queries, out_grad, *blocks[b]],
            [shape((rows, 2 * hd)), shape((rows, tall))],
            14,
            (11 * product, 16 * rows * columns),
            [p_buf, *sums],
            before,
        )
        if b == min(2, n - 1):
            own, score_grads[0] = own_call([part])
        for other in parts[b]:
            part = merge(part, other, rows, [own] if b == 2 else [])
        before = [part]
        to = b & (b - 1)
        parts[to].append(swap(part, b & -b))
    return own, parts[0], [blocks[b][0] for b in range(n)], score_grads, before


def query_gradients(key_blocks, score_grads, columns, after):
    n = len(key_blocks)
    rows = key_blocks[0].shape[0]
    return whole_call(
        functools.partial(query_kernel, n),
        "query_gradients",
        [],
        [*key_blocks, *score_grads],
        [shape((rows, columns)), shape((8, 128), F32)],
        5 + 3 * n,
        (2 * n * rows * rows * columns, 16 * rows * columns),
        [],
        after,
    )


def pack_top(top):
    high = jnp.minimum(top, BF16_MAX).astype(BF16).astype(F32)
    rest = top - high
    middle = rest.astype(BF16).astype(F32)
    low = rest - middle
    return (high + pltpu.roll(middle, PACK_LANES, 1) + pltpu.roll(low, 2 * PACK_LANES, 1)).astype(BF16)


def unpack_top(ref, at):
    x = ref[at : at + TOP_ROWS, :TOP_LANES].astype(F32)
    total = x + (pltpu.roll(x, TOP_LANES - PACK_LANES, 1) + pltpu.roll(x, TOP_LANES - 2 * PACK_LANES, 1))
    lane = lax.broadcasted_iota(jnp.int32, x.shape, 1)
    return jnp.where(lane < PACK_LANES, total, 0.0)


def tile_of(step, me_dp, bits, flip):
    mask = flip
    for j in range(1, bits):
        if not (step >> (bits - 1 - j)) & 1:
            mask |= 1 << j
    return me_dp ^ mask


def reversed_step(step, bits):
    return sum(((step >> (bits - 1 - j)) & 1) << (j - 1) for j in range(1, bits))


def corrected_tile(chosen, dest, grads, a_ref, e_ref, top_ref):
    _, n_ctx, sets, rows_set, rows = a_ref.shape
    tall = n_ctx * rows_set
    a = a_ref[dest, :, chosen].reshape(tall, rows)
    e = e_ref[dest, :, chosen].reshape(tall, e_ref.shape[4])
    c = jnp.dot(a, grads, preferred_element_type=F32) + e

    mags = jnp.max(jnp.abs(c).reshape(tall // QROWS, QROWS, c.shape[1]), axis=1)
    mags = jnp.max(mags, axis=1, keepdims=True)
    per_set = rows_set // QROWS
    block = lax.broadcasted_iota(jnp.int32, (tall // QROWS, TOP_LANES), 0)
    lane = lax.broadcasted_iota(jnp.int32, (tall // QROWS, TOP_LANES), 1)
    shift = per_set.bit_length() - 1
    place = ((block >> shift) * (sets * per_set)) + chosen * per_set + (block & (per_set - 1))
    top = jnp.max(jnp.where(lane == place, mags, 0.0), axis=0, keepdims=True)
    top_ref[pl.ds(dest, 1), :] = jnp.maximum(top_ref[pl.ds(dest, 1), :], top)
    return c


def send_rows(bits, shrink, chosen, me_ref, total, a_ref, e_ref, out_ref, top_ref, packed):
    tall = a_ref.shape[1] * a_ref.shape[3]
    steps = a_ref.shape[0] // 2
    for step in range(steps):
        dest = tile_of(step, me_ref[0], bits, 1)
        c = corrected_tile(chosen, dest, total, a_ref, e_ref, top_ref)
        out_ref[step * tall : (step + 1) * tall, :] = (c * shrink).astype(BF16)
    if packed:
        out_ref[steps * tall :, :TOP_LANES] = pack_top(top_ref[...])
        out_ref[steps * tall :, TOP_LANES:] = jnp.zeros((TOP_ROWS, out_ref.shape[1] - TOP_LANES), BF16)


def first_send_kernel(bits, shrink, n_parts, me_ref, own_ref, *refs):
    part_refs = refs[:n_parts]
    a_ref, e_ref, out_ref, top_ref, kg_ref, vg_ref, grads_ref = refs[n_parts:]
    total = own_ref[...]
    for part in part_refs:
        total = total + part[: total.shape[0], :].astype(F32)
    total = total.astype(BF16)
    hd = total.shape[1] // 2
    kg_ref[...] = total[:, :hd]
    vg_ref[...] = total[:, hd:]
    grads_ref[...] = total
    top_ref[...] = jnp.zeros_like(top_ref)
    send_rows(bits, shrink, 0, me_ref, total, a_ref, e_ref, out_ref, top_ref, False)


def next_send_kernel(bits, shrink, chosen, packed, me_ref, grads_ref, before_ref, a_ref, e_ref, out_ref, top_ref):
    top_ref[...] = before_ref[...]
    send_rows(bits, shrink, chosen, me_ref, grads_ref[...], a_ref, e_ref, out_ref, top_ref, packed)


def kept_kernel(bits, shrink, me_ref, grads_ref, before_ref, a_ref, e_ref, *outs):
    *kept, top_ref = outs
    top_ref[...] = before_ref[...]
    total = grads_ref[...]
    for chosen, out_ref in enumerate(kept):
        for step in range(out_ref.shape[0]):
            dest = tile_of(step, me_ref[0], bits, 0)
            out_ref[step] = corrected_tile(chosen, dest, total, a_ref, e_ref, top_ref) * shrink


def split_kernel(bits, n_tops, kept, got, *refs):
    steps, tall, width = kept.shape
    half = steps // 2
    hd = width // 2
    tops = refs[:n_tops]
    low_away, low_stay, high_away, high_stay, *top_out = refs[n_tops:]
    for step in range(steps):
        c = (kept[step] + got[step * tall : (step + 1) * tall, :].astype(F32)).astype(BF16)
        back = reversed_step(step, bits)
        for at, part, away, stay in ((step, c[:, :hd], low_away, low_stay), (back, c[:, hd:], high_away, high_stay)):
            if at < half:
                away[at * tall : (at + 1) * tall, :] = part
            else:
                stay[(at - half) * tall : (at - half + 1) * tall, :] = part
    if tops:
        top = largest(tops, got, steps * tall)
        top_out[0][...] = top
        low_away[half * tall :, :] = pack_top(top)


def largest(tops, low_got, size):
    found = [top[...] for top in tops]
    if low_got.shape[0] > size:
        found.append(unpack_top(low_got, size))
    return functools.reduce(jnp.maximum, found)


def add_kernel(n_tops, low, low_got, high, high_got, *refs):
    tops = refs[:n_tops]
    low_away, low_stay, high_away, high_stay, *top_out = refs[n_tops:]
    size = low.shape[0]
    half = size // 2
    for mine, got, away, stay in ((low, low_got, low_away, low_stay), (high, high_got, high_away, high_stay)):
        away[:half, :] = (mine[:half, :].astype(F32) + got[:half, :].astype(F32)).astype(BF16)
        stay[...] = (mine[half:, :].astype(F32) + got[half:size, :].astype(F32)).astype(BF16)
    if tops:
        top = largest(tops, low_got, size)
        top_out[0][...] = top
        if low_away.shape[0] > half:
            low_away[half:, :] = pack_top(top)


def last_kernel(n_ctx, n_tops, me_ref, low, low_got, high, high_got, *refs):
    tops = refs[:n_tops]
    outs, top_out = refs[n_tops : n_tops + n_ctx], refs[n_tops + n_ctx :]
    size, hd = low.shape
    rows_set = size // n_ctx
    if tops:
        top = largest(tops, low_got, size)
        top_out[0][...] = top
        packed = pack_top(top)
    for b in range(n_ctx):
        part = pl.ds(pl.multiple_of((me_ref[0] ^ b) * rows_set, rows_set), rows_set)
        for at, mine, got in ((0, low, low_got), (rows_set, high, high_got)):
            total = mine[part, :].astype(F32) + got[part, :].astype(F32)
            outs[b][at : at + rows_set, :] = total.astype(outs[b].dtype)
        if b > 0:
            tail = outs[b].shape[0] - 2 * rows_set
            outs[b][2 * rows_set :, :] = packed if tops else jnp.zeros((tail, hd), BF16)


def final_kernel(sets, n_ctx, gain, me_dp_ref, me_ctx_ref, *refs):
    groups = [refs[chosen * n_ctx : (chosen + 1) * n_ctx] for chosen in range(sets)][::-1]
    top_ref, out_ref, scale_ref, all_tops = refs[sets * n_ctx :]
    n_dp, lanes = scale_ref.shape
    rows_set, hd = groups[0][0].shape[0] // 2, groups[0][0].shape[1]
    scale = top_ref[...]
    for other in groups[-1][1:]:
        scale = jnp.maximum(scale, unpack_top(other, 2 * rows_set))
    scale = scale + 1e-06
    all_tops[...] = scale
    scale_ref[...] = scale[:n_dp, :lanes]
    factors = gain / all_tops[pl.ds(me_dp_ref[0], 1), :]
    lane = lax.broadcasted_iota(jnp.int32, factors.shape, 1)
    per_set = rows_set // QROWS
    first = me_ctx_ref[0] * (sets * per_set)
    for chosen, group in enumerate(groups):
        for r in range(per_set):
            mine = jnp.where(lane == first + (chosen * per_set + r), factors, 0.0)
            factor = jnp.sum(mine, axis=1, keepdims=True)
            at = chosen * rows_set + r * QROWS
            for h in range(2):
                part = slice(h * rows_set + r * QROWS, h * rows_set + (r + 1) * QROWS)
                total = group[0][part, :]
                for other in group[1:]:
                    total = total + other[part, :].astype(F32)
                out_ref[at : at + QROWS, h * hd : (h + 1) * hd] = total * factor


def local(n_dp, n_ctx, sets, span_order, queries, keys, values, out_grad, activations, error_feedback):
    rows, hd = keys.shape
    width = 2 * hd
    model = activations.shape[1]
    rows_set = model // (n_dp * n_ctx * sets)
    tall = n_ctx * rows_set
    me_dp = lax.axis_index("dp").astype(jnp.int32)[None]
    me_ctx = lax.axis_index("context").astype(jnp.int32)[None]
    bits = n_dp.bit_length() - 1

    def swap_dp(x, mask):
        return lax.ppermute(x, "dp", xor_perm(n_dp, mask))

    def swap_ctx(x, mask):
        return lax.ppermute(x, "context", xor_perm(n_ctx, mask))

    own, parts, key_blocks, score_grads, last_part = attention(
        me_ctx, span_order[0], queries, out_grad, keys, values, swap_ctx, n_ctx
    )
    acts = prepare(activations, last_part)

    shrink = 1.0 / (n_dp * n_ctx)
    acts = acts.reshape(n_dp, n_ctx, sets, rows_set, rows)
    errors = error_feedback.reshape(n_dp, n_ctx, sets, rows_set, width)
    tops = shape((TOP_ROWS, TOP_LANES), F32)
    steps = n_dp // 2
    cost = (2 * steps * tall * rows * width, steps * tall * (2 * rows + 6 * width))
    out, top, key_grad, value_grad, grads = whole_call(
        functools.partial(first_send_kernel, bits, shrink, len(parts)),
        "send_tiles",
        [me_dp],
        [own, *parts, acts, errors],
        [shape((steps * tall, width)), tops, shape((rows, hd)), shape((rows, hd)), shape((rows, width))],
        18,
        cost,
    )
    got = [swap_dp(out, 1)]
    *kept, top = whole_call(
        functools.partial(kept_kernel, bits, shrink),
        "kept_tiles",
        [me_dp],
        [grads, top, acts, errors],
        [shape((steps, tall, width), F32)] * sets + [tops],
        20,
        (sets * cost[0], sets * cost[1]),
    )
    for chosen in range(1, sets):
        extra = TOP_ROWS if chosen == sets - 1 else 0
        out, top = whole_call(
            functools.partial(next_send_kernel, bits, shrink, chosen, extra > 0),
            "send_tiles",
            [me_dp],
            [grads, top, acts, errors],
            [shape((steps * tall + extra, width)), tops],
            18,
            cost,
        )
        got.append(swap_dp(out, 1))

    halves = []
    for chosen in range(sets):
        half = steps // 2 * tall
        last = chosen == sets - 1
        arrays = whole_call(
            functools.partial(split_kernel, bits, int(last)),
            "split_tiles",
            [],
            [kept[chosen], got[chosen]] + [top] * last,
            [shape((half + TOP_ROWS * last, hd))] + [shape((half, hd))] * 3 + [tops] * last,
            10,
            (4 * half * width, 12 * half * width),
        )
        halves.append(arrays[:4])
    gathered = [arrays[4]]
    query_grad, mark = query_gradients(key_blocks, score_grads, queries.shape[1], [arrays[1]])
    groups = []
    for chosen in range(sets):
        low_away, low, high_away, high = halves[chosen]
        extra = TOP_ROWS if chosen == sets - 1 else 0
        for stage in range(1, bits):
            low_got = swap_dp(low_away, 1 << stage)
            high_got = swap_dp(high_away, 1 << (bits - stage))
            with_tops = extra > 0
            operands = [low, low_got, high, high_got] + (gathered if with_tops else [])
            n_tops = len(operands) - 4
            size = low.shape[0]
            cost = (4 * size * hd, 12 * size * hd)
            if stage < bits - 1:
                low_away, low, high_away, high, *top_out = whole_call(
                    functools.partial(add_kernel, n_tops),
                    "add_stage",
                    [],
                    operands,
                    [shape((size // 2 + extra, hd))] + [shape((size // 2, hd))] * 3 + [tops] * with_tops,
                    8,
                    cost,
                    after=[mark] if chosen == 0 and stage == 1 else [],
                )
            else:
                outs = whole_call(
                    functools.partial(last_kernel, n_ctx, n_tops),
                    "last_stage",
                    [me_ctx],
                    operands,
                    [shape((2 * rows_set, hd), F32)]
                    + [shape((2 * rows_set + (extra or 2 * TOP_ROWS), hd))] * (n_ctx - 1)
                    + [tops] * with_tops,
                    8,
                    cost,
                )
                mine, away, top_out = outs[0], outs[1:n_ctx], outs[n_ctx:]
            if with_tops:
                gathered = list(top_out)
        groups.append([mine] + [swap_ctx(away[b - 1], b) for b in range(n_ctx - 1, 0, -1)])
    payload, scale = whole_call(
        functools.partial(final_kernel, sets, n_ctx, 7.0 / shrink),
        "final_stage",
        [me_dp, me_ctx],
        [x for group in groups[::-1] for x in group] + gathered,
        [shape((sets * rows_set, width), F32), shape((n_dp, sets * tall // QROWS), F32)],
        8,
        (4 * sets * tall * width, 16 * sets * rows_set * width),
        [pltpu.VMEM((TOP_ROWS, TOP_LANES), F32)],
    )
    return query_grad, key_grad, value_grad, payload, scale.reshape(-1)


def solution(mesh):
    tokens = P(("dp", "context"), None)
    return jax.shard_map(
        functools.partial(local, mesh.shape["dp"], mesh.shape["context"], 2),
        mesh=mesh,
        in_specs=(P("dp", None), tokens, tokens, tokens, tokens, tokens, P("dp", "context", None, None)),
        out_specs=(tokens, tokens, tokens, tokens, P()),
        check_vma=False,
    )
```

```python
import functools

import jax
import jax.numpy as jnp
from jax import lax
from jax.experimental import pallas as pl
from jax.experimental.pallas import tpu as pltpu
from jax.sharding import PartitionSpec as P

QROWS = 32
LOG2E = 1.4426950408889634
FAR = 1e30
MIB = 1024 * 1024
CHUNK = 256
TOP_ROWS, TOP_LANES, PACK_LANES = 16, 128, 32
BF16, F32 = jnp.bfloat16, jnp.float32
BF16_MAX = float(jnp.finfo(jnp.bfloat16).max)
NT = (((1,), (1,)), ((), ()))
TN = (((0,), (0,)), ((), ()))


def xor_perm(size, mask):
    return [(i, i ^ mask) for i in range(size)]


def whole(x):
    return pl.BlockSpec(x.shape, lambda *_: (0,) * len(x.shape))


def shape(dims, dtype=BF16):
    return jax.ShapeDtypeStruct(dims, dtype)


def whole_call(kernel, name, scalars, operands, out_shape, mib, cost, scratch=(), after=()):
    def body(*refs):
        first = len(scalars) + len(operands)
        kernel(*refs[:first], *refs[first + len(after) :])

    return pl.pallas_call(
        body,
        grid_spec=pltpu.PrefetchScalarGridSpec(
            num_scalar_prefetch=len(scalars),
            grid=(1,),
            in_specs=[whole(x) for x in operands] + [pl.BlockSpec(memory_space=pl.ANY)] * len(after),
            out_specs=[whole(x) for x in out_shape],
            scratch_shapes=list(scratch),
        ),
        out_shape=out_shape,
        compiler_params=pltpu.CompilerParams(vmem_limit_bytes=mib * MIB),
        cost_estimate=pl.CostEstimate(flops=cost[0], bytes_accessed=cost[1], transcendentals=0),
        name=name,
    )(*scalars, *operands, *after)


def begin_kernel(out_ref):
    out_ref[...] = jnp.zeros_like(out_ref)


def begin():
    mark = [shape((8, 128), F32)]
    return whole_call(begin_kernel, "begin", [], [], mark, 4, (20_000_000_000, 0))[0]


def prepare_kernel(pieces, a_ref, a_out):
    tile = a_ref.shape[1] // pieces
    for i in range(pieces):
        a_out[i * tile : (i + 1) * tile, :] = a_ref[:, i * tile : (i + 1) * tile].T


def prepare(activations, after):
    rows, model = activations.shape
    outs = [shape((model, rows))]
    cost = (0, 0)
    kernel = functools.partial(prepare_kernel, 8)
    return whole_call(kernel, "prepare", [], [activations], outs, 16, cost, [], after)[0]


def head_pair(ref, i, hd):
    at = i * (2 * hd)
    first = ref[:, pl.ds(pl.multiple_of(at, hd), hd)]
    second = ref[:, pl.ds(pl.multiple_of(at + hd, hd), hd)]
    return jnp.concatenate([first, second], axis=0)


def score_chunk(k, v, q, do, own, first_lane):
    s = lax.dot_general(k, q, NT, preferred_element_type=F32)
    dp = lax.dot_general(v, do, NT, preferred_element_type=F32)
    if own:
        rows = k.shape[0]
        key_at = lax.broadcasted_iota(jnp.int32, s.shape, 0)
        query_at = lax.broadcasted_iota(jnp.int32, s.shape, 1) + first_lane
        query_at = jnp.where(query_at >= rows, query_at - rows, query_at)
        s = jnp.where(key_at <= query_at, s, -FAR)
    return s, dp


def counted(b, flags):
    lane = lax.broadcasted_iota(jnp.int32, flags.shape, 1)
    return jnp.max(jnp.where(lane == b, flags[...], 0.0)) > 0.5


def stats_of_block(b, q_ref, do_ref, k_ref, v_ref, before, out):
    k, v = k_ref[...], v_ref[...]
    rows, hd = k.shape
    pair = 2 * rows
    factor = LOG2E / hd**0.5

    def heads(i, carry):
        q, do = head_pair(q_ref, i, hd), head_pair(do_ref, i, hd)
        for t in range(pair // CHUNK):
            part = slice(t * CHUNK, (t + 1) * CHUNK)
            lanes = pl.ds(pl.multiple_of(i * pair + t * CHUNK, CHUNK), CHUNK)
            s, dp = score_chunk(k, v, q[part], do[part], b == 0, t * CHUNK)
            top = jnp.max(s, axis=0, keepdims=True) * factor
            e = jnp.exp2(s * factor - top)
            total = jnp.sum(e, axis=0, keepdims=True)
            weighted = jnp.sum(e * dp, axis=0, keepdims=True)
            if b > 0:
                old = before[0:1, lanes]
                both = jnp.maximum(old, top)
                old_part, new_part = jnp.exp2(old - both), jnp.exp2(top - both)
                total = before[1:2, lanes] * old_part + total * new_part
                weighted = before[2:3, lanes] * old_part + weighted * new_part
                top = both
            out[0:1, lanes] = top
            out[1:2, lanes] = total
            out[2:3, lanes] = weighted
        return carry

    lax.fori_loop(0, q_ref.shape[1] // (2 * hd), heads, 0, unroll=True)


def first_stats_kernel(n, me_ref, span_ref, q_ref, do_ref, k_ref, v_ref, out, q_out, do_out, k_out, v_out, flags):
    me = me_ref[0]
    lane = lax.broadcasted_iota(jnp.int32, flags.shape, 1)
    found = jnp.zeros(flags.shape, F32)
    for b in range(1, n):
        found = jnp.where((lane == b) & (span_ref[me ^ b] < span_ref[me]), 1.0, found)
    flags[...] = found
    q_out[...] = q_ref[...]
    do_out[...] = do_ref[...]
    k_out[...] = k_ref[...]
    v_out[...] = v_ref[...]
    stats_of_block(0, q_ref, do_ref, k_ref, v_ref, None, out)


def next_stats_kernel(b, flags, q_ref, do_ref, k_ref, v_ref, before, out):
    keep = counted(b, flags)

    @pl.when(keep)
    def _():
        stats_of_block(b, q_ref, do_ref, k_ref, v_ref, before, out)

    @pl.when(jnp.logical_not(keep))
    def _():
        out[...] = before[...]


def block_gradients(own, stats, q_ref, do_ref, k_ref, v_ref, p_buf, ds_ref, dk, dv):
    k, v = k_ref[...], v_ref[...]
    rows, hd = k.shape
    pair = 2 * rows
    factor = LOG2E / hd**0.5
    dk[...] = jnp.zeros_like(dk)
    dv[...] = jnp.zeros_like(dv)

    def heads(i, carry):
        q, do = head_pair(q_ref, i, hd), head_pair(do_ref, i, hd)
        for t in range(pair // CHUNK):
            part = slice(t * CHUNK, (t + 1) * CHUNK)
            lanes = pl.ds(pl.multiple_of(i * pair + t * CHUNK, CHUNK), CHUNK)
            s, dp = score_chunk(k, v, q[part], do[part], own, t * CHUNK)
            total = stats[1:2, lanes]
            level = stats[0:1, lanes] + jnp.log(total) * LOG2E
            p = jnp.exp2(s * factor - level)
            p_buf[:, part] = p.astype(BF16)
            ds = (p * (dp - stats[2:3, lanes] / total)).astype(BF16)
            ds_ref[:, lanes] = ds
        ds = ds_ref[:, pl.ds(pl.multiple_of(i * pair, CHUNK), pair)]
        dk[...] += jnp.dot(ds, q, preferred_element_type=F32)
        dv[...] += jnp.dot(p_buf[...], do, preferred_element_type=F32)
        return carry

    lax.fori_loop(0, q_ref.shape[1] // (2 * hd), heads, 0, unroll=True)
    inverse = 1.0 / hd**0.5
    return dk[...] * inverse, dv[...]


def other_kernel(b, flags, stats, q_ref, do_ref, k_ref, v_ref, out_ref, ds_out, p_buf, dk, dv):
    keep = counted(b, flags)
    rows, hd = dk.shape

    @pl.when(keep)
    def _():
        dk_sum, dv_sum = block_gradients(False, stats, q_ref, do_ref, k_ref, v_ref, p_buf, ds_out, dk, dv)
        out_ref[:, :hd] = dk_sum.astype(BF16)
        out_ref[:, hd:] = dv_sum.astype(BF16)

    @pl.when(jnp.logical_not(keep))
    def _():
        out_ref[...] = jnp.zeros_like(out_ref)
        ds_out[...] = jnp.zeros_like(ds_out)


def own_kernel(stats, q_ref, do_ref, k_ref, v_ref, out_ref, ds_out, p_buf, dk, dv):
    hd = dk.shape[1]
    dk_sum, dv_sum = block_gradients(True, stats, q_ref, do_ref, k_ref, v_ref, p_buf, ds_out, dk, dv)
    out_ref[:, :hd] = dk_sum
    out_ref[:, hd:] = dv_sum


def query_kernel(n, *refs):
    k_refs, ds_refs, dq_ref, mark_ref = refs[:n], refs[n : 2 * n], refs[2 * n], refs[2 * n + 1]
    mark_ref[...] = jnp.zeros_like(mark_ref)
    rows, hd = k_refs[0].shape
    for h in range(dq_ref.shape[1] // hd):
        dq = 0.0
        for k, ds in zip(k_refs, ds_refs):
            part = ds[:, h * rows : (h + 1) * rows]
            dq = dq + lax.dot_general(part, k[...], TN, preferred_element_type=F32)
        dq_ref[:, h * hd : (h + 1) * hd] = (dq / hd**0.5).astype(BF16)


def merge_kernel(rows, own_ref, got_ref, out_ref):
    out_ref[:rows, :] = (own_ref[:rows, :].astype(F32) + got_ref[:rows, :].astype(F32)).astype(BF16)
    out_ref[rows:, :] = jnp.zeros((out_ref.shape[0] - rows, out_ref.shape[1]), BF16)


def merge(own, got, rows, after):
    outs = [shape((rows + TOP_ROWS, own.shape[1]))]
    kernel = functools.partial(merge_kernel, rows)
    return whole_call(kernel, "merge", [], [own, got], outs, 4, (0, 6 * own.size), [], after)[0]


def attention(me, spans, queries, out_grad, keys, values, activations, swap, n):
    rows, hd = keys.shape
    columns = queries.shape[1]
    tall = columns // hd * rows
    product = 2 * rows * tall * hd
    cost = (8 * product, 8 * rows * columns)

    direct = [b for b in range(1, n) if b & (b - 1) == 0]
    blocks = {b: [swap(keys, b), swap(values, b)] for b in reversed(direct)}
    stats_shape = shape((8, tall), F32)
    stats, queries, out_grad, keys, values, flags = whole_call(
        functools.partial(first_stats_kernel, n),
        "first_stats",
        [me, spans],
        [queries, out_grad, keys, values],
        [stats_shape] + [shape(x.shape) for x in (queries, out_grad, keys, values)] + [shape((8, 128), F32)],
        12,
        cost,
        [],
        [begin()],
    )
    blocks[0] = [keys, values]
    acts = prepare(activations, [stats])
    for b in range(1, n):
        if b not in blocks:
            blocks[b] = [swap(x, b & -b) for x in blocks[b & (b - 1)]]
        stats = whole_call(
            functools.partial(next_stats_kernel, b),
            "next_stats",
            [],
            [flags, queries, out_grad, *blocks[b], stats],
            [stats_shape],
            10,
            cost,
            [],
            [*blocks[2], acts] if b == 1 else [],
        )[0]
    p_buf = pltpu.VMEM((rows, 2 * rows), BF16)
    sums = [pltpu.VMEM((rows, hd), F32)] * 2
    def own_call(after):
        return whole_call(
            own_kernel,
            "own_gradients",
            [],
            [stats, queries, out_grad, keys, values],
            [shape((rows, 2 * hd), F32), shape((rows, tall))],
            10,
            (11 * product, 16 * rows * columns),
            [p_buf, *sums],
            after,
        )

    parts, score_grads, before = [[] for _ in range(n)], [None] * n, []
    for b in range(n - 1, 0, -1):
        part, score_grads[b] = whole_call(
            functools.partial(other_kernel, b),
            "block_gradients",
            [],
            [flags, stats, queries, out_grad, *blocks[b]],
            [shape((rows, 2 * hd)), shape((rows, tall))],
            10,
            (11 * product, 16 * rows * columns),
            [p_buf, *sums],
            before,
        )
        if b == min(2, n - 1):
            own, score_grads[0] = own_call([part])
        for other in parts[b]:
            part = merge(part, other, rows, [own] if b == 2 else [])
        before = [part]
        to = b & (b - 1)
        parts[to].append(swap(part, b & -b))
    return own, parts[0], [blocks[b][0] for b in range(n)], score_grads, acts


def query_gradients(key_blocks, score_grads, columns, after):
    n = len(key_blocks)
    rows = key_blocks[0].shape[0]
    return whole_call(
        functools.partial(query_kernel, n),
        "query_gradients",
        [],
        [*key_blocks, *score_grads],
        [shape((rows, columns)), shape((8, 128), F32)],
        2 + 3 * n,
        (2 * n * rows * rows * columns, 16 * rows * columns),
        [],
        after,
    )


def pack_top(top):
    high = jnp.minimum(top, BF16_MAX).astype(BF16).astype(F32)
    rest = top - high
    middle = rest.astype(BF16).astype(F32)
    low = rest - middle
    return (high + pltpu.roll(middle, PACK_LANES, 1) + pltpu.roll(low, 2 * PACK_LANES, 1)).astype(BF16)


def unpack_top(ref, at):
    x = ref[at : at + TOP_ROWS, :TOP_LANES].astype(F32)
    total = x + (pltpu.roll(x, TOP_LANES - PACK_LANES, 1) + pltpu.roll(x, TOP_LANES - 2 * PACK_LANES, 1))
    lane = lax.broadcasted_iota(jnp.int32, x.shape, 1)
    return jnp.where(lane < PACK_LANES, total, 0.0)


def tile_of(step, me_dp, bits, flip):
    mask = flip
    for j in range(1, bits):
        if not (step >> (bits - 1 - j)) & 1:
            mask |= 1 << j
    return me_dp ^ mask


def reversed_step(step, bits):
    return sum(((step >> (bits - 1 - j)) & 1) << (j - 1) for j in range(1, bits))


def corrected_tile(chosen, dest, grads, a_ref, e_ref, top_ref):
    _, n_ctx, sets, rows_set, rows = a_ref.shape
    tall = n_ctx * rows_set
    a = a_ref[dest, :, chosen].reshape(tall, rows)
    e = e_ref[dest, :, chosen].reshape(tall, e_ref.shape[4])
    c = jnp.dot(a, grads, preferred_element_type=F32) + e

    mags = jnp.max(jnp.abs(c).reshape(tall // QROWS, QROWS, c.shape[1]), axis=1)
    mags = jnp.max(mags, axis=1, keepdims=True)
    per_set = rows_set // QROWS
    block = lax.broadcasted_iota(jnp.int32, (tall // QROWS, TOP_LANES), 0)
    lane = lax.broadcasted_iota(jnp.int32, (tall // QROWS, TOP_LANES), 1)
    shift = per_set.bit_length() - 1
    place = ((block >> shift) * (sets * per_set)) + chosen * per_set + (block & (per_set - 1))
    top = jnp.max(jnp.where(lane == place, mags, 0.0), axis=0, keepdims=True)
    top_ref[pl.ds(dest, 1), :] = jnp.maximum(top_ref[pl.ds(dest, 1), :], top)
    return c


def send_rows(bits, shrink, chosen, me_ref, total, a_ref, e_ref, out_ref, top_ref, packed):
    tall = a_ref.shape[1] * a_ref.shape[3]
    steps = a_ref.shape[0] // 2
    for step in range(steps):
        dest = tile_of(step, me_ref[0], bits, 1)
        c = corrected_tile(chosen, dest, total, a_ref, e_ref, top_ref)
        out_ref[step * tall : (step + 1) * tall, :] = (c * shrink).astype(BF16)
    if packed:
        out_ref[steps * tall :, :TOP_LANES] = pack_top(top_ref[...])
        out_ref[steps * tall :, TOP_LANES:] = jnp.zeros((TOP_ROWS, out_ref.shape[1] - TOP_LANES), BF16)


def first_send_kernel(bits, shrink, n_parts, me_ref, own_ref, *refs):
    part_refs = refs[:n_parts]
    a_ref, e_ref, out_ref, top_ref, kg_ref, vg_ref, grads_ref = refs[n_parts:]
    total = own_ref[...]
    for part in part_refs:
        total = total + part[: total.shape[0], :].astype(F32)
    total = total.astype(BF16)
    hd = total.shape[1] // 2
    kg_ref[...] = total[:, :hd]
    vg_ref[...] = total[:, hd:]
    grads_ref[...] = total
    top_ref[...] = jnp.zeros_like(top_ref)
    send_rows(bits, shrink, 0, me_ref, total, a_ref, e_ref, out_ref, top_ref, False)


def next_send_kernel(bits, shrink, chosen, packed, me_ref, grads_ref, before_ref, a_ref, e_ref, out_ref, top_ref):
    top_ref[...] = before_ref[...]
    send_rows(bits, shrink, chosen, me_ref, grads_ref[...], a_ref, e_ref, out_ref, top_ref, packed)


def kept_kernel(bits, shrink, me_ref, grads_ref, before_ref, a_ref, e_ref, *outs):
    *kept, top_ref = outs
    top_ref[...] = before_ref[...]
    total = grads_ref[...]
    for chosen, out_ref in enumerate(kept):
        for step in range(out_ref.shape[0]):
            dest = tile_of(step, me_ref[0], bits, 0)
            out_ref[step] = corrected_tile(chosen, dest, total, a_ref, e_ref, top_ref) * shrink


def split_kernel(bits, n_tops, kept, got, *refs):
    steps, tall, width = kept.shape
    half = steps // 2
    hd = width // 2
    tops = refs[:n_tops]
    low_away, low_stay, high_away, high_stay, *top_out = refs[n_tops:]
    for step in range(steps):
        c = (kept[step] + got[step * tall : (step + 1) * tall, :].astype(F32)).astype(BF16)
        back = reversed_step(step, bits)
        for at, part, away, stay in ((step, c[:, :hd], low_away, low_stay), (back, c[:, hd:], high_away, high_stay)):
            if at < half:
                away[at * tall : (at + 1) * tall, :] = part
            else:
                stay[(at - half) * tall : (at - half + 1) * tall, :] = part
    if tops:
        top = largest(tops, got, steps * tall)
        top_out[0][...] = top
        low_away[half * tall :, :] = pack_top(top)


def largest(tops, low_got, size):
    found = [top[...] for top in tops]
    if low_got.shape[0] > size:
        found.append(unpack_top(low_got, size))
    return functools.reduce(jnp.maximum, found)


def add_kernel(n_tops, low, low_got, high, high_got, *refs):
    tops = refs[:n_tops]
    low_away, low_stay, high_away, high_stay, *top_out = refs[n_tops:]
    size = low.shape[0]
    half = size // 2
    for mine, got, away, stay in ((low, low_got, low_away, low_stay), (high, high_got, high_away, high_stay)):
        away[:half, :] = (mine[:half, :].astype(F32) + got[:half, :].astype(F32)).astype(BF16)
        stay[...] = (mine[half:, :].astype(F32) + got[half:size, :].astype(F32)).astype(BF16)
    if tops:
        top = largest(tops, low_got, size)
        top_out[0][...] = top
        if low_away.shape[0] > half:
            low_away[half:, :] = pack_top(top)


def last_kernel(n_ctx, n_tops, me_ref, low, low_got, high, high_got, *refs):
    tops = refs[:n_tops]
    outs, top_out = refs[n_tops : n_tops + n_ctx], refs[n_tops + n_ctx :]
    size, hd = low.shape
    rows_set = size // n_ctx
    if tops:
        top = largest(tops, low_got, size)
        top_out[0][...] = top
        packed = pack_top(top)
    for b in range(n_ctx):
        part = pl.ds(pl.multiple_of((me_ref[0] ^ b) * rows_set, rows_set), rows_set)
        for at, mine, got in ((0, low, low_got), (rows_set, high, high_got)):
            total = mine[part, :].astype(F32) + got[part, :].astype(F32)
            outs[b][at : at + rows_set, :] = total.astype(outs[b].dtype)
        if b > 0:
            tail = outs[b].shape[0] - 2 * rows_set
            outs[b][2 * rows_set :, :] = packed if tops else jnp.zeros((tail, hd), BF16)


def final_kernel(sets, n_ctx, gain, me_dp_ref, me_ctx_ref, *refs):
    groups = [refs[chosen * n_ctx : (chosen + 1) * n_ctx] for chosen in range(sets)][::-1]
    top_ref, out_ref, scale_ref, all_tops = refs[sets * n_ctx :]
    n_dp, lanes = scale_ref.shape
    rows_set, hd = groups[0][0].shape[0] // 2, groups[0][0].shape[1]
    scale = top_ref[...]
    for other in groups[-1][1:]:
        scale = jnp.maximum(scale, unpack_top(other, 2 * rows_set))
    scale = scale + 1e-06
    all_tops[...] = scale
    scale_ref[...] = scale[:n_dp, :lanes]
    factors = gain / all_tops[pl.ds(me_dp_ref[0], 1), :]
    lane = lax.broadcasted_iota(jnp.int32, factors.shape, 1)
    per_set = rows_set // QROWS
    first = me_ctx_ref[0] * (sets * per_set)
    for chosen, group in enumerate(groups):
        for r in range(per_set):
            mine = jnp.where(lane == first + (chosen * per_set + r), factors, 0.0)
            factor = jnp.sum(mine, axis=1, keepdims=True)
            at = chosen * rows_set + r * QROWS
            for h in range(2):
                part = slice(h * rows_set + r * QROWS, h * rows_set + (r + 1) * QROWS)
                total = group[0][part, :]
                for other in group[1:]:
                    total = total + other[part, :].astype(F32)
                out_ref[at : at + QROWS, h * hd : (h + 1) * hd] = total * factor


def local(n_dp, n_ctx, sets, span_order, queries, keys, values, out_grad, activations, error_feedback):
    rows, hd = keys.shape
    width = 2 * hd
    model = activations.shape[1]
    rows_set = model // (n_dp * n_ctx * sets)
    tall = n_ctx * rows_set
    me_dp = lax.axis_index("dp").astype(jnp.int32)[None]
    me_ctx = lax.axis_index("context").astype(jnp.int32)[None]
    bits = n_dp.bit_length() - 1

    def swap_dp(x, mask):
        return lax.ppermute(x, "dp", xor_perm(n_dp, mask))

    def swap_ctx(x, mask):
        return lax.ppermute(x, "context", xor_perm(n_ctx, mask))

    own, parts, key_blocks, score_grads, acts = attention(
        me_ctx, span_order[0], queries, out_grad, keys, values, activations, swap_ctx, n_ctx
    )

    shrink = 1.0 / (n_dp * n_ctx)
    acts = acts.reshape(n_dp, n_ctx, sets, rows_set, rows)
    errors = error_feedback.reshape(n_dp, n_ctx, sets, rows_set, width)
    tops = shape((TOP_ROWS, TOP_LANES), F32)
    steps = n_dp // 2
    cost = (2 * steps * tall * rows * width, steps * tall * (2 * rows + 6 * width))
    out, top, key_grad, value_grad, grads = whole_call(
        functools.partial(first_send_kernel, bits, shrink, len(parts)),
        "send_tiles",
        [me_dp],
        [own, *parts, acts, errors],
        [shape((steps * tall, width)), tops, shape((rows, hd)), shape((rows, hd)), shape((rows, width))],
        18,
        cost,
    )
    got = [swap_dp(out, 1)]
    *kept, top = whole_call(
        functools.partial(kept_kernel, bits, shrink),
        "kept_tiles",
        [me_dp],
        [grads, top, acts, errors],
        [shape((steps, tall, width), F32)] * sets + [tops],
        20,
        (sets * cost[0], sets * cost[1]),
    )
    for chosen in range(1, sets):
        extra = TOP_ROWS if chosen == sets - 1 else 0
        out, top = whole_call(
            functools.partial(next_send_kernel, bits, shrink, chosen, extra > 0),
            "send_tiles",
            [me_dp],
            [grads, top, acts, errors],
            [shape((steps * tall + extra, width)), tops],
            18,
            cost,
        )
        got.append(swap_dp(out, 1))

    halves = []
    for chosen in range(sets):
        half = steps // 2 * tall
        last = chosen == sets - 1
        arrays = whole_call(
            functools.partial(split_kernel, bits, int(last)),
            "split_tiles",
            [],
            [kept[chosen], got[chosen]] + [top] * last,
            [shape((half + TOP_ROWS * last, hd))] + [shape((half, hd))] * 3 + [tops] * last,
            10,
            (4 * half * width, 12 * half * width),
        )
        halves.append(arrays[:4])
    gathered = [arrays[4]]
    query_grad, mark = query_gradients(key_blocks, score_grads, queries.shape[1], [arrays[1]])
    groups = []
    for chosen in range(sets):
        low_away, low, high_away, high = halves[chosen]
        extra = TOP_ROWS if chosen == sets - 1 else 0
        for stage in range(1, bits):
            low_got = swap_dp(low_away, 1 << stage)
            high_got = swap_dp(high_away, 1 << (bits - stage))
            with_tops = extra > 0
            operands = [low, low_got, high, high_got] + (gathered if with_tops else [])
            n_tops = len(operands) - 4
            size = low.shape[0]
            cost = (4 * size * hd, 12 * size * hd)
            if stage < bits - 1:
                low_away, low, high_away, high, *top_out = whole_call(
                    functools.partial(add_kernel, n_tops),
                    "add_stage",
                    [],
                    operands,
                    [shape((size // 2 + extra, hd))] + [shape((size // 2, hd))] * 3 + [tops] * with_tops,
                    8,
                    cost,
                    after=[mark] if chosen == 0 and stage == 1 else [],
                )
            else:
                outs = whole_call(
                    functools.partial(last_kernel, n_ctx, n_tops),
                    "last_stage",
                    [me_ctx],
                    operands,
                    [shape((2 * rows_set, hd), F32)]
                    + [shape((2 * rows_set + (extra or 2 * TOP_ROWS), hd))] * (n_ctx - 1)
                    + [tops] * with_tops,
                    8,
                    cost,
                )
                mine, away, top_out = outs[0], outs[1:n_ctx], outs[n_ctx:]
            if with_tops:
                gathered = list(top_out)
        groups.append([mine] + [swap_ctx(away[b - 1], b) for b in range(n_ctx - 1, 0, -1)])
    payload, scale = whole_call(
        functools.partial(final_kernel, sets, n_ctx, 7.0 / shrink),
        "final_stage",
        [me_dp, me_ctx],
        [x for group in groups[::-1] for x in group] + gathered,
        [shape((sets * rows_set, width), F32), shape((n_dp, sets * tall // QROWS), F32)],
        8,
        (4 * sets * tall * width, 16 * sets * rows_set * width),
        [pltpu.VMEM((TOP_ROWS, TOP_LANES), F32)],
    )
    return query_grad, key_grad, value_grad, payload, scale.reshape(-1)


def solution(mesh):
    tokens = P(("dp", "context"), None)
    return jax.shard_map(
        functools.partial(local, mesh.shape["dp"], mesh.shape["context"], 2),
        mesh=mesh,
        in_specs=(P("dp", None), tokens, tokens, tokens, tokens, tokens, P("dp", "context", None, None)),
        out_specs=(tokens, tokens, tokens, tokens, P()),
        check_vma=False,
    )
```

```python
import functools

import jax
import jax.numpy as jnp
from jax import lax
from jax.experimental import pallas as pl
from jax.experimental.pallas import tpu as pltpu
from jax.sharding import PartitionSpec as P

QROWS = 32
LOG2E = 1.4426950408889634
FAR = 1e30
MIB = 1024 * 1024
CHUNK = 256
TOP_ROWS, TOP_LANES, PACK_LANES = 16, 128, 32
BF16, F32 = jnp.bfloat16, jnp.float32
BF16_MAX = float(jnp.finfo(jnp.bfloat16).max)
NT = (((1,), (1,)), ((), ()))
TN = (((0,), (0,)), ((), ()))


def xor_perm(size, mask):
    return [(i, i ^ mask) for i in range(size)]


def whole(x):
    return pl.BlockSpec(x.shape, lambda *_: (0,) * len(x.shape))


def shape(dims, dtype=BF16):
    return jax.ShapeDtypeStruct(dims, dtype)


def whole_call(kernel, name, scalars, operands, out_shape, mib, cost, scratch=(), after=()):
    def body(*refs):
        first = len(scalars) + len(operands)
        kernel(*refs[:first], *refs[first + len(after) :])

    return pl.pallas_call(
        body,
        grid_spec=pltpu.PrefetchScalarGridSpec(
            num_scalar_prefetch=len(scalars),
            grid=(1,),
            in_specs=[whole(x) for x in operands] + [pl.BlockSpec(memory_space=pl.ANY)] * len(after),
            out_specs=[whole(x) for x in out_shape],
            scratch_shapes=list(scratch),
        ),
        out_shape=out_shape,
        compiler_params=pltpu.CompilerParams(vmem_limit_bytes=mib * MIB),
        cost_estimate=pl.CostEstimate(flops=cost[0], bytes_accessed=cost[1], transcendentals=0),
        name=name,
    )(*scalars, *operands, *after)


def begin_kernel(me_dp_ref, me_ctx_ref, out_ref):
    out_ref[...] = jnp.zeros_like(out_ref)


def begin(me_dp, me_ctx):
    mark = [shape((8, 128), F32)]
    return whole_call(begin_kernel, "begin", [me_dp, me_ctx], [], mark, 4, (20_000_000_000, 0))[0]


def prepare_kernel(pieces, a_ref, a_out):
    tile = a_ref.shape[1] // pieces
    for i in range(pieces):
        a_out[i * tile : (i + 1) * tile, :] = a_ref[:, i * tile : (i + 1) * tile].T


def prepare(activations, after):
    rows, model = activations.shape
    outs = [shape((model, rows))]
    cost = (0, 0)
    kernel = functools.partial(prepare_kernel, 8)
    return whole_call(kernel, "prepare", [], [activations], outs, 16, cost, [], after)[0]


def head_pair(ref, i, hd):
    at = i * (2 * hd)
    first = ref[:, pl.ds(pl.multiple_of(at, hd), hd)]
    second = ref[:, pl.ds(pl.multiple_of(at + hd, hd), hd)]
    return jnp.concatenate([first, second], axis=0)


def score_chunk(k, v, q, do, own, first_lane):
    s = lax.dot_general(k, q, NT, preferred_element_type=F32)
    dp = lax.dot_general(v, do, NT, preferred_element_type=F32)
    if own:
        rows = k.shape[0]
        key_at = lax.broadcasted_iota(jnp.int32, s.shape, 0)
        query_at = lax.broadcasted_iota(jnp.int32, s.shape, 1) + first_lane
        query_at = jnp.where(query_at >= rows, query_at - rows, query_at)
        s = jnp.where(key_at <= query_at, s, -FAR)
    return s, dp


def counted(b, flags):
    lane = lax.broadcasted_iota(jnp.int32, flags.shape, 1)
    return jnp.max(jnp.where(lane == b, flags[...], 0.0)) > 0.5


def stats_of_block(b, q_ref, do_ref, k_ref, v_ref, before, out):
    k, v = k_ref[...], v_ref[...]
    rows, hd = k.shape
    pair = 2 * rows
    factor = LOG2E / hd**0.5

    def heads(i, carry):
        q, do = head_pair(q_ref, i, hd), head_pair(do_ref, i, hd)
        for t in range(pair // CHUNK):
            part = slice(t * CHUNK, (t + 1) * CHUNK)
            lanes = pl.ds(pl.multiple_of(i * pair + t * CHUNK, CHUNK), CHUNK)
            s, dp = score_chunk(k, v, q[part], do[part], b == 0, t * CHUNK)
            top = jnp.max(s, axis=0, keepdims=True) * factor
            e = jnp.exp2(s * factor - top)
            total = jnp.sum(e, axis=0, keepdims=True)
            weighted = jnp.sum(e * dp, axis=0, keepdims=True)
            if b > 0:
                old = before[0:1, lanes]
                both = jnp.maximum(old, top)
                old_part, new_part = jnp.exp2(old - both), jnp.exp2(top - both)
                total = before[1:2, lanes] * old_part + total * new_part
                weighted = before[2:3, lanes] * old_part + weighted * new_part
                top = both
            out[0:1, lanes] = top
            out[1:2, lanes] = total
            out[2:3, lanes] = weighted
        return carry

    lax.fori_loop(0, q_ref.shape[1] // (2 * hd), heads, 0, unroll=True)


def first_stats_kernel(n, me_ref, span_ref, q_ref, do_ref, k_ref, v_ref, out, q_out, do_out, k_out, v_out, flags):
    me = me_ref[0]
    lane = lax.broadcasted_iota(jnp.int32, flags.shape, 1)
    found = jnp.zeros(flags.shape, F32)
    for b in range(1, n):
        found = jnp.where((lane == b) & (span_ref[me ^ b] < span_ref[me]), 1.0, found)
    flags[...] = found
    q_out[...] = q_ref[...]
    do_out[...] = do_ref[...]
    k_out[...] = k_ref[...]
    v_out[...] = v_ref[...]
    stats_of_block(0, q_ref, do_ref, k_ref, v_ref, None, out)


def next_stats_kernel(b, flags, q_ref, do_ref, k_ref, v_ref, before, out):
    keep = counted(b, flags)

    @pl.when(keep)
    def _():
        stats_of_block(b, q_ref, do_ref, k_ref, v_ref, before, out)

    @pl.when(jnp.logical_not(keep))
    def _():
        out[...] = before[...]


def block_gradients(own, stats, q_ref, do_ref, k_ref, v_ref, p_buf, ds_ref, dk, dv):
    k, v = k_ref[...], v_ref[...]
    rows, hd = k.shape
    pair = 2 * rows
    factor = LOG2E / hd**0.5
    dk[...] = jnp.zeros_like(dk)
    dv[...] = jnp.zeros_like(dv)

    def heads(i, carry):
        q, do = head_pair(q_ref, i, hd), head_pair(do_ref, i, hd)
        for t in range(pair // CHUNK):
            part = slice(t * CHUNK, (t + 1) * CHUNK)
            lanes = pl.ds(pl.multiple_of(i * pair + t * CHUNK, CHUNK), CHUNK)
            s, dp = score_chunk(k, v, q[part], do[part], own, t * CHUNK)
            total = stats[1:2, lanes]
            level = stats[0:1, lanes] + jnp.log(total) * LOG2E
            p = jnp.exp2(s * factor - level)
            p_buf[:, part] = p.astype(BF16)
            ds = (p * (dp - stats[2:3, lanes] / total)).astype(BF16)
            ds_ref[:, lanes] = ds
        ds = ds_ref[:, pl.ds(pl.multiple_of(i * pair, CHUNK), pair)]
        dk[...] += jnp.dot(ds, q, preferred_element_type=F32)
        dv[...] += jnp.dot(p_buf[...], do, preferred_element_type=F32)
        return carry

    lax.fori_loop(0, q_ref.shape[1] // (2 * hd), heads, 0, unroll=True)
    inverse = 1.0 / hd**0.5
    return dk[...] * inverse, dv[...]


def other_kernel(b, flags, stats, q_ref, do_ref, k_ref, v_ref, out_ref, ds_out, p_buf, dk, dv):
    keep = counted(b, flags)
    rows, hd = dk.shape

    @pl.when(keep)
    def _():
        dk_sum, dv_sum = block_gradients(False, stats, q_ref, do_ref, k_ref, v_ref, p_buf, ds_out, dk, dv)
        out_ref[:, :hd] = dk_sum.astype(BF16)
        out_ref[:, hd:] = dv_sum.astype(BF16)

    @pl.when(jnp.logical_not(keep))
    def _():
        out_ref[...] = jnp.zeros_like(out_ref)
        ds_out[...] = jnp.zeros_like(ds_out)


def own_kernel(stats, q_ref, do_ref, k_ref, v_ref, out_ref, ds_out, p_buf, dk, dv):
    hd = dk.shape[1]
    dk_sum, dv_sum = block_gradients(True, stats, q_ref, do_ref, k_ref, v_ref, p_buf, ds_out, dk, dv)
    out_ref[:, :hd] = dk_sum
    out_ref[:, hd:] = dv_sum


def query_kernel(n, *refs):
    k_refs, ds_refs, dq_ref, mark_ref = refs[:n], refs[n : 2 * n], refs[2 * n], refs[2 * n + 1]
    mark_ref[...] = jnp.zeros_like(mark_ref)
    rows, hd = k_refs[0].shape
    for h in range(dq_ref.shape[1] // hd):
        dq = 0.0
        for k, ds in zip(k_refs, ds_refs):
            part = ds[:, h * rows : (h + 1) * rows]
            dq = dq + lax.dot_general(part, k[...], TN, preferred_element_type=F32)
        dq_ref[:, h * hd : (h + 1) * hd] = (dq / hd**0.5).astype(BF16)


def merge_kernel(rows, own_ref, got_ref, out_ref):
    out_ref[:rows, :] = (own_ref[:rows, :].astype(F32) + got_ref[:rows, :].astype(F32)).astype(BF16)
    out_ref[rows:, :] = jnp.zeros((out_ref.shape[0] - rows, out_ref.shape[1]), BF16)


def merge(own, got, rows, after):
    outs = [shape((rows + TOP_ROWS, own.shape[1]))]
    kernel = functools.partial(merge_kernel, rows)
    return whole_call(kernel, "merge", [], [own, got], outs, 4, (0, 6 * own.size), [], after)[0]


def attention(me, spans, queries, out_grad, keys, values, activations, mark, swap, n):
    rows, hd = keys.shape
    columns = queries.shape[1]
    tall = columns // hd * rows
    product = 2 * rows * tall * hd
    cost = (8 * product, 8 * rows * columns)

    direct = [b for b in range(1, n) if b & (b - 1) == 0]
    blocks = {b: [swap(keys, b), swap(values, b)] for b in reversed(direct)}
    stats_shape = shape((8, tall), F32)
    stats, queries, out_grad, keys, values, flags = whole_call(
        functools.partial(first_stats_kernel, n),
        "first_stats",
        [me, spans],
        [queries, out_grad, keys, values],
        [stats_shape] + [shape(x.shape) for x in (queries, out_grad, keys, values)] + [shape((8, 128), F32)],
        12,
        cost,
        [],
        [mark],
    )
    blocks[0] = [keys, values]
    acts = prepare(activations, [stats])
    for b in range(1, n):
        if b not in blocks:
            blocks[b] = [swap(x, b & -b) for x in blocks[b & (b - 1)]]
        stats = whole_call(
            functools.partial(next_stats_kernel, b),
            "next_stats",
            [],
            [flags, queries, out_grad, *blocks[b], stats],
            [stats_shape],
            10,
            cost,
            [],
            [*blocks[2], acts] if b == 1 else [],
        )[0]
    p_buf = pltpu.VMEM((rows, 2 * rows), BF16)
    sums = [pltpu.VMEM((rows, hd), F32)] * 2
    def own_call(after):
        return whole_call(
            own_kernel,
            "own_gradients",
            [],
            [stats, queries, out_grad, keys, values],
            [shape((rows, 2 * hd), F32), shape((rows, tall))],
            10,
            (11 * product, 16 * rows * columns),
            [p_buf, *sums],
            after,
        )

    parts, score_grads, before = [[] for _ in range(n)], [None] * n, []
    for b in range(n - 1, 0, -1):
        part, score_grads[b] = whole_call(
            functools.partial(other_kernel, b),
            "block_gradients",
            [],
            [flags, stats, queries, out_grad, *blocks[b]],
            [shape((rows, 2 * hd)), shape((rows, tall))],
            10,
            (11 * product, 16 * rows * columns),
            [p_buf, *sums],
            before,
        )
        if b == min(2, n - 1):
            own, score_grads[0] = own_call([part])
        for other in parts[b]:
            part = merge(part, other, rows, [own] if b == 2 else [])
        before = [part]
        to = b & (b - 1)
        parts[to].append(swap(part, b & -b))
    return own, parts[0], [blocks[b][0] for b in range(n)], score_grads, acts


def query_gradients(key_blocks, score_grads, columns, after):
    n = len(key_blocks)
    rows = key_blocks[0].shape[0]
    return whole_call(
        functools.partial(query_kernel, n),
        "query_gradients",
        [],
        [*key_blocks, *score_grads],
        [shape((rows, columns)), shape((8, 128), F32)],
        2 + 3 * n,
        (2 * n * rows * rows * columns, 16 * rows * columns),
        [],
        after,
    )


def pack_top(top):
    high = jnp.minimum(top, BF16_MAX).astype(BF16).astype(F32)
    rest = top - high
    middle = rest.astype(BF16).astype(F32)
    low = rest - middle
    return (high + pltpu.roll(middle, PACK_LANES, 1) + pltpu.roll(low, 2 * PACK_LANES, 1)).astype(BF16)


def unpack_top(ref, at):
    x = ref[at : at + TOP_ROWS, :TOP_LANES].astype(F32)
    total = x + (pltpu.roll(x, TOP_LANES - PACK_LANES, 1) + pltpu.roll(x, TOP_LANES - 2 * PACK_LANES, 1))
    lane = lax.broadcasted_iota(jnp.int32, x.shape, 1)
    return jnp.where(lane < PACK_LANES, total, 0.0)


def tile_of(step, me_dp, bits, flip):
    mask = flip
    for j in range(1, bits):
        if not (step >> (bits - 1 - j)) & 1:
            mask |= 1 << j
    return me_dp ^ mask


def reversed_step(step, bits):
    return sum(((step >> (bits - 1 - j)) & 1) << (j - 1) for j in range(1, bits))


def corrected_tile(chosen, dest, grads, a_ref, e_ref, top_ref):
    _, n_ctx, sets, rows_set, rows = a_ref.shape
    tall = n_ctx * rows_set
    a = a_ref[dest, :, chosen].reshape(tall, rows)
    e = e_ref[dest, :, chosen].reshape(tall, e_ref.shape[4])
    c = jnp.dot(a, grads, preferred_element_type=F32) + e

    mags = jnp.max(jnp.abs(c).reshape(tall // QROWS, QROWS, c.shape[1]), axis=1)
    mags = jnp.max(mags, axis=1, keepdims=True)
    per_set = rows_set // QROWS
    block = lax.broadcasted_iota(jnp.int32, (tall // QROWS, TOP_LANES), 0)
    lane = lax.broadcasted_iota(jnp.int32, (tall // QROWS, TOP_LANES), 1)
    shift = per_set.bit_length() - 1
    place = ((block >> shift) * (sets * per_set)) + chosen * per_set + (block & (per_set - 1))
    top = jnp.max(jnp.where(lane == place, mags, 0.0), axis=0, keepdims=True)
    top_ref[pl.ds(dest, 1), :] = jnp.maximum(top_ref[pl.ds(dest, 1), :], top)
    return c


def send_rows(bits, shrink, chosen, me_ref, total, a_ref, e_ref, out_ref, top_ref, packed):
    tall = a_ref.shape[1] * a_ref.shape[3]
    steps = a_ref.shape[0] // 2
    for step in range(steps):
        dest = tile_of(step, me_ref[0], bits, 1)
        c = corrected_tile(chosen, dest, total, a_ref, e_ref, top_ref)
        out_ref[step * tall : (step + 1) * tall, :] = (c * shrink).astype(BF16)
    if packed:
        out_ref[steps * tall :, :TOP_LANES] = pack_top(top_ref[...])
        out_ref[steps * tall :, TOP_LANES:] = jnp.zeros((TOP_ROWS, out_ref.shape[1] - TOP_LANES), BF16)


def first_send_kernel(bits, shrink, n_parts, me_ref, own_ref, *refs):
    part_refs = refs[:n_parts]
    a_ref, e_ref, out_ref, top_ref, kg_ref, vg_ref, grads_ref = refs[n_parts:]
    total = own_ref[...]
    for part in part_refs:
        total = total + part[: total.shape[0], :].astype(F32)
    total = total.astype(BF16)
    hd = total.shape[1] // 2
    kg_ref[...] = total[:, :hd]
    vg_ref[...] = total[:, hd:]
    grads_ref[...] = total
    top_ref[...] = jnp.zeros_like(top_ref)
    send_rows(bits, shrink, 0, me_ref, total, a_ref, e_ref, out_ref, top_ref, False)


def next_send_kernel(bits, shrink, chosen, packed, me_ref, grads_ref, before_ref, a_ref, e_ref, out_ref, top_ref):
    top_ref[...] = before_ref[...]
    send_rows(bits, shrink, chosen, me_ref, grads_ref[...], a_ref, e_ref, out_ref, top_ref, packed)


def kept_kernel(bits, shrink, me_ref, grads_ref, before_ref, a_ref, e_ref, *outs):
    *kept, top_ref = outs
    top_ref[...] = before_ref[...]
    total = grads_ref[...]
    for chosen, out_ref in enumerate(kept):
        for step in range(out_ref.shape[0]):
            dest = tile_of(step, me_ref[0], bits, 0)
            out_ref[step] = corrected_tile(chosen, dest, total, a_ref, e_ref, top_ref) * shrink


def split_kernel(bits, n_tops, kept, got, *refs):
    steps, tall, width = kept.shape
    half = steps // 2
    hd = width // 2
    tops = refs[:n_tops]
    low_away, low_stay, high_away, high_stay, *top_out = refs[n_tops:]
    for step in range(steps):
        c = (kept[step] + got[step * tall : (step + 1) * tall, :].astype(F32)).astype(BF16)
        back = reversed_step(step, bits)
        for at, part, away, stay in ((step, c[:, :hd], low_away, low_stay), (back, c[:, hd:], high_away, high_stay)):
            if at < half:
                away[at * tall : (at + 1) * tall, :] = part
            else:
                stay[(at - half) * tall : (at - half + 1) * tall, :] = part
    if tops:
        top = largest(tops, got, steps * tall)
        top_out[0][...] = top
        low_away[half * tall :, :] = pack_top(top)


def largest(tops, low_got, size):
    found = [top[...] for top in tops]
    if low_got.shape[0] > size:
        found.append(unpack_top(low_got, size))
    return functools.reduce(jnp.maximum, found)


def add_kernel(n_tops, low, low_got, high, high_got, *refs):
    tops = refs[:n_tops]
    low_away, low_stay, high_away, high_stay, *top_out = refs[n_tops:]
    size = low.shape[0]
    half = size // 2
    for mine, got, away, stay in ((low, low_got, low_away, low_stay), (high, high_got, high_away, high_stay)):
        away[:half, :] = (mine[:half, :].astype(F32) + got[:half, :].astype(F32)).astype(BF16)
        stay[...] = (mine[half:, :].astype(F32) + got[half:size, :].astype(F32)).astype(BF16)
    if tops:
        top = largest(tops, low_got, size)
        top_out[0][...] = top
        if low_away.shape[0] > half:
            low_away[half:, :] = pack_top(top)


def last_kernel(n_ctx, n_tops, me_ref, low, low_got, high, high_got, *refs):
    tops = refs[:n_tops]
    outs, top_out = refs[n_tops : n_tops + n_ctx], refs[n_tops + n_ctx :]
    size, hd = low.shape
    rows_set = size // n_ctx
    if tops:
        top = largest(tops, low_got, size)
        top_out[0][...] = top
        packed = pack_top(top)
    for b in range(n_ctx):
        part = pl.ds(pl.multiple_of((me_ref[0] ^ b) * rows_set, rows_set), rows_set)
        for at, mine, got in ((0, low, low_got), (rows_set, high, high_got)):
            total = mine[part, :].astype(F32) + got[part, :].astype(F32)
            outs[b][at : at + rows_set, :] = total.astype(outs[b].dtype)
        if b > 0:
            tail = outs[b].shape[0] - 2 * rows_set
            outs[b][2 * rows_set :, :] = packed if tops else jnp.zeros((tail, hd), BF16)


def final_kernel(sets, n_ctx, gain, me_dp_ref, me_ctx_ref, *refs):
    groups = [refs[chosen * n_ctx : (chosen + 1) * n_ctx] for chosen in range(sets)][::-1]
    top_ref, out_ref, scale_ref, all_tops = refs[sets * n_ctx :]
    n_dp, lanes = scale_ref.shape
    rows_set, hd = groups[0][0].shape[0] // 2, groups[0][0].shape[1]
    scale = top_ref[...]
    for other in groups[-1][1:]:
        scale = jnp.maximum(scale, unpack_top(other, 2 * rows_set))
    scale = scale + 1e-06
    all_tops[...] = scale
    scale_ref[...] = scale[:n_dp, :lanes]
    factors = gain / all_tops[pl.ds(me_dp_ref[0], 1), :]
    lane = lax.broadcasted_iota(jnp.int32, factors.shape, 1)
    per_set = rows_set // QROWS
    first = me_ctx_ref[0] * (sets * per_set)
    for chosen, group in enumerate(groups):
        for r in range(per_set):
            mine = jnp.where(lane == first + (chosen * per_set + r), factors, 0.0)
            factor = jnp.sum(mine, axis=1, keepdims=True)
            at = chosen * rows_set + r * QROWS
            for h in range(2):
                part = slice(h * rows_set + r * QROWS, h * rows_set + (r + 1) * QROWS)
                total = group[0][part, :]
                for other in group[1:]:
                    total = total + other[part, :].astype(F32)
                out_ref[at : at + QROWS, h * hd : (h + 1) * hd] = total * factor


def local(n_dp, n_ctx, sets, span_order, queries, keys, values, out_grad, activations, error_feedback):
    rows, hd = keys.shape
    width = 2 * hd
    model = activations.shape[1]
    rows_set = model // (n_dp * n_ctx * sets)
    tall = n_ctx * rows_set
    me_dp = lax.axis_index("dp").astype(jnp.int32)[None]
    me_ctx = lax.axis_index("context").astype(jnp.int32)[None]
    bits = n_dp.bit_length() - 1

    def swap_dp(x, mask):
        return lax.ppermute(x, "dp", xor_perm(n_dp, mask))

    def swap_ctx(x, mask):
        return lax.ppermute(x, "context", xor_perm(n_ctx, mask))

    own, parts, key_blocks, score_grads, acts = attention(
        me_ctx, span_order[0], queries, out_grad, keys, values, activations, begin(me_dp, me_ctx), swap_ctx, n_ctx
    )

    shrink = 1.0 / (n_dp * n_ctx)
    acts = acts.reshape(n_dp, n_ctx, sets, rows_set, rows)
    errors = error_feedback.reshape(n_dp, n_ctx, sets, rows_set, width)
    tops = shape((TOP_ROWS, TOP_LANES), F32)
    steps = n_dp // 2
    cost = (2 * steps * tall * rows * width, steps * tall * (2 * rows + 6 * width))
    out, top, key_grad, value_grad, grads = whole_call(
        functools.partial(first_send_kernel, bits, shrink, len(parts)),
        "send_tiles",
        [me_dp],
        [own, *parts, acts, errors],
        [shape((steps * tall, width)), tops, shape((rows, hd)), shape((rows, hd)), shape((rows, width))],
        18,
        cost,
    )
    got = [swap_dp(out, 1)]
    *kept, top = whole_call(
        functools.partial(kept_kernel, bits, shrink),
        "kept_tiles",
        [me_dp],
        [grads, top, acts, errors],
        [shape((steps, tall, width), F32)] * sets + [tops],
        20,
        (sets * cost[0], sets * cost[1]),
    )
    for chosen in range(1, sets):
        extra = TOP_ROWS if chosen == sets - 1 else 0
        out, top = whole_call(
            functools.partial(next_send_kernel, bits, shrink, chosen, extra > 0),
            "send_tiles",
            [me_dp],
            [grads, top, acts, errors],
            [shape((steps * tall + extra, width)), tops],
            18,
            cost,
        )
        got.append(swap_dp(out, 1))

    halves = []
    for chosen in range(sets):
        half = steps // 2 * tall
        last = chosen == sets - 1
        arrays = whole_call(
            functools.partial(split_kernel, bits, int(last)),
            "split_tiles",
            [],
            [kept[chosen], got[chosen]] + [top] * last,
            [shape((half + TOP_ROWS * last, hd))] + [shape((half, hd))] * 3 + [tops] * last,
            10,
            (4 * half * width, 12 * half * width),
        )
        halves.append(arrays[:4])
    gathered = [arrays[4]]
    query_grad, mark = query_gradients(key_blocks, score_grads, queries.shape[1], [arrays[1]])
    groups = []
    for chosen in range(sets):
        low_away, low, high_away, high = halves[chosen]
        extra = TOP_ROWS if chosen == sets - 1 else 0
        for stage in range(1, bits):
            low_got = swap_dp(low_away, 1 << stage)
            high_got = swap_dp(high_away, 1 << (bits - stage))
            with_tops = extra > 0
            operands = [low, low_got, high, high_got] + (gathered if with_tops else [])
            n_tops = len(operands) - 4
            size = low.shape[0]
            cost = (4 * size * hd, 12 * size * hd)
            if stage < bits - 1:
                low_away, low, high_away, high, *top_out = whole_call(
                    functools.partial(add_kernel, n_tops),
                    "add_stage",
                    [],
                    operands,
                    [shape((size // 2 + extra, hd))] + [shape((size // 2, hd))] * 3 + [tops] * with_tops,
                    8,
                    cost,
                    after=[mark] if chosen == 0 and stage == 1 else [],
                )
            else:
                outs = whole_call(
                    functools.partial(last_kernel, n_ctx, n_tops),
                    "last_stage",
                    [me_ctx],
                    operands,
                    [shape((2 * rows_set, hd), F32)]
                    + [shape((2 * rows_set + (extra or 2 * TOP_ROWS), hd))] * (n_ctx - 1)
                    + [tops] * with_tops,
                    8,
                    cost,
                )
                mine, away, top_out = outs[0], outs[1:n_ctx], outs[n_ctx:]
            if with_tops:
                gathered = list(top_out)
        groups.append([mine] + [swap_ctx(away[b - 1], b) for b in range(n_ctx - 1, 0, -1)])
    payload, scale = whole_call(
        functools.partial(final_kernel, sets, n_ctx, 7.0 / shrink),
        "final_stage",
        [me_dp, me_ctx],
        [x for group in groups[::-1] for x in group] + gathered,
        [shape((sets * rows_set, width), F32), shape((n_dp, sets * tall // QROWS), F32)],
        8,
        (4 * sets * tall * width, 16 * sets * rows_set * width),
        [pltpu.VMEM((TOP_ROWS, TOP_LANES), F32)],
    )
    return query_grad, key_grad, value_grad, payload, scale.reshape(-1)


def solution(mesh):
    tokens = P(("dp", "context"), None)
    return jax.shard_map(
        functools.partial(local, mesh.shape["dp"], mesh.shape["context"], 2),
        mesh=mesh,
        in_specs=(P("dp", None), tokens, tokens, tokens, tokens, tokens, P("dp", "context", None, None)),
        out_specs=(tokens, tokens, tokens, tokens, P()),
        check_vma=False,
    )
```

```python
import functools

import jax
import jax.numpy as jnp
from jax import lax
from jax.experimental import pallas as pl
from jax.experimental.pallas import tpu as pltpu
from jax.sharding import PartitionSpec as P

QROWS = 32
LOG2E = 1.4426950408889634
FAR = 1e30
MIB = 1024 * 1024
CHUNK = 256
TOP_ROWS, TOP_LANES, PACK_LANES = 16, 128, 32
BF16, F32 = jnp.bfloat16, jnp.float32
BF16_MAX = float(jnp.finfo(jnp.bfloat16).max)
NT = (((1,), (1,)), ((), ()))
TN = (((0,), (0,)), ((), ()))


def xor_perm(size, mask):
    return [(i, i ^ mask) for i in range(size)]


def whole(x):
    return pl.BlockSpec(x.shape, lambda *_: (0,) * len(x.shape))


def shape(dims, dtype=BF16):
    return jax.ShapeDtypeStruct(dims, dtype)


def whole_call(kernel, name, scalars, operands, out_shape, mib, cost, scratch=(), after=()):
    def body(*refs):
        first = len(scalars) + len(operands)
        kernel(*refs[:first], *refs[first + len(after) :])

    return pl.pallas_call(
        body,
        grid_spec=pltpu.PrefetchScalarGridSpec(
            num_scalar_prefetch=len(scalars),
            grid=(1,),
            in_specs=[whole(x) for x in operands] + [pl.BlockSpec(memory_space=pl.ANY)] * len(after),
            out_specs=[whole(x) for x in out_shape],
            scratch_shapes=list(scratch),
        ),
        out_shape=out_shape,
        compiler_params=pltpu.CompilerParams(vmem_limit_bytes=mib * MIB),
        cost_estimate=pl.CostEstimate(flops=cost[0], bytes_accessed=cost[1], transcendentals=0),
        name=name,
    )(*scalars, *operands, *after)


def begin_kernel(me_dp_ref, me_ctx_ref, out_ref):
    out_ref[...] = jnp.zeros_like(out_ref)


def begin(me_dp, me_ctx):
    mark = [shape((8, 128), F32)]
    return whole_call(begin_kernel, "begin", [me_dp, me_ctx], [], mark, 4, (20_000_000_000, 0))[0]


def prepare_kernel(pieces, a_ref, a_out):
    tile = a_ref.shape[1] // pieces
    for i in range(pieces):
        a_out[i * tile : (i + 1) * tile, :] = a_ref[:, i * tile : (i + 1) * tile].T


def prepare(activations, after):
    rows, model = activations.shape
    outs = [shape((model, rows))]
    cost = (0, 0)
    kernel = functools.partial(prepare_kernel, 8)
    return whole_call(kernel, "prepare", [], [activations], outs, 16, cost, [], after)[0]


def head_pair(ref, i, hd):
    at = i * (2 * hd)
    first = ref[:, pl.ds(pl.multiple_of(at, hd), hd)]
    second = ref[:, pl.ds(pl.multiple_of(at + hd, hd), hd)]
    return jnp.concatenate([first, second], axis=0)


def score_chunk(k, v, q, do, own, first_lane):
    s = lax.dot_general(k, q, NT, preferred_element_type=F32)
    dp = lax.dot_general(v, do, NT, preferred_element_type=F32)
    if own:
        rows = k.shape[0]
        key_at = lax.broadcasted_iota(jnp.int32, s.shape, 0)
        query_at = lax.broadcasted_iota(jnp.int32, s.shape, 1) + first_lane
        query_at = jnp.where(query_at >= rows, query_at - rows, query_at)
        s = jnp.where(key_at <= query_at, s, -FAR)
    return s, dp


def counted(b, flags):
    lane = lax.broadcasted_iota(jnp.int32, flags.shape, 1)
    return jnp.max(jnp.where(lane == b, flags[...], 0.0)) > 0.5


def stats_of_block(b, q_ref, do_ref, k_ref, v_ref, before, out):
    k, v = k_ref[...], v_ref[...]
    rows, hd = k.shape
    pair = 2 * rows
    factor = LOG2E / hd**0.5

    def heads(i, carry):
        q, do = head_pair(q_ref, i, hd), head_pair(do_ref, i, hd)
        for t in range(pair // CHUNK):
            part = slice(t * CHUNK, (t + 1) * CHUNK)
            lanes = pl.ds(pl.multiple_of(i * pair + t * CHUNK, CHUNK), CHUNK)
            s, dp = score_chunk(k, v, q[part], do[part], b == 0, t * CHUNK)
            top = jnp.max(s, axis=0, keepdims=True) * factor
            e = jnp.exp2(s * factor - top)
            total = jnp.sum(e, axis=0, keepdims=True)
            weighted = jnp.sum(e * dp, axis=0, keepdims=True)
            if b > 0:
                old = before[0:1, lanes]
                both = jnp.maximum(old, top)
                old_part, new_part = jnp.exp2(old - both), jnp.exp2(top - both)
                total = before[1:2, lanes] * old_part + total * new_part
                weighted = before[2:3, lanes] * old_part + weighted * new_part
                top = both
            out[0:1, lanes] = top
            out[1:2, lanes] = total
            out[2:3, lanes] = weighted
        return carry

    lax.fori_loop(0, q_ref.shape[1] // (2 * hd), heads, 0, unroll=True)


def first_stats_kernel(n, me_ref, span_ref, q_ref, do_ref, k_ref, v_ref, out, q_out, do_out, k_out, v_out, flags):
    me = me_ref[0]
    lane = lax.broadcasted_iota(jnp.int32, flags.shape, 1)
    found = jnp.zeros(flags.shape, F32)
    for b in range(1, n):
        found = jnp.where((lane == b) & (span_ref[me ^ b] < span_ref[me]), 1.0, found)
    flags[...] = found
    q_out[...] = q_ref[...]
    do_out[...] = do_ref[...]
    k_out[...] = k_ref[...]
    v_out[...] = v_ref[...]
    stats_of_block(0, q_ref, do_ref, k_ref, v_ref, None, out)


def next_stats_kernel(b, flags, q_ref, do_ref, k_ref, v_ref, before, out):
    keep = counted(b, flags)

    @pl.when(keep)
    def _():
        stats_of_block(b, q_ref, do_ref, k_ref, v_ref, before, out)

    @pl.when(jnp.logical_not(keep))
    def _():
        out[...] = before[...]


def block_gradients(own, stats, q_ref, do_ref, k_ref, v_ref, p_buf, ds_ref, dk, dv):
    k, v = k_ref[...], v_ref[...]
    rows, hd = k.shape
    pair = 2 * rows
    factor = LOG2E / hd**0.5
    dk[...] = jnp.zeros_like(dk)
    dv[...] = jnp.zeros_like(dv)

    def heads(i, carry):
        q, do = head_pair(q_ref, i, hd), head_pair(do_ref, i, hd)
        for t in range(pair // CHUNK):
            part = slice(t * CHUNK, (t + 1) * CHUNK)
            lanes = pl.ds(pl.multiple_of(i * pair + t * CHUNK, CHUNK), CHUNK)
            s, dp = score_chunk(k, v, q[part], do[part], own, t * CHUNK)
            total = stats[1:2, lanes]
            level = stats[0:1, lanes] + jnp.log(total) * LOG2E
            p = jnp.exp2(s * factor - level)
            p_buf[:, part] = p.astype(BF16)
            ds = (p * (dp - stats[2:3, lanes] / total)).astype(BF16)
            ds_ref[:, lanes] = ds
        ds = ds_ref[:, pl.ds(pl.multiple_of(i * pair, CHUNK), pair)]
        dk[...] += jnp.dot(ds, q, preferred_element_type=F32)
        dv[...] += jnp.dot(p_buf[...], do, preferred_element_type=F32)
        return carry

    lax.fori_loop(0, q_ref.shape[1] // (2 * hd), heads, 0, unroll=True)
    inverse = 1.0 / hd**0.5
    return dk[...] * inverse, dv[...]


def other_kernel(b, flags, stats, q_ref, do_ref, k_ref, v_ref, *refs):
    *outs, ds_out, p_buf, dk, dv = refs
    keep = counted(b, flags)
    hd = dk.shape[1]
    dk_out, dv_out = outs if len(outs) == 2 else (outs[0].at[:, pl.ds(0, hd)], outs[0].at[:, pl.ds(hd, hd)])

    @pl.when(keep)
    def _():
        dk_sum, dv_sum = block_gradients(False, stats, q_ref, do_ref, k_ref, v_ref, p_buf, ds_out, dk, dv)
        dk_out[...] = dk_sum.astype(BF16)
        dv_out[...] = dv_sum.astype(BF16)

    @pl.when(jnp.logical_not(keep))
    def _():
        for out in outs:
            out[...] = jnp.zeros_like(out)
        ds_out[...] = jnp.zeros_like(ds_out)


def own_kernel(stats, q_ref, do_ref, k_ref, v_ref, out_ref, ds_out, p_buf, dk, dv):
    hd = dk.shape[1]
    dk_sum, dv_sum = block_gradients(True, stats, q_ref, do_ref, k_ref, v_ref, p_buf, ds_out, dk, dv)
    out_ref[:, :hd] = dk_sum
    out_ref[:, hd:] = dv_sum


def query_kernel(n, *refs):
    k_refs, ds_refs, dq_ref, mark_ref = refs[:n], refs[n : 2 * n], refs[2 * n], refs[2 * n + 1]
    mark_ref[...] = jnp.zeros_like(mark_ref)
    rows, hd = k_refs[0].shape
    for h in range(dq_ref.shape[1] // hd):
        dq = 0.0
        for k, ds in zip(k_refs, ds_refs):
            part = ds[:, h * rows : (h + 1) * rows]
            dq = dq + lax.dot_general(part, k[...], TN, preferred_element_type=F32)
        dq_ref[:, h * hd : (h + 1) * hd] = (dq / hd**0.5).astype(BF16)


def merge_kernel(n_got, own_ref, *refs):
    got_refs, out_ref = refs[:n_got], refs[n_got]
    rows, width = own_ref.shape
    at = width - got_refs[0].shape[1]
    total = own_ref[:, at:].astype(F32)
    for got in got_refs:
        total = total + got[...].astype(F32)
    out_ref[:rows, at:] = total.astype(BF16)
    if at:
        out_ref[:rows, :at] = own_ref[:, :at]
    if out_ref.shape[0] > rows:
        out_ref[rows:, :] = jnp.zeros((out_ref.shape[0] - rows, width), BF16)


def merge(own, got, extra, after):
    outs = [shape((own.shape[0] + extra, own.shape[1]))]
    kernel = functools.partial(merge_kernel, len(got))
    return whole_call(kernel, "merge", [], [own, *got], outs, 4, (0, 0), [], after)[0]


def attention(me, spans, queries, out_grad, keys, values, activations, mark, swap, n):
    rows, hd = keys.shape
    columns = queries.shape[1]
    tall = columns // hd * rows
    product = 2 * rows * tall * hd
    cost = (8 * product, 8 * rows * columns)

    direct = [b for b in range(1, n) if b & (b - 1) == 0]
    blocks = {b: [swap(keys, b), swap(values, b)] for b in reversed(direct)}
    stats_shape = shape((8, tall), F32)
    stats, queries, out_grad, keys, values, flags = whole_call(
        functools.partial(first_stats_kernel, n),
        "first_stats",
        [me, spans],
        [queries, out_grad, keys, values],
        [stats_shape] + [shape(x.shape) for x in (queries, out_grad, keys, values)] + [shape((8, 128), F32)],
        12,
        cost,
        [],
        [mark],
    )
    blocks[0] = [keys, values]
    acts = prepare(activations, [stats])
    for b in range(1, n):
        if b not in blocks:
            blocks[b] = [swap(x, b & -b) for x in blocks[b & (b - 1)]]
        stats = whole_call(
            functools.partial(next_stats_kernel, b),
            "next_stats",
            [],
            [flags, queries, out_grad, *blocks[b], stats],
            [stats_shape],
            10,
            cost,
            [],
            [*blocks[2], acts] if b == 1 else [],
        )[0]
    p_buf = pltpu.VMEM((rows, 2 * rows), BF16)
    sums = [pltpu.VMEM((rows, hd), F32)] * 2
    parts, straight, score_grads, before = [[] for _ in range(n)], [], [None] * n, []
    for b in range(n - 1, 0, -1):
        far = b & (b - 1)
        outs = [shape((rows, hd))] * 2 if far else [shape((rows, 2 * hd))]
        *part, score_grads[b] = whole_call(
            functools.partial(other_kernel, b),
            "block_gradients",
            [],
            [flags, stats, queries, out_grad, *blocks[b]],
            outs + [shape((rows, tall))],
            10,
            (0, 0),
            [p_buf, *sums],
            before if far or b > 1 else [*before, *straight],
        )
        before = part[:1]
        if far:
            straight.append(swap(part[0], b))
        part = part[-1]
        if parts[b]:
            part = merge(part, parts[b], 0 if far else TOP_ROWS, [])
            before = [part]
        parts[far].append(swap(part, b & -b))
    own, score_grads[0] = whole_call(
        own_kernel,
        "own_gradients",
        [],
        [stats, queries, out_grad, keys, values],
        [shape((rows, 2 * hd), F32), shape((rows, tall))],
        10,
        (0, 0),
        [p_buf, *sums],
        before,
    )
    return own, [*straight, *parts[0]], [blocks[b][0] for b in range(n)], score_grads, acts


def query_gradients(key_blocks, score_grads, columns, after):
    n = len(key_blocks)
    rows = key_blocks[0].shape[0]
    return whole_call(
        functools.partial(query_kernel, n),
        "query_gradients",
        [],
        [*key_blocks, *score_grads],
        [shape((rows, columns)), shape((8, 128), F32)],
        2 + 3 * n,
        (2 * n * rows * rows * columns, 16 * rows * columns),
        [],
        after,
    )


def pack_top(top):
    high = jnp.minimum(top, BF16_MAX).astype(BF16).astype(F32)
    rest = top - high
    middle = rest.astype(BF16).astype(F32)
    low = rest - middle
    return (high + pltpu.roll(middle, PACK_LANES, 1) + pltpu.roll(low, 2 * PACK_LANES, 1)).astype(BF16)


def unpack_top(ref, at):
    x = ref[at : at + TOP_ROWS, :TOP_LANES].astype(F32)
    total = x + (pltpu.roll(x, TOP_LANES - PACK_LANES, 1) + pltpu.roll(x, TOP_LANES - 2 * PACK_LANES, 1))
    lane = lax.broadcasted_iota(jnp.int32, x.shape, 1)
    return jnp.where(lane < PACK_LANES, total, 0.0)


def tile_of(step, me_dp, bits, flip):
    mask = flip
    for j in range(1, bits):
        if not (step >> (bits - 1 - j)) & 1:
            mask |= 1 << j
    return me_dp ^ mask


def reversed_step(step, bits):
    return sum(((step >> (bits - 1 - j)) & 1) << (j - 1) for j in range(1, bits))


def corrected_tile(chosen, dest, grads, a_ref, e_ref, top_ref):
    _, n_ctx, sets, rows_set, rows = a_ref.shape
    tall = n_ctx * rows_set
    a = a_ref[dest, :, chosen].reshape(tall, rows)
    e = e_ref[dest, :, chosen].reshape(tall, e_ref.shape[4])
    c = jnp.dot(a, grads, preferred_element_type=F32) + e

    mags = jnp.max(jnp.abs(c).reshape(tall // QROWS, QROWS, c.shape[1]), axis=1)
    mags = jnp.max(mags, axis=1, keepdims=True)
    per_set = rows_set // QROWS
    block = lax.broadcasted_iota(jnp.int32, (tall // QROWS, TOP_LANES), 0)
    lane = lax.broadcasted_iota(jnp.int32, (tall // QROWS, TOP_LANES), 1)
    shift = per_set.bit_length() - 1
    place = ((block >> shift) * (sets * per_set)) + chosen * per_set + (block & (per_set - 1))
    top = jnp.max(jnp.where(lane == place, mags, 0.0), axis=0, keepdims=True)
    top_ref[pl.ds(dest, 1), :] = jnp.maximum(top_ref[pl.ds(dest, 1), :], top)
    return c


def send_rows(bits, shrink, chosen, me_ref, total, a_ref, e_ref, out_ref, top_ref, packed):
    tall = a_ref.shape[1] * a_ref.shape[3]
    steps = a_ref.shape[0] // 2
    for step in range(steps):
        dest = tile_of(step, me_ref[0], bits, 1)
        c = corrected_tile(chosen, dest, total, a_ref, e_ref, top_ref)
        out_ref[step * tall : (step + 1) * tall, :] = (c * shrink).astype(BF16)
    out_ref[steps * tall :, :] = jnp.zeros((out_ref.shape[0] - steps * tall, out_ref.shape[1]), BF16)
    if packed:
        out_ref[steps * tall :, :TOP_LANES] = pack_top(top_ref[...])


def first_send_kernel(bits, shrink, n_parts, me_ref, own_ref, *refs):
    part_refs = refs[:n_parts]
    a_ref, e_ref, out_ref, top_ref, kg_ref, vg_ref, grads_ref = refs[n_parts:]
    total = own_ref[...]
    for part in part_refs:
        got = part[: total.shape[0], :].astype(F32)
        if got.shape[1] < total.shape[1]:
            got = jnp.concatenate([got, jnp.zeros_like(got)], axis=1)
        total = total + got
    total = total.astype(BF16)
    hd = total.shape[1] // 2
    kg_ref[...] = total[:, :hd]
    vg_ref[...] = total[:, hd:]
    grads_ref[...] = total
    top_ref[...] = jnp.zeros_like(top_ref)
    send_rows(bits, shrink, 0, me_ref, total, a_ref, e_ref, out_ref, top_ref, False)


def next_send_kernel(bits, shrink, chosen, packed, me_ref, grads_ref, before_ref, a_ref, e_ref, out_ref, top_ref):
    top_ref[...] = before_ref[...]
    send_rows(bits, shrink, chosen, me_ref, grads_ref[...], a_ref, e_ref, out_ref, top_ref, packed)


def kept_kernel(bits, shrink, me_ref, grads_ref, before_ref, a_ref, e_ref, *outs):
    *kept, top_ref = outs
    top_ref[...] = before_ref[...]
    total = grads_ref[...]
    for chosen, out_ref in enumerate(kept):
        for step in range(out_ref.shape[0]):
            dest = tile_of(step, me_ref[0], bits, 0)
            out_ref[step] = corrected_tile(chosen, dest, total, a_ref, e_ref, top_ref) * shrink


def split_kernel(bits, n_tops, kept, got, *refs):
    steps, tall, width = kept.shape
    half = steps // 2
    hd = width // 2
    tops = refs[:n_tops]
    low_away, low_stay, high_away, high_stay, *top_out = refs[n_tops:]
    for step in range(steps):
        c = (kept[step] + got[step * tall : (step + 1) * tall, :].astype(F32)).astype(BF16)
        back = reversed_step(step, bits)
        for at, part, away, stay in ((step, c[:, :hd], low_away, low_stay), (back, c[:, hd:], high_away, high_stay)):
            if at < half:
                away[at * tall : (at + 1) * tall, :] = part
            else:
                stay[(at - half) * tall : (at - half + 1) * tall, :] = part
    if tops:
        top = largest(tops, got, steps * tall)
        top_out[0][...] = top
        low_away[half * tall :, :] = pack_top(top)
    else:
        low_away[half * tall :, :] = jnp.zeros((low_away.shape[0] - half * tall, hd), BF16)


def largest(tops, low_got, size):
    found = [top[...] for top in tops]
    if low_got.shape[0] > size:
        found.append(unpack_top(low_got, size))
    return functools.reduce(jnp.maximum, found)


def add_kernel(n_tops, low, low_got, high, high_got, *refs):
    tops = refs[:n_tops]
    low_away, low_stay, high_away, high_stay, *top_out = refs[n_tops:]
    size = low.shape[0]
    half = size // 2
    for mine, got, away, stay in ((low, low_got, low_away, low_stay), (high, high_got, high_away, high_stay)):
        away[:half, :] = (mine[:half, :].astype(F32) + got[:half, :].astype(F32)).astype(BF16)
        stay[...] = (mine[half:, :].astype(F32) + got[half:size, :].astype(F32)).astype(BF16)
    if tops:
        top = largest(tops, low_got, size)
        top_out[0][...] = top
        low_away[half:, :] = pack_top(top)
    else:
        low_away[half:, :] = jnp.zeros((low_away.shape[0] - half, low_away.shape[1]), BF16)


def context_masks(n_ctx):
    bits = n_ctx.bit_length() - 1
    return [sum((1 << j) for j in range(bits) if not (step >> (bits - 1 - j)) & 1) for step in range(n_ctx)]


def last_kernel(n_ctx, n_tops, me_ref, low, low_got, high, high_got, *refs):
    tops = refs[:n_tops]
    away, stay, *top_out = refs[n_tops:]
    size, hd = low.shape
    rows_set = size // n_ctx
    half = n_ctx // 2
    for i, mask in enumerate(context_masks(n_ctx)):
        part = pl.ds(pl.multiple_of((me_ref[0] ^ mask) * rows_set, rows_set), rows_set)
        out, at = (away, i) if i < half else (stay, i - half)
        at = 2 * at * rows_set
        for mine, got in ((low, low_got), (high, high_got)):
            total = mine[part, :].astype(F32) + got[part, :].astype(F32)
            out[at : at + rows_set, :] = total.astype(BF16)
            at += rows_set
    if tops:
        top = largest(tops, low_got, size)
        top_out[0][...] = top
        away[half * 2 * rows_set :, :] = pack_top(top)
    else:
        away[half * 2 * rows_set :, :] = jnp.zeros((away.shape[0] - half * 2 * rows_set, hd), BF16)


def halve_kernel(n_tops, mine, got, *refs):
    tops = refs[:n_tops]
    away, stay, *top_out = refs[n_tops:]
    size = mine.shape[0]
    half = size // 2
    away[:half, :] = (mine[:half, :].astype(F32) + got[:half, :].astype(F32)).astype(BF16)
    stay[...] = (mine[half:, :].astype(F32) + got[half:size, :].astype(F32)).astype(stay.dtype)
    if tops:
        top = largest(tops, got, size)
        top_out[0][...] = top
        away[half:, :] = pack_top(top)
    else:
        away[half:, :] = jnp.zeros((away.shape[0] - half, away.shape[1]), BF16)


def final_kernel(sets, gain, me_dp_ref, me_ctx_ref, *refs):
    groups = [refs[2 * chosen : 2 * chosen + 2] for chosen in range(sets)][::-1]
    top_ref, out_ref, scale_ref, all_tops = refs[2 * sets :]
    n_dp, lanes = scale_ref.shape
    rows_set, hd = groups[0][0].shape[0] // 2, groups[0][0].shape[1]
    scale = jnp.maximum(top_ref[...], unpack_top(groups[-1][1], 2 * rows_set)) + 1e-06
    all_tops[...] = scale
    scale_ref[...] = scale[:n_dp, :lanes]
    factors = gain / all_tops[pl.ds(me_dp_ref[0], 1), :]
    lane = lax.broadcasted_iota(jnp.int32, factors.shape, 1)
    per_set = rows_set // QROWS
    first = me_ctx_ref[0] * (sets * per_set)
    for chosen, (mine_ref, got_ref) in enumerate(groups):
        for r in range(per_set):
            mine = jnp.where(lane == first + (chosen * per_set + r), factors, 0.0)
            factor = jnp.sum(mine, axis=1, keepdims=True)
            at = chosen * rows_set + r * QROWS
            for h in range(2):
                part = slice(h * rows_set + r * QROWS, h * rows_set + (r + 1) * QROWS)
                total = mine_ref[part, :] + got_ref[part, :].astype(F32)
                out_ref[at : at + QROWS, h * hd : (h + 1) * hd] = total * factor


def local(n_dp, n_ctx, sets, span_order, queries, keys, values, out_grad, activations, error_feedback):
    rows, hd = keys.shape
    width = 2 * hd
    model = activations.shape[1]
    rows_set = model // (n_dp * n_ctx * sets)
    tall = n_ctx * rows_set
    me_dp = lax.axis_index("dp").astype(jnp.int32)[None]
    me_ctx = lax.axis_index("context").astype(jnp.int32)[None]
    bits = n_dp.bit_length() - 1

    def swap_dp(x, mask):
        return lax.ppermute(x, "dp", xor_perm(n_dp, mask))

    def swap_ctx(x, mask):
        return lax.ppermute(x, "context", xor_perm(n_ctx, mask))

    own, parts, key_blocks, score_grads, acts = attention(
        me_ctx, span_order[0], queries, out_grad, keys, values, activations, begin(me_dp, me_ctx), swap_ctx, n_ctx
    )

    shrink = 1.0 / (n_dp * n_ctx)
    acts = acts.reshape(n_dp, n_ctx, sets, rows_set, rows)
    errors = error_feedback.reshape(n_dp, n_ctx, sets, rows_set, width)
    tops = shape((TOP_ROWS, TOP_LANES), F32)
    steps = n_dp // 2
    cost = (2 * steps * tall * rows * width, steps * tall * (2 * rows + 6 * width))
    out, top, key_grad, value_grad, grads = whole_call(
        functools.partial(first_send_kernel, bits, shrink, len(parts)),
        "send_tiles",
        [me_dp],
        [own, *parts, acts, errors],
        [shape((steps * tall + 2 * TOP_ROWS, width)), tops, shape((rows, hd)), shape((rows, hd)), shape((rows, width))],
        18,
        cost,
    )
    got = [swap_dp(out, 1)]
    *kept, top = whole_call(
        functools.partial(kept_kernel, bits, shrink),
        "kept_tiles",
        [me_dp],
        [grads, top, acts, errors],
        [shape((steps, tall, width), F32)] * sets + [tops],
        20,
        (sets * cost[0], sets * cost[1]),
    )
    for chosen in range(1, sets):
        extra = TOP_ROWS if chosen == sets - 1 else 0
        out, top = whole_call(
            functools.partial(next_send_kernel, bits, shrink, chosen, extra > 0),
            "send_tiles",
            [me_dp],
            [grads, top, acts, errors],
            [shape((steps * tall + extra, width)), tops],
            18,
            cost,
        )
        got.append(swap_dp(out, 1))

    halves = []
    for chosen in range(sets):
        half = steps // 2 * tall
        last = chosen == sets - 1
        arrays = whole_call(
            functools.partial(split_kernel, bits, int(last)),
            "split_tiles",
            [],
            [kept[chosen], got[chosen]] + [top] * last,
            [shape((half + (1 if last else 2) * TOP_ROWS, hd))] + [shape((half, hd))] * 3 + [tops] * last,
            10,
            (4 * half * width, 12 * half * width),
        )
        halves.append(arrays[:4])
    gathered = [arrays[4]]
    query_grad, mark = query_gradients(key_blocks, score_grads, queries.shape[1], [arrays[1]])
    groups = []
    for chosen in range(sets):
        low_away, low, high_away, high = halves[chosen]
        extra = TOP_ROWS if chosen == sets - 1 else 0
        tail = extra or 2 * TOP_ROWS
        for stage in range(1, bits):
            low_got = swap_dp(low_away, 1 << stage)
            high_got = swap_dp(high_away, 1 << (bits - stage))
            with_tops = extra > 0
            operands = [low, low_got, high, high_got] + (gathered if with_tops else [])
            n_tops = len(operands) - 4
            size = low.shape[0]
            cost = (4 * size * hd, 12 * size * hd)
            if stage < bits - 1:
                low_away, low, high_away, high, *top_out = whole_call(
                    functools.partial(add_kernel, n_tops),
                    "add_stage",
                    [],
                    operands,
                    [shape((size // 2 + tail, hd))] + [shape((size // 2, hd))] * 3 + [tops] * with_tops,
                    8,
                    cost,
                    after=[mark] if chosen == 0 and stage == 1 else [],
                )
            else:
                chunk = 2 * rows_set
                away, stay, *top_out = whole_call(
                    functools.partial(last_kernel, n_ctx, n_tops),
                    "last_stage",
                    [me_ctx],
                    operands,
                    [shape((n_ctx // 2 * chunk + tail, hd)), shape((n_ctx // 2 * chunk, hd))] + [tops] * with_tops,
                    8,
                    cost,
                )
            if with_tops:
                gathered = list(top_out)
        mask = 1
        while mask < n_ctx // 2:
            size = stay.shape[0]
            away, stay, *top_out = whole_call(
                functools.partial(halve_kernel, int(with_tops)),
                "halve_context",
                [],
                [stay, swap_ctx(away, mask)] + (gathered if with_tops else []),
                [shape((size // 2 + tail, hd)), shape((size // 2, hd), F32 if size == 2 * chunk else BF16)]
                + [tops] * with_tops,
                8,
                (0, 0),
            )
            if with_tops:
                gathered = list(top_out)
            mask *= 2
        groups = [stay, swap_ctx(away, mask), *groups]
    payload, scale = whole_call(
        functools.partial(final_kernel, sets, 7.0 / shrink),
        "final_stage",
        [me_dp, me_ctx],
        groups + gathered,
        [shape((sets * rows_set, width), F32), shape((n_dp, sets * tall // QROWS), F32)],
        8,
        (0, 0),
        [pltpu.VMEM((TOP_ROWS, TOP_LANES), F32)],
    )
    return query_grad, key_grad, value_grad, payload, scale.reshape(-1)


def solution(mesh):
    tokens = P(("dp", "context"), None)
    return jax.shard_map(
        functools.partial(local, mesh.shape["dp"], mesh.shape["context"], 2),
        mesh=mesh,
        in_specs=(P("dp", None), tokens, tokens, tokens, tokens, tokens, P("dp", "context", None, None)),
        out_specs=(tokens, tokens, tokens, tokens, P()),
        check_vma=False,
    )
```

```python
import functools

import jax
import jax.numpy as jnp
from jax import lax
from jax.experimental import pallas as pl
from jax.experimental.pallas import tpu as pltpu
from jax.sharding import PartitionSpec as P

QROWS = 32
LOG2E = 1.4426950408889634
FAR = 1e30
MIB = 1024 * 1024
CHUNK = 256
TOP_ROWS, TOP_LANES, PACK_LANES = 16, 128, 32
BF16, F32 = jnp.bfloat16, jnp.float32
BF16_MAX = float(jnp.finfo(jnp.bfloat16).max)
NT = (((1,), (1,)), ((), ()))
TN = (((0,), (0,)), ((), ()))


def xor_perm(size, mask):
    return [(i, i ^ mask) for i in range(size)]


def whole(x):
    return pl.BlockSpec(x.shape, lambda *_: (0,) * len(x.shape))


def shape(dims, dtype=BF16):
    return jax.ShapeDtypeStruct(dims, dtype)


def whole_call(kernel, name, scalars, operands, out_shape, mib, cost, scratch=(), after=()):
    def body(*refs):
        first = len(scalars) + len(operands)
        kernel(*refs[:first], *refs[first + len(after) :])

    return pl.pallas_call(
        body,
        grid_spec=pltpu.PrefetchScalarGridSpec(
            num_scalar_prefetch=len(scalars),
            grid=(1,),
            in_specs=[whole(x) for x in operands] + [pl.BlockSpec(memory_space=pl.ANY)] * len(after),
            out_specs=[whole(x) for x in out_shape],
            scratch_shapes=list(scratch),
        ),
        out_shape=out_shape,
        compiler_params=pltpu.CompilerParams(vmem_limit_bytes=mib * MIB),
        cost_estimate=pl.CostEstimate(flops=cost[0], bytes_accessed=cost[1], transcendentals=0),
        name=name,
    )(*scalars, *operands, *after)


def begin_kernel(me_dp_ref, me_ctx_ref, out_ref):
    out_ref[...] = jnp.zeros_like(out_ref)


def begin(me_dp, me_ctx):
    mark = [shape((8, 128), F32)]
    return whole_call(begin_kernel, "begin", [me_dp, me_ctx], [], mark, 4, (20_000_000_000, 0))[0]


def prepare_kernel(pieces, a_ref, a_out):
    tile = a_ref.shape[1] // pieces
    for i in range(pieces):
        a_out[i * tile : (i + 1) * tile, :] = a_ref[:, i * tile : (i + 1) * tile].T


def prepare(activations, after):
    rows, model = activations.shape
    outs = [shape((model, rows))]
    cost = (0, 0)
    kernel = functools.partial(prepare_kernel, 8)
    return whole_call(kernel, "prepare", [], [activations], outs, 16, cost, [], after)[0]


def head_pair(ref, i, hd):
    at = i * (2 * hd)
    first = ref[:, pl.ds(pl.multiple_of(at, hd), hd)]
    second = ref[:, pl.ds(pl.multiple_of(at + hd, hd), hd)]
    return jnp.concatenate([first, second], axis=0)


def score_chunk(k, v, q, do, own, first_lane):
    s = lax.dot_general(k, q, NT, preferred_element_type=F32)
    dp = lax.dot_general(v, do, NT, preferred_element_type=F32)
    if own:
        rows = k.shape[0]
        key_at = lax.broadcasted_iota(jnp.int32, s.shape, 0)
        query_at = lax.broadcasted_iota(jnp.int32, s.shape, 1) + first_lane
        query_at = jnp.where(query_at >= rows, query_at - rows, query_at)
        s = jnp.where(key_at <= query_at, s, -FAR)
    return s, dp


def counted(b, flags):
    lane = lax.broadcasted_iota(jnp.int32, flags.shape, 1)
    return jnp.max(jnp.where(lane == b, flags[...], 0.0)) > 0.5


def stats_of_block(b, q_ref, do_ref, k_ref, v_ref, before, out):
    k, v = k_ref[...], v_ref[...]
    rows, hd = k.shape
    pair = 2 * rows
    factor = LOG2E / hd**0.5

    def heads(i, carry):
        q, do = head_pair(q_ref, i, hd), head_pair(do_ref, i, hd)
        for t in range(pair // CHUNK):
            part = slice(t * CHUNK, (t + 1) * CHUNK)
            lanes = pl.ds(pl.multiple_of(i * pair + t * CHUNK, CHUNK), CHUNK)
            s, dp = score_chunk(k, v, q[part], do[part], b == 0, t * CHUNK)
            top = jnp.max(s, axis=0, keepdims=True) * factor
            e = jnp.exp2(s * factor - top)
            total = jnp.sum(e, axis=0, keepdims=True)
            weighted = jnp.sum(e * dp, axis=0, keepdims=True)
            if b > 0:
                old = before[0:1, lanes]
                both = jnp.maximum(old, top)
                old_part, new_part = jnp.exp2(old - both), jnp.exp2(top - both)
                total = before[1:2, lanes] * old_part + total * new_part
                weighted = before[2:3, lanes] * old_part + weighted * new_part
                top = both
            out[0:1, lanes] = top
            out[1:2, lanes] = total
            out[2:3, lanes] = weighted
        return carry

    lax.fori_loop(0, q_ref.shape[1] // (2 * hd), heads, 0, unroll=True)


def first_stats_kernel(n, me_ref, span_ref, q_ref, do_ref, k_ref, v_ref, out, q_out, do_out, k_out, v_out, flags):
    me = me_ref[0]
    lane = lax.broadcasted_iota(jnp.int32, flags.shape, 1)
    found = jnp.zeros(flags.shape, F32)
    for b in range(1, n):
        found = jnp.where((lane == b) & (span_ref[me ^ b] < span_ref[me]), 1.0, found)
    flags[...] = found
    q_out[...] = q_ref[...]
    do_out[...] = do_ref[...]
    k_out[...] = k_ref[...]
    v_out[...] = v_ref[...]
    stats_of_block(0, q_ref, do_ref, k_ref, v_ref, None, out)


def next_stats_kernel(b, flags, q_ref, do_ref, k_ref, v_ref, before, out):
    keep = counted(b, flags)

    @pl.when(keep)
    def _():
        stats_of_block(b, q_ref, do_ref, k_ref, v_ref, before, out)

    @pl.when(jnp.logical_not(keep))
    def _():
        out[...] = before[...]


def block_gradients(own, stats, q_ref, do_ref, k_ref, v_ref, p_buf, ds_ref, dk, dv):
    k, v = k_ref[...], v_ref[...]
    rows, hd = k.shape
    pair = 2 * rows
    factor = LOG2E / hd**0.5
    dk[...] = jnp.zeros_like(dk)
    dv[...] = jnp.zeros_like(dv)

    def heads(i, carry):
        q, do = head_pair(q_ref, i, hd), head_pair(do_ref, i, hd)
        for t in range(pair // CHUNK):
            part = slice(t * CHUNK, (t + 1) * CHUNK)
            lanes = pl.ds(pl.multiple_of(i * pair + t * CHUNK, CHUNK), CHUNK)
            s, dp = score_chunk(k, v, q[part], do[part], own, t * CHUNK)
            total = stats[1:2, lanes]
            level = stats[0:1, lanes] + jnp.log(total) * LOG2E
            p = jnp.exp2(s * factor - level)
            p_buf[:, part] = p.astype(BF16)
            ds = (p * (dp - stats[2:3, lanes] / total)).astype(BF16)
            ds_ref[:, lanes] = ds
        ds = ds_ref[:, pl.ds(pl.multiple_of(i * pair, CHUNK), pair)]
        dk[...] += jnp.dot(ds, q, preferred_element_type=F32)
        dv[...] += jnp.dot(p_buf[...], do, preferred_element_type=F32)
        return carry

    lax.fori_loop(0, q_ref.shape[1] // (2 * hd), heads, 0, unroll=True)
    inverse = 1.0 / hd**0.5
    return dk[...] * inverse, dv[...]


def other_kernel(b, flags, stats, q_ref, do_ref, k_ref, v_ref, dk_out, dv_out, ds_out, p_buf, dk, dv):
    keep = counted(b, flags)
    rows = dk.shape[0]

    @pl.when(keep)
    def _():
        dk_sum, dv_sum = block_gradients(False, stats, q_ref, do_ref, k_ref, v_ref, p_buf, ds_out, dk, dv)
        dk_out[...] = dk_sum.astype(BF16)
        dv_out[:rows, :] = dv_sum.astype(BF16)
        dv_out[rows:, :] = jnp.zeros((dv_out.shape[0] - rows, dv.shape[1]), BF16)

    @pl.when(jnp.logical_not(keep))
    def _():
        dk_out[...] = jnp.zeros_like(dk_out)
        dv_out[...] = jnp.zeros_like(dv_out)
        ds_out[...] = jnp.zeros_like(ds_out)


def own_kernel(stats, q_ref, do_ref, k_ref, v_ref, out_ref, ds_out, p_buf, dk, dv):
    hd = dk.shape[1]
    dk_sum, dv_sum = block_gradients(True, stats, q_ref, do_ref, k_ref, v_ref, p_buf, ds_out, dk, dv)
    out_ref[:, :hd] = dk_sum
    out_ref[:, hd:] = dv_sum


def query_kernel(n, *refs):
    k_refs, ds_refs, dq_ref, mark_ref = refs[:n], refs[n : 2 * n], refs[2 * n], refs[2 * n + 1]
    mark_ref[...] = jnp.zeros_like(mark_ref)
    rows, hd = k_refs[0].shape
    for h in range(dq_ref.shape[1] // hd):
        dq = 0.0
        for k, ds in zip(k_refs, ds_refs):
            part = ds[:, h * rows : (h + 1) * rows]
            dq = dq + lax.dot_general(part, k[...], TN, preferred_element_type=F32)
        dq_ref[:, h * hd : (h + 1) * hd] = (dq / hd**0.5).astype(BF16)


def merge_kernel(rows, *refs):
    *terms, out_ref = refs
    total = functools.reduce(jnp.add, [term[:rows, :].astype(F32) for term in terms])
    out_ref[:rows, :] = total.astype(BF16)
    if out_ref.shape[0] > rows:
        out_ref[rows:, :] = jnp.zeros((out_ref.shape[0] - rows, out_ref.shape[1]), BF16)


def merge(rows, terms, after):
    outs = [shape(terms[0].shape)]
    return whole_call(functools.partial(merge_kernel, rows), "merge", [], terms, outs, 4, (0, 0), [], after)[0]


def attention(me, spans, queries, out_grad, keys, values, activations, mark, swap, n):
    rows, hd = keys.shape
    columns = queries.shape[1]
    tall = columns // hd * rows
    product = 2 * rows * tall * hd
    cost = (8 * product, 8 * rows * columns)

    direct = [b for b in range(1, n) if b & (b - 1) == 0]
    blocks = {b: [swap(keys, b), swap(values, b)] for b in reversed(direct)}
    stats_shape = shape((8, tall), F32)
    stats, queries, out_grad, keys, values, flags = whole_call(
        functools.partial(first_stats_kernel, n),
        "first_stats",
        [me, spans],
        [queries, out_grad, keys, values],
        [stats_shape] + [shape(x.shape) for x in (queries, out_grad, keys, values)] + [shape((8, 128), F32)],
        12,
        cost,
        [],
        [mark],
    )
    blocks[0] = [keys, values]
    acts = prepare(activations, [stats])
    for b in range(1, n):
        if b not in blocks:
            blocks[b] = [swap(x, b & -b) for x in blocks[b & (b - 1)]]
        stats = whole_call(
            functools.partial(next_stats_kernel, b),
            "next_stats",
            [],
            [flags, queries, out_grad, *blocks[b], stats],
            [stats_shape],
            10,
            cost,
            [],
            [*blocks[2], acts] if b == 1 else [],
        )[0]
    p_buf = pltpu.VMEM((rows, 2 * rows), BF16)
    sums = [pltpu.VMEM((rows, hd), F32)] * 2
    key_parts, value_parts = [[] for _ in range(n)], [[] for _ in range(n)]
    score_grads, own_parts, before = [None] * n, {}, []
    for b in range(n - 1, 0, -1):
        dk, dv, score_grads[b] = whole_call(
            functools.partial(other_kernel, b),
            "block_gradients",
            [],
            [flags, stats, queries, out_grad, *blocks[b]],
            [shape((rows, hd)), shape((rows + TOP_ROWS, hd)), shape((rows, tall))],
            10,
            (0, 0),
            [p_buf, *sums],
            before,
        )
        own_parts[b] = dk
        if value_parts[b]:
            dv = merge(rows, [dv, *value_parts[b]], [])
        value_parts[b & (b - 1)].append(swap(dv, b & -b))
        before = [dv]
    for b in range(n - 1, 0, -1):
        dk = own_parts[b]
        if key_parts[b]:
            dk = merge(rows, [dk, *key_parts[b]], before)
        key_parts[b & (b - 1)].append(swap(dk, b & -b))
    own, score_grads[0] = whole_call(
        own_kernel,
        "own_gradients",
        [],
        [stats, queries, out_grad, keys, values],
        [shape((rows, 2 * hd), F32), shape((rows, tall))],
        10,
        (0, 0),
        [p_buf, *sums],
        before,
    )
    return own, key_parts[0], value_parts[0], [blocks[b][0] for b in range(n)], score_grads, acts


def query_gradients(key_blocks, score_grads, columns, after):
    n = len(key_blocks)
    rows = key_blocks[0].shape[0]
    return whole_call(
        functools.partial(query_kernel, n),
        "query_gradients",
        [],
        [*key_blocks, *score_grads],
        [shape((rows, columns)), shape((8, 128), F32)],
        2 + 3 * n,
        (2 * n * rows * rows * columns, 16 * rows * columns),
        [],
        after,
    )


def pack_top(top):
    high = jnp.minimum(top, BF16_MAX).astype(BF16).astype(F32)
    rest = top - high
    middle = rest.astype(BF16).astype(F32)
    low = rest - middle
    return (high + pltpu.roll(middle, PACK_LANES, 1) + pltpu.roll(low, 2 * PACK_LANES, 1)).astype(BF16)


def unpack_top(ref, at):
    x = ref[at : at + TOP_ROWS, :TOP_LANES].astype(F32)
    total = x + (pltpu.roll(x, TOP_LANES - PACK_LANES, 1) + pltpu.roll(x, TOP_LANES - 2 * PACK_LANES, 1))
    lane = lax.broadcasted_iota(jnp.int32, x.shape, 1)
    return jnp.where(lane < PACK_LANES, total, 0.0)


def tile_of(step, me_dp, bits, flip):
    mask = flip
    for j in range(1, bits):
        if not (step >> (bits - 1 - j)) & 1:
            mask |= 1 << j
    return me_dp ^ mask


def reversed_step(step, bits):
    return sum(((step >> (bits - 1 - j)) & 1) << (j - 1) for j in range(1, bits))


def corrected_tile(at, dest, grads, a_ref, e_ref, top_ref):
    _, n_ctx, rows_ctx, rows = a_ref.shape
    tall = n_ctx * rows_ctx
    hd = grads.shape[1]
    a = a_ref[dest].reshape(tall, rows)
    e = e_ref[dest, :, :, at : at + hd].reshape(tall, hd)
    c = jnp.dot(a, grads, preferred_element_type=F32) + e
    mags = jnp.max(jnp.abs(c).reshape(tall // QROWS, QROWS, hd), axis=1)
    mags = jnp.max(mags, axis=1, keepdims=True)
    block = lax.broadcasted_iota(jnp.int32, (tall // QROWS, TOP_LANES), 0)
    lane = lax.broadcasted_iota(jnp.int32, (tall // QROWS, TOP_LANES), 1)
    top = jnp.max(jnp.where(lane == block, mags, 0.0), axis=0, keepdims=True)
    top_ref[pl.ds(dest, 1), :] = jnp.maximum(top_ref[pl.ds(dest, 1), :], top)
    return c


def summed_grads(at, own_ref, part_refs):
    rows, hd = own_ref.shape[0], own_ref.shape[1] // 2
    total = own_ref[:, at : at + hd]
    for part in part_refs:
        total = total + part[:rows, :].astype(F32)
    return total.astype(BF16)


def send_rows(bits, shrink, at, me_ref, total, a_ref, e_ref, out_ref, top_ref, packed):
    tall = a_ref.shape[1] * a_ref.shape[2]
    steps = a_ref.shape[0] // 2
    for step in range(steps):
        dest = tile_of(step, me_ref[0], bits, 1)
        c = corrected_tile(at, dest, total, a_ref, e_ref, top_ref)
        out_ref[step * tall : (step + 1) * tall, :] = (c * shrink).astype(BF16)
    tail = jnp.zeros((out_ref.shape[0] - steps * tall, out_ref.shape[1]), BF16)
    out_ref[steps * tall :, :] = pack_top(top_ref[...]) if packed else tail


def kept_rows(bits, shrink, at, me_ref, total, a_ref, e_ref, out_ref, top_ref):
    for step in range(out_ref.shape[0]):
        dest = tile_of(step, me_ref[0], bits, 0)
        out_ref[step] = corrected_tile(at, dest, total, a_ref, e_ref, top_ref) * shrink


def first_send_kernel(bits, shrink, at, n_parts, me_ref, own_ref, *refs):
    a_ref, e_ref, out_ref, top_ref, grads_ref, grads_out = refs[n_parts:]
    total = summed_grads(at, own_ref, refs[:n_parts])
    grads_ref[...] = total
    grads_out[...] = total
    top_ref[...] = jnp.zeros_like(top_ref)
    send_rows(bits, shrink, at, me_ref, total, a_ref, e_ref, out_ref, top_ref, False)


def next_kept_kernel(bits, shrink, at, me_ref, grads_ref, before_ref, a_ref, e_ref, out_ref, top_ref):
    top_ref[...] = before_ref[...]
    kept_rows(bits, shrink, at, me_ref, grads_ref[...], a_ref, e_ref, out_ref, top_ref)


def first_kept_kernel(bits, shrink, at, n_parts, me_ref, own_ref, *refs):
    before_ref, a_ref, e_ref, out_ref, top_ref, grads_ref, grads_out = refs[n_parts:]
    total = summed_grads(at, own_ref, refs[:n_parts])
    grads_ref[...] = total
    grads_out[...] = total
    top_ref[...] = before_ref[...]
    kept_rows(bits, shrink, at, me_ref, total, a_ref, e_ref, out_ref, top_ref)


def next_send_kernel(bits, shrink, at, me_ref, grads_ref, before_ref, a_ref, e_ref, out_ref, top_ref):
    top_ref[...] = before_ref[...]
    send_rows(bits, shrink, at, me_ref, grads_ref[...], a_ref, e_ref, out_ref, top_ref, True)


def split_kernel(bits, n_ctx, n_tops, kept, got, *refs):
    steps, tall, hd = kept.shape
    half = steps // 2
    part_tall = tall // 2
    tops = refs[:n_tops]
    low_away, low_stay, high_away, high_stay, *top_out = refs[n_tops:]
    for step in range(steps):
        c = (kept[step] + got[step * tall : (step + 1) * tall, :].astype(F32)).astype(BF16)
        c = c.reshape(n_ctx, 2, part_tall // n_ctx, hd)
        back = reversed_step(step, bits)
        for at, i, away, stay in ((step, 0, low_away, low_stay), (back, 1, high_away, high_stay)):
            part = c[:, i].reshape(part_tall, hd)
            if at < half:
                away[at * part_tall : (at + 1) * part_tall, :] = part
            else:
                stay[(at - half) * part_tall : (at - half + 1) * part_tall, :] = part
    if tops:
        top = largest(tops, got, steps * tall)
        top_out[0][...] = top
        low_away[half * part_tall :, :] = pack_top(top)
    else:
        low_away[half * part_tall :, :] = jnp.zeros((low_away.shape[0] - half * part_tall, hd), BF16)


def largest(tops, low_got, size):
    found = [top[...] for top in tops]
    if low_got.shape[0] > size:
        found.append(unpack_top(low_got, size))
    return functools.reduce(jnp.maximum, found)


def add_kernel(n_tops, low, low_got, high, high_got, *refs):
    tops = refs[:n_tops]
    low_away, low_stay, high_away, high_stay, *top_out = refs[n_tops:]
    size = low.shape[0]
    half = size // 2
    for mine, got, away, stay in ((low, low_got, low_away, low_stay), (high, high_got, high_away, high_stay)):
        away[:half, :] = (mine[:half, :].astype(F32) + got[:half, :].astype(F32)).astype(BF16)
        stay[...] = (mine[half:, :].astype(F32) + got[half:size, :].astype(F32)).astype(BF16)
    if tops:
        top = largest(tops, low_got, size)
        top_out[0][...] = top
        low_away[half:, :] = pack_top(top)
    else:
        low_away[half:, :] = jnp.zeros((low_away.shape[0] - half, low_away.shape[1]), BF16)


def context_masks(n_ctx):
    bits = n_ctx.bit_length() - 1
    return [sum((1 << j) for j in range(bits) if not (step >> (bits - 1 - j)) & 1) for step in range(n_ctx)]


def last_kernel(n_ctx, n_tops, me_ref, low, low_got, high, high_got, *refs):
    tops = refs[:n_tops]
    away, stay, *top_out = refs[n_tops:]
    size, hd = low.shape
    rows_set = size // n_ctx
    half = n_ctx // 2
    for i, mask in enumerate(context_masks(n_ctx)):
        part = pl.ds(pl.multiple_of((me_ref[0] ^ mask) * rows_set, rows_set), rows_set)
        out, at = (away, i) if i < half else (stay, i - half)
        at = 2 * at * rows_set
        for mine, got in ((low, low_got), (high, high_got)):
            total = mine[part, :].astype(F32) + got[part, :].astype(F32)
            out[at : at + rows_set, :] = total.astype(BF16)
            at += rows_set
    if tops:
        top = largest(tops, low_got, size)
        top_out[0][...] = top
        away[half * 2 * rows_set :, :] = pack_top(top)
    else:
        away[half * 2 * rows_set :, :] = jnp.zeros((away.shape[0] - half * 2 * rows_set, hd), BF16)


def halve_kernel(n_tops, mine, got, *refs):
    tops = refs[:n_tops]
    away, stay, *top_out = refs[n_tops:]
    size = mine.shape[0]
    half = size // 2
    away[:half, :] = (mine[:half, :].astype(F32) + got[:half, :].astype(F32)).astype(BF16)
    stay[...] = (mine[half:, :].astype(F32) + got[half:size, :].astype(F32)).astype(stay.dtype)
    if tops:
        top = largest(tops, got, size)
        top_out[0][...] = top
        away[half:, :] = pack_top(top)
    else:
        away[half:, :] = jnp.zeros((away.shape[0] - half, away.shape[1]), BF16)


def final_kernel(columns, gain, me_dp_ref, me_ctx_ref, *refs):
    sets = len(columns)
    groups = [refs[2 * chosen : 2 * chosen + 2] for chosen in range(sets)]
    top_ref, out_ref, scale_ref, all_tops = refs[2 * sets :]
    n_dp, lanes = scale_ref.shape
    rows_ctx, hd = groups[0][0].shape
    scale = jnp.maximum(top_ref[...], unpack_top(groups[0][1], rows_ctx)) + 1e-06
    all_tops[...] = scale
    scale_ref[...] = scale[:n_dp, :lanes]
    factors = gain / all_tops[pl.ds(me_dp_ref[0], 1), :]
    lane = lax.broadcasted_iota(jnp.int32, factors.shape, 1)
    blocks = rows_ctx // QROWS
    for r in range(blocks):
        mine = jnp.where(lane == me_ctx_ref[0] * blocks + r, factors, 0.0)
        factor = jnp.sum(mine, axis=1, keepdims=True)
        part = slice(r * QROWS, (r + 1) * QROWS)
        for at, (mine_ref, got_ref) in zip(columns, groups):
            out_ref[part, at : at + hd] = (mine_ref[part, :] + got_ref[part, :].astype(F32)) * factor


def local(n_dp, n_ctx, span_order, queries, keys, values, out_grad, activations, error_feedback):
    rows, hd = keys.shape
    width = 2 * hd
    model = activations.shape[1]
    rows_ctx = model // (n_dp * n_ctx)
    tall = n_ctx * rows_ctx
    me_dp = lax.axis_index("dp").astype(jnp.int32)[None]
    me_ctx = lax.axis_index("context").astype(jnp.int32)[None]
    bits = n_dp.bit_length() - 1

    def swap_dp(x, mask):
        return lax.ppermute(x, "dp", xor_perm(n_dp, mask))

    def swap_ctx(x, mask):
        return lax.ppermute(x, "context", xor_perm(n_ctx, mask))

    own, key_parts, value_parts, key_blocks, score_grads, acts = attention(
        me_ctx, span_order[0], queries, out_grad, keys, values, activations, begin(me_dp, me_ctx), swap_ctx, n_ctx
    )

    shrink = 1.0 / (n_dp * n_ctx)
    acts = acts.reshape(n_dp, n_ctx, rows_ctx, rows)
    errors = error_feedback.reshape(n_dp, n_ctx, rows_ctx, width)
    tops = shape((TOP_ROWS, TOP_LANES), F32)
    steps = n_dp // 2
    cost = (0, 0)
    kept_shape, grad_shape = shape((steps, tall, hd), F32), shape((rows, hd))

    def tiles(kernel, name, operands, outs, after=()):
        return whole_call(kernel, name, [me_dp], [*operands, acts, errors], outs, 18, cost, [], after)

    sets = 2
    half = steps // 2 * (tall // 2)

    def split(last, kept, got, top):
        return whole_call(
            functools.partial(split_kernel, bits, n_ctx, int(last)),
            "split_tiles",
            [],
            [kept, got] + [top] * last,
            [shape((half + (1 if last else 2) * TOP_ROWS, hd))] + [shape((half, hd))] * 3 + [tops] * last,
            10,
            cost,
        )

    out, top, grads, value_grad = tiles(
        functools.partial(first_send_kernel, bits, shrink, hd, len(value_parts)),
        "send_tiles",
        [own, *value_parts],
        [shape((steps * tall + 2 * TOP_ROWS, hd)), tops, grad_shape, grad_shape],
    )
    got = swap_dp(out, 1)
    kept, top = tiles(
        functools.partial(next_kept_kernel, bits, shrink, hd), "kept_tiles", [grads, top], [kept_shape, tops]
    )
    halves = [split(False, kept, got, None)]
    kept, top, grads, key_grad = tiles(
        functools.partial(first_kept_kernel, bits, shrink, 0, len(key_parts)),
        "kept_tiles",
        [own, *key_parts, top],
        [kept_shape, tops, grad_shape, grad_shape],
        halves[0][1:2],
    )
    out, top = tiles(
        functools.partial(next_send_kernel, bits, shrink, 0),
        "send_tiles",
        [grads, top],
        [shape((steps * tall + TOP_ROWS, hd)), tops],
    )
    arrays = split(True, kept, swap_dp(out, 1), top)
    halves.append(arrays[:4])
    gathered = [arrays[4]]
    query_grad, mark = query_gradients(key_blocks, score_grads, queries.shape[1], [arrays[1]])
    groups = []
    for chosen in range(sets):
        low_away, low, high_away, high = halves[chosen]
        extra = TOP_ROWS if chosen == sets - 1 else 0
        tail = extra or 2 * TOP_ROWS
        for stage in range(1, bits):
            low_got = swap_dp(low_away, 1 << stage)
            high_got = swap_dp(high_away, 1 << (bits - stage))
            with_tops = extra > 0
            operands = [low, low_got, high, high_got] + (gathered if with_tops else [])
            n_tops = len(operands) - 4
            size = low.shape[0]
            if stage < bits - 1:
                low_away, low, high_away, high, *top_out = whole_call(
                    functools.partial(add_kernel, n_tops),
                    "add_stage",
                    [],
                    operands,
                    [shape((size // 2 + tail, hd))] + [shape((size // 2, hd))] * 3 + [tops] * with_tops,
                    8,
                    cost,
                    after=[mark] if chosen == 0 and stage == 1 else [],
                )
            else:
                chunk = rows_ctx
                away, stay, *top_out = whole_call(
                    functools.partial(last_kernel, n_ctx, n_tops),
                    "last_stage",
                    [me_ctx],
                    operands,
                    [shape((n_ctx // 2 * chunk + tail, hd)), shape((n_ctx // 2 * chunk, hd))] + [tops] * with_tops,
                    8,
                    cost,
                )
            if with_tops:
                gathered = list(top_out)
        mask = 1
        while mask < n_ctx // 2:
            size = stay.shape[0]
            away, stay, *top_out = whole_call(
                functools.partial(halve_kernel, int(with_tops)),
                "halve_context",
                [],
                [stay, swap_ctx(away, mask)] + (gathered if with_tops else []),
                [shape((size // 2 + tail, hd)), shape((size // 2, hd), F32 if size == 2 * chunk else BF16)]
                + [tops] * with_tops,
                8,
                (0, 0),
            )
            if with_tops:
                gathered = list(top_out)
            mask *= 2
        groups = [stay, swap_ctx(away, mask), *groups]
    payload, scale = whole_call(
        functools.partial(final_kernel, (0, hd), 7.0 / shrink),
        "final_stage",
        [me_dp, me_ctx],
        groups + gathered,
        [shape((rows_ctx, width), F32), shape((n_dp, tall // QROWS), F32)],
        8,
        (0, 0),
        [pltpu.VMEM((TOP_ROWS, TOP_LANES), F32)],
    )
    return query_grad, key_grad, value_grad, payload, scale.reshape(-1)


def solution(mesh):
    tokens = P(("dp", "context"), None)
    return jax.shard_map(
        functools.partial(local, mesh.shape["dp"], mesh.shape["context"]),
        mesh=mesh,
        in_specs=(P("dp", None), tokens, tokens, tokens, tokens, tokens, P("dp", "context", None, None)),
        out_specs=(tokens, tokens, tokens, tokens, P()),
        check_vma=False,
    )
```

```python
import functools

import jax
import jax.numpy as jnp
from jax import lax
from jax.experimental import pallas as pl
from jax.experimental.pallas import tpu as pltpu
from jax.sharding import PartitionSpec as P

QROWS = 32
LOG2E = 1.4426950408889634
FAR = 1e30
MIB = 1024 * 1024
CHUNK = 256
TOP_ROWS, TOP_LANES, PACK_LANES = 16, 128, 32
BF16, F32 = jnp.bfloat16, jnp.float32
BF16_MAX = float(jnp.finfo(jnp.bfloat16).max)
NT = (((1,), (1,)), ((), ()))
TN = (((0,), (0,)), ((), ()))


def xor_perm(size, mask):
    return [(i, i ^ mask) for i in range(size)]


def whole(x):
    return pl.BlockSpec(x.shape, lambda *_: (0,) * len(x.shape))


def shape(dims, dtype=BF16):
    return jax.ShapeDtypeStruct(dims, dtype)


def whole_call(kernel, name, scalars, operands, out_shape, mib, cost, scratch=(), after=()):
    def body(*refs):
        first = len(scalars) + len(operands)
        kernel(*refs[:first], *refs[first + len(after) :])

    return pl.pallas_call(
        body,
        grid_spec=pltpu.PrefetchScalarGridSpec(
            num_scalar_prefetch=len(scalars),
            grid=(1,),
            in_specs=[whole(x) for x in operands] + [pl.BlockSpec(memory_space=pl.ANY)] * len(after),
            out_specs=[whole(x) for x in out_shape],
            scratch_shapes=list(scratch),
        ),
        out_shape=out_shape,
        compiler_params=pltpu.CompilerParams(vmem_limit_bytes=mib * MIB),
        cost_estimate=pl.CostEstimate(flops=cost[0], bytes_accessed=cost[1], transcendentals=0),
        name=name,
    )(*scalars, *operands, *after)


def begin_kernel(me_dp_ref, me_ctx_ref, out_ref):
    out_ref[...] = jnp.zeros_like(out_ref)


def begin(me_dp, me_ctx):
    mark = [shape((8, 128), F32)]
    return whole_call(begin_kernel, "begin", [me_dp, me_ctx], [], mark, 4, (20_000_000_000, 0))[0]


def prepare_kernel(pieces, a_ref, a_out):
    tile = a_ref.shape[1] // pieces
    for i in range(pieces):
        a_out[i * tile : (i + 1) * tile, :] = a_ref[:, i * tile : (i + 1) * tile].T


def prepare(activations, after):
    rows, model = activations.shape
    outs = [shape((model, rows))]
    cost = (0, 0)
    kernel = functools.partial(prepare_kernel, 8)
    return whole_call(kernel, "prepare", [], [activations], outs, 16, cost, [], after)[0]


def head_pair(ref, i, hd):
    at = i * (2 * hd)
    first = ref[:, pl.ds(pl.multiple_of(at, hd), hd)]
    second = ref[:, pl.ds(pl.multiple_of(at + hd, hd), hd)]
    return jnp.concatenate([first, second], axis=0)


def score_chunk(k, v, q, do, own, first_lane):
    s = lax.dot_general(k, q, NT, preferred_element_type=F32)
    dp = lax.dot_general(v, do, NT, preferred_element_type=F32)
    if own:
        rows = k.shape[0]
        key_at = lax.broadcasted_iota(jnp.int32, s.shape, 0)
        query_at = lax.broadcasted_iota(jnp.int32, s.shape, 1) + first_lane
        query_at = jnp.where(query_at >= rows, query_at - rows, query_at)
        s = jnp.where(key_at <= query_at, s, -FAR)
    return s, dp


def counted(b, flags):
    lane = lax.broadcasted_iota(jnp.int32, flags.shape, 1)
    return jnp.max(jnp.where(lane == b, flags[...], 0.0)) > 0.5


def stats_of_block(b, q_ref, do_ref, k_ref, v_ref, before, out):
    k, v = k_ref[...], v_ref[...]
    rows, hd = k.shape
    pair = 2 * rows
    factor = LOG2E / hd**0.5

    def heads(i, carry):
        q, do = head_pair(q_ref, i, hd), head_pair(do_ref, i, hd)
        for t in range(pair // CHUNK):
            part = slice(t * CHUNK, (t + 1) * CHUNK)
            lanes = pl.ds(pl.multiple_of(i * pair + t * CHUNK, CHUNK), CHUNK)
            s, dp = score_chunk(k, v, q[part], do[part], b == 0, t * CHUNK)
            top = jnp.max(s, axis=0, keepdims=True) * factor
            e = jnp.exp2(s * factor - top)
            total = jnp.sum(e, axis=0, keepdims=True)
            weighted = jnp.sum(e * dp, axis=0, keepdims=True)
            if b > 0:
                old = before[0:1, lanes]
                both = jnp.maximum(old, top)
                old_part, new_part = jnp.exp2(old - both), jnp.exp2(top - both)
                total = before[1:2, lanes] * old_part + total * new_part
                weighted = before[2:3, lanes] * old_part + weighted * new_part
                top = both
            out[0:1, lanes] = top
            out[1:2, lanes] = total
            out[2:3, lanes] = weighted
        return carry

    lax.fori_loop(0, q_ref.shape[1] // (2 * hd), heads, 0, unroll=True)


def first_stats_kernel(n, me_ref, span_ref, q_ref, do_ref, k_ref, v_ref, out, q_out, do_out, k_out, v_out, flags):
    me = me_ref[0]
    lane = lax.broadcasted_iota(jnp.int32, flags.shape, 1)
    found = jnp.zeros(flags.shape, F32)
    for b in range(1, n):
        found = jnp.where((lane == b) & (span_ref[me ^ b] < span_ref[me]), 1.0, found)
    flags[...] = found
    q_out[...] = q_ref[...]
    do_out[...] = do_ref[...]
    k_out[...] = k_ref[...]
    v_out[...] = v_ref[...]
    stats_of_block(0, q_ref, do_ref, k_ref, v_ref, None, out)


def next_stats_kernel(b, flags, q_ref, do_ref, k_ref, v_ref, before, out):
    keep = counted(b, flags)

    @pl.when(keep)
    def _():
        stats_of_block(b, q_ref, do_ref, k_ref, v_ref, before, out)

    @pl.when(jnp.logical_not(keep))
    def _():
        out[...] = before[...]


def block_gradients(own, stats, q_ref, do_ref, k_ref, v_ref, p_buf, ds_ref, dk, dv):
    k, v = k_ref[...], v_ref[...]
    rows, hd = k.shape
    pair = 2 * rows
    factor = LOG2E / hd**0.5
    dk[...] = jnp.zeros_like(dk)
    dv[...] = jnp.zeros_like(dv)

    def heads(i, carry):
        q, do = head_pair(q_ref, i, hd), head_pair(do_ref, i, hd)
        for t in range(pair // CHUNK):
            part = slice(t * CHUNK, (t + 1) * CHUNK)
            lanes = pl.ds(pl.multiple_of(i * pair + t * CHUNK, CHUNK), CHUNK)
            s, dp = score_chunk(k, v, q[part], do[part], own, t * CHUNK)
            total = stats[1:2, lanes]
            level = stats[0:1, lanes] + jnp.log(total) * LOG2E
            p = jnp.exp2(s * factor - level)
            p_buf[:, part] = p.astype(BF16)
            ds = (p * (dp - stats[2:3, lanes] / total)).astype(BF16)
            ds_ref[:, lanes] = ds
        ds = ds_ref[:, pl.ds(pl.multiple_of(i * pair, CHUNK), pair)]
        dk[...] += jnp.dot(ds, q, preferred_element_type=F32)
        dv[...] += jnp.dot(p_buf[...], do, preferred_element_type=F32)
        return carry

    lax.fori_loop(0, q_ref.shape[1] // (2 * hd), heads, 0, unroll=True)
    inverse = 1.0 / hd**0.5
    return dk[...] * inverse, dv[...]


def other_kernel(b, flags, stats, q_ref, do_ref, k_ref, v_ref, dk_out, dv_out, ds_out, p_buf, dk, dv):
    keep = counted(b, flags)
    rows = dk.shape[0]

    @pl.when(keep)
    def _():
        dk_sum, dv_sum = block_gradients(False, stats, q_ref, do_ref, k_ref, v_ref, p_buf, ds_out, dk, dv)
        dk_out[...] = dk_sum.astype(BF16)
        dv_out[:rows, :] = dv_sum.astype(BF16)
        dv_out[rows:, :] = jnp.zeros((dv_out.shape[0] - rows, dv.shape[1]), BF16)

    @pl.when(jnp.logical_not(keep))
    def _():
        dk_out[...] = jnp.zeros_like(dk_out)
        dv_out[...] = jnp.zeros_like(dv_out)
        ds_out[...] = jnp.zeros_like(ds_out)


def own_kernel(stats, q_ref, do_ref, k_ref, v_ref, out_ref, ds_out, p_buf, dk, dv):
    hd = dk.shape[1]
    dk_sum, dv_sum = block_gradients(True, stats, q_ref, do_ref, k_ref, v_ref, p_buf, ds_out, dk, dv)
    out_ref[:, :hd] = dk_sum
    out_ref[:, hd:] = dv_sum


def query_kernel(n, *refs):
    k_refs, ds_refs, dq_ref, mark_ref = refs[:n], refs[n : 2 * n], refs[2 * n], refs[2 * n + 1]
    mark_ref[...] = jnp.zeros_like(mark_ref)
    rows, hd = k_refs[0].shape
    for h in range(dq_ref.shape[1] // hd):
        dq = 0.0
        for k, ds in zip(k_refs, ds_refs):
            part = ds[:, h * rows : (h + 1) * rows]
            dq = dq + lax.dot_general(part, k[...], TN, preferred_element_type=F32)
        dq_ref[:, h * hd : (h + 1) * hd] = (dq / hd**0.5).astype(BF16)


def merge_kernel(rows, *refs):
    *terms, out_ref = refs
    total = functools.reduce(jnp.add, [term[:rows, :].astype(F32) for term in terms])
    out_ref[:rows, :] = total.astype(BF16)
    if out_ref.shape[0] > rows:
        out_ref[rows:, :] = jnp.zeros((out_ref.shape[0] - rows, out_ref.shape[1]), BF16)


def merge(rows, terms, after):
    outs = [shape(terms[0].shape)]
    return whole_call(functools.partial(merge_kernel, rows), "merge", [], terms, outs, 4, (0, 0), [], after)[0]


def attention(me, spans, queries, out_grad, keys, values, activations, mark, swap, n):
    rows, hd = keys.shape
    columns = queries.shape[1]
    tall = columns // hd * rows
    product = 2 * rows * tall * hd
    cost = (8 * product, 8 * rows * columns)

    direct = [b for b in range(1, n) if b & (b - 1) == 0]
    blocks = {b: [swap(keys, b), swap(values, b)] for b in reversed(direct)}
    stats_shape = shape((8, tall), F32)
    stats, queries, out_grad, keys, values, flags = whole_call(
        functools.partial(first_stats_kernel, n),
        "first_stats",
        [me, spans],
        [queries, out_grad, keys, values],
        [stats_shape] + [shape(x.shape) for x in (queries, out_grad, keys, values)] + [shape((8, 128), F32)],
        12,
        cost,
        [],
        [mark],
    )
    blocks[0] = [keys, values]
    acts = prepare(activations, [stats])
    for b in range(1, n):
        if b not in blocks:
            blocks[b] = [swap(x, b & -b) for x in blocks[b & (b - 1)]]
        stats = whole_call(
            functools.partial(next_stats_kernel, b),
            "next_stats",
            [],
            [flags, queries, out_grad, *blocks[b], stats],
            [stats_shape],
            10,
            cost,
            [],
            [*blocks[2], acts] if b == 1 else [],
        )[0]
    p_buf = pltpu.VMEM((rows, 2 * rows), BF16)
    sums = [pltpu.VMEM((rows, hd), F32)] * 2
    key_parts, value_parts = [[] for _ in range(n)], [[] for _ in range(n)]
    score_grads, before = [None] * n, []
    for b in range(n - 1, 0, -1):
        dk, dv, score_grads[b] = whole_call(
            functools.partial(other_kernel, b),
            "block_gradients",
            [],
            [flags, stats, queries, out_grad, *blocks[b]],
            [shape((rows, hd)), shape((rows + TOP_ROWS, hd)), shape((rows, tall))],
            10,
            (0, 0),
            [p_buf, *sums],
            before,
        )
        if value_parts[b]:
            dv = merge(rows, [dv, *value_parts[b]], [])
        value_parts[b & (b - 1)].append(swap(dv, b & -b))
        if key_parts[b]:
            dk = merge(rows, [dk, *key_parts[b]], [dv])
        key_parts[b & (b - 1)].append(swap(dk, b & -b))
        before = [dv, dk]
    own, score_grads[0] = whole_call(
        own_kernel,
        "own_gradients",
        [],
        [stats, queries, out_grad, keys, values],
        [shape((rows, 2 * hd), F32), shape((rows, tall))],
        10,
        (0, 0),
        [p_buf, *sums],
        before,
    )
    return own, key_parts[0], value_parts[0], [blocks[b][0] for b in range(n)], score_grads, acts


def query_gradients(key_blocks, score_grads, columns, after):
    n = len(key_blocks)
    rows = key_blocks[0].shape[0]
    return whole_call(
        functools.partial(query_kernel, n),
        "query_gradients",
        [],
        [*key_blocks, *score_grads],
        [shape((rows, columns)), shape((8, 128), F32)],
        2 + 3 * n,
        (2 * n * rows * rows * columns, 16 * rows * columns),
        [],
        after,
    )


def pack_top(top):
    high = jnp.minimum(top, BF16_MAX).astype(BF16).astype(F32)
    rest = top - high
    middle = rest.astype(BF16).astype(F32)
    low = rest - middle
    return (high + pltpu.roll(middle, PACK_LANES, 1) + pltpu.roll(low, 2 * PACK_LANES, 1)).astype(BF16)


def unpack_top(ref, at):
    x = ref[at : at + TOP_ROWS, :TOP_LANES].astype(F32)
    total = x + (pltpu.roll(x, TOP_LANES - PACK_LANES, 1) + pltpu.roll(x, TOP_LANES - 2 * PACK_LANES, 1))
    lane = lax.broadcasted_iota(jnp.int32, x.shape, 1)
    return jnp.where(lane < PACK_LANES, total, 0.0)


def tile_of(step, me_dp, bits, flip):
    mask = flip
    for j in range(1, bits):
        if not (step >> (bits - 1 - j)) & 1:
            mask |= 1 << j
    return me_dp ^ mask


def reversed_step(step, bits):
    return sum(((step >> (bits - 1 - j)) & 1) << (j - 1) for j in range(1, bits))


def corrected_tile(at, dest, grads, a_ref, e_ref, top_ref):
    _, n_ctx, rows_ctx, rows = a_ref.shape
    tall = n_ctx * rows_ctx
    hd = grads.shape[1]
    a = a_ref[dest].reshape(tall, rows)
    e = e_ref[dest, :, :, at : at + hd].reshape(tall, hd)
    c = jnp.dot(a, grads, preferred_element_type=F32) + e
    mags = jnp.max(jnp.abs(c).reshape(tall // QROWS, QROWS, hd), axis=1)
    mags = jnp.max(mags, axis=1, keepdims=True)
    block = lax.broadcasted_iota(jnp.int32, (tall // QROWS, TOP_LANES), 0)
    lane = lax.broadcasted_iota(jnp.int32, (tall // QROWS, TOP_LANES), 1)
    top = jnp.max(jnp.where(lane == block, mags, 0.0), axis=0, keepdims=True)
    top_ref[pl.ds(dest, 1), :] = jnp.maximum(top_ref[pl.ds(dest, 1), :], top)
    return c


def summed_grads(at, own_ref, part_refs):
    rows, hd = own_ref.shape[0], own_ref.shape[1] // 2
    total = own_ref[:, at : at + hd]
    for part in part_refs:
        total = total + part[:rows, :].astype(F32)
    return total.astype(BF16)


def send_rows(bits, shrink, at, me_ref, total, a_ref, e_ref, out_ref, top_ref, packed):
    tall = a_ref.shape[1] * a_ref.shape[2]
    steps = a_ref.shape[0] // 2
    for step in range(steps):
        dest = tile_of(step, me_ref[0], bits, 1)
        c = corrected_tile(at, dest, total, a_ref, e_ref, top_ref)
        out_ref[step * tall : (step + 1) * tall, :] = (c * shrink).astype(BF16)
    tail = jnp.zeros((out_ref.shape[0] - steps * tall, out_ref.shape[1]), BF16)
    out_ref[steps * tall :, :] = pack_top(top_ref[...]) if packed else tail


def kept_rows(bits, shrink, at, me_ref, total, a_ref, e_ref, out_ref, top_ref):
    for step in range(out_ref.shape[0]):
        dest = tile_of(step, me_ref[0], bits, 0)
        out_ref[step] = corrected_tile(at, dest, total, a_ref, e_ref, top_ref) * shrink


def first_send_kernel(bits, shrink, at, n_parts, me_ref, own_ref, *refs):
    a_ref, e_ref, out_ref, top_ref, grads_ref, grads_out = refs[n_parts:]
    total = summed_grads(at, own_ref, refs[:n_parts])
    grads_ref[...] = total
    grads_out[...] = total
    top_ref[...] = jnp.zeros_like(top_ref)
    send_rows(bits, shrink, at, me_ref, total, a_ref, e_ref, out_ref, top_ref, False)


def next_kept_kernel(bits, shrink, at, me_ref, grads_ref, before_ref, a_ref, e_ref, out_ref, top_ref):
    top_ref[...] = before_ref[...]
    kept_rows(bits, shrink, at, me_ref, grads_ref[...], a_ref, e_ref, out_ref, top_ref)


def first_kept_kernel(bits, shrink, at, n_parts, me_ref, own_ref, *refs):
    before_ref, a_ref, e_ref, out_ref, top_ref, grads_ref, grads_out = refs[n_parts:]
    total = summed_grads(at, own_ref, refs[:n_parts])
    grads_ref[...] = total
    grads_out[...] = total
    top_ref[...] = before_ref[...]
    kept_rows(bits, shrink, at, me_ref, total, a_ref, e_ref, out_ref, top_ref)


def next_send_kernel(bits, shrink, at, me_ref, grads_ref, before_ref, a_ref, e_ref, out_ref, top_ref):
    top_ref[...] = before_ref[...]
    send_rows(bits, shrink, at, me_ref, grads_ref[...], a_ref, e_ref, out_ref, top_ref, True)


def split_kernel(bits, n_ctx, n_tops, kept, got, *refs):
    steps, tall, hd = kept.shape
    half = steps // 2
    part_tall = tall // 2
    tops = refs[:n_tops]
    low_away, low_stay, high_away, high_stay, *top_out = refs[n_tops:]
    for step in range(steps):
        c = (kept[step] + got[step * tall : (step + 1) * tall, :].astype(F32)).astype(BF16)
        c = c.reshape(n_ctx, 2, part_tall // n_ctx, hd)
        back = reversed_step(step, bits)
        for at, i, away, stay in ((step, 0, low_away, low_stay), (back, 1, high_away, high_stay)):
            part = c[:, i].reshape(part_tall, hd)
            if at < half:
                away[at * part_tall : (at + 1) * part_tall, :] = part
            else:
                stay[(at - half) * part_tall : (at - half + 1) * part_tall, :] = part
    if tops:
        top = largest(tops, got, steps * tall)
        top_out[0][...] = top
        low_away[half * part_tall :, :] = pack_top(top)
    else:
        low_away[half * part_tall :, :] = jnp.zeros((low_away.shape[0] - half * part_tall, hd), BF16)


def largest(tops, low_got, size):
    found = [top[...] for top in tops]
    if low_got.shape[0] > size:
        found.append(unpack_top(low_got, size))
    return functools.reduce(jnp.maximum, found)


def add_kernel(n_tops, low, low_got, high, high_got, *refs):
    tops = refs[:n_tops]
    low_away, low_stay, high_away, high_stay, *top_out = refs[n_tops:]
    size = low.shape[0]
    half = size // 2
    for mine, got, away, stay in ((low, low_got, low_away, low_stay), (high, high_got, high_away, high_stay)):
        away[:half, :] = (mine[:half, :].astype(F32) + got[:half, :].astype(F32)).astype(BF16)
        stay[...] = (mine[half:, :].astype(F32) + got[half:size, :].astype(F32)).astype(BF16)
    if tops:
        top = largest(tops, low_got, size)
        top_out[0][...] = top
        low_away[half:, :] = pack_top(top)
    else:
        low_away[half:, :] = jnp.zeros((low_away.shape[0] - half, low_away.shape[1]), BF16)


def context_masks(n_ctx):
    bits = n_ctx.bit_length() - 1
    return [sum((1 << j) for j in range(bits) if not (step >> (bits - 1 - j)) & 1) for step in range(n_ctx)]


def last_kernel(n_ctx, n_tops, me_ref, low, low_got, high, high_got, *refs):
    tops = refs[:n_tops]
    away, stay, *top_out = refs[n_tops:]
    size, hd = low.shape
    rows_set = size // n_ctx
    half = n_ctx // 2
    for i, mask in enumerate(context_masks(n_ctx)):
        part = pl.ds(pl.multiple_of((me_ref[0] ^ mask) * rows_set, rows_set), rows_set)
        out, at = (away, i) if i < half else (stay, i - half)
        at = 2 * at * rows_set
        for mine, got in ((low, low_got), (high, high_got)):
            total = mine[part, :].astype(F32) + got[part, :].astype(F32)
            out[at : at + rows_set, :] = total.astype(BF16)
            at += rows_set
    if tops:
        top = largest(tops, low_got, size)
        top_out[0][...] = top
        away[half * 2 * rows_set :, :] = pack_top(top)
    else:
        away[half * 2 * rows_set :, :] = jnp.zeros((away.shape[0] - half * 2 * rows_set, hd), BF16)


def halve_kernel(n_tops, mine, got, *refs):
    tops = refs[:n_tops]
    away, stay, *top_out = refs[n_tops:]
    size = mine.shape[0]
    half = size // 2
    away[:half, :] = (mine[:half, :].astype(F32) + got[:half, :].astype(F32)).astype(BF16)
    stay[...] = (mine[half:, :].astype(F32) + got[half:size, :].astype(F32)).astype(stay.dtype)
    if tops:
        top = largest(tops, got, size)
        top_out[0][...] = top
        away[half:, :] = pack_top(top)
    else:
        away[half:, :] = jnp.zeros((away.shape[0] - half, away.shape[1]), BF16)


def final_kernel(columns, gain, me_dp_ref, me_ctx_ref, *refs):
    sets = len(columns)
    groups = [refs[2 * chosen : 2 * chosen + 2] for chosen in range(sets)]
    top_ref, out_ref, scale_ref, all_tops = refs[2 * sets :]
    n_dp, lanes = scale_ref.shape
    rows_ctx, hd = groups[0][0].shape
    scale = jnp.maximum(top_ref[...], unpack_top(groups[0][1], rows_ctx)) + 1e-06
    all_tops[...] = scale
    scale_ref[...] = scale[:n_dp, :lanes]
    factors = gain / all_tops[pl.ds(me_dp_ref[0], 1), :]
    lane = lax.broadcasted_iota(jnp.int32, factors.shape, 1)
    blocks = rows_ctx // QROWS
    for r in range(blocks):
        mine = jnp.where(lane == me_ctx_ref[0] * blocks + r, factors, 0.0)
        factor = jnp.sum(mine, axis=1, keepdims=True)
        part = slice(r * QROWS, (r + 1) * QROWS)
        for at, (mine_ref, got_ref) in zip(columns, groups):
            out_ref[part, at : at + hd] = (mine_ref[part, :] + got_ref[part, :].astype(F32)) * factor


def local(n_dp, n_ctx, span_order, queries, keys, values, out_grad, activations, error_feedback):
    rows, hd = keys.shape
    width = 2 * hd
    model = activations.shape[1]
    rows_ctx = model // (n_dp * n_ctx)
    tall = n_ctx * rows_ctx
    me_dp = lax.axis_index("dp").astype(jnp.int32)[None]
    me_ctx = lax.axis_index("context").astype(jnp.int32)[None]
    bits = n_dp.bit_length() - 1

    def swap_dp(x, mask):
        return lax.ppermute(x, "dp", xor_perm(n_dp, mask))

    def swap_ctx(x, mask):
        return lax.ppermute(x, "context", xor_perm(n_ctx, mask))

    own, key_parts, value_parts, key_blocks, score_grads, acts = attention(
        me_ctx, span_order[0], queries, out_grad, keys, values, activations, begin(me_dp, me_ctx), swap_ctx, n_ctx
    )

    shrink = 1.0 / (n_dp * n_ctx)
    acts = acts.reshape(n_dp, n_ctx, rows_ctx, rows)
    errors = error_feedback.reshape(n_dp, n_ctx, rows_ctx, width)
    tops = shape((TOP_ROWS, TOP_LANES), F32)
    steps = n_dp // 2
    cost = (0, 0)
    kept_shape, grad_shape = shape((steps, tall, hd), F32), shape((rows, hd))

    def tiles(kernel, name, operands, outs, after=()):
        return whole_call(kernel, name, [me_dp], [*operands, acts, errors], outs, 18, cost, [], after)

    sets = 2
    half = steps // 2 * (tall // 2)

    def split(last, kept, got, top):
        return whole_call(
            functools.partial(split_kernel, bits, n_ctx, int(last)),
            "split_tiles",
            [],
            [kept, got] + [top] * last,
            [shape((half + (1 if last else 2) * TOP_ROWS, hd))] + [shape((half, hd))] * 3 + [tops] * last,
            10,
            cost,
        )

    out, top, grads, value_grad = tiles(
        functools.partial(first_send_kernel, bits, shrink, hd, len(value_parts)),
        "send_tiles",
        [own, *value_parts],
        [shape((steps * tall + 2 * TOP_ROWS, hd)), tops, grad_shape, grad_shape],
    )
    got = swap_dp(out, 1)
    kept, top = tiles(
        functools.partial(next_kept_kernel, bits, shrink, hd), "kept_tiles", [grads, top], [kept_shape, tops]
    )
    halves = [split(False, kept, got, None)]
    kept, top, grads, key_grad = tiles(
        functools.partial(first_kept_kernel, bits, shrink, 0, len(key_parts)),
        "kept_tiles",
        [own, *key_parts, top],
        [kept_shape, tops, grad_shape, grad_shape],
    )
    out, top = tiles(
        functools.partial(next_send_kernel, bits, shrink, 0),
        "send_tiles",
        [grads, top],
        [shape((steps * tall + TOP_ROWS, hd)), tops],
    )
    arrays = split(True, kept, swap_dp(out, 1), top)
    halves.append(arrays[:4])
    gathered = [arrays[4]]
    query_grad, mark = query_gradients(key_blocks, score_grads, queries.shape[1], [arrays[1]])
    groups = []
    for chosen in range(sets):
        low_away, low, high_away, high = halves[chosen]
        extra = TOP_ROWS if chosen == sets - 1 else 0
        tail = extra or 2 * TOP_ROWS
        for stage in range(1, bits):
            low_got = swap_dp(low_away, 1 << stage)
            high_got = swap_dp(high_away, 1 << (bits - stage))
            with_tops = extra > 0
            operands = [low, low_got, high, high_got] + (gathered if with_tops else [])
            n_tops = len(operands) - 4
            size = low.shape[0]
            if stage < bits - 1:
                low_away, low, high_away, high, *top_out = whole_call(
                    functools.partial(add_kernel, n_tops),
                    "add_stage",
                    [],
                    operands,
                    [shape((size // 2 + tail, hd))] + [shape((size // 2, hd))] * 3 + [tops] * with_tops,
                    8,
                    cost,
                    after=[mark] if chosen == 0 and stage == 1 else [],
                )
            else:
                chunk = rows_ctx
                away, stay, *top_out = whole_call(
                    functools.partial(last_kernel, n_ctx, n_tops),
                    "last_stage",
                    [me_ctx],
                    operands,
                    [shape((n_ctx // 2 * chunk + tail, hd)), shape((n_ctx // 2 * chunk, hd))] + [tops] * with_tops,
                    8,
                    cost,
                )
            if with_tops:
                gathered = list(top_out)
        mask = 1
        while mask < n_ctx // 2:
            size = stay.shape[0]
            away, stay, *top_out = whole_call(
                functools.partial(halve_kernel, int(with_tops)),
                "halve_context",
                [],
                [stay, swap_ctx(away, mask)] + (gathered if with_tops else []),
                [shape((size // 2 + tail, hd)), shape((size // 2, hd), F32 if size == 2 * chunk else BF16)]
                + [tops] * with_tops,
                8,
                (0, 0),
            )
            if with_tops:
                gathered = list(top_out)
            mask *= 2
        groups = [stay, swap_ctx(away, mask), *groups]
    payload, scale = whole_call(
        functools.partial(final_kernel, (0, hd), 7.0 / shrink),
        "final_stage",
        [me_dp, me_ctx],
        groups + gathered,
        [shape((rows_ctx, width), F32), shape((n_dp, tall // QROWS), F32)],
        8,
        (0, 0),
        [pltpu.VMEM((TOP_ROWS, TOP_LANES), F32)],
    )
    return query_grad, key_grad, value_grad, payload, scale.reshape(-1)


def solution(mesh):
    tokens = P(("dp", "context"), None)
    return jax.shard_map(
        functools.partial(local, mesh.shape["dp"], mesh.shape["context"]),
        mesh=mesh,
        in_specs=(P("dp", None), tokens, tokens, tokens, tokens, tokens, P("dp", "context", None, None)),
        out_specs=(tokens, tokens, tokens, tokens, P()),
        check_vma=False,
    )
```

```python
import functools

import jax
import jax.numpy as jnp
from jax import lax
from jax.experimental import pallas as pl
from jax.experimental.pallas import tpu as pltpu
from jax.sharding import PartitionSpec as P

QROWS = 32
LOG2E = 1.4426950408889634
FAR = 1e30
MIB = 1024 * 1024
CHUNK = 256
TOP_ROWS, TOP_LANES, PACK_LANES = 16, 128, 32
BF16, F32 = jnp.bfloat16, jnp.float32
BF16_MAX = float(jnp.finfo(jnp.bfloat16).max)
NT = (((1,), (1,)), ((), ()))
TN = (((0,), (0,)), ((), ()))


def xor_perm(size, mask):
    return [(i, i ^ mask) for i in range(size)]


def whole(x):
    return pl.BlockSpec(x.shape, lambda *_: (0,) * len(x.shape))


def shape(dims, dtype=BF16):
    return jax.ShapeDtypeStruct(dims, dtype)


def whole_call(kernel, name, scalars, operands, out_shape, mib, cost, scratch=(), after=()):
    def body(*refs):
        first = len(scalars) + len(operands)
        kernel(*refs[:first], *refs[first + len(after) :])

    return pl.pallas_call(
        body,
        grid_spec=pltpu.PrefetchScalarGridSpec(
            num_scalar_prefetch=len(scalars),
            grid=(1,),
            in_specs=[whole(x) for x in operands] + [pl.BlockSpec(memory_space=pl.ANY)] * len(after),
            out_specs=[whole(x) for x in out_shape],
            scratch_shapes=list(scratch),
        ),
        out_shape=out_shape,
        compiler_params=pltpu.CompilerParams(vmem_limit_bytes=mib * MIB),
        cost_estimate=pl.CostEstimate(flops=cost[0], bytes_accessed=cost[1], transcendentals=0),
        name=name,
    )(*scalars, *operands, *after)


def begin_kernel(me_dp_ref, me_ctx_ref, out_ref):
    out_ref[...] = jnp.zeros_like(out_ref)


def begin(me_dp, me_ctx):
    mark = [shape((8, 128), F32)]
    return whole_call(begin_kernel, "begin", [me_dp, me_ctx], [], mark, 4, (20_000_000_000, 0))[0]


def prepare_kernel(pieces, a_ref, a_out):
    tile = a_ref.shape[1] // pieces
    for i in range(pieces):
        a_out[i * tile : (i + 1) * tile, :] = a_ref[:, i * tile : (i + 1) * tile].T


def prepare(activations, after):
    rows, model = activations.shape
    outs = [shape((model, rows))]
    cost = (0, 0)
    kernel = functools.partial(prepare_kernel, 8)
    return whole_call(kernel, "prepare", [], [activations], outs, 16, cost, [], after)[0]


def head_pair(ref, i, hd):
    at = i * (2 * hd)
    first = ref[:, pl.ds(pl.multiple_of(at, hd), hd)]
    second = ref[:, pl.ds(pl.multiple_of(at + hd, hd), hd)]
    return jnp.concatenate([first, second], axis=0)


def score_chunk(k, v, q, do, own, first_lane):
    s = lax.dot_general(k, q, NT, preferred_element_type=F32)
    dp = lax.dot_general(v, do, NT, preferred_element_type=F32)
    if own:
        rows = k.shape[0]
        key_at = lax.broadcasted_iota(jnp.int32, s.shape, 0)
        query_at = lax.broadcasted_iota(jnp.int32, s.shape, 1) + first_lane
        query_at = jnp.where(query_at >= rows, query_at - rows, query_at)
        s = jnp.where(key_at <= query_at, s, -FAR)
    return s, dp


def counted(b, flags):
    lane = lax.broadcasted_iota(jnp.int32, flags.shape, 1)
    return jnp.max(jnp.where(lane == b, flags[...], 0.0)) > 0.5


def stats_of_block(b, q_ref, do_ref, k_ref, v_ref, before, out):
    k, v = k_ref[...], v_ref[...]
    rows, hd = k.shape
    pair = 2 * rows
    factor = LOG2E / hd**0.5

    def heads(i, carry):
        q, do = head_pair(q_ref, i, hd), head_pair(do_ref, i, hd)
        for t in range(pair // CHUNK):
            part = slice(t * CHUNK, (t + 1) * CHUNK)
            lanes = pl.ds(pl.multiple_of(i * pair + t * CHUNK, CHUNK), CHUNK)
            s, dp = score_chunk(k, v, q[part], do[part], b == 0, t * CHUNK)
            top = jnp.max(s, axis=0, keepdims=True) * factor
            e = jnp.exp2(s * factor - top)
            total = jnp.sum(e, axis=0, keepdims=True)
            weighted = jnp.sum(e * dp, axis=0, keepdims=True)
            if b > 0:
                old = before[0:1, lanes]
                both = jnp.maximum(old, top)
                old_part, new_part = jnp.exp2(old - both), jnp.exp2(top - both)
                total = before[1:2, lanes] * old_part + total * new_part
                weighted = before[2:3, lanes] * old_part + weighted * new_part
                top = both
            out[0:1, lanes] = top
            out[1:2, lanes] = total
            out[2:3, lanes] = weighted
        return carry

    lax.fori_loop(0, q_ref.shape[1] // (2 * hd), heads, 0, unroll=True)


def first_stats_kernel(n, me_ref, span_ref, q_ref, do_ref, k_ref, v_ref, out, q_out, do_out, k_out, v_out, flags):
    me = me_ref[0]
    lane = lax.broadcasted_iota(jnp.int32, flags.shape, 1)
    found = jnp.zeros(flags.shape, F32)
    for b in range(1, n):
        found = jnp.where((lane == b) & (span_ref[me ^ b] < span_ref[me]), 1.0, found)
    flags[...] = found
    q_out[...] = q_ref[...]
    do_out[...] = do_ref[...]
    k_out[...] = k_ref[...]
    v_out[...] = v_ref[...]
    stats_of_block(0, q_ref, do_ref, k_ref, v_ref, None, out)


def next_stats_kernel(b, flags, q_ref, do_ref, k_ref, v_ref, before, out):
    keep = counted(b, flags)

    @pl.when(keep)
    def _():
        stats_of_block(b, q_ref, do_ref, k_ref, v_ref, before, out)

    @pl.when(jnp.logical_not(keep))
    def _():
        out[...] = before[...]


def block_gradients(own, stats, q_ref, do_ref, k_ref, v_ref, p_buf, ds_ref, dk, dv):
    k, v = k_ref[...], v_ref[...]
    rows, hd = k.shape
    pair = 2 * rows
    factor = LOG2E / hd**0.5
    dk[...] = jnp.zeros_like(dk)
    dv[...] = jnp.zeros_like(dv)

    def heads(i, carry):
        q, do = head_pair(q_ref, i, hd), head_pair(do_ref, i, hd)
        for t in range(pair // CHUNK):
            part = slice(t * CHUNK, (t + 1) * CHUNK)
            lanes = pl.ds(pl.multiple_of(i * pair + t * CHUNK, CHUNK), CHUNK)
            s, dp = score_chunk(k, v, q[part], do[part], own, t * CHUNK)
            total = stats[1:2, lanes]
            level = stats[0:1, lanes] + jnp.log(total) * LOG2E
            p = jnp.exp2(s * factor - level)
            p_buf[:, part] = p.astype(BF16)
            ds = (p * (dp - stats[2:3, lanes] / total)).astype(BF16)
            ds_ref[:, lanes] = ds
        ds = ds_ref[:, pl.ds(pl.multiple_of(i * pair, CHUNK), pair)]
        dk[...] += jnp.dot(ds, q, preferred_element_type=F32)
        dv[...] += jnp.dot(p_buf[...], do, preferred_element_type=F32)
        return carry

    lax.fori_loop(0, q_ref.shape[1] // (2 * hd), heads, 0, unroll=True)
    inverse = 1.0 / hd**0.5
    return dk[...] * inverse, dv[...]


def other_kernel(b, flags, stats, q_ref, do_ref, k_ref, v_ref, dk_out, dv_out, ds_out, p_buf, dk, dv):
    keep = counted(b, flags)
    rows = dk.shape[0]

    @pl.when(keep)
    def _():
        dk_sum, dv_sum = block_gradients(False, stats, q_ref, do_ref, k_ref, v_ref, p_buf, ds_out, dk, dv)
        dk_out[...] = dk_sum.astype(BF16)
        dv_out[:rows, :] = dv_sum.astype(BF16)
        dv_out[rows:, :] = jnp.zeros((dv_out.shape[0] - rows, dv.shape[1]), BF16)

    @pl.when(jnp.logical_not(keep))
    def _():
        dk_out[...] = jnp.zeros_like(dk_out)
        dv_out[...] = jnp.zeros_like(dv_out)
        ds_out[...] = jnp.zeros_like(ds_out)


def own_kernel(stats, q_ref, do_ref, k_ref, v_ref, out_ref, ds_out, p_buf, dk, dv):
    hd = dk.shape[1]
    dk_sum, dv_sum = block_gradients(True, stats, q_ref, do_ref, k_ref, v_ref, p_buf, ds_out, dk, dv)
    out_ref[:, :hd] = dk_sum
    out_ref[:, hd:] = dv_sum


def query_kernel(n, *refs):
    k_refs, ds_refs, dq_ref, mark_ref = refs[:n], refs[n : 2 * n], refs[2 * n], refs[2 * n + 1]
    mark_ref[...] = jnp.zeros_like(mark_ref)
    rows, hd = k_refs[0].shape
    for h in range(dq_ref.shape[1] // hd):
        dq = 0.0
        for k, ds in zip(k_refs, ds_refs):
            part = ds[:, h * rows : (h + 1) * rows]
            dq = dq + lax.dot_general(part, k[...], TN, preferred_element_type=F32)
        dq_ref[:, h * hd : (h + 1) * hd] = (dq / hd**0.5).astype(BF16)


def merge_kernel(rows, *refs):
    *terms, out_ref = refs
    total = functools.reduce(jnp.add, [term[:rows, :].astype(F32) for term in terms])
    out_ref[:rows, :] = total.astype(BF16)
    if out_ref.shape[0] > rows:
        out_ref[rows:, :] = jnp.zeros((out_ref.shape[0] - rows, out_ref.shape[1]), BF16)


def merge(rows, terms, after):
    outs = [shape(terms[0].shape)]
    return whole_call(functools.partial(merge_kernel, rows), "merge", [], terms, outs, 4, (0, 0), [], after)[0]


def attention(me, spans, queries, out_grad, keys, values, activations, mark, swap, n):
    rows, hd = keys.shape
    columns = queries.shape[1]
    tall = columns // hd * rows
    product = 2 * rows * tall * hd
    cost = (8 * product, 8 * rows * columns)

    direct = [b for b in range(1, n) if b & (b - 1) == 0]
    blocks = {b: [swap(keys, b), swap(values, b)] for b in reversed(direct)}
    stats_shape = shape((8, tall), F32)
    stats, queries, out_grad, keys, values, flags = whole_call(
        functools.partial(first_stats_kernel, n),
        "first_stats",
        [me, spans],
        [queries, out_grad, keys, values],
        [stats_shape] + [shape(x.shape) for x in (queries, out_grad, keys, values)] + [shape((8, 128), F32)],
        12,
        cost,
        [],
        [mark],
    )
    blocks[0] = [keys, values]
    acts = prepare(activations, [stats])
    for b in range(1, n):
        if b not in blocks:
            blocks[b] = [swap(x, b & -b) for x in blocks[b & (b - 1)]]
        stats = whole_call(
            functools.partial(next_stats_kernel, b),
            "next_stats",
            [],
            [flags, queries, out_grad, *blocks[b], stats],
            [stats_shape],
            10,
            cost,
            [],
            [*blocks[2], acts] if b == 1 else [],
        )[0]
    p_buf = pltpu.VMEM((rows, 2 * rows), BF16)
    sums = [pltpu.VMEM((rows, hd), F32)] * 2
    key_parts, value_parts = [[] for _ in range(n)], [[] for _ in range(n)]
    score_grads, own_parts, before = [None] * n, {}, []
    for b in range(n - 1, 0, -1):
        dk, dv, score_grads[b] = whole_call(
            functools.partial(other_kernel, b),
            "block_gradients",
            [],
            [flags, stats, queries, out_grad, *blocks[b]],
            [shape((rows, hd)), shape((rows + TOP_ROWS, hd)), shape((rows, tall))],
            10,
            (0, 0),
            [p_buf, *sums],
            before,
        )
        if value_parts[b]:
            dv = merge(rows, [dv, *value_parts[b]], [])
        value_parts[b & (b - 1)].append(swap(dv, b & -b))
        own_parts[b] = dk
        before = [dv]
    for b in range(n - 1, 0, -1):
        dk = own_parts[b]
        if key_parts[b]:
            dk = merge(rows, [dk, *key_parts[b]], before)
        key_parts[b & (b - 1)].append(swap(dk, b & -b))
    own, score_grads[0] = whole_call(
        own_kernel,
        "own_gradients",
        [],
        [stats, queries, out_grad, keys, values],
        [shape((rows, 2 * hd), F32), shape((rows, tall))],
        10,
        (0, 0),
        [p_buf, *sums],
        before,
    )
    return own, key_parts[0], value_parts[0], [blocks[b][0] for b in range(n)], score_grads, acts


def query_gradients(key_blocks, score_grads, columns, after):
    n = len(key_blocks)
    rows = key_blocks[0].shape[0]
    return whole_call(
        functools.partial(query_kernel, n),
        "query_gradients",
        [],
        [*key_blocks, *score_grads],
        [shape((rows, columns)), shape((8, 128), F32)],
        2 + 3 * n,
        (2 * n * rows * rows * columns, 16 * rows * columns),
        [],
        after,
    )


def pack_top(top):
    high = jnp.minimum(top, BF16_MAX).astype(BF16).astype(F32)
    rest = top - high
    middle = rest.astype(BF16).astype(F32)
    low = rest - middle
    return (high + pltpu.roll(middle, PACK_LANES, 1) + pltpu.roll(low, 2 * PACK_LANES, 1)).astype(BF16)


def unpack_top(ref, at):
    x = ref[at : at + TOP_ROWS, :TOP_LANES].astype(F32)
    total = x + (pltpu.roll(x, TOP_LANES - PACK_LANES, 1) + pltpu.roll(x, TOP_LANES - 2 * PACK_LANES, 1))
    lane = lax.broadcasted_iota(jnp.int32, x.shape, 1)
    return jnp.where(lane < PACK_LANES, total, 0.0)


def tile_of(step, me_dp, bits, flip):
    mask = flip
    for j in range(1, bits):
        if not (step >> (bits - 1 - j)) & 1:
            mask |= 1 << j
    return me_dp ^ mask


def reversed_step(step, bits):
    return sum(((step >> (bits - 1 - j)) & 1) << (j - 1) for j in range(1, bits))


def corrected_tile(at, dest, grads, a_ref, e_ref, top_ref):
    _, n_ctx, rows_ctx, rows = a_ref.shape
    tall = n_ctx * rows_ctx
    hd = grads.shape[1]
    a = a_ref[dest].reshape(tall, rows)
    e = e_ref[dest, :, :, at : at + hd].reshape(tall, hd)
    c = jnp.dot(a, grads, preferred_element_type=F32) + e
    mags = jnp.max(jnp.abs(c).reshape(tall // QROWS, QROWS, hd), axis=1)
    mags = jnp.max(mags, axis=1, keepdims=True)
    block = lax.broadcasted_iota(jnp.int32, (tall // QROWS, TOP_LANES), 0)
    lane = lax.broadcasted_iota(jnp.int32, (tall // QROWS, TOP_LANES), 1)
    top = jnp.max(jnp.where(lane == block, mags, 0.0), axis=0, keepdims=True)
    top_ref[pl.ds(dest, 1), :] = jnp.maximum(top_ref[pl.ds(dest, 1), :], top)
    return c


def summed_grads(at, own_ref, part_refs):
    rows, hd = own_ref.shape[0], own_ref.shape[1] // 2
    total = own_ref[:, at : at + hd]
    for part in part_refs:
        total = total + part[:rows, :].astype(F32)
    return total.astype(BF16)


def send_rows(bits, shrink, at, me_ref, total, a_ref, e_ref, out_ref, top_ref, packed):
    tall = a_ref.shape[1] * a_ref.shape[2]
    steps = a_ref.shape[0] // 2
    for step in range(steps):
        dest = tile_of(step, me_ref[0], bits, 1)
        c = corrected_tile(at, dest, total, a_ref, e_ref, top_ref)
        out_ref[step * tall : (step + 1) * tall, :] = (c * shrink).astype(BF16)
    tail = jnp.zeros((out_ref.shape[0] - steps * tall, out_ref.shape[1]), BF16)
    out_ref[steps * tall :, :] = pack_top(top_ref[...]) if packed else tail


def kept_rows(bits, shrink, at, me_ref, total, a_ref, e_ref, out_ref, top_ref):
    for step in range(out_ref.shape[0]):
        dest = tile_of(step, me_ref[0], bits, 0)
        out_ref[step] = corrected_tile(at, dest, total, a_ref, e_ref, top_ref) * shrink


def first_send_kernel(bits, shrink, at, n_parts, me_ref, own_ref, *refs):
    a_ref, e_ref, out_ref, top_ref, grads_ref, grads_out = refs[n_parts:]
    total = summed_grads(at, own_ref, refs[:n_parts])
    grads_ref[...] = total
    grads_out[...] = total
    top_ref[...] = jnp.zeros_like(top_ref)
    send_rows(bits, shrink, at, me_ref, total, a_ref, e_ref, out_ref, top_ref, False)


def next_kept_kernel(bits, shrink, at, me_ref, grads_ref, before_ref, a_ref, e_ref, out_ref, top_ref):
    top_ref[...] = before_ref[...]
    kept_rows(bits, shrink, at, me_ref, grads_ref[...], a_ref, e_ref, out_ref, top_ref)


def first_kept_kernel(bits, shrink, at, n_parts, me_ref, own_ref, *refs):
    before_ref, a_ref, e_ref, out_ref, top_ref, grads_ref, grads_out = refs[n_parts:]
    total = summed_grads(at, own_ref, refs[:n_parts])
    grads_ref[...] = total
    grads_out[...] = total
    top_ref[...] = before_ref[...]
    kept_rows(bits, shrink, at, me_ref, total, a_ref, e_ref, out_ref, top_ref)


def next_send_kernel(bits, shrink, at, me_ref, grads_ref, before_ref, a_ref, e_ref, out_ref, top_ref):
    top_ref[...] = before_ref[...]
    send_rows(bits, shrink, at, me_ref, grads_ref[...], a_ref, e_ref, out_ref, top_ref, True)


def split_kernel(bits, n_ctx, n_tops, kept, got, *refs):
    steps, tall, hd = kept.shape
    half = steps // 2
    part_tall = tall // 2
    tops = refs[:n_tops]
    low_away, low_stay, high_away, high_stay, *top_out = refs[n_tops:]
    for step in range(steps):
        c = (kept[step] + got[step * tall : (step + 1) * tall, :].astype(F32)).astype(BF16)
        c = c.reshape(n_ctx, 2, part_tall // n_ctx, hd)
        back = reversed_step(step, bits)
        for at, i, away, stay in ((step, 0, low_away, low_stay), (back, 1, high_away, high_stay)):
            part = c[:, i].reshape(part_tall, hd)
            if at < half:
                away[at * part_tall : (at + 1) * part_tall, :] = part
            else:
                stay[(at - half) * part_tall : (at - half + 1) * part_tall, :] = part
    if tops:
        top = largest(tops, got, steps * tall)
        top_out[0][...] = top
        low_away[half * part_tall :, :] = pack_top(top)
    else:
        low_away[half * part_tall :, :] = jnp.zeros((low_away.shape[0] - half * part_tall, hd), BF16)


def largest(tops, low_got, size):
    found = [top[...] for top in tops]
    if low_got.shape[0] > size:
        found.append(unpack_top(low_got, size))
    return functools.reduce(jnp.maximum, found)


def add_kernel(n_tops, low, low_got, high, high_got, *refs):
    tops = refs[:n_tops]
    low_away, low_stay, high_away, high_stay, *top_out = refs[n_tops:]
    size = low.shape[0]
    half = size // 2
    for mine, got, away, stay in ((low, low_got, low_away, low_stay), (high, high_got, high_away, high_stay)):
        away[:half, :] = (mine[:half, :].astype(F32) + got[:half, :].astype(F32)).astype(BF16)
        stay[...] = (mine[half:, :].astype(F32) + got[half:size, :].astype(F32)).astype(BF16)
    if tops:
        top = largest(tops, low_got, size)
        top_out[0][...] = top
        low_away[half:, :] = pack_top(top)
    else:
        low_away[half:, :] = jnp.zeros((low_away.shape[0] - half, low_away.shape[1]), BF16)


def context_masks(n_ctx):
    bits = n_ctx.bit_length() - 1
    return [sum((1 << j) for j in range(bits) if not (step >> (bits - 1 - j)) & 1) for step in range(n_ctx)]


def last_kernel(n_ctx, n_tops, me_ref, low, low_got, high, high_got, *refs):
    tops = refs[:n_tops]
    away, stay, *top_out = refs[n_tops:]
    size, hd = low.shape
    rows_set = size // n_ctx
    half = n_ctx // 2
    for i, mask in enumerate(context_masks(n_ctx)):
        part = pl.ds(pl.multiple_of((me_ref[0] ^ mask) * rows_set, rows_set), rows_set)
        out, at = (away, i) if i < half else (stay, i - half)
        at = 2 * at * rows_set
        for mine, got in ((low, low_got), (high, high_got)):
            total = mine[part, :].astype(F32) + got[part, :].astype(F32)
            out[at : at + rows_set, :] = total.astype(BF16)
            at += rows_set
    if tops:
        top = largest(tops, low_got, size)
        top_out[0][...] = top
        away[half * 2 * rows_set :, :] = pack_top(top)
    else:
        away[half * 2 * rows_set :, :] = jnp.zeros((away.shape[0] - half * 2 * rows_set, hd), BF16)


def halve_kernel(n_tops, mine, got, *refs):
    tops = refs[:n_tops]
    away, stay, *top_out = refs[n_tops:]
    size = mine.shape[0]
    half = size // 2
    away[:half, :] = (mine[:half, :].astype(F32) + got[:half, :].astype(F32)).astype(BF16)
    stay[...] = (mine[half:, :].astype(F32) + got[half:size, :].astype(F32)).astype(stay.dtype)
    if tops:
        top = largest(tops, got, size)
        top_out[0][...] = top
        away[half:, :] = pack_top(top)
    else:
        away[half:, :] = jnp.zeros((away.shape[0] - half, away.shape[1]), BF16)


def final_kernel(columns, n_ctx, gain, me_dp_ref, me_ctx_ref, *refs):
    sets = len(columns)
    groups = [refs[2 * chosen : 2 * chosen + 2] for chosen in range(sets)]
    top_ref, out_ref, scale_ref, all_tops = refs[2 * sets :]
    rows_ctx, hd = groups[0][0].shape
    scale = jnp.maximum(top_ref[...], unpack_top(groups[0][1], rows_ctx)) + 1e-06
    all_tops[...] = scale
    blocks = rows_ctx // QROWS
    lanes = n_ctx * blocks
    per_row = TOP_LANES // lanes
    lane = lax.broadcasted_iota(jnp.int32, scale.shape, 1)
    group = jnp.where(lane < lanes, scale, 0.0)
    moved = [group] + [pltpu.roll(group, k * lanes, 1) for k in range(1, per_row)]
    for r in range(scale_ref.shape[0]):
        row = [moved[k][r * per_row + k : r * per_row + k + 1, :] for k in range(per_row)]
        scale_ref[r : r + 1, :] = functools.reduce(jnp.add, row)
    factors = gain / all_tops[pl.ds(me_dp_ref[0], 1), :]
    lane = lax.broadcasted_iota(jnp.int32, factors.shape, 1)
    for r in range(blocks):
        mine = jnp.where(lane == me_ctx_ref[0] * blocks + r, factors, 0.0)
        factor = jnp.sum(mine, axis=1, keepdims=True)
        part = slice(r * QROWS, (r + 1) * QROWS)
        for at, (mine_ref, got_ref) in zip(columns, groups):
            out_ref[part, at : at + hd] = (mine_ref[part, :] + got_ref[part, :].astype(F32)) * factor


def local(n_dp, n_ctx, span_order, queries, keys, values, out_grad, activations, error_feedback):
    rows, hd = keys.shape
    width = 2 * hd
    model = activations.shape[1]
    rows_ctx = model // (n_dp * n_ctx)
    tall = n_ctx * rows_ctx
    me_dp = lax.axis_index("dp").astype(jnp.int32)[None]
    me_ctx = lax.axis_index("context").astype(jnp.int32)[None]
    bits = n_dp.bit_length() - 1

    def swap_dp(x, mask):
        return lax.ppermute(x, "dp", xor_perm(n_dp, mask))

    def swap_ctx(x, mask):
        return lax.ppermute(x, "context", xor_perm(n_ctx, mask))

    own, key_parts, value_parts, key_blocks, score_grads, acts = attention(
        me_ctx, span_order[0], queries, out_grad, keys, values, activations, begin(me_dp, me_ctx), swap_ctx, n_ctx
    )

    shrink = 1.0 / (n_dp * n_ctx)
    acts = acts.reshape(n_dp, n_ctx, rows_ctx, rows)
    errors = error_feedback.reshape(n_dp, n_ctx, rows_ctx, width)
    tops = shape((TOP_ROWS, TOP_LANES), F32)
    steps = n_dp // 2
    cost = (0, 0)
    kept_shape, grad_shape = shape((steps, tall, hd), F32), shape((rows, hd))

    def tiles(kernel, name, operands, outs, after=()):
        return whole_call(kernel, name, [me_dp], [*operands, acts, errors], outs, 18, cost, [], after)

    sets = 2
    half = steps // 2 * (tall // 2)

    def split(last, kept, got, top):
        return whole_call(
            functools.partial(split_kernel, bits, n_ctx, int(last)),
            "split_tiles",
            [],
            [kept, got] + [top] * last,
            [shape((half + (1 if last else 2) * TOP_ROWS, hd))] + [shape((half, hd))] * 3 + [tops] * last,
            10,
            cost,
        )

    out, top, grads, value_grad = tiles(
        functools.partial(first_send_kernel, bits, shrink, hd, len(value_parts)),
        "send_tiles",
        [own, *value_parts],
        [shape((steps * tall + 2 * TOP_ROWS, hd)), tops, grad_shape, grad_shape],
    )
    got = swap_dp(out, 1)
    kept, top = tiles(
        functools.partial(next_kept_kernel, bits, shrink, hd), "kept_tiles", [grads, top], [kept_shape, tops]
    )
    halves = [split(False, kept, got, None)]
    kept, top, grads, key_grad = tiles(
        functools.partial(first_kept_kernel, bits, shrink, 0, len(key_parts)),
        "kept_tiles",
        [own, *key_parts, top],
        [kept_shape, tops, grad_shape, grad_shape],
    )
    out, top = tiles(
        functools.partial(next_send_kernel, bits, shrink, 0),
        "send_tiles",
        [grads, top],
        [shape((steps * tall + TOP_ROWS, hd)), tops],
    )
    arrays = split(True, kept, swap_dp(out, 1), top)
    halves.append(arrays[:4])
    gathered = [arrays[4]]
    query_grad, mark = query_gradients(key_blocks, score_grads, queries.shape[1], [arrays[1]])
    groups = []
    for chosen in range(sets):
        low_away, low, high_away, high = halves[chosen]
        extra = TOP_ROWS if chosen == sets - 1 else 0
        tail = extra or 2 * TOP_ROWS
        for stage in range(1, bits):
            low_got = swap_dp(low_away, 1 << stage)
            high_got = swap_dp(high_away, 1 << (bits - stage))
            with_tops = extra > 0
            operands = [low, low_got, high, high_got] + (gathered if with_tops else [])
            n_tops = len(operands) - 4
            size = low.shape[0]
            if stage < bits - 1:
                low_away, low, high_away, high, *top_out = whole_call(
                    functools.partial(add_kernel, n_tops),
                    "add_stage",
                    [],
                    operands,
                    [shape((size // 2 + tail, hd))] + [shape((size // 2, hd))] * 3 + [tops] * with_tops,
                    8,
                    cost,
                    after=[mark] if chosen == 0 and stage == 1 else [],
                )
            else:
                chunk = rows_ctx
                away, stay, *top_out = whole_call(
                    functools.partial(last_kernel, n_ctx, n_tops),
                    "last_stage",
                    [me_ctx],
                    operands,
                    [shape((n_ctx // 2 * chunk + tail, hd)), shape((n_ctx // 2 * chunk, hd))] + [tops] * with_tops,
                    8,
                    cost,
                )
            if with_tops:
                gathered = list(top_out)
        mask = 1
        while mask < n_ctx // 2:
            size = stay.shape[0]
            away, stay, *top_out = whole_call(
                functools.partial(halve_kernel, int(with_tops)),
                "halve_context",
                [],
                [stay, swap_ctx(away, mask)] + (gathered if with_tops else []),
                [shape((size // 2 + tail, hd)), shape((size // 2, hd), F32 if size == 2 * chunk else BF16)]
                + [tops] * with_tops,
                8,
                (0, 0),
            )
            if with_tops:
                gathered = list(top_out)
            mask *= 2
        groups = [stay, swap_ctx(away, mask), *groups]
    payload, scale = whole_call(
        functools.partial(final_kernel, (0, hd), n_ctx, 7.0 / shrink),
        "final_stage",
        [me_dp, me_ctx],
        groups + gathered,
        [shape((rows_ctx, width), F32), shape((model // QROWS // TOP_LANES, TOP_LANES), F32)],
        8,
        (0, 0),
        [pltpu.VMEM((TOP_ROWS, TOP_LANES), F32)],
    )
    return query_grad, key_grad, value_grad, payload, scale.reshape(-1)


def solution(mesh):
    tokens = P(("dp", "context"), None)
    return jax.shard_map(
        functools.partial(local, mesh.shape["dp"], mesh.shape["context"]),
        mesh=mesh,
        in_specs=(P("dp", None), tokens, tokens, tokens, tokens, tokens, P("dp", "context", None, None)),
        out_specs=(tokens, tokens, tokens, tokens, P()),
        check_vma=False,
    )
```

```python
import functools

import jax
import jax.numpy as jnp
from jax import lax
from jax.experimental import pallas as pl
from jax.experimental.pallas import tpu as pltpu
from jax.sharding import PartitionSpec as P

QROWS = 32
LOG2E = 1.4426950408889634
FAR = 1e30
MIB = 1024 * 1024
CHUNK = 256
TOP_ROWS, TOP_LANES, PACK_LANES = 16, 128, 32
BF16, F32 = jnp.bfloat16, jnp.float32
BF16_MAX = float(jnp.finfo(jnp.bfloat16).max)
NT = (((1,), (1,)), ((), ()))
TN = (((0,), (0,)), ((), ()))


def xor_perm(size, mask):
    return [(i, i ^ mask) for i in range(size)]


def whole(x):
    return pl.BlockSpec(x.shape, lambda *_: (0,) * len(x.shape))


def shape(dims, dtype=BF16):
    return jax.ShapeDtypeStruct(dims, dtype)


def whole_call(kernel, name, scalars, operands, out_shape, mib, cost, scratch=(), after=()):
    def body(*refs):
        first = len(scalars) + len(operands)
        kernel(*refs[:first], *refs[first + len(after) :])

    return pl.pallas_call(
        body,
        grid_spec=pltpu.PrefetchScalarGridSpec(
            num_scalar_prefetch=len(scalars),
            grid=(1,),
            in_specs=[whole(x) for x in operands] + [pl.BlockSpec(memory_space=pl.ANY)] * len(after),
            out_specs=[whole(x) for x in out_shape],
            scratch_shapes=list(scratch),
        ),
        out_shape=out_shape,
        compiler_params=pltpu.CompilerParams(vmem_limit_bytes=mib * MIB),
        cost_estimate=pl.CostEstimate(flops=cost[0], bytes_accessed=cost[1], transcendentals=0),
        name=name,
    )(*scalars, *operands, *after)


def begin_kernel(me_dp_ref, me_ctx_ref, out_ref):
    out_ref[...] = jnp.zeros_like(out_ref)


def begin(me_dp, me_ctx):
    mark = [shape((8, 128), F32)]
    return whole_call(begin_kernel, "begin", [me_dp, me_ctx], [], mark, 4, (20_000_000_000, 0))[0]


def prepare_kernel(pieces, a_ref, a_out):
    tile = a_ref.shape[1] // pieces
    for i in range(pieces):
        a_out[i * tile : (i + 1) * tile, :] = a_ref[:, i * tile : (i + 1) * tile].T


def prepare(activations, after):
    rows, model = activations.shape
    outs = [shape((model, rows))]
    cost = (0, 0)
    kernel = functools.partial(prepare_kernel, 8)
    return whole_call(kernel, "prepare", [], [activations], outs, 16, cost, [], after)[0]


def head_pair(ref, i, hd):
    at = i * (2 * hd)
    first = ref[:, pl.ds(pl.multiple_of(at, hd), hd)]
    second = ref[:, pl.ds(pl.multiple_of(at + hd, hd), hd)]
    return jnp.concatenate([first, second], axis=0)


def score_chunk(k, v, q, do, own, first_lane):
    s = lax.dot_general(k, q, NT, preferred_element_type=F32)
    dp = lax.dot_general(v, do, NT, preferred_element_type=F32)
    if own:
        rows = k.shape[0]
        key_at = lax.broadcasted_iota(jnp.int32, s.shape, 0)
        query_at = lax.broadcasted_iota(jnp.int32, s.shape, 1) + first_lane
        query_at = jnp.where(query_at >= rows, query_at - rows, query_at)
        s = jnp.where(key_at <= query_at, s, -FAR)
    return s, dp


def counted(b, flags):
    lane = lax.broadcasted_iota(jnp.int32, flags.shape, 1)
    return jnp.max(jnp.where(lane == b, flags[...], 0.0)) > 0.5


def stats_of_block(b, q_ref, do_ref, k_ref, v_ref, before, out, held=None):
    k, v = k_ref[...], v_ref[...]
    rows, hd = k.shape
    pair = 2 * rows
    factor = LOG2E / hd**0.5

    def heads(i, carry):
        q, do = head_pair(q_ref, i, hd), head_pair(do_ref, i, hd)
        for t in range(pair // CHUNK):
            part = slice(t * CHUNK, (t + 1) * CHUNK)
            lanes = pl.ds(pl.multiple_of(i * pair + t * CHUNK, CHUNK), CHUNK)
            s, dp = score_chunk(k, v, q[part], do[part], b == 0, t * CHUNK)
            if held:
                held[0][:, lanes] = s
                held[1][:, lanes] = dp
            top = jnp.max(s, axis=0, keepdims=True) * factor
            e = jnp.exp2(s * factor - top)
            total = jnp.sum(e, axis=0, keepdims=True)
            weighted = jnp.sum(e * dp, axis=0, keepdims=True)
            if b > 0:
                old = before[0:1, lanes]
                both = jnp.maximum(old, top)
                old_part, new_part = jnp.exp2(old - both), jnp.exp2(top - both)
                total = before[1:2, lanes] * old_part + total * new_part
                weighted = before[2:3, lanes] * old_part + weighted * new_part
                top = both
            out[0:1, lanes] = top
            out[1:2, lanes] = total
            out[2:3, lanes] = weighted
        return carry

    lax.fori_loop(0, q_ref.shape[1] // (2 * hd), heads, 0, unroll=True)


def first_stats_kernel(n, me_ref, span_ref, q_ref, do_ref, k_ref, v_ref, out, q_out, do_out, k_out, v_out, flags):
    me = me_ref[0]
    lane = lax.broadcasted_iota(jnp.int32, flags.shape, 1)
    found = jnp.zeros(flags.shape, F32)
    for b in range(1, n):
        found = jnp.where((lane == b) & (span_ref[me ^ b] < span_ref[me]), 1.0, found)
    flags[...] = found
    q_out[...] = q_ref[...]
    do_out[...] = do_ref[...]
    k_out[...] = k_ref[...]
    v_out[...] = v_ref[...]
    stats_of_block(0, q_ref, do_ref, k_ref, v_ref, None, out)


def next_stats_kernel(b, flags, q_ref, do_ref, k_ref, v_ref, before, out):
    keep = counted(b, flags)

    @pl.when(keep)
    def _():
        stats_of_block(b, q_ref, do_ref, k_ref, v_ref, before, out)

    @pl.when(jnp.logical_not(keep))
    def _():
        out[...] = before[...]


def block_gradients(own, stats, q_ref, do_ref, k_ref, v_ref, p_buf, ds_ref, dk, dv, held=None):
    k, v = k_ref[...], v_ref[...]
    rows, hd = k.shape
    pair = 2 * rows
    factor = LOG2E / hd**0.5
    dk[...] = jnp.zeros_like(dk)
    dv[...] = jnp.zeros_like(dv)

    def heads(i, carry):
        q, do = head_pair(q_ref, i, hd), head_pair(do_ref, i, hd)
        for t in range(pair // CHUNK):
            part = slice(t * CHUNK, (t + 1) * CHUNK)
            lanes = pl.ds(pl.multiple_of(i * pair + t * CHUNK, CHUNK), CHUNK)
            if held:
                s, dp = held[0][:, lanes], held[1][:, lanes]
            else:
                s, dp = score_chunk(k, v, q[part], do[part], own, t * CHUNK)
            total = stats[1:2, lanes]
            level = stats[0:1, lanes] + jnp.log(total) * LOG2E
            p = jnp.exp2(s * factor - level)
            p_buf[:, part] = p.astype(BF16)
            ds = (p * (dp - stats[2:3, lanes] / total)).astype(BF16)
            ds_ref[:, lanes] = ds
        ds = ds_ref[:, pl.ds(pl.multiple_of(i * pair, CHUNK), pair)]
        dk[...] += jnp.dot(ds, q, preferred_element_type=F32)
        dv[...] += jnp.dot(p_buf[...], do, preferred_element_type=F32)
        return carry

    lax.fori_loop(0, q_ref.shape[1] // (2 * hd), heads, 0, unroll=True)
    inverse = 1.0 / hd**0.5
    return dk[...] * inverse, dv[...]


def other_kernel(b, flags, stats, q_ref, do_ref, k_ref, v_ref, dk_out, dv_out, ds_out, *refs):
    *refs, p_buf, dk, dv = refs
    keep = counted(b, flags)
    rows = dk.shape[0]
    held, before = None, stats
    if refs:
        stats, *held = refs

    @pl.when(keep)
    def _():
        if held:
            stats_of_block(b, q_ref, do_ref, k_ref, v_ref, before, stats, held)
        dk_sum, dv_sum = block_gradients(False, stats, q_ref, do_ref, k_ref, v_ref, p_buf, ds_out, dk, dv, held)
        dk_out[...] = dk_sum.astype(BF16)
        dv_out[:rows, :] = dv_sum.astype(BF16)
        dv_out[rows:, :] = jnp.zeros((dv_out.shape[0] - rows, dv.shape[1]), BF16)

    @pl.when(jnp.logical_not(keep))
    def _():
        if held:
            stats[...] = before[...]
        dk_out[...] = jnp.zeros_like(dk_out)
        dv_out[...] = jnp.zeros_like(dv_out)
        ds_out[...] = jnp.zeros_like(ds_out)


def own_kernel(stats, q_ref, do_ref, k_ref, v_ref, out_ref, ds_out, p_buf, dk, dv):
    hd = dk.shape[1]
    dk_sum, dv_sum = block_gradients(True, stats, q_ref, do_ref, k_ref, v_ref, p_buf, ds_out, dk, dv)
    out_ref[:, :hd] = dk_sum
    out_ref[:, hd:] = dv_sum


def query_kernel(n, *refs):
    k_refs, ds_refs, dq_ref, mark_ref = refs[:n], refs[n : 2 * n], refs[2 * n], refs[2 * n + 1]
    mark_ref[...] = jnp.zeros_like(mark_ref)
    rows, hd = k_refs[0].shape
    for h in range(dq_ref.shape[1] // hd):
        dq = 0.0
        for k, ds in zip(k_refs, ds_refs):
            part = ds[:, h * rows : (h + 1) * rows]
            dq = dq + lax.dot_general(part, k[...], TN, preferred_element_type=F32)
        dq_ref[:, h * hd : (h + 1) * hd] = (dq / hd**0.5).astype(BF16)


def merge_kernel(rows, *refs):
    *terms, out_ref = refs
    total = functools.reduce(jnp.add, [term[:rows, :].astype(F32) for term in terms])
    out_ref[:rows, :] = total.astype(BF16)
    if out_ref.shape[0] > rows:
        out_ref[rows:, :] = jnp.zeros((out_ref.shape[0] - rows, out_ref.shape[1]), BF16)


def merge(rows, terms, after):
    outs = [shape(terms[0].shape)]
    return whole_call(functools.partial(merge_kernel, rows), "merge", [], terms, outs, 4, (0, 0), [], after)[0]


def attention(me, spans, queries, out_grad, keys, values, activations, mark, swap, n):
    rows, hd = keys.shape
    columns = queries.shape[1]
    tall = columns // hd * rows
    product = 2 * rows * tall * hd
    cost = (8 * product, 8 * rows * columns)

    direct = [b for b in range(1, n) if b & (b - 1) == 0]
    blocks = {b: [swap(keys, b), swap(values, b)] for b in reversed(direct)}
    stats_shape = shape((8, tall), F32)
    stats, queries, out_grad, keys, values, flags = whole_call(
        functools.partial(first_stats_kernel, n),
        "first_stats",
        [me, spans],
        [queries, out_grad, keys, values],
        [stats_shape] + [shape(x.shape) for x in (queries, out_grad, keys, values)] + [shape((8, 128), F32)],
        12,
        cost,
        [],
        [mark],
    )
    blocks[0] = [keys, values]
    acts = prepare(activations, [stats])
    for b in range(1, n):
        if b not in blocks:
            blocks[b] = [swap(x, b & -b) for x in blocks[b & (b - 1)]]
        if b == n - 1:
            break
        stats = whole_call(
            functools.partial(next_stats_kernel, b),
            "next_stats",
            [],
            [flags, queries, out_grad, *blocks[b], stats],
            [stats_shape],
            10,
            cost,
            [],
            [*blocks[2], acts] if b == 1 else [],
        )[0]
    p_buf = pltpu.VMEM((rows, 2 * rows), BF16)
    sums = [pltpu.VMEM((rows, hd), F32)] * 2
    key_parts, value_parts = [[] for _ in range(n)], [[] for _ in range(n)]
    score_grads, own_parts, before = [None] * n, {}, []
    for b in range(n - 1, 0, -1):
        last = b == n - 1
        held = pltpu.VMEM((rows, tall), F32)
        dk, dv, score_grads[b], *total = whole_call(
            functools.partial(other_kernel, b),
            "block_gradients",
            [],
            [flags, stats, queries, out_grad, *blocks[b]],
            [shape((rows, hd)), shape((rows + TOP_ROWS, hd)), shape((rows, tall))] + [stats_shape] * last,
            20 if last else 10,
            (0, 0),
            [held, held] * last + [p_buf, *sums],
            before,
        )
        if last:
            stats = total[0]
        if value_parts[b]:
            dv = merge(rows, [dv, *value_parts[b]], [])
        value_parts[b & (b - 1)].append(swap(dv, b & -b))
        own_parts[b] = dk
        before = [dv]
    for b in range(n - 1, 0, -1):
        dk = own_parts[b]
        if key_parts[b]:
            dk = merge(rows, [dk, *key_parts[b]], before)
        key_parts[b & (b - 1)].append(swap(dk, b & -b))
    own, score_grads[0] = whole_call(
        own_kernel,
        "own_gradients",
        [],
        [stats, queries, out_grad, keys, values],
        [shape((rows, 2 * hd), F32), shape((rows, tall))],
        10,
        (0, 0),
        [p_buf, *sums],
        before,
    )
    return own, key_parts[0], value_parts[0], [blocks[b][0] for b in range(n)], score_grads, acts


def query_gradients(key_blocks, score_grads, columns, after):
    n = len(key_blocks)
    rows = key_blocks[0].shape[0]
    return whole_call(
        functools.partial(query_kernel, n),
        "query_gradients",
        [],
        [*key_blocks, *score_grads],
        [shape((rows, columns)), shape((8, 128), F32)],
        2 + 3 * n,
        (2 * n * rows * rows * columns, 16 * rows * columns),
        [],
        after,
    )


def pack_top(top):
    high = jnp.minimum(top, BF16_MAX).astype(BF16).astype(F32)
    rest = top - high
    middle = rest.astype(BF16).astype(F32)
    low = rest - middle
    return (high + pltpu.roll(middle, PACK_LANES, 1) + pltpu.roll(low, 2 * PACK_LANES, 1)).astype(BF16)


def unpack_top(ref, at):
    x = ref[at : at + TOP_ROWS, :TOP_LANES].astype(F32)
    total = x + (pltpu.roll(x, TOP_LANES - PACK_LANES, 1) + pltpu.roll(x, TOP_LANES - 2 * PACK_LANES, 1))
    lane = lax.broadcasted_iota(jnp.int32, x.shape, 1)
    return jnp.where(lane < PACK_LANES, total, 0.0)


def tile_of(step, me_dp, bits, flip):
    mask = flip
    for j in range(1, bits):
        if not (step >> (bits - 1 - j)) & 1:
            mask |= 1 << j
    return me_dp ^ mask


def reversed_step(step, bits):
    return sum(((step >> (bits - 1 - j)) & 1) << (j - 1) for j in range(1, bits))


def corrected_tile(at, dest, grads, a_ref, e_ref, top_ref):
    _, n_ctx, rows_ctx, rows = a_ref.shape
    tall = n_ctx * rows_ctx
    hd = grads.shape[1]
    a = a_ref[dest].reshape(tall, rows)
    e = e_ref[dest, :, :, at : at + hd].reshape(tall, hd)
    c = jnp.dot(a, grads, preferred_element_type=F32) + e
    mags = jnp.max(jnp.abs(c).reshape(tall // QROWS, QROWS, hd), axis=1)
    mags = jnp.max(mags, axis=1, keepdims=True)
    block = lax.broadcasted_iota(jnp.int32, (tall // QROWS, TOP_LANES), 0)
    lane = lax.broadcasted_iota(jnp.int32, (tall // QROWS, TOP_LANES), 1)
    top = jnp.max(jnp.where(lane == block, mags, 0.0), axis=0, keepdims=True)
    top_ref[pl.ds(dest, 1), :] = jnp.maximum(top_ref[pl.ds(dest, 1), :], top)
    return c


def summed_grads(at, own_ref, part_refs):
    rows, hd = own_ref.shape[0], own_ref.shape[1] // 2
    total = own_ref[:, at : at + hd]
    for part in part_refs:
        total = total + part[:rows, :].astype(F32)
    return total.astype(BF16)


def send_rows(bits, shrink, at, me_ref, total, a_ref, e_ref, out_ref, top_ref, packed):
    tall = a_ref.shape[1] * a_ref.shape[2]
    steps = a_ref.shape[0] // 2
    for step in range(steps):
        dest = tile_of(step, me_ref[0], bits, 1)
        c = corrected_tile(at, dest, total, a_ref, e_ref, top_ref)
        out_ref[step * tall : (step + 1) * tall, :] = (c * shrink).astype(BF16)
    tail = jnp.zeros((out_ref.shape[0] - steps * tall, out_ref.shape[1]), BF16)
    out_ref[steps * tall :, :] = pack_top(top_ref[...]) if packed else tail


def kept_rows(bits, shrink, at, me_ref, total, a_ref, e_ref, out_ref, top_ref):
    for step in range(out_ref.shape[0]):
        dest = tile_of(step, me_ref[0], bits, 0)
        out_ref[step] = corrected_tile(at, dest, total, a_ref, e_ref, top_ref) * shrink


def first_send_kernel(bits, shrink, at, n_parts, me_ref, own_ref, *refs):
    a_ref, e_ref, out_ref, top_ref, grads_ref, grads_out = refs[n_parts:]
    total = summed_grads(at, own_ref, refs[:n_parts])
    grads_ref[...] = total
    grads_out[...] = total
    top_ref[...] = jnp.zeros_like(top_ref)
    send_rows(bits, shrink, at, me_ref, total, a_ref, e_ref, out_ref, top_ref, False)


def next_kept_kernel(bits, shrink, at, me_ref, grads_ref, before_ref, a_ref, e_ref, out_ref, top_ref):
    top_ref[...] = before_ref[...]
    kept_rows(bits, shrink, at, me_ref, grads_ref[...], a_ref, e_ref, out_ref, top_ref)


def first_kept_kernel(bits, shrink, at, n_parts, me_ref, own_ref, *refs):
    before_ref, a_ref, e_ref, out_ref, top_ref, grads_ref, grads_out = refs[n_parts:]
    total = summed_grads(at, own_ref, refs[:n_parts])
    grads_ref[...] = total
    grads_out[...] = total
    top_ref[...] = before_ref[...]
    kept_rows(bits, shrink, at, me_ref, total, a_ref, e_ref, out_ref, top_ref)


def next_send_kernel(bits, shrink, at, me_ref, grads_ref, before_ref, a_ref, e_ref, out_ref, top_ref):
    top_ref[...] = before_ref[...]
    send_rows(bits, shrink, at, me_ref, grads_ref[...], a_ref, e_ref, out_ref, top_ref, True)


def split_kernel(bits, n_ctx, n_tops, kept, got, *refs):
    steps, tall, hd = kept.shape
    half = steps // 2
    part_tall = tall // 2
    tops = refs[:n_tops]
    low_away, low_stay, high_away, high_stay, *top_out = refs[n_tops:]
    for step in range(steps):
        c = (kept[step] + got[step * tall : (step + 1) * tall, :].astype(F32)).astype(BF16)
        c = c.reshape(n_ctx, 2, part_tall // n_ctx, hd)
        back = reversed_step(step, bits)
        for at, i, away, stay in ((step, 0, low_away, low_stay), (back, 1, high_away, high_stay)):
            part = c[:, i].reshape(part_tall, hd)
            if at < half:
                away[at * part_tall : (at + 1) * part_tall, :] = part
            else:
                stay[(at - half) * part_tall : (at - half + 1) * part_tall, :] = part
    if tops:
        top = largest(tops, got, steps * tall)
        top_out[0][...] = top
        low_away[half * part_tall :, :] = pack_top(top)
    else:
        low_away[half * part_tall :, :] = jnp.zeros((low_away.shape[0] - half * part_tall, hd), BF16)


def largest(tops, low_got, size):
    found = [top[...] for top in tops]
    if low_got.shape[0] > size:
        found.append(unpack_top(low_got, size))
    return functools.reduce(jnp.maximum, found)


def add_kernel(n_tops, low, low_got, high, high_got, *refs):
    tops = refs[:n_tops]
    low_away, low_stay, high_away, high_stay, *top_out = refs[n_tops:]
    size = low.shape[0]
    half = size // 2
    for mine, got, away, stay in ((low, low_got, low_away, low_stay), (high, high_got, high_away, high_stay)):
        away[:half, :] = (mine[:half, :].astype(F32) + got[:half, :].astype(F32)).astype(BF16)
        stay[...] = (mine[half:, :].astype(F32) + got[half:size, :].astype(F32)).astype(BF16)
    if tops:
        top = largest(tops, low_got, size)
        top_out[0][...] = top
        low_away[half:, :] = pack_top(top)
    else:
        low_away[half:, :] = jnp.zeros((low_away.shape[0] - half, low_away.shape[1]), BF16)


def context_masks(n_ctx):
    bits = n_ctx.bit_length() - 1
    return [sum((1 << j) for j in range(bits) if not (step >> (bits - 1 - j)) & 1) for step in range(n_ctx)]


def last_kernel(n_ctx, n_tops, me_ref, low, low_got, high, high_got, *refs):
    tops = refs[:n_tops]
    away, stay, *top_out = refs[n_tops:]
    size, hd = low.shape
    rows_set = size // n_ctx
    half = n_ctx // 2
    for i, mask in enumerate(context_masks(n_ctx)):
        part = pl.ds(pl.multiple_of((me_ref[0] ^ mask) * rows_set, rows_set), rows_set)
        out, at = (away, i) if i < half else (stay, i - half)
        at = 2 * at * rows_set
        for mine, got in ((low, low_got), (high, high_got)):
            total = mine[part, :].astype(F32) + got[part, :].astype(F32)
            out[at : at + rows_set, :] = total.astype(BF16)
            at += rows_set
    if tops:
        top = largest(tops, low_got, size)
        top_out[0][...] = top
        away[half * 2 * rows_set :, :] = pack_top(top)
    else:
        away[half * 2 * rows_set :, :] = jnp.zeros((away.shape[0] - half * 2 * rows_set, hd), BF16)


def halve_kernel(n_tops, mine, got, *refs):
    tops = refs[:n_tops]
    away, stay, *top_out = refs[n_tops:]
    size = mine.shape[0]
    half = size // 2
    away[:half, :] = (mine[:half, :].astype(F32) + got[:half, :].astype(F32)).astype(BF16)
    stay[...] = (mine[half:, :].astype(F32) + got[half:size, :].astype(F32)).astype(stay.dtype)
    if tops:
        top = largest(tops, got, size)
        top_out[0][...] = top
        away[half:, :] = pack_top(top)
    else:
        away[half:, :] = jnp.zeros((away.shape[0] - half, away.shape[1]), BF16)


def final_kernel(columns, n_ctx, gain, me_dp_ref, me_ctx_ref, *refs):
    sets = len(columns)
    groups = [refs[2 * chosen : 2 * chosen + 2] for chosen in range(sets)]
    top_ref, out_ref, scale_ref, all_tops = refs[2 * sets :]
    rows_ctx, hd = groups[0][0].shape
    scale = jnp.maximum(top_ref[...], unpack_top(groups[0][1], rows_ctx)) + 1e-06
    all_tops[...] = scale
    blocks = rows_ctx // QROWS
    lanes = n_ctx * blocks
    per_row = TOP_LANES // lanes
    lane = lax.broadcasted_iota(jnp.int32, scale.shape, 1)
    group = jnp.where(lane < lanes, scale, 0.0)
    moved = [group] + [pltpu.roll(group, k * lanes, 1) for k in range(1, per_row)]
    for r in range(scale_ref.shape[0]):
        row = [moved[k][r * per_row + k : r * per_row + k + 1, :] for k in range(per_row)]
        scale_ref[r : r + 1, :] = functools.reduce(jnp.add, row)
    factors = gain / all_tops[pl.ds(me_dp_ref[0], 1), :]
    lane = lax.broadcasted_iota(jnp.int32, factors.shape, 1)
    for r in range(blocks):
        mine = jnp.where(lane == me_ctx_ref[0] * blocks + r, factors, 0.0)
        factor = jnp.sum(mine, axis=1, keepdims=True)
        part = slice(r * QROWS, (r + 1) * QROWS)
        for at, (mine_ref, got_ref) in zip(columns, groups):
            out_ref[part, at : at + hd] = (mine_ref[part, :] + got_ref[part, :].astype(F32)) * factor


def local(n_dp, n_ctx, span_order, queries, keys, values, out_grad, activations, error_feedback):
    rows, hd = keys.shape
    width = 2 * hd
    model = activations.shape[1]
    rows_ctx = model // (n_dp * n_ctx)
    tall = n_ctx * rows_ctx
    me_dp = lax.axis_index("dp").astype(jnp.int32)[None]
    me_ctx = lax.axis_index("context").astype(jnp.int32)[None]
    bits = n_dp.bit_length() - 1

    def swap_dp(x, mask):
        return lax.ppermute(x, "dp", xor_perm(n_dp, mask))

    def swap_ctx(x, mask):
        return lax.ppermute(x, "context", xor_perm(n_ctx, mask))

    own, key_parts, value_parts, key_blocks, score_grads, acts = attention(
        me_ctx, span_order[0], queries, out_grad, keys, values, activations, begin(me_dp, me_ctx), swap_ctx, n_ctx
    )

    shrink = 1.0 / (n_dp * n_ctx)
    acts = acts.reshape(n_dp, n_ctx, rows_ctx, rows)
    errors = error_feedback.reshape(n_dp, n_ctx, rows_ctx, width)
    tops = shape((TOP_ROWS, TOP_LANES), F32)
    steps = n_dp // 2
    cost = (0, 0)
    kept_shape, grad_shape = shape((steps, tall, hd), F32), shape((rows, hd))

    def tiles(kernel, name, operands, outs, after=()):
        return whole_call(kernel, name, [me_dp], [*operands, acts, errors], outs, 18, cost, [], after)

    sets = 2
    half = steps // 2 * (tall // 2)

    def split(last, kept, got, top):
        return whole_call(
            functools.partial(split_kernel, bits, n_ctx, int(last)),
            "split_tiles",
            [],
            [kept, got] + [top] * last,
            [shape((half + (1 if last else 2) * TOP_ROWS, hd))] + [shape((half, hd))] * 3 + [tops] * last,
            10,
            cost,
        )

    out, top, grads, value_grad = tiles(
        functools.partial(first_send_kernel, bits, shrink, hd, len(value_parts)),
        "send_tiles",
        [own, *value_parts],
        [shape((steps * tall + 2 * TOP_ROWS, hd)), tops, grad_shape, grad_shape],
    )
    got = swap_dp(out, 1)
    kept, top = tiles(
        functools.partial(next_kept_kernel, bits, shrink, hd), "kept_tiles", [grads, top], [kept_shape, tops]
    )
    halves = [split(False, kept, got, None)]
    kept, top, grads, key_grad = tiles(
        functools.partial(first_kept_kernel, bits, shrink, 0, len(key_parts)),
        "kept_tiles",
        [own, *key_parts, top],
        [kept_shape, tops, grad_shape, grad_shape],
    )
    out, top = tiles(
        functools.partial(next_send_kernel, bits, shrink, 0),
        "send_tiles",
        [grads, top],
        [shape((steps * tall + TOP_ROWS, hd)), tops],
    )
    arrays = split(True, kept, swap_dp(out, 1), top)
    halves.append(arrays[:4])
    gathered = [arrays[4]]
    query_grad, mark = query_gradients(key_blocks, score_grads, queries.shape[1], [arrays[1]])
    groups = []
    for chosen in range(sets):
        low_away, low, high_away, high = halves[chosen]
        extra = TOP_ROWS if chosen == sets - 1 else 0
        tail = extra or 2 * TOP_ROWS
        for stage in range(1, bits):
            low_got = swap_dp(low_away, 1 << stage)
            high_got = swap_dp(high_away, 1 << (bits - stage))
            with_tops = extra > 0
            operands = [low, low_got, high, high_got] + (gathered if with_tops else [])
            n_tops = len(operands) - 4
            size = low.shape[0]
            if stage < bits - 1:
                low_away, low, high_away, high, *top_out = whole_call(
                    functools.partial(add_kernel, n_tops),
                    "add_stage",
                    [],
                    operands,
                    [shape((size // 2 + tail, hd))] + [shape((size // 2, hd))] * 3 + [tops] * with_tops,
                    8,
                    cost,
                    after=[mark] if chosen == 0 and stage == 1 else [],
                )
            else:
                chunk = rows_ctx
                away, stay, *top_out = whole_call(
                    functools.partial(last_kernel, n_ctx, n_tops),
                    "last_stage",
                    [me_ctx],
                    operands,
                    [shape((n_ctx // 2 * chunk + tail, hd)), shape((n_ctx // 2 * chunk, hd))] + [tops] * with_tops,
                    8,
                    cost,
                )
            if with_tops:
                gathered = list(top_out)
        mask = 1
        while mask < n_ctx // 2:
            size = stay.shape[0]
            away, stay, *top_out = whole_call(
                functools.partial(halve_kernel, int(with_tops)),
                "halve_context",
                [],
                [stay, swap_ctx(away, mask)] + (gathered if with_tops else []),
                [shape((size // 2 + tail, hd)), shape((size // 2, hd), F32 if size == 2 * chunk else BF16)]
                + [tops] * with_tops,
                8,
                (0, 0),
            )
            if with_tops:
                gathered = list(top_out)
            mask *= 2
        groups = [stay, swap_ctx(away, mask), *groups]
    payload, scale = whole_call(
        functools.partial(final_kernel, (0, hd), n_ctx, 7.0 / shrink),
        "final_stage",
        [me_dp, me_ctx],
        groups + gathered,
        [shape((rows_ctx, width), F32), shape((model // QROWS // TOP_LANES, TOP_LANES), F32)],
        8,
        (0, 0),
        [pltpu.VMEM((TOP_ROWS, TOP_LANES), F32)],
    )
    return query_grad, key_grad, value_grad, payload, scale.reshape(-1)


def solution(mesh):
    tokens = P(("dp", "context"), None)
    return jax.shard_map(
        functools.partial(local, mesh.shape["dp"], mesh.shape["context"]),
        mesh=mesh,
        in_specs=(P("dp", None), tokens, tokens, tokens, tokens, tokens, P("dp", "context", None, None)),
        out_specs=(tokens, tokens, tokens, tokens, P()),
        check_vma=False,
    )
```

```python
import functools

import jax
import jax.numpy as jnp
from jax import lax
from jax.experimental import pallas as pl
from jax.experimental.pallas import tpu as pltpu
from jax.sharding import PartitionSpec as P

QROWS = 32
LOG2E = 1.4426950408889634
FAR = 1e30
MIB = 1024 * 1024
CHUNK = 256
TOP_ROWS, TOP_LANES, PACK_LANES = 16, 128, 32
BF16, F32 = jnp.bfloat16, jnp.float32
BF16_MAX = float(jnp.finfo(jnp.bfloat16).max)
NT = (((1,), (1,)), ((), ()))
TN = (((0,), (0,)), ((), ()))


def xor_perm(size, mask):
    return [(i, i ^ mask) for i in range(size)]


def whole(x):
    return pl.BlockSpec(x.shape, lambda *_: (0,) * len(x.shape))


def shape(dims, dtype=BF16):
    return jax.ShapeDtypeStruct(dims, dtype)


def whole_call(kernel, name, scalars, operands, out_shape, mib, cost, scratch=(), after=()):
    def body(*refs):
        first = len(scalars) + len(operands)
        kernel(*refs[:first], *refs[first + len(after) :])

    return pl.pallas_call(
        body,
        grid_spec=pltpu.PrefetchScalarGridSpec(
            num_scalar_prefetch=len(scalars),
            grid=(1,),
            in_specs=[whole(x) for x in operands] + [pl.BlockSpec(memory_space=pl.ANY)] * len(after),
            out_specs=[whole(x) for x in out_shape],
            scratch_shapes=list(scratch),
        ),
        out_shape=out_shape,
        compiler_params=pltpu.CompilerParams(vmem_limit_bytes=mib * MIB),
        cost_estimate=pl.CostEstimate(flops=cost[0], bytes_accessed=cost[1], transcendentals=0),
        name=name,
    )(*scalars, *operands, *after)


def begin_kernel(me_dp_ref, me_ctx_ref, out_ref):
    out_ref[...] = jnp.zeros_like(out_ref)


def begin(me_dp, me_ctx):
    mark = [shape((8, 128), F32)]
    return whole_call(begin_kernel, "begin", [me_dp, me_ctx], [], mark, 4, (20_000_000_000, 0))[0]


def prepare_kernel(pieces, a_ref, a_out):
    tile = a_ref.shape[1] // pieces
    for i in range(pieces):
        a_out[i * tile : (i + 1) * tile, :] = a_ref[:, i * tile : (i + 1) * tile].T


def prepare(activations, after):
    rows, model = activations.shape
    outs = [shape((model, rows))]
    cost = (0, 0)
    kernel = functools.partial(prepare_kernel, 8)
    return whole_call(kernel, "prepare", [], [activations], outs, 16, cost, [], after)[0]


def head_pair(ref, i, hd):
    at = i * (2 * hd)
    first = ref[:, pl.ds(pl.multiple_of(at, hd), hd)]
    second = ref[:, pl.ds(pl.multiple_of(at + hd, hd), hd)]
    return jnp.concatenate([first, second], axis=0)


def score_chunk(k, v, q, do, own, first_lane):
    s = lax.dot_general(k, q, NT, preferred_element_type=F32)
    dp = lax.dot_general(v, do, NT, preferred_element_type=F32)
    if own:
        rows = k.shape[0]
        key_at = lax.broadcasted_iota(jnp.int32, s.shape, 0)
        query_at = lax.broadcasted_iota(jnp.int32, s.shape, 1) + first_lane
        query_at = jnp.where(query_at >= rows, query_at - rows, query_at)
        s = jnp.where(key_at <= query_at, s, -FAR)
    return s, dp


def counted(b, flags):
    lane = lax.broadcasted_iota(jnp.int32, flags.shape, 1)
    return jnp.max(jnp.where(lane == b, flags[...], 0.0)) > 0.5


def stats_of_block(b, q_ref, do_ref, k_ref, v_ref, before, out, held=None):
    k, v = k_ref[...], v_ref[...]
    rows, hd = k.shape
    pair = 2 * rows
    factor = LOG2E / hd**0.5

    def heads(i, carry):
        q, do = head_pair(q_ref, i, hd), head_pair(do_ref, i, hd)
        for t in range(pair // CHUNK):
            part = slice(t * CHUNK, (t + 1) * CHUNK)
            lanes = pl.ds(pl.multiple_of(i * pair + t * CHUNK, CHUNK), CHUNK)
            s, dp = score_chunk(k, v, q[part], do[part], b == 0, t * CHUNK)
            if held:
                held[0][:, lanes] = s
                held[1][:, lanes] = dp
            top = jnp.max(s, axis=0, keepdims=True) * factor
            e = jnp.exp2(s * factor - top)
            total = jnp.sum(e, axis=0, keepdims=True)
            weighted = jnp.sum(e * dp, axis=0, keepdims=True)
            if b > 0:
                old = before[0:1, lanes]
                both = jnp.maximum(old, top)
                old_part, new_part = jnp.exp2(old - both), jnp.exp2(top - both)
                total = before[1:2, lanes] * old_part + total * new_part
                weighted = before[2:3, lanes] * old_part + weighted * new_part
                top = both
            out[0:1, lanes] = top
            out[1:2, lanes] = total
            out[2:3, lanes] = weighted
        return carry

    lax.fori_loop(0, q_ref.shape[1] // (2 * hd), heads, 0, unroll=True)


def first_stats_kernel(n, me_ref, span_ref, q_ref, do_ref, k_ref, v_ref, out, q_out, do_out, k_out, v_out, flags):
    me = me_ref[0]
    lane = lax.broadcasted_iota(jnp.int32, flags.shape, 1)
    found = jnp.zeros(flags.shape, F32)
    for b in range(1, n):
        found = jnp.where((lane == b) & (span_ref[me ^ b] < span_ref[me]), 1.0, found)
    flags[...] = found
    q_out[...] = q_ref[...]
    do_out[...] = do_ref[...]
    k_out[...] = k_ref[...]
    v_out[...] = v_ref[...]
    stats_of_block(0, q_ref, do_ref, k_ref, v_ref, None, out)


def next_stats_kernel(b, flags, q_ref, do_ref, k_ref, v_ref, before, out):
    keep = counted(b, flags)

    @pl.when(keep)
    def _():
        stats_of_block(b, q_ref, do_ref, k_ref, v_ref, before, out)

    @pl.when(jnp.logical_not(keep))
    def _():
        out[...] = before[...]


def block_gradients(own, stats, q_ref, do_ref, k_ref, v_ref, p_buf, ds_ref, dk, dv, held=None):
    k, v = k_ref[...], v_ref[...]
    rows, hd = k.shape
    pair = 2 * rows
    factor = LOG2E / hd**0.5
    dk[...] = jnp.zeros_like(dk)
    dv[...] = jnp.zeros_like(dv)

    def heads(i, carry):
        q, do = head_pair(q_ref, i, hd), head_pair(do_ref, i, hd)
        for t in range(pair // CHUNK):
            part = slice(t * CHUNK, (t + 1) * CHUNK)
            lanes = pl.ds(pl.multiple_of(i * pair + t * CHUNK, CHUNK), CHUNK)
            if held:
                s, dp = held[0][:, lanes], held[1][:, lanes]
            else:
                s, dp = score_chunk(k, v, q[part], do[part], own, t * CHUNK)
            total = stats[1:2, lanes]
            level = stats[0:1, lanes] + jnp.log(total) * LOG2E
            p = jnp.exp2(s * factor - level)
            p_buf[:, part] = p.astype(BF16)
            ds = (p * (dp - stats[2:3, lanes] / total)).astype(BF16)
            ds_ref[:, lanes] = ds
        ds = ds_ref[:, pl.ds(pl.multiple_of(i * pair, CHUNK), pair)]
        dk[...] += jnp.dot(ds, q, preferred_element_type=F32)
        dv[...] += jnp.dot(p_buf[...], do, preferred_element_type=F32)
        return carry

    lax.fori_loop(0, q_ref.shape[1] // (2 * hd), heads, 0, unroll=True)
    inverse = 1.0 / hd**0.5
    return dk[...] * inverse, dv[...]


def other_kernel(b, flags, stats, q_ref, do_ref, k_ref, v_ref, dk_out, dv_out, ds_out, *refs):
    *refs, p_buf, dk, dv = refs
    keep = counted(b, flags)
    rows = dk.shape[0]
    held, before = None, stats
    if refs:
        stats, *held = refs

    @pl.when(keep)
    def _():
        if held:
            stats_of_block(b, q_ref, do_ref, k_ref, v_ref, before, stats, held)
        dk_sum, dv_sum = block_gradients(False, stats, q_ref, do_ref, k_ref, v_ref, p_buf, ds_out, dk, dv, held)
        dk_out[...] = dk_sum.astype(BF16)
        dv_out[:rows, :] = dv_sum.astype(BF16)
        dv_out[rows:, :] = jnp.zeros((dv_out.shape[0] - rows, dv.shape[1]), BF16)

    @pl.when(jnp.logical_not(keep))
    def _():
        if held:
            stats[...] = before[...]
        dk_out[...] = jnp.zeros_like(dk_out)
        dv_out[...] = jnp.zeros_like(dv_out)
        ds_out[...] = jnp.zeros_like(ds_out)


def own_kernel(stats, q_ref, do_ref, k_ref, v_ref, out_ref, ds_out, p_buf, dk, dv):
    hd = dk.shape[1]
    dk_sum, dv_sum = block_gradients(True, stats, q_ref, do_ref, k_ref, v_ref, p_buf, ds_out, dk, dv)
    out_ref[:, :hd] = dk_sum
    out_ref[:, hd:] = dv_sum


def query_kernel(n, *refs):
    k_refs, ds_refs, dq_ref, mark_ref = refs[:n], refs[n : 2 * n], refs[2 * n], refs[2 * n + 1]
    mark_ref[...] = jnp.zeros_like(mark_ref)
    rows, hd = k_refs[0].shape
    for h in range(dq_ref.shape[1] // hd):
        dq = 0.0
        for k, ds in zip(k_refs, ds_refs):
            part = ds[:, h * rows : (h + 1) * rows]
            dq = dq + lax.dot_general(part, k[...], TN, preferred_element_type=F32)
        dq_ref[:, h * hd : (h + 1) * hd] = (dq / hd**0.5).astype(BF16)


def merge_kernel(rows, *refs):
    *terms, out_ref = refs
    total = functools.reduce(jnp.add, [term[:rows, :].astype(F32) for term in terms])
    out_ref[:rows, :] = total.astype(BF16)
    if out_ref.shape[0] > rows:
        out_ref[rows:, :] = jnp.zeros((out_ref.shape[0] - rows, out_ref.shape[1]), BF16)


def merge(rows, terms, after):
    outs = [shape(terms[0].shape)]
    return whole_call(functools.partial(merge_kernel, rows), "merge", [], terms, outs, 4, (0, 0), [], after)[0]


def attention(me, spans, queries, out_grad, keys, values, activations, mark, swap, n):
    rows, hd = keys.shape
    columns = queries.shape[1]
    tall = columns // hd * rows
    product = 2 * rows * tall * hd
    cost = (8 * product, 8 * rows * columns)

    direct = [b for b in range(1, n) if b & (b - 1) == 0]
    blocks = {b: [swap(keys, b), swap(values, b)] for b in reversed(direct)}
    stats_shape = shape((8, tall), F32)
    stats, queries, out_grad, keys, values, flags = whole_call(
        functools.partial(first_stats_kernel, n),
        "first_stats",
        [me, spans],
        [queries, out_grad, keys, values],
        [stats_shape] + [shape(x.shape) for x in (queries, out_grad, keys, values)] + [shape((8, 128), F32)],
        12,
        cost,
        [],
        [mark],
    )
    blocks[0] = [keys, values]
    acts = prepare(activations, [stats])
    for b in range(1, n):
        if b not in blocks:
            blocks[b] = [swap(x, b & -b) for x in blocks[b & (b - 1)]]
        if b == n - 1:
            break
        stats = whole_call(
            functools.partial(next_stats_kernel, b),
            "next_stats",
            [],
            [flags, queries, out_grad, *blocks[b], stats],
            [stats_shape],
            10,
            cost,
            [],
            [*blocks[2], acts] if b == 1 else [],
        )[0]
    p_buf = pltpu.VMEM((rows, 2 * rows), BF16)
    sums = [pltpu.VMEM((rows, hd), F32)] * 2
    key_parts, value_parts = [[] for _ in range(n)], [[] for _ in range(n)]
    score_grads, own_parts, before = [None] * n, {}, []
    for b in range(n - 1, 0, -1):
        last = b == n - 1
        held = pltpu.VMEM((rows, tall), F32)
        dk, dv, score_grads[b], *total = whole_call(
            functools.partial(other_kernel, b),
            "block_gradients",
            [],
            [flags, stats, queries, out_grad, *blocks[b]],
            [shape((rows, hd)), shape((rows + TOP_ROWS, hd)), shape((rows, tall))] + [stats_shape] * last,
            20 if last else 10,
            (0, 0),
            [held, held] * last + [p_buf, *sums],
            before,
        )
        if last:
            stats = total[0]
        if value_parts[b]:
            dv = merge(rows, [dv, *value_parts[b]], [])
        value_parts[b & (b - 1)].append(swap(dv, b & -b))
        own_parts[b] = dk
        before = [dv]
    for b in range(n - 1, 0, -1):
        dk = own_parts[b]
        if key_parts[b]:
            dk = merge(rows, [dk, *key_parts[b]], before)
        key_parts[b & (b - 1)].append(swap(dk, b & -b))
    own, score_grads[0] = whole_call(
        own_kernel,
        "own_gradients",
        [],
        [stats, queries, out_grad, keys, values],
        [shape((rows, 2 * hd), F32), shape((rows, tall))],
        10,
        (0, 0),
        [p_buf, *sums],
        before,
    )
    return own, key_parts[0], value_parts[0], [blocks[b][0] for b in range(n)], score_grads, acts


def query_gradients(key_blocks, score_grads, columns, after):
    n = len(key_blocks)
    rows = key_blocks[0].shape[0]
    return whole_call(
        functools.partial(query_kernel, n),
        "query_gradients",
        [],
        [*key_blocks, *score_grads],
        [shape((rows, columns)), shape((8, 128), F32)],
        2 + 3 * n,
        (2 * n * rows * rows * columns, 16 * rows * columns),
        [],
        after,
    )


def pack_top(top):
    high = jnp.minimum(top, BF16_MAX).astype(BF16).astype(F32)
    rest = top - high
    middle = rest.astype(BF16).astype(F32)
    low = rest - middle
    return (high + pltpu.roll(middle, PACK_LANES, 1) + pltpu.roll(low, 2 * PACK_LANES, 1)).astype(BF16)


def unpack_top(ref, at):
    x = ref[at : at + TOP_ROWS, :TOP_LANES].astype(F32)
    total = x + (pltpu.roll(x, TOP_LANES - PACK_LANES, 1) + pltpu.roll(x, TOP_LANES - 2 * PACK_LANES, 1))
    lane = lax.broadcasted_iota(jnp.int32, x.shape, 1)
    return jnp.where(lane < PACK_LANES, total, 0.0)


def tile_of(step, me_dp, bits, flip):
    mask = flip
    for j in range(1, bits):
        if not (step >> (bits - 1 - j)) & 1:
            mask |= 1 << j
    return me_dp ^ mask


def reversed_step(step, bits):
    return sum(((step >> (bits - 1 - j)) & 1) << (j - 1) for j in range(1, bits))


def corrected_tile(at, dest, grads, a_ref, e_ref, top_ref):
    _, n_ctx, rows_ctx, rows = a_ref.shape
    tall = n_ctx * rows_ctx
    hd = grads.shape[1]
    a = a_ref[dest].reshape(tall, rows)
    e = e_ref[dest, :, :, at : at + hd].reshape(tall, hd)
    c = jnp.dot(a, grads, preferred_element_type=F32) + e
    mags = jnp.max(jnp.abs(c).reshape(tall // QROWS, QROWS, hd), axis=1)
    mags = jnp.max(mags, axis=1, keepdims=True)
    block = lax.broadcasted_iota(jnp.int32, (tall // QROWS, TOP_LANES), 0)
    lane = lax.broadcasted_iota(jnp.int32, (tall // QROWS, TOP_LANES), 1)
    top = jnp.max(jnp.where(lane == block, mags, 0.0), axis=0, keepdims=True)
    top_ref[pl.ds(dest, 1), :] = jnp.maximum(top_ref[pl.ds(dest, 1), :], top)
    return c


def summed_grads(at, own_ref, part_refs):
    rows, hd = own_ref.shape[0], own_ref.shape[1] // 2
    total = own_ref[:, at : at + hd]
    for part in part_refs:
        total = total + part[:rows, :].astype(F32)
    return total.astype(BF16)


def kept_rows(bits, shrink, at, me_ref, total, a_ref, e_ref, out_ref, top_ref):
    for step in range(out_ref.shape[0]):
        dest = tile_of(step, me_ref[0], bits, 0)
        out_ref[step] = corrected_tile(at, dest, total, a_ref, e_ref, top_ref) * shrink


def send_kernel(bits, shrink, at, n_parts, me_ref, own_ref, *refs):
    *before, a_ref, e_ref, out_ref, top_ref, grads_ref, grads_out = refs[n_parts:]
    total = summed_grads(at, own_ref, refs[:n_parts])
    grads_ref[...] = total
    grads_out[...] = total
    top_ref[...] = before[0][...] if before else jnp.zeros_like(top_ref)
    steps = a_ref.shape[0] // 2
    tall = a_ref.shape[1] * a_ref.shape[2]
    for step in range(steps):
        dest = tile_of(step, me_ref[0], bits, 1)
        c = corrected_tile(at, dest, total, a_ref, e_ref, top_ref)
        out_ref[step * tall : (step + 1) * tall, :] = (c * shrink).astype(BF16)
    if out_ref.shape[0] > steps * tall:
        out_ref[steps * tall :, :] = jnp.zeros((out_ref.shape[0] - steps * tall, out_ref.shape[1]), BF16)


def kept_kernel(bits, shrink, at, me_ref, grads_ref, before_ref, a_ref, e_ref, out_ref, top_ref):
    top_ref[...] = before_ref[...]
    kept_rows(bits, shrink, at, me_ref, grads_ref[...], a_ref, e_ref, out_ref, top_ref)


def split_kernel(bits, n_ctx, n_tops, kept, got, *refs):
    steps, tall, hd = kept.shape
    half = steps // 2
    part_tall = tall // 2
    tops = refs[:n_tops]
    low_away, low_stay, high_away, high_stay, *top_out = refs[n_tops:]
    for step in range(steps):
        c = (kept[step] + got[step * tall : (step + 1) * tall, :].astype(F32)).astype(BF16)
        c = c.reshape(n_ctx, 2, part_tall // n_ctx, hd)
        back = reversed_step(step, bits)
        for at, i, away, stay in ((step, 0, low_away, low_stay), (back, 1, high_away, high_stay)):
            part = c[:, i].reshape(part_tall, hd)
            if at < half:
                away[at * part_tall : (at + 1) * part_tall, :] = part
            else:
                stay[(at - half) * part_tall : (at - half + 1) * part_tall, :] = part
    if tops:
        top = largest(tops, got, steps * tall)
        top_out[0][...] = top
        low_away[half * part_tall :, :] = pack_top(top)
    else:
        tail = jnp.zeros((low_away.shape[0] - half * part_tall, hd), BF16)
        low_away[half * part_tall :, :] = tail
        high_away[half * part_tall :, :] = tail


def largest(tops, low_got, size):
    found = [top[...] for top in tops]
    if low_got.shape[0] > size:
        found.append(unpack_top(low_got, size))
    return functools.reduce(jnp.maximum, found)


def add_kernel(n_tops, low, low_got, high, high_got, *refs):
    tops = refs[:n_tops]
    low_away, low_stay, high_away, high_stay, *top_out = refs[n_tops:]
    size = low.shape[0]
    half = size // 2
    for mine, got, away, stay in ((low, low_got, low_away, low_stay), (high, high_got, high_away, high_stay)):
        away[:half, :] = (mine[:half, :].astype(F32) + got[:half, :].astype(F32)).astype(BF16)
        stay[...] = (mine[half:, :].astype(F32) + got[half:size, :].astype(F32)).astype(BF16)
    if tops:
        top = largest(tops, low_got, size)
        top_out[0][...] = top
        low_away[half:, :] = pack_top(top)
    else:
        low_away[half:, :] = jnp.zeros((low_away.shape[0] - half, low_away.shape[1]), BF16)


def context_masks(n_ctx):
    bits = n_ctx.bit_length() - 1
    return [sum((1 << j) for j in range(bits) if not (step >> (bits - 1 - j)) & 1) for step in range(n_ctx)]


def last_kernel(n_ctx, n_tops, me_ref, low, low_got, high, high_got, *refs):
    tops = refs[:n_tops]
    away, stay, *top_out = refs[n_tops:]
    size, hd = low.shape
    rows_set = size // n_ctx
    half = n_ctx // 2
    for i, mask in enumerate(context_masks(n_ctx)):
        part = pl.ds(pl.multiple_of((me_ref[0] ^ mask) * rows_set, rows_set), rows_set)
        out, at = (away, i) if i < half else (stay, i - half)
        at = 2 * at * rows_set
        for mine, got in ((low, low_got), (high, high_got)):
            total = mine[part, :].astype(F32) + got[part, :].astype(F32)
            out[at : at + rows_set, :] = total.astype(BF16)
            at += rows_set
    if tops:
        top = largest(tops, low_got, size)
        top_out[0][...] = top
        away[half * 2 * rows_set :, :] = pack_top(top)
    else:
        away[half * 2 * rows_set :, :] = jnp.zeros((away.shape[0] - half * 2 * rows_set, hd), BF16)


def halve_kernel(n_tops, mine, got, *refs):
    tops = refs[:n_tops]
    away, stay, *top_out = refs[n_tops:]
    size = mine.shape[0]
    half = size // 2
    away[:half, :] = (mine[:half, :].astype(F32) + got[:half, :].astype(F32)).astype(BF16)
    stay[...] = (mine[half:, :].astype(F32) + got[half:size, :].astype(F32)).astype(stay.dtype)
    if tops:
        top = largest(tops, got, size)
        top_out[0][...] = top
        away[half:, :] = pack_top(top)
    else:
        away[half:, :] = jnp.zeros((away.shape[0] - half, away.shape[1]), BF16)


def final_kernel(columns, n_ctx, gain, me_dp_ref, me_ctx_ref, *refs):
    sets = len(columns)
    groups = [refs[2 * chosen : 2 * chosen + 2] for chosen in range(sets)]
    top_ref, out_ref, scale_ref, all_tops = refs[2 * sets :]
    rows_ctx, hd = groups[0][0].shape
    scale = jnp.maximum(top_ref[...], unpack_top(groups[0][1], rows_ctx)) + 1e-06
    all_tops[...] = scale
    blocks = rows_ctx // QROWS
    lanes = n_ctx * blocks
    per_row = TOP_LANES // lanes
    lane = lax.broadcasted_iota(jnp.int32, scale.shape, 1)
    group = jnp.where(lane < lanes, scale, 0.0)
    moved = [group] + [pltpu.roll(group, k * lanes, 1) for k in range(1, per_row)]
    for r in range(scale_ref.shape[0]):
        row = [moved[k][r * per_row + k : r * per_row + k + 1, :] for k in range(per_row)]
        scale_ref[r : r + 1, :] = functools.reduce(jnp.add, row)
    factors = gain / all_tops[pl.ds(me_dp_ref[0], 1), :]
    lane = lax.broadcasted_iota(jnp.int32, factors.shape, 1)
    for r in range(blocks):
        mine = jnp.where(lane == me_ctx_ref[0] * blocks + r, factors, 0.0)
        factor = jnp.sum(mine, axis=1, keepdims=True)
        part = slice(r * QROWS, (r + 1) * QROWS)
        for at, (mine_ref, got_ref) in zip(columns, groups):
            out_ref[part, at : at + hd] = (mine_ref[part, :] + got_ref[part, :].astype(F32)) * factor


def local(n_dp, n_ctx, span_order, queries, keys, values, out_grad, activations, error_feedback):
    rows, hd = keys.shape
    width = 2 * hd
    model = activations.shape[1]
    rows_ctx = model // (n_dp * n_ctx)
    tall = n_ctx * rows_ctx
    me_dp = lax.axis_index("dp").astype(jnp.int32)[None]
    me_ctx = lax.axis_index("context").astype(jnp.int32)[None]
    bits = n_dp.bit_length() - 1

    def swap_dp(x, mask):
        return lax.ppermute(x, "dp", xor_perm(n_dp, mask))

    def swap_ctx(x, mask):
        return lax.ppermute(x, "context", xor_perm(n_ctx, mask))

    own, key_parts, value_parts, key_blocks, score_grads, acts = attention(
        me_ctx, span_order[0], queries, out_grad, keys, values, activations, begin(me_dp, me_ctx), swap_ctx, n_ctx
    )

    shrink = 1.0 / (n_dp * n_ctx)
    acts = acts.reshape(n_dp, n_ctx, rows_ctx, rows)
    errors = error_feedback.reshape(n_dp, n_ctx, rows_ctx, width)
    tops = shape((TOP_ROWS, TOP_LANES), F32)
    steps = n_dp // 2
    cost = (0, 0)
    kept_shape, grad_shape = shape((steps, tall, hd), F32), shape((rows, hd))

    def tiles(kernel, name, operands, outs, after=()):
        return whole_call(kernel, name, [me_dp], [*operands, acts, errors], outs, 18, cost, [], after)

    sets = 2
    half = steps // 2 * (tall // 2)

    def split(last, kept, got, top):
        return whole_call(
            functools.partial(split_kernel, bits, n_ctx, len(top)),
            "split_tiles",
            [],
            [kept, got, *top],
            [
                shape((half + (1 if last else 2) * TOP_ROWS, hd)),
                shape((half, hd)),
                shape((half + (0 if last else 2) * TOP_ROWS, hd)),
                shape((half, hd)),
            ]
            + [tops] * last,
            10,
            cost,
        )

    out, top, grads, value_grad = tiles(
        functools.partial(send_kernel, bits, shrink, hd, len(value_parts)),
        "send_tiles",
        [own, *value_parts],
        [shape((steps * tall + 2 * TOP_ROWS, hd)), tops, grad_shape, grad_shape],
    )
    got = swap_dp(out, 1)
    kept, top = tiles(
        functools.partial(kept_kernel, bits, shrink, hd), "kept_tiles", [grads, top], [kept_shape, tops]
    )
    out, top, grads, key_grad = tiles(
        functools.partial(send_kernel, bits, shrink, 0, len(key_parts)),
        "send_tiles",
        [own, *key_parts, top],
        [shape((steps * tall, hd)), tops, grad_shape, grad_shape],
    )
    halves = [split(False, kept, got, [])]
    got = swap_dp(out, 1)
    kept, top = tiles(
        functools.partial(kept_kernel, bits, shrink, 0),
        "kept_tiles",
        [grads, top],
        [kept_shape, tops],
        halves[0][1:2],
    )
    arrays = split(True, kept, got, [top, swap_dp(top, 1)])
    halves.append(arrays[:4])
    gathered = [arrays[4]]
    query_grad, mark = query_gradients(key_blocks, score_grads, queries.shape[1], [arrays[1]])
    groups = []
    for chosen in range(sets):
        low_away, low, high_away, high = halves[chosen]
        extra = TOP_ROWS if chosen == sets - 1 else 0
        tail = extra or 2 * TOP_ROWS
        for stage in range(1, bits):
            low_got = swap_dp(low_away, 1 << stage)
            high_got = swap_dp(high_away, 1 << (bits - stage))
            with_tops = extra > 0
            operands = [low, low_got, high, high_got] + (gathered if with_tops else [])
            n_tops = len(operands) - 4
            size = low.shape[0]
            if stage < bits - 1:
                low_away, low, high_away, high, *top_out = whole_call(
                    functools.partial(add_kernel, n_tops),
                    "add_stage",
                    [],
                    operands,
                    [shape((size // 2 + tail, hd))] + [shape((size // 2, hd))] * 3 + [tops] * with_tops,
                    8,
                    cost,
                    after=[mark] if chosen == 0 and stage == 1 else [],
                )
            else:
                chunk = rows_ctx
                away, stay, *top_out = whole_call(
                    functools.partial(last_kernel, n_ctx, n_tops),
                    "last_stage",
                    [me_ctx],
                    operands,
                    [shape((n_ctx // 2 * chunk + tail, hd)), shape((n_ctx // 2 * chunk, hd))] + [tops] * with_tops,
                    8,
                    cost,
                )
            if with_tops:
                gathered = list(top_out)
        mask = 1
        while mask < n_ctx // 2:
            size = stay.shape[0]
            away, stay, *top_out = whole_call(
                functools.partial(halve_kernel, int(with_tops)),
                "halve_context",
                [],
                [stay, swap_ctx(away, mask)] + (gathered if with_tops else []),
                [shape((size // 2 + tail, hd)), shape((size // 2, hd), F32 if size == 2 * chunk else BF16)]
                + [tops] * with_tops,
                8,
                (0, 0),
            )
            if with_tops:
                gathered = list(top_out)
            mask *= 2
        groups = [stay, swap_ctx(away, mask), *groups]
    payload, scale = whole_call(
        functools.partial(final_kernel, (0, hd), n_ctx, 7.0 / shrink),
        "final_stage",
        [me_dp, me_ctx],
        groups + gathered,
        [shape((rows_ctx, width), F32), shape((model // QROWS // TOP_LANES, TOP_LANES), F32)],
        8,
        (0, 0),
        [pltpu.VMEM((TOP_ROWS, TOP_LANES), F32)],
    )
    return query_grad, key_grad, value_grad, payload, scale.reshape(-1)


def solution(mesh):
    tokens = P(("dp", "context"), None)
    return jax.shard_map(
        functools.partial(local, mesh.shape["dp"], mesh.shape["context"]),
        mesh=mesh,
        in_specs=(P("dp", None), tokens, tokens, tokens, tokens, tokens, P("dp", "context", None, None)),
        out_specs=(tokens, tokens, tokens, tokens, P()),
        check_vma=False,
    )
```

```python
import functools

import jax
import jax.numpy as jnp
from jax import lax
from jax.experimental import pallas as pl
from jax.experimental.pallas import tpu as pltpu
from jax.sharding import PartitionSpec as P

QROWS = 32
LOG2E = 1.4426950408889634
FAR = 1e30
MIB = 1024 * 1024
CHUNK = 256
TOP_ROWS, TOP_LANES, PACK_LANES = 16, 128, 32
BF16, F32 = jnp.bfloat16, jnp.float32
BF16_MAX = float(jnp.finfo(jnp.bfloat16).max)
NT = (((1,), (1,)), ((), ()))
TN = (((0,), (0,)), ((), ()))


def xor_perm(size, mask):
    return [(i, i ^ mask) for i in range(size)]


def whole(x):
    return pl.BlockSpec(x.shape, lambda *_: (0,) * len(x.shape))


def shape(dims, dtype=BF16):
    return jax.ShapeDtypeStruct(dims, dtype)


def whole_call(kernel, name, scalars, operands, out_shape, mib, cost, scratch=(), after=()):
    def body(*refs):
        first = len(scalars) + len(operands)
        kernel(*refs[:first], *refs[first + len(after) :])

    return pl.pallas_call(
        body,
        grid_spec=pltpu.PrefetchScalarGridSpec(
            num_scalar_prefetch=len(scalars),
            grid=(1,),
            in_specs=[whole(x) for x in operands] + [pl.BlockSpec(memory_space=pl.ANY)] * len(after),
            out_specs=[whole(x) for x in out_shape],
            scratch_shapes=list(scratch),
        ),
        out_shape=out_shape,
        compiler_params=pltpu.CompilerParams(vmem_limit_bytes=mib * MIB),
        cost_estimate=pl.CostEstimate(flops=cost[0], bytes_accessed=cost[1], transcendentals=0),
        name=name,
    )(*scalars, *operands, *after)


def begin_kernel(me_dp_ref, me_ctx_ref, out_ref):
    out_ref[...] = jnp.zeros_like(out_ref)


def begin(me_dp, me_ctx):
    mark = [shape((8, 128), F32)]
    return whole_call(begin_kernel, "begin", [me_dp, me_ctx], [], mark, 4, (20_000_000_000, 0))[0]


def prepare_kernel(pieces, a_ref, a_out):
    tile = a_ref.shape[1] // pieces
    for i in range(pieces):
        a_out[i * tile : (i + 1) * tile, :] = a_ref[:, i * tile : (i + 1) * tile].T


def prepare(activations, after):
    rows, model = activations.shape
    outs = [shape((model, rows))]
    cost = (0, 0)
    kernel = functools.partial(prepare_kernel, 8)
    return whole_call(kernel, "prepare", [], [activations], outs, 16, cost, [], after)[0]


def head_pair(ref, i, hd):
    at = i * (2 * hd)
    first = ref[:, pl.ds(pl.multiple_of(at, hd), hd)]
    second = ref[:, pl.ds(pl.multiple_of(at + hd, hd), hd)]
    return jnp.concatenate([first, second], axis=0)


def score_chunk(k, v, q, do, own, first_lane):
    s = lax.dot_general(k, q, NT, preferred_element_type=F32)
    dp = lax.dot_general(v, do, NT, preferred_element_type=F32)
    if own:
        rows = k.shape[0]
        key_at = lax.broadcasted_iota(jnp.int32, s.shape, 0)
        query_at = lax.broadcasted_iota(jnp.int32, s.shape, 1) + first_lane
        query_at = jnp.where(query_at >= rows, query_at - rows, query_at)
        s = jnp.where(key_at <= query_at, s, -FAR)
    return s, dp


def counted(b, flags):
    lane = lax.broadcasted_iota(jnp.int32, flags.shape, 1)
    return jnp.max(jnp.where(lane == b, flags[...], 0.0)) > 0.5


def stats_of_block(b, q_ref, do_ref, k_ref, v_ref, before, out, held=None):
    k, v = k_ref[...], v_ref[...]
    rows, hd = k.shape
    pair = 2 * rows
    factor = LOG2E / hd**0.5

    def heads(i, carry):
        q, do = head_pair(q_ref, i, hd), head_pair(do_ref, i, hd)
        for t in range(pair // CHUNK):
            part = slice(t * CHUNK, (t + 1) * CHUNK)
            lanes = pl.ds(pl.multiple_of(i * pair + t * CHUNK, CHUNK), CHUNK)
            s, dp = score_chunk(k, v, q[part], do[part], b == 0, t * CHUNK)
            if held:
                held[0][:, lanes] = s
                held[1][:, lanes] = dp
            top = jnp.max(s, axis=0, keepdims=True) * factor
            e = jnp.exp2(s * factor - top)
            total = jnp.sum(e, axis=0, keepdims=True)
            weighted = jnp.sum(e * dp, axis=0, keepdims=True)
            if b > 0:
                old = before[0:1, lanes]
                both = jnp.maximum(old, top)
                old_part, new_part = jnp.exp2(old - both), jnp.exp2(top - both)
                total = before[1:2, lanes] * old_part + total * new_part
                weighted = before[2:3, lanes] * old_part + weighted * new_part
                top = both
            out[0:1, lanes] = top
            out[1:2, lanes] = total
            out[2:3, lanes] = weighted
        return carry

    lax.fori_loop(0, q_ref.shape[1] // (2 * hd), heads, 0, unroll=True)


def first_stats_kernel(n, me_ref, span_ref, q_ref, do_ref, k_ref, v_ref, out, q_out, do_out, k_out, v_out, flags):
    me = me_ref[0]
    lane = lax.broadcasted_iota(jnp.int32, flags.shape, 1)
    found = jnp.zeros(flags.shape, F32)
    for b in range(1, n):
        found = jnp.where((lane == b) & (span_ref[me ^ b] < span_ref[me]), 1.0, found)
    flags[...] = found
    q_out[...] = q_ref[...]
    do_out[...] = do_ref[...]
    k_out[...] = k_ref[...]
    v_out[...] = v_ref[...]
    stats_of_block(0, q_ref, do_ref, k_ref, v_ref, None, out)


def next_stats_kernel(b, flags, q_ref, do_ref, k_ref, v_ref, before, out):
    keep = counted(b, flags)

    @pl.when(keep)
    def _():
        stats_of_block(b, q_ref, do_ref, k_ref, v_ref, before, out)

    @pl.when(jnp.logical_not(keep))
    def _():
        out[...] = before[...]


def block_gradients(own, stats, q_ref, do_ref, k_ref, v_ref, p_buf, ds_ref, dk, dv, held=None):
    k, v = k_ref[...], v_ref[...]
    rows, hd = k.shape
    pair = 2 * rows
    factor = LOG2E / hd**0.5
    dk[...] = jnp.zeros_like(dk)
    dv[...] = jnp.zeros_like(dv)

    def heads(i, carry):
        q, do = head_pair(q_ref, i, hd), head_pair(do_ref, i, hd)
        for t in range(pair // CHUNK):
            part = slice(t * CHUNK, (t + 1) * CHUNK)
            lanes = pl.ds(pl.multiple_of(i * pair + t * CHUNK, CHUNK), CHUNK)
            if held:
                s, dp = held[0][:, lanes], held[1][:, lanes]
            else:
                s, dp = score_chunk(k, v, q[part], do[part], own, t * CHUNK)
            total = stats[1:2, lanes]
            level = stats[0:1, lanes] + jnp.log(total) * LOG2E
            p = jnp.exp2(s * factor - level)
            p_buf[:, part] = p.astype(BF16)
            ds = (p * (dp - stats[2:3, lanes] / total)).astype(BF16)
            ds_ref[:, lanes] = ds
        ds = ds_ref[:, pl.ds(pl.multiple_of(i * pair, CHUNK), pair)]
        dk[...] += jnp.dot(ds, q, preferred_element_type=F32)
        dv[...] += jnp.dot(p_buf[...], do, preferred_element_type=F32)
        return carry

    lax.fori_loop(0, q_ref.shape[1] // (2 * hd), heads, 0, unroll=True)
    inverse = 1.0 / hd**0.5
    return dk[...] * inverse, dv[...]


def other_kernel(b, flags, stats, q_ref, do_ref, k_ref, v_ref, dk_out, dv_out, ds_out, *refs):
    *refs, p_buf, dk, dv = refs
    keep = counted(b, flags)
    rows = dk.shape[0]
    held, before = None, stats
    if refs:
        stats, *held = refs

    @pl.when(keep)
    def _():
        if held:
            stats_of_block(b, q_ref, do_ref, k_ref, v_ref, before, stats, held)
        dk_sum, dv_sum = block_gradients(False, stats, q_ref, do_ref, k_ref, v_ref, p_buf, ds_out, dk, dv, held)
        dk_out[...] = dk_sum.astype(BF16)
        dv_out[:rows, :] = dv_sum.astype(BF16)
        dv_out[rows:, :] = jnp.zeros((dv_out.shape[0] - rows, dv.shape[1]), BF16)

    @pl.when(jnp.logical_not(keep))
    def _():
        if held:
            stats[...] = before[...]
        dk_out[...] = jnp.zeros_like(dk_out)
        dv_out[...] = jnp.zeros_like(dv_out)
        ds_out[...] = jnp.zeros_like(ds_out)


def own_kernel(stats, q_ref, do_ref, k_ref, v_ref, out_ref, ds_out, p_buf, dk, dv):
    hd = dk.shape[1]
    dk_sum, dv_sum = block_gradients(True, stats, q_ref, do_ref, k_ref, v_ref, p_buf, ds_out, dk, dv)
    out_ref[:, :hd] = dk_sum
    out_ref[:, hd:] = dv_sum


def query_kernel(n, *refs):
    k_refs, ds_refs = refs[:n], refs[n : 2 * n]
    *done, dq_ref, mark_ref = refs[2 * n :]
    mark_ref[...] = jnp.zeros_like(mark_ref)
    rows, hd = k_refs[0].shape
    first = 0
    if done:
        first = done[0].shape[1] // hd
        dq_ref[:, : first * hd] = done[0][...]
    for h in range(first, dq_ref.shape[1] // hd):
        dq = 0.0
        for k, ds in zip(k_refs, ds_refs):
            part = ds[:, h * rows : (h + 1) * rows]
            dq = dq + lax.dot_general(part, k[...], TN, preferred_element_type=F32)
        dq_ref[:, h * hd : (h + 1) * hd] = (dq / hd**0.5).astype(BF16)


def merge_kernel(rows, *refs):
    *terms, out_ref = refs
    total = functools.reduce(jnp.add, [term[:rows, :].astype(F32) for term in terms])
    out_ref[:rows, :] = total.astype(BF16)
    if out_ref.shape[0] > rows:
        out_ref[rows:, :] = jnp.zeros((out_ref.shape[0] - rows, out_ref.shape[1]), BF16)


def merge(rows, terms, after):
    outs = [shape(terms[0].shape)]
    return whole_call(functools.partial(merge_kernel, rows), "merge", [], terms, outs, 4, (0, 0), [], after)[0]


def attention(me, spans, queries, out_grad, keys, values, activations, mark, swap, n):
    rows, hd = keys.shape
    columns = queries.shape[1]
    tall = columns // hd * rows
    product = 2 * rows * tall * hd
    cost = (8 * product, 8 * rows * columns)

    direct = [b for b in range(1, n) if b & (b - 1) == 0]
    blocks = {b: [swap(keys, b), swap(values, b)] for b in reversed(direct)}
    stats_shape = shape((8, tall), F32)
    stats, queries, out_grad, keys, values, flags = whole_call(
        functools.partial(first_stats_kernel, n),
        "first_stats",
        [me, spans],
        [queries, out_grad, keys, values],
        [stats_shape] + [shape(x.shape) for x in (queries, out_grad, keys, values)] + [shape((8, 128), F32)],
        12,
        cost,
        [],
        [mark],
    )
    blocks[0] = [keys, values]
    acts = prepare(activations, [stats])
    for b in range(1, n):
        if b not in blocks:
            blocks[b] = [swap(x, b & -b) for x in blocks[b & (b - 1)]]
        if b == n - 1:
            break
        stats = whole_call(
            functools.partial(next_stats_kernel, b),
            "next_stats",
            [],
            [flags, queries, out_grad, *blocks[b], stats],
            [stats_shape],
            10,
            cost,
            [],
            [*blocks[2], acts] if b == 1 else [],
        )[0]
    p_buf = pltpu.VMEM((rows, 2 * rows), BF16)
    sums = [pltpu.VMEM((rows, hd), F32)] * 2
    key_parts, value_parts = [[] for _ in range(n)], [[] for _ in range(n)]
    score_grads, own_parts, before = [None] * n, {}, []
    for b in range(n - 1, 0, -1):
        last = b == n - 1
        held = pltpu.VMEM((rows, tall), F32)
        dk, dv, score_grads[b], *total = whole_call(
            functools.partial(other_kernel, b),
            "block_gradients",
            [],
            [flags, stats, queries, out_grad, *blocks[b]],
            [shape((rows, hd)), shape((rows + TOP_ROWS, hd)), shape((rows, tall))] + [stats_shape] * last,
            20 if last else 10,
            (0, 0),
            [held, held] * last + [p_buf, *sums],
            before,
        )
        if last:
            stats = total[0]
        if value_parts[b]:
            dv = merge(rows, [dv, *value_parts[b]], [])
        value_parts[b & (b - 1)].append(swap(dv, b & -b))
        own_parts[b] = dk
        before = [dv]
    for b in range(n - 1, 0, -1):
        dk = own_parts[b]
        if key_parts[b]:
            dk = merge(rows, [dk, *key_parts[b]], before)
        key_parts[b & (b - 1)].append(swap(dk, b & -b))
    own, score_grads[0] = whole_call(
        own_kernel,
        "own_gradients",
        [],
        [stats, queries, out_grad, keys, values],
        [shape((rows, 2 * hd), F32), shape((rows, tall))],
        10,
        (0, 0),
        [p_buf, *sums],
        before,
    )
    return own, key_parts[0], value_parts[0], [blocks[b][0] for b in range(n)], score_grads, acts


def query_gradients(key_blocks, score_grads, done, columns, after):
    n = len(key_blocks)
    rows = key_blocks[0].shape[0]
    return whole_call(
        functools.partial(query_kernel, n),
        "query_gradients",
        [],
        [*key_blocks, *score_grads, *done],
        [shape((rows, columns)), shape((8, 128), F32)],
        2 + 3 * n,
        (0, 0),
        [],
        after,
    )


def pack_top(top):
    high = jnp.minimum(top, BF16_MAX).astype(BF16).astype(F32)
    rest = top - high
    middle = rest.astype(BF16).astype(F32)
    low = rest - middle
    return (high + pltpu.roll(middle, PACK_LANES, 1) + pltpu.roll(low, 2 * PACK_LANES, 1)).astype(BF16)


def unpack_top(ref, at):
    x = ref[at : at + TOP_ROWS, :TOP_LANES].astype(F32)
    total = x + (pltpu.roll(x, TOP_LANES - PACK_LANES, 1) + pltpu.roll(x, TOP_LANES - 2 * PACK_LANES, 1))
    lane = lax.broadcasted_iota(jnp.int32, x.shape, 1)
    return jnp.where(lane < PACK_LANES, total, 0.0)


def tile_of(step, me_dp, bits, flip):
    mask = flip
    for j in range(1, bits):
        if not (step >> (bits - 1 - j)) & 1:
            mask |= 1 << j
    return me_dp ^ mask


def reversed_step(step, bits):
    return sum(((step >> (bits - 1 - j)) & 1) << (j - 1) for j in range(1, bits))


def corrected_tile(at, dest, grads, a_ref, e_ref, top_ref):
    _, n_ctx, rows_ctx, rows = a_ref.shape
    tall = n_ctx * rows_ctx
    hd = grads.shape[1]
    a = a_ref[dest].reshape(tall, rows)
    e = e_ref[dest, :, :, at : at + hd].reshape(tall, hd)
    c = jnp.dot(a, grads, preferred_element_type=F32) + e
    mags = jnp.max(jnp.abs(c).reshape(tall // QROWS, QROWS, hd), axis=1)
    mags = jnp.max(mags, axis=1, keepdims=True)
    block = lax.broadcasted_iota(jnp.int32, (tall // QROWS, TOP_LANES), 0)
    lane = lax.broadcasted_iota(jnp.int32, (tall // QROWS, TOP_LANES), 1)
    top = jnp.max(jnp.where(lane == block, mags, 0.0), axis=0, keepdims=True)
    top_ref[pl.ds(dest, 1), :] = jnp.maximum(top_ref[pl.ds(dest, 1), :], top)
    return c


def summed_grads(at, own_ref, part_refs):
    rows, hd = own_ref.shape[0], own_ref.shape[1] // 2
    total = own_ref[:, at : at + hd]
    for part in part_refs:
        total = total + part[:rows, :].astype(F32)
    return total.astype(BF16)


def kept_rows(bits, shrink, at, me_ref, total, a_ref, e_ref, out_ref, top_ref):
    for step in range(out_ref.shape[0]):
        dest = tile_of(step, me_ref[0], bits, 0)
        out_ref[step] = corrected_tile(at, dest, total, a_ref, e_ref, top_ref) * shrink


def send_kernel(bits, shrink, at, n_parts, me_ref, own_ref, *refs):
    *before, a_ref, e_ref, out_ref, top_ref, grads_ref, grads_out = refs[n_parts:]
    total = summed_grads(at, own_ref, refs[:n_parts])
    grads_ref[...] = total
    grads_out[...] = total
    top_ref[...] = before[0][...] if before else jnp.zeros_like(top_ref)
    steps = a_ref.shape[0] // 2
    tall = a_ref.shape[1] * a_ref.shape[2]
    for step in range(steps):
        dest = tile_of(step, me_ref[0], bits, 1)
        c = corrected_tile(at, dest, total, a_ref, e_ref, top_ref)
        out_ref[step * tall : (step + 1) * tall, :] = (c * shrink).astype(BF16)
    if out_ref.shape[0] > steps * tall:
        out_ref[steps * tall :, :] = jnp.zeros((out_ref.shape[0] - steps * tall, out_ref.shape[1]), BF16)


def kept_kernel(bits, shrink, at, me_ref, grads_ref, before_ref, a_ref, e_ref, out_ref, top_ref):
    top_ref[...] = before_ref[...]
    kept_rows(bits, shrink, at, me_ref, grads_ref[...], a_ref, e_ref, out_ref, top_ref)


def split_kernel(bits, n_ctx, n_tops, kept, got, *refs):
    steps, tall, hd = kept.shape
    half = steps // 2
    part_tall = tall // 2
    tops = refs[:n_tops]
    low_away, low_stay, high_away, high_stay, *top_out = refs[n_tops:]
    for step in range(steps):
        c = (kept[step] + got[step * tall : (step + 1) * tall, :].astype(F32)).astype(BF16)
        c = c.reshape(n_ctx, 2, part_tall // n_ctx, hd)
        back = reversed_step(step, bits)
        for at, i, away, stay in ((step, 0, low_away, low_stay), (back, 1, high_away, high_stay)):
            part = c[:, i].reshape(part_tall, hd)
            if at < half:
                away[at * part_tall : (at + 1) * part_tall, :] = part
            else:
                stay[(at - half) * part_tall : (at - half + 1) * part_tall, :] = part
    if tops:
        top = largest(tops, got, steps * tall)
        top_out[0][...] = top
        low_away[half * part_tall :, :] = pack_top(top)
    else:
        tail = jnp.zeros((low_away.shape[0] - half * part_tall, hd), BF16)
        low_away[half * part_tall :, :] = tail
        high_away[half * part_tall :, :] = tail


def largest(tops, low_got, size):
    found = [top[...] for top in tops]
    if low_got.shape[0] > size:
        found.append(unpack_top(low_got, size))
    return functools.reduce(jnp.maximum, found)


def add_kernel(n_tops, low, low_got, high, high_got, *refs):
    tops = refs[:n_tops]
    low_away, low_stay, high_away, high_stay, *top_out = refs[n_tops:]
    size = low.shape[0]
    half = size // 2
    for mine, got, away, stay in ((low, low_got, low_away, low_stay), (high, high_got, high_away, high_stay)):
        away[:half, :] = (mine[:half, :].astype(F32) + got[:half, :].astype(F32)).astype(BF16)
        stay[...] = (mine[half:, :].astype(F32) + got[half:size, :].astype(F32)).astype(BF16)
    if tops:
        top = largest(tops, low_got, size)
        top_out[0][...] = top
        low_away[half:, :] = pack_top(top)
    else:
        low_away[half:, :] = jnp.zeros((low_away.shape[0] - half, low_away.shape[1]), BF16)


def context_masks(n_ctx):
    bits = n_ctx.bit_length() - 1
    return [sum((1 << j) for j in range(bits) if not (step >> (bits - 1 - j)) & 1) for step in range(n_ctx)]


def last_kernel(n_ctx, n_tops, me_ref, low, low_got, high, high_got, *refs):
    tops = refs[:n_tops]
    away, stay, *top_out = refs[n_tops:]
    size, hd = low.shape
    rows_set = size // n_ctx
    half = n_ctx // 2
    for i, mask in enumerate(context_masks(n_ctx)):
        part = pl.ds(pl.multiple_of((me_ref[0] ^ mask) * rows_set, rows_set), rows_set)
        out, at = (away, i) if i < half else (stay, i - half)
        at = 2 * at * rows_set
        for mine, got in ((low, low_got), (high, high_got)):
            total = mine[part, :].astype(F32) + got[part, :].astype(F32)
            out[at : at + rows_set, :] = total.astype(BF16)
            at += rows_set
    if tops:
        top = largest(tops, low_got, size)
        top_out[0][...] = top
        away[half * 2 * rows_set :, :] = pack_top(top)
    else:
        away[half * 2 * rows_set :, :] = jnp.zeros((away.shape[0] - half * 2 * rows_set, hd), BF16)


def halve_kernel(n_tops, mine, got, *refs):
    tops = refs[:n_tops]
    away, stay, *top_out = refs[n_tops:]
    size = mine.shape[0]
    half = size // 2
    away[:half, :] = (mine[:half, :].astype(F32) + got[:half, :].astype(F32)).astype(BF16)
    stay[...] = (mine[half:, :].astype(F32) + got[half:size, :].astype(F32)).astype(stay.dtype)
    if tops:
        top = largest(tops, got, size)
        top_out[0][...] = top
        away[half:, :] = pack_top(top)
    else:
        away[half:, :] = jnp.zeros((away.shape[0] - half, away.shape[1]), BF16)


def final_kernel(columns, n_ctx, gain, me_dp_ref, me_ctx_ref, *refs):
    sets = len(columns)
    groups = [refs[2 * chosen : 2 * chosen + 2] for chosen in range(sets)]
    top_ref, out_ref, scale_ref, all_tops = refs[2 * sets :]
    rows_ctx, hd = groups[0][0].shape
    scale = jnp.maximum(top_ref[...], unpack_top(groups[0][1], rows_ctx)) + 1e-06
    all_tops[...] = scale
    blocks = rows_ctx // QROWS
    lanes = n_ctx * blocks
    per_row = TOP_LANES // lanes
    lane = lax.broadcasted_iota(jnp.int32, scale.shape, 1)
    group = jnp.where(lane < lanes, scale, 0.0)
    moved = [group] + [pltpu.roll(group, k * lanes, 1) for k in range(1, per_row)]
    for r in range(scale_ref.shape[0]):
        row = [moved[k][r * per_row + k : r * per_row + k + 1, :] for k in range(per_row)]
        scale_ref[r : r + 1, :] = functools.reduce(jnp.add, row)
    factors = gain / all_tops[pl.ds(me_dp_ref[0], 1), :]
    lane = lax.broadcasted_iota(jnp.int32, factors.shape, 1)
    for r in range(blocks):
        mine = jnp.where(lane == me_ctx_ref[0] * blocks + r, factors, 0.0)
        factor = jnp.sum(mine, axis=1, keepdims=True)
        part = slice(r * QROWS, (r + 1) * QROWS)
        for at, (mine_ref, got_ref) in zip(columns, groups):
            out_ref[part, at : at + hd] = (mine_ref[part, :] + got_ref[part, :].astype(F32)) * factor


def local(n_dp, n_ctx, span_order, queries, keys, values, out_grad, activations, error_feedback):
    rows, hd = keys.shape
    width = 2 * hd
    model = activations.shape[1]
    rows_ctx = model // (n_dp * n_ctx)
    tall = n_ctx * rows_ctx
    me_dp = lax.axis_index("dp").astype(jnp.int32)[None]
    me_ctx = lax.axis_index("context").astype(jnp.int32)[None]
    bits = n_dp.bit_length() - 1

    def swap_dp(x, mask):
        return lax.ppermute(x, "dp", xor_perm(n_dp, mask))

    def swap_ctx(x, mask):
        return lax.ppermute(x, "context", xor_perm(n_ctx, mask))

    own, key_parts, value_parts, key_blocks, score_grads, acts = attention(
        me_ctx, span_order[0], queries, out_grad, keys, values, activations, begin(me_dp, me_ctx), swap_ctx, n_ctx
    )

    shrink = 1.0 / (n_dp * n_ctx)
    acts = acts.reshape(n_dp, n_ctx, rows_ctx, rows)
    errors = error_feedback.reshape(n_dp, n_ctx, rows_ctx, width)
    tops = shape((TOP_ROWS, TOP_LANES), F32)
    steps = n_dp // 2
    cost = (0, 0)
    kept_shape, grad_shape = shape((steps, tall, hd), F32), shape((rows, hd))

    def tiles(kernel, name, operands, outs, after=()):
        return whole_call(kernel, name, [me_dp], [*operands, acts, errors], outs, 18, cost, [], after)

    sets = 2
    half = steps // 2 * (tall // 2)

    def split(last, kept, got, top):
        return whole_call(
            functools.partial(split_kernel, bits, n_ctx, len(top)),
            "split_tiles",
            [],
            [kept, got, *top],
            [
                shape((half + (1 if last else 2) * TOP_ROWS, hd)),
                shape((half, hd)),
                shape((half + (0 if last else 2) * TOP_ROWS, hd)),
                shape((half, hd)),
            ]
            + [tops] * last,
            10,
            cost,
        )

    out, top, grads, value_grad = tiles(
        functools.partial(send_kernel, bits, shrink, hd, len(value_parts)),
        "send_tiles",
        [own, *value_parts],
        [shape((steps * tall + 2 * TOP_ROWS, hd)), tops, grad_shape, grad_shape],
    )
    got = swap_dp(out, 1)
    kept, top = tiles(
        functools.partial(kept_kernel, bits, shrink, hd), "kept_tiles", [grads, top], [kept_shape, tops]
    )
    out, top, grads, key_grad = tiles(
        functools.partial(send_kernel, bits, shrink, 0, len(key_parts)),
        "send_tiles",
        [own, *key_parts, top],
        [shape((steps * tall, hd)), tops, grad_shape, grad_shape],
    )
    halves = [split(False, kept, got, [])]
    got = swap_dp(out, 1)
    kept, top = tiles(
        functools.partial(kept_kernel, bits, shrink, 0),
        "kept_tiles",
        [grads, top],
        [kept_shape, tops],
        halves[0][1:2],
    )
    arrays = split(True, kept, got, [top, swap_dp(top, 1)])
    halves.append(arrays[:4])
    gathered = [arrays[4]]
    query_half, mark = query_gradients(key_blocks, score_grads, [], queries.shape[1] // 2, [arrays[1]])
    groups = []
    for chosen in range(sets):
        low_away, low, high_away, high = halves[chosen]
        extra = TOP_ROWS if chosen == sets - 1 else 0
        tail = extra or 2 * TOP_ROWS
        for stage in range(1, bits):
            low_got = swap_dp(low_away, 1 << stage)
            high_got = swap_dp(high_away, 1 << (bits - stage))
            with_tops = extra > 0
            operands = [low, low_got, high, high_got] + (gathered if with_tops else [])
            n_tops = len(operands) - 4
            size = low.shape[0]
            if stage < bits - 1:
                low_away, low, high_away, high, *top_out = whole_call(
                    functools.partial(add_kernel, n_tops),
                    "add_stage",
                    [],
                    operands,
                    [shape((size // 2 + tail, hd))] + [shape((size // 2, hd))] * 3 + [tops] * with_tops,
                    8,
                    cost,
                    after=[mark] if stage == 1 else [],
                )
                if chosen == 0 and stage == 1:
                    query_grad, mark = query_gradients(
                        key_blocks, score_grads, [query_half], queries.shape[1], [low]
                    )
            else:
                chunk = rows_ctx
                away, stay, *top_out = whole_call(
                    functools.partial(last_kernel, n_ctx, n_tops),
                    "last_stage",
                    [me_ctx],
                    operands,
                    [shape((n_ctx // 2 * chunk + tail, hd)), shape((n_ctx // 2 * chunk, hd))] + [tops] * with_tops,
                    8,
                    cost,
                )
            if with_tops:
                gathered = list(top_out)
        mask = 1
        while mask < n_ctx // 2:
            size = stay.shape[0]
            away, stay, *top_out = whole_call(
                functools.partial(halve_kernel, int(with_tops)),
                "halve_context",
                [],
                [stay, swap_ctx(away, mask)] + (gathered if with_tops else []),
                [shape((size // 2 + tail, hd)), shape((size // 2, hd), F32 if size == 2 * chunk else BF16)]
                + [tops] * with_tops,
                8,
                (0, 0),
            )
            if with_tops:
                gathered = list(top_out)
            mask *= 2
        groups = [stay, swap_ctx(away, mask), *groups]
    payload, scale = whole_call(
        functools.partial(final_kernel, (0, hd), n_ctx, 7.0 / shrink),
        "final_stage",
        [me_dp, me_ctx],
        groups + gathered,
        [shape((rows_ctx, width), F32), shape((model // QROWS // TOP_LANES, TOP_LANES), F32)],
        8,
        (0, 0),
        [pltpu.VMEM((TOP_ROWS, TOP_LANES), F32)],
    )
    return query_grad, key_grad, value_grad, payload, scale.reshape(-1)


def solution(mesh):
    tokens = P(("dp", "context"), None)
    return jax.shard_map(
        functools.partial(local, mesh.shape["dp"], mesh.shape["context"]),
        mesh=mesh,
        in_specs=(P("dp", None), tokens, tokens, tokens, tokens, tokens, P("dp", "context", None, None)),
        out_specs=(tokens, tokens, tokens, tokens, P()),
        check_vma=False,
    )
```

```python
import functools

import jax
import jax.numpy as jnp
from jax import lax
from jax.experimental import pallas as pl
from jax.experimental.pallas import tpu as pltpu
from jax.sharding import PartitionSpec as P

QROWS = 32
LOG2E = 1.4426950408889634
FAR = 1e30
MIB = 1024 * 1024
CHUNK = 256
TOP_ROWS, TOP_LANES, PACK_LANES = 16, 128, 32
BF16, F32 = jnp.bfloat16, jnp.float32
BF16_MAX = float(jnp.finfo(jnp.bfloat16).max)
NT = (((1,), (1,)), ((), ()))
TN = (((0,), (0,)), ((), ()))


def xor_perm(size, mask):
    return [(i, i ^ mask) for i in range(size)]


def whole(x):
    return pl.BlockSpec(x.shape, lambda *_: (0,) * len(x.shape))


def shape(dims, dtype=BF16):
    return jax.ShapeDtypeStruct(dims, dtype)


def whole_call(kernel, name, scalars, operands, out_shape, mib, cost, scratch=(), after=()):
    def body(*refs):
        first = len(scalars) + len(operands)
        kernel(*refs[:first], *refs[first + len(after) :])

    return pl.pallas_call(
        body,
        grid_spec=pltpu.PrefetchScalarGridSpec(
            num_scalar_prefetch=len(scalars),
            grid=(1,),
            in_specs=[whole(x) for x in operands] + [pl.BlockSpec(memory_space=pl.ANY)] * len(after),
            out_specs=[whole(x) for x in out_shape],
            scratch_shapes=list(scratch),
        ),
        out_shape=out_shape,
        compiler_params=pltpu.CompilerParams(vmem_limit_bytes=mib * MIB),
        cost_estimate=pl.CostEstimate(flops=cost[0], bytes_accessed=cost[1], transcendentals=0),
        name=name,
    )(*scalars, *operands, *after)


def begin_kernel(me_dp_ref, me_ctx_ref, out_ref):
    out_ref[...] = jnp.zeros_like(out_ref)


def begin(me_dp, me_ctx):
    mark = [shape((8, 128), F32)]
    return whole_call(begin_kernel, "begin", [me_dp, me_ctx], [], mark, 4, (20_000_000_000, 0))[0]


def prepare_kernel(pieces, a_ref, a_out):
    tile = a_ref.shape[1] // pieces
    for i in range(pieces):
        a_out[i * tile : (i + 1) * tile, :] = a_ref[:, i * tile : (i + 1) * tile].T


def prepare(activations, after):
    rows, model = activations.shape
    outs = [shape((model, rows))]
    cost = (0, 0)
    kernel = functools.partial(prepare_kernel, 8)
    return whole_call(kernel, "prepare", [], [activations], outs, 16, cost, [], after)[0]


def head_pair(ref, i, hd):
    at = i * (2 * hd)
    first = ref[:, pl.ds(pl.multiple_of(at, hd), hd)]
    second = ref[:, pl.ds(pl.multiple_of(at + hd, hd), hd)]
    return jnp.concatenate([first, second], axis=0)


def score_chunk(k, v, q, do, own, first_lane):
    s = lax.dot_general(k, q, NT, preferred_element_type=F32)
    dp = lax.dot_general(v, do, NT, preferred_element_type=F32)
    if own:
        rows = k.shape[0]
        key_at = lax.broadcasted_iota(jnp.int32, s.shape, 0)
        query_at = lax.broadcasted_iota(jnp.int32, s.shape, 1) + first_lane
        query_at = jnp.where(query_at >= rows, query_at - rows, query_at)
        s = jnp.where(key_at <= query_at, s, -FAR)
    return s, dp


def counted(b, flags):
    lane = lax.broadcasted_iota(jnp.int32, flags.shape, 1)
    return jnp.max(jnp.where(lane == b, flags[...], 0.0)) > 0.5


def stats_of_block(b, q_ref, do_ref, k_ref, v_ref, before, out, held=None):
    k, v = k_ref[...], v_ref[...]
    rows, hd = k.shape
    pair = 2 * rows
    factor = LOG2E / hd**0.5

    def heads(i, carry):
        q, do = head_pair(q_ref, i, hd), head_pair(do_ref, i, hd)
        for t in range(pair // CHUNK):
            part = slice(t * CHUNK, (t + 1) * CHUNK)
            lanes = pl.ds(pl.multiple_of(i * pair + t * CHUNK, CHUNK), CHUNK)
            s, dp = score_chunk(k, v, q[part], do[part], b == 0, t * CHUNK)
            if held:
                held[0][:, lanes] = s
                held[1][:, lanes] = dp
            top = jnp.max(s, axis=0, keepdims=True) * factor
            e = jnp.exp2(s * factor - top)
            total = jnp.sum(e, axis=0, keepdims=True)
            weighted = jnp.sum(e * dp, axis=0, keepdims=True)
            if b > 0:
                old = before[0:1, lanes]
                both = jnp.maximum(old, top)
                old_part, new_part = jnp.exp2(old - both), jnp.exp2(top - both)
                total = before[1:2, lanes] * old_part + total * new_part
                weighted = before[2:3, lanes] * old_part + weighted * new_part
                top = both
            out[0:1, lanes] = top
            out[1:2, lanes] = total
            out[2:3, lanes] = weighted
        return carry

    lax.fori_loop(0, q_ref.shape[1] // (2 * hd), heads, 0, unroll=True)


def first_stats_kernel(n, me_ref, span_ref, q_ref, do_ref, k_ref, v_ref, out, q_out, do_out, k_out, v_out, flags):
    me = me_ref[0]
    lane = lax.broadcasted_iota(jnp.int32, flags.shape, 1)
    found = jnp.zeros(flags.shape, F32)
    for b in range(1, n):
        found = jnp.where((lane == b) & (span_ref[me ^ b] < span_ref[me]), 1.0, found)
    flags[...] = found
    q_out[...] = q_ref[...]
    do_out[...] = do_ref[...]
    k_out[...] = k_ref[...]
    v_out[...] = v_ref[...]
    stats_of_block(0, q_ref, do_ref, k_ref, v_ref, None, out)


def next_stats_kernel(b, flags, q_ref, do_ref, k_ref, v_ref, before, out):
    keep = counted(b, flags)

    @pl.when(keep)
    def _():
        stats_of_block(b, q_ref, do_ref, k_ref, v_ref, before, out)

    @pl.when(jnp.logical_not(keep))
    def _():
        out[...] = before[...]


def block_gradients(own, stats, q_ref, do_ref, k_ref, v_ref, p_buf, ds_ref, dk, dv, held=None):
    k, v = k_ref[...], v_ref[...]
    rows, hd = k.shape
    pair = 2 * rows
    factor = LOG2E / hd**0.5
    dk[...] = jnp.zeros_like(dk)
    dv[...] = jnp.zeros_like(dv)

    def heads(i, carry):
        q, do = head_pair(q_ref, i, hd), head_pair(do_ref, i, hd)
        for t in range(pair // CHUNK):
            part = slice(t * CHUNK, (t + 1) * CHUNK)
            lanes = pl.ds(pl.multiple_of(i * pair + t * CHUNK, CHUNK), CHUNK)
            if held:
                s, dp = held[0][:, lanes], held[1][:, lanes]
            else:
                s, dp = score_chunk(k, v, q[part], do[part], own, t * CHUNK)
            total = stats[1:2, lanes]
            level = stats[0:1, lanes] + jnp.log(total) * LOG2E
            p = jnp.exp2(s * factor - level)
            p_buf[:, part] = p.astype(BF16)
            ds = (p * (dp - stats[2:3, lanes] / total)).astype(BF16)
            ds_ref[:, lanes] = ds
        ds = ds_ref[:, pl.ds(pl.multiple_of(i * pair, CHUNK), pair)]
        dk[...] += jnp.dot(ds, q, preferred_element_type=F32)
        dv[...] += jnp.dot(p_buf[...], do, preferred_element_type=F32)
        return carry

    lax.fori_loop(0, q_ref.shape[1] // (2 * hd), heads, 0, unroll=True)
    inverse = 1.0 / hd**0.5
    return dk[...] * inverse, dv[...]


def other_kernel(b, flags, stats, q_ref, do_ref, k_ref, v_ref, *refs):
    if b & (b - 1):
        both, ds_out, *refs = refs
        hd = both.shape[1] // 2
        dk_out, dv_out = both.at[:, pl.ds(0, hd)], both.at[:, pl.ds(hd, hd)]
    else:
        dk_out, dv_out, ds_out, *refs = refs
    *refs, p_buf, dk, dv = refs
    keep = counted(b, flags)
    rows = dk.shape[0]
    held, before = None, stats
    if refs:
        stats, *held = refs

    @pl.when(keep)
    def _():
        if held:
            stats_of_block(b, q_ref, do_ref, k_ref, v_ref, before, stats, held)
        dk_sum, dv_sum = block_gradients(False, stats, q_ref, do_ref, k_ref, v_ref, p_buf, ds_out, dk, dv, held)
        for out, total in ((dk_out, dk_sum), (dv_out, dv_sum)):
            out[:rows, :] = total.astype(BF16)
            if out.shape[0] > rows:
                out[rows:, :] = jnp.zeros((out.shape[0] - rows, total.shape[1]), BF16)

    @pl.when(jnp.logical_not(keep))
    def _():
        if held:
            stats[...] = before[...]
        dk_out[...] = jnp.zeros(dk_out.shape, BF16)
        dv_out[...] = jnp.zeros(dv_out.shape, BF16)
        ds_out[...] = jnp.zeros_like(ds_out)


def own_kernel(stats, q_ref, do_ref, k_ref, v_ref, out_ref, ds_out, p_buf, dk, dv):
    hd = dk.shape[1]
    dk_sum, dv_sum = block_gradients(True, stats, q_ref, do_ref, k_ref, v_ref, p_buf, ds_out, dk, dv)
    out_ref[:, :hd] = dk_sum
    out_ref[:, hd:] = dv_sum


def query_kernel(n, *refs):
    k_refs, ds_refs = refs[:n], refs[n : 2 * n]
    *done, dq_ref, mark_ref = refs[2 * n :]
    mark_ref[...] = jnp.zeros_like(mark_ref)
    rows, hd = k_refs[0].shape
    first = 0
    if done:
        first = done[0].shape[1] // hd
        dq_ref[:, : first * hd] = done[0][...]
    for h in range(first, dq_ref.shape[1] // hd):
        dq = 0.0
        for k, ds in zip(k_refs, ds_refs):
            part = ds[:, h * rows : (h + 1) * rows]
            dq = dq + lax.dot_general(part, k[...], TN, preferred_element_type=F32)
        dq_ref[:, h * hd : (h + 1) * hd] = (dq / hd**0.5).astype(BF16)


def merge_kernel(rows, at, own, *refs):
    *got, out_ref = refs
    total = own[:rows, :].astype(F32)
    for part in got:
        total = total + part[:rows, at : at + total.shape[1]].astype(F32)
    out_ref[:rows, :] = total.astype(BF16)
    if out_ref.shape[0] > rows:
        out_ref[rows:, :] = jnp.zeros((out_ref.shape[0] - rows, out_ref.shape[1]), BF16)


def merge(rows, at, own, got, after):
    outs = [shape(own.shape)]
    kernel = functools.partial(merge_kernel, rows, at)
    return whole_call(kernel, "merge", [], [own, *got], outs, 4, (0, 0), [], after)[0]


def attention(me, spans, queries, out_grad, keys, values, activations, mark, swap, n):
    rows, hd = keys.shape
    columns = queries.shape[1]
    tall = columns // hd * rows
    product = 2 * rows * tall * hd
    cost = (8 * product, 8 * rows * columns)

    direct = [b for b in range(1, n) if b & (b - 1) == 0]
    blocks = {b: [swap(keys, b), swap(values, b)] for b in reversed(direct)}
    stats_shape = shape((8, tall), F32)
    stats, queries, out_grad, keys, values, flags = whole_call(
        functools.partial(first_stats_kernel, n),
        "first_stats",
        [me, spans],
        [queries, out_grad, keys, values],
        [stats_shape] + [shape(x.shape) for x in (queries, out_grad, keys, values)] + [shape((8, 128), F32)],
        12,
        cost,
        [],
        [mark],
    )
    blocks[0] = [keys, values]
    acts = prepare(activations, [stats])
    for b in range(1, n):
        if b not in blocks:
            blocks[b] = [swap(x, b & -b) for x in blocks[b & (b - 1)]]
        if b == n - 1:
            break
        stats = whole_call(
            functools.partial(next_stats_kernel, b),
            "next_stats",
            [],
            [flags, queries, out_grad, *blocks[b], stats],
            [stats_shape],
            10,
            cost,
            [],
            [*blocks[2], acts] if b == 1 else [],
        )[0]
    p_buf = pltpu.VMEM((rows, 2 * rows), BF16)
    sums = [pltpu.VMEM((rows, hd), F32)] * 2
    far_parts, key_parts, value_parts = [[] for _ in range(n)], [], []
    score_grads, made, before = [None] * n, {}, []
    for b in range(n - 1, 0, -1):
        last = b == n - 1
        held = pltpu.VMEM((rows, tall), F32)
        longer = rows + TOP_ROWS
        outs = [shape((longer, 2 * hd))] if b & (b - 1) else [shape((rows, hd)), shape((longer, hd))]
        results = whole_call(
            functools.partial(other_kernel, b),
            "block_gradients",
            [],
            [flags, stats, queries, out_grad, *blocks[b]],
            outs + [shape((rows, tall))] + [stats_shape] * last,
            20 if last else 10,
            (0, 0),
            [held, held] * last + [p_buf, *sums],
            before,
        )
        made[b] = results[: len(outs)]
        score_grads[b] = results[len(outs)]
        if last:
            stats = results[-1]
        before = made[b][-1:]
    for b in range(n - 1, 0, -1):
        got, to = far_parts[b], b & (b - 1)
        if to:
            part = merge(rows, 0, made[b][0], got, before) if got else made[b][0]
            far_parts[to].append(swap(part, b & -b))
            continue
        dk, dv = made[b]
        if got:
            dv = merge(rows, hd, dv, got, before)
        value_parts.append(swap(dv, b))
        if got:
            dk = merge(rows, 0, dk, got, [dv])
        key_parts.append(swap(dk, b))
    own, score_grads[0] = whole_call(
        own_kernel,
        "own_gradients",
        [],
        [stats, queries, out_grad, keys, values],
        [shape((rows, 2 * hd), F32), shape((rows, tall))],
        10,
        (0, 0),
        [p_buf, *sums],
        before,
    )
    return own, key_parts, value_parts, [blocks[b][0] for b in range(n)], score_grads, acts


def query_gradients(key_blocks, score_grads, done, columns, after):
    n = len(key_blocks)
    rows = key_blocks[0].shape[0]
    return whole_call(
        functools.partial(query_kernel, n),
        "query_gradients",
        [],
        [*key_blocks, *score_grads, *done],
        [shape((rows, columns)), shape((8, 128), F32)],
        2 + 3 * n,
        (0, 0),
        [],
        after,
    )


def pack_top(top):
    high = jnp.minimum(top, BF16_MAX).astype(BF16).astype(F32)
    rest = top - high
    middle = rest.astype(BF16).astype(F32)
    low = rest - middle
    return (high + pltpu.roll(middle, PACK_LANES, 1) + pltpu.roll(low, 2 * PACK_LANES, 1)).astype(BF16)


def unpack_top(ref, at):
    x = ref[at : at + TOP_ROWS, :TOP_LANES].astype(F32)
    total = x + (pltpu.roll(x, TOP_LANES - PACK_LANES, 1) + pltpu.roll(x, TOP_LANES - 2 * PACK_LANES, 1))
    lane = lax.broadcasted_iota(jnp.int32, x.shape, 1)
    return jnp.where(lane < PACK_LANES, total, 0.0)


def tile_of(step, me_dp, bits, flip):
    mask = flip
    for j in range(1, bits):
        if not (step >> (bits - 1 - j)) & 1:
            mask |= 1 << j
    return me_dp ^ mask


def reversed_step(step, bits):
    return sum(((step >> (bits - 1 - j)) & 1) << (j - 1) for j in range(1, bits))


def corrected_tile(at, dest, grads, a_ref, e_ref, top_ref):
    _, n_ctx, rows_ctx, rows = a_ref.shape
    tall = n_ctx * rows_ctx
    hd = grads.shape[1]
    a = a_ref[dest].reshape(tall, rows)
    e = e_ref[dest, :, :, at : at + hd].reshape(tall, hd)
    c = jnp.dot(a, grads, preferred_element_type=F32) + e
    mags = jnp.max(jnp.abs(c).reshape(tall // QROWS, QROWS, hd), axis=1)
    mags = jnp.max(mags, axis=1, keepdims=True)
    block = lax.broadcasted_iota(jnp.int32, (tall // QROWS, TOP_LANES), 0)
    lane = lax.broadcasted_iota(jnp.int32, (tall // QROWS, TOP_LANES), 1)
    top = jnp.max(jnp.where(lane == block, mags, 0.0), axis=0, keepdims=True)
    top_ref[pl.ds(dest, 1), :] = jnp.maximum(top_ref[pl.ds(dest, 1), :], top)
    return c


def summed_grads(at, own_ref, part_refs):
    rows, hd = own_ref.shape[0], own_ref.shape[1] // 2
    total = own_ref[:, at : at + hd]
    for part in part_refs:
        total = total + part[:rows, :].astype(F32)
    return total.astype(BF16)


def kept_rows(bits, shrink, at, me_ref, total, a_ref, e_ref, out_ref, top_ref):
    for step in range(out_ref.shape[0]):
        dest = tile_of(step, me_ref[0], bits, 0)
        out_ref[step] = corrected_tile(at, dest, total, a_ref, e_ref, top_ref) * shrink


def send_kernel(bits, shrink, at, n_parts, me_ref, own_ref, *refs):
    *before, a_ref, e_ref, out_ref, top_ref, grads_ref, grads_out = refs[n_parts:]
    total = summed_grads(at, own_ref, refs[:n_parts])
    grads_ref[...] = total
    grads_out[...] = total
    top_ref[...] = before[0][...] if before else jnp.zeros_like(top_ref)
    steps = a_ref.shape[0] // 2
    tall = a_ref.shape[1] * a_ref.shape[2]
    for step in range(steps):
        dest = tile_of(step, me_ref[0], bits, 1)
        c = corrected_tile(at, dest, total, a_ref, e_ref, top_ref)
        out_ref[step * tall : (step + 1) * tall, :] = (c * shrink).astype(BF16)
    if out_ref.shape[0] > steps * tall:
        out_ref[steps * tall :, :] = jnp.zeros((out_ref.shape[0] - steps * tall, out_ref.shape[1]), BF16)


def kept_kernel(bits, shrink, at, me_ref, grads_ref, before_ref, a_ref, e_ref, out_ref, top_ref):
    top_ref[...] = before_ref[...]
    kept_rows(bits, shrink, at, me_ref, grads_ref[...], a_ref, e_ref, out_ref, top_ref)


def split_kernel(bits, n_ctx, n_tops, kept, got, *refs):
    steps, tall, hd = kept.shape
    half = steps // 2
    part_tall = tall // 2
    tops = refs[:n_tops]
    low_away, low_stay, high_away, high_stay, *top_out = refs[n_tops:]
    for step in range(steps):
        c = (kept[step] + got[step * tall : (step + 1) * tall, :].astype(F32)).astype(BF16)
        c = c.reshape(n_ctx, 2, part_tall // n_ctx, hd)
        back = reversed_step(step, bits)
        for at, i, away, stay in ((step, 0, low_away, low_stay), (back, 1, high_away, high_stay)):
            part = c[:, i].reshape(part_tall, hd)
            if at < half:
                away[at * part_tall : (at + 1) * part_tall, :] = part
            else:
                stay[(at - half) * part_tall : (at - half + 1) * part_tall, :] = part
    if tops:
        top = largest(tops, got, steps * tall)
        top_out[0][...] = top
        low_away[half * part_tall :, :] = pack_top(top)
    else:
        tail = jnp.zeros((low_away.shape[0] - half * part_tall, hd), BF16)
        low_away[half * part_tall :, :] = tail
        high_away[half * part_tall :, :] = tail


def largest(tops, low_got, size):
    found = [top[...] for top in tops]
    if low_got.shape[0] > size:
        found.append(unpack_top(low_got, size))
    return functools.reduce(jnp.maximum, found)


def add_kernel(n_tops, low, low_got, high, high_got, *refs):
    tops = refs[:n_tops]
    low_away, low_stay, high_away, high_stay, *top_out = refs[n_tops:]
    size = low.shape[0]
    half = size // 2
    for mine, got, away, stay in ((low, low_got, low_away, low_stay), (high, high_got, high_away, high_stay)):
        away[:half, :] = (mine[:half, :].astype(F32) + got[:half, :].astype(F32)).astype(BF16)
        stay[...] = (mine[half:, :].astype(F32) + got[half:size, :].astype(F32)).astype(BF16)
    if tops:
        top = largest(tops, low_got, size)
        top_out[0][...] = top
        low_away[half:, :] = pack_top(top)
    else:
        low_away[half:, :] = jnp.zeros((low_away.shape[0] - half, low_away.shape[1]), BF16)


def context_masks(n_ctx):
    bits = n_ctx.bit_length() - 1
    return [sum((1 << j) for j in range(bits) if not (step >> (bits - 1 - j)) & 1) for step in range(n_ctx)]


def last_kernel(n_ctx, n_tops, me_ref, low, low_got, high, high_got, *refs):
    tops = refs[:n_tops]
    away, stay, *top_out = refs[n_tops:]
    size, hd = low.shape
    rows_set = size // n_ctx
    half = n_ctx // 2
    for i, mask in enumerate(context_masks(n_ctx)):
        part = pl.ds(pl.multiple_of((me_ref[0] ^ mask) * rows_set, rows_set), rows_set)
        out, at = (away, i) if i < half else (stay, i - half)
        at = 2 * at * rows_set
        for mine, got in ((low, low_got), (high, high_got)):
            total = mine[part, :].astype(F32) + got[part, :].astype(F32)
            out[at : at + rows_set, :] = total.astype(BF16)
            at += rows_set
    if tops:
        top = largest(tops, low_got, size)
        top_out[0][...] = top
        away[half * 2 * rows_set :, :] = pack_top(top)
    else:
        away[half * 2 * rows_set :, :] = jnp.zeros((away.shape[0] - half * 2 * rows_set, hd), BF16)


def halve_kernel(n_tops, mine, got, *refs):
    tops = refs[:n_tops]
    away, stay, *top_out = refs[n_tops:]
    size = mine.shape[0]
    half = size // 2
    away[:half, :] = (mine[:half, :].astype(F32) + got[:half, :].astype(F32)).astype(BF16)
    stay[...] = (mine[half:, :].astype(F32) + got[half:size, :].astype(F32)).astype(stay.dtype)
    if tops:
        top = largest(tops, got, size)
        top_out[0][...] = top
        away[half:, :] = pack_top(top)
    else:
        away[half:, :] = jnp.zeros((away.shape[0] - half, away.shape[1]), BF16)


def final_kernel(columns, n_ctx, gain, me_dp_ref, me_ctx_ref, *refs):
    sets = len(columns)
    groups = [refs[2 * chosen : 2 * chosen + 2] for chosen in range(sets)]
    top_ref, out_ref, scale_ref, all_tops = refs[2 * sets :]
    rows_ctx, hd = groups[0][0].shape
    scale = jnp.maximum(top_ref[...], unpack_top(groups[0][1], rows_ctx)) + 1e-06
    all_tops[...] = scale
    blocks = rows_ctx // QROWS
    lanes = n_ctx * blocks
    per_row = TOP_LANES // lanes
    lane = lax.broadcasted_iota(jnp.int32, scale.shape, 1)
    group = jnp.where(lane < lanes, scale, 0.0)
    moved = [group] + [pltpu.roll(group, k * lanes, 1) for k in range(1, per_row)]
    for r in range(scale_ref.shape[0]):
        row = [moved[k][r * per_row + k : r * per_row + k + 1, :] for k in range(per_row)]
        scale_ref[r : r + 1, :] = functools.reduce(jnp.add, row)
    factors = gain / all_tops[pl.ds(me_dp_ref[0], 1), :]
    lane = lax.broadcasted_iota(jnp.int32, factors.shape, 1)
    for r in range(blocks):
        mine = jnp.where(lane == me_ctx_ref[0] * blocks + r, factors, 0.0)
        factor = jnp.sum(mine, axis=1, keepdims=True)
        part = slice(r * QROWS, (r + 1) * QROWS)
        for at, (mine_ref, got_ref) in zip(columns, groups):
            out_ref[part, at : at + hd] = (mine_ref[part, :] + got_ref[part, :].astype(F32)) * factor


def local(n_dp, n_ctx, span_order, queries, keys, values, out_grad, activations, error_feedback):
    rows, hd = keys.shape
    width = 2 * hd
    model = activations.shape[1]
    rows_ctx = model // (n_dp * n_ctx)
    tall = n_ctx * rows_ctx
    me_dp = lax.axis_index("dp").astype(jnp.int32)[None]
    me_ctx = lax.axis_index("context").astype(jnp.int32)[None]
    bits = n_dp.bit_length() - 1

    def swap_dp(x, mask):
        return lax.ppermute(x, "dp", xor_perm(n_dp, mask))

    def swap_ctx(x, mask):
        return lax.ppermute(x, "context", xor_perm(n_ctx, mask))

    own, key_parts, value_parts, key_blocks, score_grads, acts = attention(
        me_ctx, span_order[0], queries, out_grad, keys, values, activations, begin(me_dp, me_ctx), swap_ctx, n_ctx
    )

    shrink = 1.0 / (n_dp * n_ctx)
    acts = acts.reshape(n_dp, n_ctx, rows_ctx, rows)
    errors = error_feedback.reshape(n_dp, n_ctx, rows_ctx, width)
    tops = shape((TOP_ROWS, TOP_LANES), F32)
    steps = n_dp // 2
    cost = (0, 0)
    kept_shape, grad_shape = shape((steps, tall, hd), F32), shape((rows, hd))

    def tiles(kernel, name, operands, outs, after=()):
        return whole_call(kernel, name, [me_dp], [*operands, acts, errors], outs, 18, cost, [], after)

    sets = 2
    half = steps // 2 * (tall // 2)

    def split(last, kept, got, top):
        return whole_call(
            functools.partial(split_kernel, bits, n_ctx, len(top)),
            "split_tiles",
            [],
            [kept, got, *top],
            [
                shape((half + (1 if last else 2) * TOP_ROWS, hd)),
                shape((half, hd)),
                shape((half + (0 if last else 2) * TOP_ROWS, hd)),
                shape((half, hd)),
            ]
            + [tops] * last,
            10,
            cost,
        )

    out, top, grads, value_grad = tiles(
        functools.partial(send_kernel, bits, shrink, hd, len(value_parts)),
        "send_tiles",
        [own, *value_parts],
        [shape((steps * tall + 2 * TOP_ROWS, hd)), tops, grad_shape, grad_shape],
    )
    got = swap_dp(out, 1)
    kept, top = tiles(
        functools.partial(kept_kernel, bits, shrink, hd), "kept_tiles", [grads, top], [kept_shape, tops]
    )
    out, top, grads, key_grad = tiles(
        functools.partial(send_kernel, bits, shrink, 0, len(key_parts)),
        "send_tiles",
        [own, *key_parts, top],
        [shape((steps * tall, hd)), tops, grad_shape, grad_shape],
    )
    halves = [split(False, kept, got, [])]
    got = swap_dp(out, 1)
    kept, top = tiles(
        functools.partial(kept_kernel, bits, shrink, 0),
        "kept_tiles",
        [grads, top],
        [kept_shape, tops],
        halves[0][1:2],
    )
    arrays = split(True, kept, got, [top, swap_dp(top, 1)])
    halves.append(arrays[:4])
    gathered = [arrays[4]]
    query_half, mark = query_gradients(key_blocks, score_grads, [], queries.shape[1] // 2, [arrays[1]])
    groups = []
    for chosen in range(sets):
        low_away, low, high_away, high = halves[chosen]
        extra = TOP_ROWS if chosen == sets - 1 else 0
        tail = extra or 2 * TOP_ROWS
        for stage in range(1, bits):
            low_got = swap_dp(low_away, 1 << stage)
            high_got = swap_dp(high_away, 1 << (bits - stage))
            with_tops = extra > 0
            operands = [low, low_got, high, high_got] + (gathered if with_tops else [])
            n_tops = len(operands) - 4
            size = low.shape[0]
            if stage < bits - 1:
                low_away, low, high_away, high, *top_out = whole_call(
                    functools.partial(add_kernel, n_tops),
                    "add_stage",
                    [],
                    operands,
                    [shape((size // 2 + tail, hd))] + [shape((size // 2, hd))] * 3 + [tops] * with_tops,
                    8,
                    cost,
                    after=[mark] if stage == 1 else [],
                )
                if chosen == 0 and stage == 1:
                    query_grad, mark = query_gradients(
                        key_blocks, score_grads, [query_half], queries.shape[1], [low]
                    )
            else:
                chunk = rows_ctx
                away, stay, *top_out = whole_call(
                    functools.partial(last_kernel, n_ctx, n_tops),
                    "last_stage",
                    [me_ctx],
                    operands,
                    [shape((n_ctx // 2 * chunk + tail, hd)), shape((n_ctx // 2 * chunk, hd))] + [tops] * with_tops,
                    8,
                    cost,
                )
            if with_tops:
                gathered = list(top_out)
        mask = 1
        while mask < n_ctx // 2:
            size = stay.shape[0]
            away, stay, *top_out = whole_call(
                functools.partial(halve_kernel, int(with_tops)),
                "halve_context",
                [],
                [stay, swap_ctx(away, mask)] + (gathered if with_tops else []),
                [shape((size // 2 + tail, hd)), shape((size // 2, hd), F32 if size == 2 * chunk else BF16)]
                + [tops] * with_tops,
                8,
                (0, 0),
            )
            if with_tops:
                gathered = list(top_out)
            mask *= 2
        groups = [stay, swap_ctx(away, mask), *groups]
    payload, scale = whole_call(
        functools.partial(final_kernel, (0, hd), n_ctx, 7.0 / shrink),
        "final_stage",
        [me_dp, me_ctx],
        groups + gathered,
        [shape((rows_ctx, width), F32), shape((model // QROWS // TOP_LANES, TOP_LANES), F32)],
        8,
        (0, 0),
        [pltpu.VMEM((TOP_ROWS, TOP_LANES), F32)],
    )
    return query_grad, key_grad, value_grad, payload, scale.reshape(-1)


def solution(mesh):
    tokens = P(("dp", "context"), None)
    return jax.shard_map(
        functools.partial(local, mesh.shape["dp"], mesh.shape["context"]),
        mesh=mesh,
        in_specs=(P("dp", None), tokens, tokens, tokens, tokens, tokens, P("dp", "context", None, None)),
        out_specs=(tokens, tokens, tokens, tokens, P()),
        check_vma=False,
    )
```

```python
import functools

import jax
import jax.numpy as jnp
from jax import lax
from jax.experimental import pallas as pl
from jax.experimental.pallas import tpu as pltpu
from jax.sharding import PartitionSpec as P

QROWS = 32
LOG2E = 1.4426950408889634
FAR = 1e30
MIB = 1024 * 1024
CHUNK = 256
TOP_ROWS, TOP_LANES, PACK_LANES = 16, 128, 32
BF16, F32 = jnp.bfloat16, jnp.float32
BF16_MAX = float(jnp.finfo(jnp.bfloat16).max)
NT = (((1,), (1,)), ((), ()))
TN = (((0,), (0,)), ((), ()))


def xor_perm(size, mask):
    return [(i, i ^ mask) for i in range(size)]


def whole(x):
    return pl.BlockSpec(x.shape, lambda *_: (0,) * len(x.shape))


def shape(dims, dtype=BF16):
    return jax.ShapeDtypeStruct(dims, dtype)


def whole_call(kernel, name, scalars, operands, out_shape, mib, cost, scratch=(), after=()):
    def body(*refs):
        first = len(scalars) + len(operands)
        kernel(*refs[:first], *refs[first + len(after) :])

    return pl.pallas_call(
        body,
        grid_spec=pltpu.PrefetchScalarGridSpec(
            num_scalar_prefetch=len(scalars),
            grid=(1,),
            in_specs=[whole(x) for x in operands] + [pl.BlockSpec(memory_space=pl.ANY)] * len(after),
            out_specs=[whole(x) for x in out_shape],
            scratch_shapes=list(scratch),
        ),
        out_shape=out_shape,
        compiler_params=pltpu.CompilerParams(vmem_limit_bytes=mib * MIB),
        cost_estimate=pl.CostEstimate(flops=cost[0], bytes_accessed=cost[1], transcendentals=0),
        name=name,
    )(*scalars, *operands, *after)


def begin_kernel(me_dp_ref, me_ctx_ref, out_ref):
    out_ref[...] = jnp.zeros_like(out_ref)


def begin(me_dp, me_ctx):
    mark = [shape((8, 128), F32)]
    return whole_call(begin_kernel, "begin", [me_dp, me_ctx], [], mark, 4, (20_000_000_000, 0))[0]


def prepare_kernel(pieces, a_ref, a_out):
    tile = a_ref.shape[1] // pieces
    for i in range(pieces):
        a_out[i * tile : (i + 1) * tile, :] = a_ref[:, i * tile : (i + 1) * tile].T


def prepare(activations, after):
    rows, model = activations.shape
    outs = [shape((model, rows))]
    cost = (0, 0)
    kernel = functools.partial(prepare_kernel, 8)
    return whole_call(kernel, "prepare", [], [activations], outs, 16, cost, [], after)[0]


def head_pair(ref, i, hd):
    at = i * (2 * hd)
    first = ref[:, pl.ds(pl.multiple_of(at, hd), hd)]
    second = ref[:, pl.ds(pl.multiple_of(at + hd, hd), hd)]
    return jnp.concatenate([first, second], axis=0)


def score_chunk(k, v, q, do, own, first_lane):
    s = lax.dot_general(k, q, NT, preferred_element_type=F32)
    dp = lax.dot_general(v, do, NT, preferred_element_type=F32)
    if own:
        rows = k.shape[0]
        key_at = lax.broadcasted_iota(jnp.int32, s.shape, 0)
        query_at = lax.broadcasted_iota(jnp.int32, s.shape, 1) + first_lane
        query_at = jnp.where(query_at >= rows, query_at - rows, query_at)
        s = jnp.where(key_at <= query_at, s, -FAR)
    return s, dp


def counted(b, flags):
    lane = lax.broadcasted_iota(jnp.int32, flags.shape, 1)
    return jnp.max(jnp.where(lane == b, flags[...], 0.0)) > 0.5


def stats_of_block(b, q_ref, do_ref, k_ref, v_ref, before, out, held=None):
    k, v = k_ref[...], v_ref[...]
    rows, hd = k.shape
    pair = 2 * rows
    factor = LOG2E / hd**0.5

    def heads(i, carry):
        q, do = head_pair(q_ref, i, hd), head_pair(do_ref, i, hd)
        for t in range(pair // CHUNK):
            part = slice(t * CHUNK, (t + 1) * CHUNK)
            lanes = pl.ds(pl.multiple_of(i * pair + t * CHUNK, CHUNK), CHUNK)
            s, dp = score_chunk(k, v, q[part], do[part], b == 0, t * CHUNK)
            if held:
                held[0][:, lanes] = s
                held[1][:, lanes] = dp
            top = jnp.max(s, axis=0, keepdims=True) * factor
            e = jnp.exp2(s * factor - top)
            total = jnp.sum(e, axis=0, keepdims=True)
            weighted = jnp.sum(e * dp, axis=0, keepdims=True)
            if b > 0:
                old = before[0:1, lanes]
                both = jnp.maximum(old, top)
                old_part, new_part = jnp.exp2(old - both), jnp.exp2(top - both)
                total = before[1:2, lanes] * old_part + total * new_part
                weighted = before[2:3, lanes] * old_part + weighted * new_part
                top = both
            out[0:1, lanes] = top
            out[1:2, lanes] = total
            out[2:3, lanes] = weighted
        return carry

    lax.fori_loop(0, q_ref.shape[1] // (2 * hd), heads, 0, unroll=True)


def first_stats_kernel(n, me_ref, span_ref, q_ref, do_ref, k_ref, v_ref, out, q_out, do_out, k_out, v_out, flags):
    me = me_ref[0]
    lane = lax.broadcasted_iota(jnp.int32, flags.shape, 1)
    found = jnp.zeros(flags.shape, F32)
    for b in range(1, n):
        found = jnp.where((lane == b) & (span_ref[me ^ b] < span_ref[me]), 1.0, found)
    flags[...] = found
    q_out[...] = q_ref[...]
    do_out[...] = do_ref[...]
    k_out[...] = k_ref[...]
    v_out[...] = v_ref[...]
    stats_of_block(0, q_ref, do_ref, k_ref, v_ref, None, out)


def next_stats_kernel(b, flags, q_ref, do_ref, k_ref, v_ref, before, out):
    keep = counted(b, flags)

    @pl.when(keep)
    def _():
        stats_of_block(b, q_ref, do_ref, k_ref, v_ref, before, out)

    @pl.when(jnp.logical_not(keep))
    def _():
        out[...] = before[...]


def block_gradients(own, stats, q_ref, do_ref, k_ref, v_ref, p_buf, ds_ref, dk, dv, held=None):
    k, v = k_ref[...], v_ref[...]
    rows, hd = k.shape
    pair = 2 * rows
    factor = LOG2E / hd**0.5
    dk[...] = jnp.zeros_like(dk)
    dv[...] = jnp.zeros_like(dv)

    def heads(i, carry):
        q, do = head_pair(q_ref, i, hd), head_pair(do_ref, i, hd)
        for t in range(pair // CHUNK):
            part = slice(t * CHUNK, (t + 1) * CHUNK)
            lanes = pl.ds(pl.multiple_of(i * pair + t * CHUNK, CHUNK), CHUNK)
            if held:
                s, dp = held[0][:, lanes], held[1][:, lanes]
            else:
                s, dp = score_chunk(k, v, q[part], do[part], own, t * CHUNK)
            total = stats[1:2, lanes]
            level = stats[0:1, lanes] + jnp.log(total) * LOG2E
            p = jnp.exp2(s * factor - level)
            p_buf[:, part] = p.astype(BF16)
            ds = (p * (dp - stats[2:3, lanes] / total)).astype(BF16)
            ds_ref[:, lanes] = ds
        ds = ds_ref[:, pl.ds(pl.multiple_of(i * pair, CHUNK), pair)]
        dk[...] += jnp.dot(ds, q, preferred_element_type=F32)
        dv[...] += jnp.dot(p_buf[...], do, preferred_element_type=F32)
        return carry

    lax.fori_loop(0, q_ref.shape[1] // (2 * hd), heads, 0, unroll=True)
    inverse = 1.0 / hd**0.5
    return dk[...] * inverse, dv[...]


def other_kernel(b, flags, stats, q_ref, do_ref, k_ref, v_ref, *refs):
    if b & (b - 1):
        both, ds_out, *refs = refs
        hd = both.shape[1] // 2
        dk_out, dv_out = both.at[:, pl.ds(0, hd)], both.at[:, pl.ds(hd, hd)]
    else:
        dk_out, dv_out, ds_out, *refs = refs
    *refs, p_buf, dk, dv = refs
    keep = counted(b, flags)
    rows = dk.shape[0]
    held, before = None, stats
    if refs:
        stats, *held = refs

    @pl.when(keep)
    def _():
        if held:
            stats_of_block(b, q_ref, do_ref, k_ref, v_ref, before, stats, held)
        dk_sum, dv_sum = block_gradients(False, stats, q_ref, do_ref, k_ref, v_ref, p_buf, ds_out, dk, dv, held)
        for out, total in ((dk_out, dk_sum), (dv_out, dv_sum)):
            out[:rows, :] = total.astype(BF16)
            if out.shape[0] > rows:
                out[rows:, :] = jnp.zeros((out.shape[0] - rows, total.shape[1]), BF16)

    @pl.when(jnp.logical_not(keep))
    def _():
        if held:
            stats[...] = before[...]
        dk_out[...] = jnp.zeros(dk_out.shape, BF16)
        dv_out[...] = jnp.zeros(dv_out.shape, BF16)
        ds_out[...] = jnp.zeros_like(ds_out)


def own_kernel(stats, q_ref, do_ref, k_ref, v_ref, out_ref, ds_out, p_buf, dk, dv):
    hd = dk.shape[1]
    dk_sum, dv_sum = block_gradients(True, stats, q_ref, do_ref, k_ref, v_ref, p_buf, ds_out, dk, dv)
    out_ref[:, :hd] = dk_sum
    out_ref[:, hd:] = dv_sum


def query_kernel(n, *refs):
    k_refs, ds_refs = refs[:n], refs[n : 2 * n]
    *done, dq_ref, mark_ref = refs[2 * n :]
    mark_ref[...] = jnp.zeros_like(mark_ref)
    rows, hd = k_refs[0].shape
    first = 0
    if done:
        first = done[0].shape[1] // hd
        dq_ref[:, : first * hd] = done[0][...]
    for h in range(first, dq_ref.shape[1] // hd):
        dq = 0.0
        for k, ds in zip(k_refs, ds_refs):
            part = ds[:, h * rows : (h + 1) * rows]
            dq = dq + lax.dot_general(part, k[...], TN, preferred_element_type=F32)
        dq_ref[:, h * hd : (h + 1) * hd] = (dq / hd**0.5).astype(BF16)


def merge_kernel(rows, at, own, *refs):
    *got, out_ref = refs
    total = own[:rows, :].astype(F32)
    for part in got:
        total = total + part[:rows, at : at + total.shape[1]].astype(F32)
    out_ref[:rows, :] = total.astype(BF16)
    if out_ref.shape[0] > rows:
        out_ref[rows:, :] = jnp.zeros((out_ref.shape[0] - rows, out_ref.shape[1]), BF16)


def merge(rows, at, own, got, after):
    outs = [shape(own.shape)]
    kernel = functools.partial(merge_kernel, rows, at)
    return whole_call(kernel, "merge", [], [own, *got], outs, 4, (0, 0), [], after)[0]


def attention(me, spans, queries, out_grad, keys, values, activations, mark, swap, n):
    rows, hd = keys.shape
    columns = queries.shape[1]
    tall = columns // hd * rows
    product = 2 * rows * tall * hd
    cost = (8 * product, 8 * rows * columns)

    direct = [b for b in range(1, n) if b & (b - 1) == 0]
    blocks = {b: [swap(keys, b), swap(values, b)] for b in reversed(direct)}
    stats_shape = shape((8, tall), F32)
    stats, queries, out_grad, keys, values, flags = whole_call(
        functools.partial(first_stats_kernel, n),
        "first_stats",
        [me, spans],
        [queries, out_grad, keys, values],
        [stats_shape] + [shape(x.shape) for x in (queries, out_grad, keys, values)] + [shape((8, 128), F32)],
        12,
        cost,
        [],
        [mark],
    )
    blocks[0] = [keys, values]
    acts = prepare(activations, [stats])
    for b in range(1, n):
        if b not in blocks:
            blocks[b] = [swap(x, b & -b) for x in blocks[b & (b - 1)]]
        if b == n - 1:
            break
        stats = whole_call(
            functools.partial(next_stats_kernel, b),
            "next_stats",
            [],
            [flags, queries, out_grad, *blocks[b], stats],
            [stats_shape],
            10,
            cost,
            [],
            [*blocks[2], acts] if b == 1 else [],
        )[0]
    p_buf = pltpu.VMEM((rows, 2 * rows), BF16)
    sums = [pltpu.VMEM((rows, hd), F32)] * 2
    far_parts, key_parts, value_parts = [[] for _ in range(n)], [], []
    score_grads, made, before = [None] * n, {}, []
    for b in range(n - 1, 0, -1):
        last = b == n - 1
        held = pltpu.VMEM((rows, tall), F32)
        longer = rows + TOP_ROWS
        outs = [shape((longer, 2 * hd))] if b & (b - 1) else [shape((rows, hd)), shape((longer, hd))]
        results = whole_call(
            functools.partial(other_kernel, b),
            "block_gradients",
            [],
            [flags, stats, queries, out_grad, *blocks[b]],
            outs + [shape((rows, tall))] + [stats_shape] * last,
            20 if last else 10,
            (0, 0),
            [held, held] * last + [p_buf, *sums],
            before,
        )
        made[b] = results[: len(outs)]
        score_grads[b] = results[len(outs)]
        if last:
            stats = results[-1]
        before = made[b][-1:]
        got, to = far_parts[b], b & (b - 1)
        if to:
            part = merge(rows, 0, made[b][0], got, before) if got else made[b][0]
            far_parts[to].append(swap(part, b & -b))
            continue
        dk, dv = made[b]
        if got:
            dv = merge(rows, hd, dv, got, before)
        value_parts.append(swap(dv, b))
        if got:
            dk = merge(rows, 0, dk, got, [dv])
        key_parts.append(swap(dk, b))
        before = [dv, dk]
    own, score_grads[0] = whole_call(
        own_kernel,
        "own_gradients",
        [],
        [stats, queries, out_grad, keys, values],
        [shape((rows, 2 * hd), F32), shape((rows, tall))],
        10,
        (0, 0),
        [p_buf, *sums],
        before,
    )
    return own, key_parts, value_parts, [blocks[b][0] for b in range(n)], score_grads, acts


def query_gradients(key_blocks, score_grads, done, columns, after):
    n = len(key_blocks)
    rows = key_blocks[0].shape[0]
    return whole_call(
        functools.partial(query_kernel, n),
        "query_gradients",
        [],
        [*key_blocks, *score_grads, *done],
        [shape((rows, columns)), shape((8, 128), F32)],
        2 + 3 * n,
        (0, 0),
        [],
        after,
    )


def pack_top(top):
    high = jnp.minimum(top, BF16_MAX).astype(BF16).astype(F32)
    rest = top - high
    middle = rest.astype(BF16).astype(F32)
    low = rest - middle
    return (high + pltpu.roll(middle, PACK_LANES, 1) + pltpu.roll(low, 2 * PACK_LANES, 1)).astype(BF16)


def unpack_top(ref, at):
    x = ref[at : at + TOP_ROWS, :TOP_LANES].astype(F32)
    total = x + (pltpu.roll(x, TOP_LANES - PACK_LANES, 1) + pltpu.roll(x, TOP_LANES - 2 * PACK_LANES, 1))
    lane = lax.broadcasted_iota(jnp.int32, x.shape, 1)
    return jnp.where(lane < PACK_LANES, total, 0.0)


def tile_of(step, me_dp, bits, flip):
    mask = flip
    for j in range(1, bits):
        if not (step >> (bits - 1 - j)) & 1:
            mask |= 1 << j
    return me_dp ^ mask


def reversed_step(step, bits):
    return sum(((step >> (bits - 1 - j)) & 1) << (j - 1) for j in range(1, bits))


def corrected_tile(at, dest, grads, a_ref, e_ref, top_ref):
    _, n_ctx, rows_ctx, rows = a_ref.shape
    tall = n_ctx * rows_ctx
    hd = grads.shape[1]
    a = a_ref[dest].reshape(tall, rows)
    e = e_ref[dest, :, :, at : at + hd].reshape(tall, hd)
    c = jnp.dot(a, grads, preferred_element_type=F32) + e
    mags = jnp.max(jnp.abs(c).reshape(tall // QROWS, QROWS, hd), axis=1)
    mags = jnp.max(mags, axis=1, keepdims=True)
    block = lax.broadcasted_iota(jnp.int32, (tall // QROWS, TOP_LANES), 0)
    lane = lax.broadcasted_iota(jnp.int32, (tall // QROWS, TOP_LANES), 1)
    top = jnp.max(jnp.where(lane == block, mags, 0.0), axis=0, keepdims=True)
    top_ref[pl.ds(dest, 1), :] = jnp.maximum(top_ref[pl.ds(dest, 1), :], top)
    return c


def summed_grads(at, own_ref, part_refs):
    rows, hd = own_ref.shape[0], own_ref.shape[1] // 2
    total = own_ref[:, at : at + hd]
    for part in part_refs:
        total = total + part[:rows, :].astype(F32)
    return total.astype(BF16)


def kept_rows(bits, shrink, at, me_ref, total, a_ref, e_ref, out_ref, top_ref):
    for step in range(out_ref.shape[0]):
        dest = tile_of(step, me_ref[0], bits, 0)
        out_ref[step] = corrected_tile(at, dest, total, a_ref, e_ref, top_ref) * shrink


def send_kernel(bits, shrink, at, n_parts, me_ref, own_ref, *refs):
    *before, a_ref, e_ref, out_ref, top_ref, grads_ref, grads_out = refs[n_parts:]
    total = summed_grads(at, own_ref, refs[:n_parts])
    grads_ref[...] = total
    grads_out[...] = total
    top_ref[...] = before[0][...] if before else jnp.zeros_like(top_ref)
    steps = a_ref.shape[0] // 2
    tall = a_ref.shape[1] * a_ref.shape[2]
    for step in range(steps):
        dest = tile_of(step, me_ref[0], bits, 1)
        c = corrected_tile(at, dest, total, a_ref, e_ref, top_ref)
        out_ref[step * tall : (step + 1) * tall, :] = (c * shrink).astype(BF16)
    if out_ref.shape[0] > steps * tall:
        out_ref[steps * tall :, :] = jnp.zeros((out_ref.shape[0] - steps * tall, out_ref.shape[1]), BF16)


def kept_kernel(bits, shrink, at, me_ref, grads_ref, before_ref, a_ref, e_ref, out_ref, top_ref):
    top_ref[...] = before_ref[...]
    kept_rows(bits, shrink, at, me_ref, grads_ref[...], a_ref, e_ref, out_ref, top_ref)


def split_kernel(bits, n_ctx, n_tops, kept, got, *refs):
    steps, tall, hd = kept.shape
    half = steps // 2
    part_tall = tall // 2
    tops = refs[:n_tops]
    low_away, low_stay, high_away, high_stay, *top_out = refs[n_tops:]
    for step in range(steps):
        c = (kept[step] + got[step * tall : (step + 1) * tall, :].astype(F32)).astype(BF16)
        c = c.reshape(n_ctx, 2, part_tall // n_ctx, hd)
        back = reversed_step(step, bits)
        for at, i, away, stay in ((step, 0, low_away, low_stay), (back, 1, high_away, high_stay)):
            part = c[:, i].reshape(part_tall, hd)
            if at < half:
                away[at * part_tall : (at + 1) * part_tall, :] = part
            else:
                stay[(at - half) * part_tall : (at - half + 1) * part_tall, :] = part
    if tops:
        top = largest(tops, got, steps * tall)
        top_out[0][...] = top
        low_away[half * part_tall :, :] = pack_top(top)
    else:
        tail = jnp.zeros((low_away.shape[0] - half * part_tall, hd), BF16)
        low_away[half * part_tall :, :] = tail
        high_away[half * part_tall :, :] = tail


def largest(tops, low_got, size):
    found = [top[...] for top in tops]
    if low_got.shape[0] > size:
        found.append(unpack_top(low_got, size))
    return functools.reduce(jnp.maximum, found)


def add_kernel(n_tops, low, low_got, high, high_got, *refs):
    tops = refs[:n_tops]
    low_away, low_stay, high_away, high_stay, *top_out = refs[n_tops:]
    size = low.shape[0]
    half = size // 2
    for mine, got, away, stay in ((low, low_got, low_away, low_stay), (high, high_got, high_away, high_stay)):
        away[:half, :] = (mine[:half, :].astype(F32) + got[:half, :].astype(F32)).astype(BF16)
        stay[...] = (mine[half:, :].astype(F32) + got[half:size, :].astype(F32)).astype(BF16)
    if tops:
        top = largest(tops, low_got, size)
        top_out[0][...] = top
        low_away[half:, :] = pack_top(top)
    else:
        low_away[half:, :] = jnp.zeros((low_away.shape[0] - half, low_away.shape[1]), BF16)


def context_masks(n_ctx):
    bits = n_ctx.bit_length() - 1
    return [sum((1 << j) for j in range(bits) if not (step >> (bits - 1 - j)) & 1) for step in range(n_ctx)]


def last_kernel(n_ctx, n_tops, me_ref, low, low_got, high, high_got, *refs):
    tops = refs[:n_tops]
    away, stay, *top_out = refs[n_tops:]
    size, hd = low.shape
    rows_set = size // n_ctx
    half = n_ctx // 2
    for i, mask in enumerate(context_masks(n_ctx)):
        part = pl.ds(pl.multiple_of((me_ref[0] ^ mask) * rows_set, rows_set), rows_set)
        out, at = (away, i) if i < half else (stay, i - half)
        at = 2 * at * rows_set
        for mine, got in ((low, low_got), (high, high_got)):
            total = mine[part, :].astype(F32) + got[part, :].astype(F32)
            out[at : at + rows_set, :] = total.astype(BF16)
            at += rows_set
    if tops:
        top = largest(tops, low_got, size)
        top_out[0][...] = top
        away[half * 2 * rows_set :, :] = pack_top(top)
    else:
        away[half * 2 * rows_set :, :] = jnp.zeros((away.shape[0] - half * 2 * rows_set, hd), BF16)


def halve_kernel(n_tops, mine, got, *refs):
    tops = refs[:n_tops]
    away, stay, *top_out = refs[n_tops:]
    size = mine.shape[0]
    half = size // 2
    away[:half, :] = (mine[:half, :].astype(F32) + got[:half, :].astype(F32)).astype(BF16)
    stay[...] = (mine[half:, :].astype(F32) + got[half:size, :].astype(F32)).astype(stay.dtype)
    if tops:
        top = largest(tops, got, size)
        top_out[0][...] = top
        away[half:, :] = pack_top(top)
    else:
        away[half:, :] = jnp.zeros((away.shape[0] - half, away.shape[1]), BF16)


def final_kernel(columns, n_ctx, gain, me_dp_ref, me_ctx_ref, *refs):
    sets = len(columns)
    groups = [refs[2 * chosen : 2 * chosen + 2] for chosen in range(sets)]
    top_ref, out_ref, scale_ref, all_tops = refs[2 * sets :]
    rows_ctx, hd = groups[0][0].shape
    scale = jnp.maximum(top_ref[...], unpack_top(groups[0][1], rows_ctx)) + 1e-06
    all_tops[...] = scale
    blocks = rows_ctx // QROWS
    lanes = n_ctx * blocks
    per_row = TOP_LANES // lanes
    lane = lax.broadcasted_iota(jnp.int32, scale.shape, 1)
    group = jnp.where(lane < lanes, scale, 0.0)
    moved = [group] + [pltpu.roll(group, k * lanes, 1) for k in range(1, per_row)]
    for r in range(scale_ref.shape[0]):
        row = [moved[k][r * per_row + k : r * per_row + k + 1, :] for k in range(per_row)]
        scale_ref[r : r + 1, :] = functools.reduce(jnp.add, row)
    factors = gain / all_tops[pl.ds(me_dp_ref[0], 1), :]
    lane = lax.broadcasted_iota(jnp.int32, factors.shape, 1)
    for r in range(blocks):
        mine = jnp.where(lane == me_ctx_ref[0] * blocks + r, factors, 0.0)
        factor = jnp.sum(mine, axis=1, keepdims=True)
        part = slice(r * QROWS, (r + 1) * QROWS)
        for at, (mine_ref, got_ref) in zip(columns, groups):
            out_ref[part, at : at + hd] = (mine_ref[part, :] + got_ref[part, :].astype(F32)) * factor


def local(n_dp, n_ctx, span_order, queries, keys, values, out_grad, activations, error_feedback):
    rows, hd = keys.shape
    width = 2 * hd
    model = activations.shape[1]
    rows_ctx = model // (n_dp * n_ctx)
    tall = n_ctx * rows_ctx
    me_dp = lax.axis_index("dp").astype(jnp.int32)[None]
    me_ctx = lax.axis_index("context").astype(jnp.int32)[None]
    bits = n_dp.bit_length() - 1

    def swap_dp(x, mask):
        return lax.ppermute(x, "dp", xor_perm(n_dp, mask))

    def swap_ctx(x, mask):
        return lax.ppermute(x, "context", xor_perm(n_ctx, mask))

    own, key_parts, value_parts, key_blocks, score_grads, acts = attention(
        me_ctx, span_order[0], queries, out_grad, keys, values, activations, begin(me_dp, me_ctx), swap_ctx, n_ctx
    )

    shrink = 1.0 / (n_dp * n_ctx)
    acts = acts.reshape(n_dp, n_ctx, rows_ctx, rows)
    errors = error_feedback.reshape(n_dp, n_ctx, rows_ctx, width)
    tops = shape((TOP_ROWS, TOP_LANES), F32)
    steps = n_dp // 2
    cost = (0, 0)
    kept_shape, grad_shape = shape((steps, tall, hd), F32), shape((rows, hd))

    def tiles(kernel, name, operands, outs, after=()):
        return whole_call(kernel, name, [me_dp], [*operands, acts, errors], outs, 18, cost, [], after)

    sets = 2
    half = steps // 2 * (tall // 2)

    def split(last, kept, got, top):
        return whole_call(
            functools.partial(split_kernel, bits, n_ctx, len(top)),
            "split_tiles",
            [],
            [kept, got, *top],
            [
                shape((half + (1 if last else 2) * TOP_ROWS, hd)),
                shape((half, hd)),
                shape((half + (0 if last else 2) * TOP_ROWS, hd)),
                shape((half, hd)),
            ]
            + [tops] * last,
            10,
            cost,
        )

    out, top, grads, value_grad = tiles(
        functools.partial(send_kernel, bits, shrink, hd, len(value_parts)),
        "send_tiles",
        [own, *value_parts],
        [shape((steps * tall + 2 * TOP_ROWS, hd)), tops, grad_shape, grad_shape],
    )
    got = swap_dp(out, 1)
    kept, top = tiles(
        functools.partial(kept_kernel, bits, shrink, hd), "kept_tiles", [grads, top], [kept_shape, tops]
    )
    out, top, grads, key_grad = tiles(
        functools.partial(send_kernel, bits, shrink, 0, len(key_parts)),
        "send_tiles",
        [own, *key_parts, top],
        [shape((steps * tall, hd)), tops, grad_shape, grad_shape],
    )
    halves = [split(False, kept, got, [])]
    got = swap_dp(out, 1)
    kept, top = tiles(
        functools.partial(kept_kernel, bits, shrink, 0),
        "kept_tiles",
        [grads, top],
        [kept_shape, tops],
        halves[0][1:2],
    )
    arrays = split(True, kept, got, [top, swap_dp(top, 1)])
    halves.append(arrays[:4])
    gathered = [arrays[4]]
    query_half, mark = query_gradients(key_blocks, score_grads, [], queries.shape[1] // 2, [arrays[1]])
    groups = []
    for chosen in range(sets):
        low_away, low, high_away, high = halves[chosen]
        extra = TOP_ROWS if chosen == sets - 1 else 0
        tail = extra or 2 * TOP_ROWS
        for stage in range(1, bits):
            low_got = swap_dp(low_away, 1 << stage)
            high_got = swap_dp(high_away, 1 << (bits - stage))
            with_tops = extra > 0
            operands = [low, low_got, high, high_got] + (gathered if with_tops else [])
            n_tops = len(operands) - 4
            size = low.shape[0]
            if stage < bits - 1:
                low_away, low, high_away, high, *top_out = whole_call(
                    functools.partial(add_kernel, n_tops),
                    "add_stage",
                    [],
                    operands,
                    [shape((size // 2 + tail, hd))] + [shape((size // 2, hd))] * 3 + [tops] * with_tops,
                    8,
                    cost,
                    after=[mark] if stage == 1 else [],
                )
                if chosen == 0 and stage == 1:
                    query_grad, mark = query_gradients(
                        key_blocks, score_grads, [query_half], queries.shape[1], [low]
                    )
            else:
                chunk = rows_ctx
                away, stay, *top_out = whole_call(
                    functools.partial(last_kernel, n_ctx, n_tops),
                    "last_stage",
                    [me_ctx],
                    operands,
                    [shape((n_ctx // 2 * chunk + tail, hd)), shape((n_ctx // 2 * chunk, hd))] + [tops] * with_tops,
                    8,
                    cost,
                )
            if with_tops:
                gathered = list(top_out)
        mask = 1
        while mask < n_ctx // 2:
            size = stay.shape[0]
            away, stay, *top_out = whole_call(
                functools.partial(halve_kernel, int(with_tops)),
                "halve_context",
                [],
                [stay, swap_ctx(away, mask)] + (gathered if with_tops else []),
                [shape((size // 2 + tail, hd)), shape((size // 2, hd), F32 if size == 2 * chunk else BF16)]
                + [tops] * with_tops,
                8,
                (0, 0),
            )
            if with_tops:
                gathered = list(top_out)
            mask *= 2
        groups = [stay, swap_ctx(away, mask), *groups]
    payload, scale = whole_call(
        functools.partial(final_kernel, (0, hd), n_ctx, 7.0 / shrink),
        "final_stage",
        [me_dp, me_ctx],
        groups + gathered,
        [shape((rows_ctx, width), F32), shape((model // QROWS // TOP_LANES, TOP_LANES), F32)],
        8,
        (0, 0),
        [pltpu.VMEM((TOP_ROWS, TOP_LANES), F32)],
    )
    return query_grad, key_grad, value_grad, payload, scale.reshape(-1)


def solution(mesh):
    tokens = P(("dp", "context"), None)
    return jax.shard_map(
        functools.partial(local, mesh.shape["dp"], mesh.shape["context"]),
        mesh=mesh,
        in_specs=(P("dp", None), tokens, tokens, tokens, tokens, tokens, P("dp", "context", None, None)),
        out_specs=(tokens, tokens, tokens, tokens, P()),
        check_vma=False,
    )
```
